32 devices in a mesh: docs: 8 (over z, x), heads: 4 (over y, core).
Axes of the slice: x: 2, y: 2, z: 4, core: 2. Of those that a mesh axis runs over, the one named last changes fastest.
Arguments:
- enc_out: bfloat16 [768, 512, 768], P('docs', 'heads'), may hold values from -6 to 6
- enc_len: int32 [384], replicated, may hold values from 64 to 512
- group_docs: int32 [8], replicated, may hold values from 1 to 96, 384 in all
- list_len: int32 [24], replicated, may hold values from 1 to 50, 384 in all
- relevance: float32 [384], replicated, may hold values from 0.1 to 10
- start_token: bfloat16 [768], replicated, may hold values from -6 to 6
- score_row: bfloat16 [768], replicated, may hold values from -6 to 6
- g_self: float32 [768], replicated, may hold values from 0.1 to 1.9
- w_value_self: bfloat16 [768, 768], P(None, 'heads'), may hold values from -0.21875 to 0.21875
- w_out_self: bfloat16 [768, 768], P('heads'), may hold values from -0.21875 to 0.21875
- g_cross: float32 [768], replicated, may hold values from 0.1 to 1.9
- w_query: bfloat16 [768, 768], P(None, 'heads'), may hold values from -0.0546875 to 0.0546875
- w_key: bfloat16 [768, 768], P(None, 'heads'), may hold values from -0.21875 to 0.21875
- w_value: bfloat16 [768, 768], P(None, 'heads'), may hold values from -0.21875 to 0.21875
- w_out: bfloat16 [768, 768], P('heads'), may hold values from -1.25 to 1.25
- g_ff: float32 [768], replicated, may hold values from 0.1 to 1.9
- w_in: bfloat16 [768, 3072], P(None, 'heads'), may hold values from -0.21875 to 0.21875
- w_down: bfloat16 [3072, 768], P('heads'), may hold values from -0.109375 to 0.109375
- g_final: float32 [768], replicated, may hold values from 0.1 to 1.9
Outputs:
- scores: float32 [384], replicated
- loss: float32 [], replicated
- enc_grad: bfloat16 [768, 512, 768], P('docs', 'heads')
- start_grad: float32 [768], replicated
- score_row_grad: float32 [768], replicated
- g_self_grad: float32 [768], replicated
- w_value_self_grad: float32 [768, 768], P(None, 'heads')
- w_out_self_grad: float32 [768, 768], P('heads')
- g_cross_grad: float32 [768], replicated
- w_query_grad: float32 [768, 768], P(None, 'heads')
- key_weight_gradient: float32 [768, 768], P(None, 'heads')
- value_weight_gradient: float32 [768, 768], P(None, 'heads')
- w_out_grad: float32 [768, 768], P('heads')
- g_ff_grad: float32 [768], replicated
- w_in_grad: float32 [768, 3072], P(None, 'heads')
- w_down_grad: float32 [3072, 768], P('heads')
- g_final_grad: float32 [768], replicated
The draws below stay inside these ranges and needn't reach their ends.
Inputs may be any that keep to these rules, and one draw needn't show every extreme that they name: Group g holds documents S_g to S_g + group_docs[g] - 1 in its first slots, S_g the sum of group_docs over earlier groups; the counts total 384. Query j's list is the next list_len[j] documents after the earlier lists; the lengths total 384.
All inputs are finite; a program needn't handle non-finite values.
Results may differ from the reference program's by a relative error of at most 0.03.
Values may be sent and summed in bfloat16 or wider, within the bound.
No kernel may reach another device: no remote copies, remote signals or barrier semaphores. Data moves between devices by JAX's collectives and lax.ppermute only.
A program may use at most 256 MiB of HBM per device.

```python
import math
import jax
import jax.numpy as jnp
import numpy as np
from jax import lax

D = 768
HEADS = 12
HEAD_DIM = 64
FF = 3072
ENC = 512
LIST_MAX = 50
HOLD = 96
GROUPS = 8
DOCS = 384
QUERY_COUNT = 24


def draw_enc_len(key, part):
    key = jax.random.fold_in(key, 11)
    first, second = jax.random.split(key)
    lengths = jax.random.randint(first, (DOCS,), ENC // 8, ENC + 1, dtype=jnp.int32)
    spot = jax.random.randint(second, (), 0, DOCS, dtype=jnp.int32)
    return lengths.at[spot].set(ENC)


def levels(own_key, shape, pieces, least, largest):
    factor_of = 1.0
    for position, shards_of in pieces:
        draws = jax.random.uniform(jax.random.fold_in(jax.random.fold_in(own_key, 6), position), (shards_of,), jnp.float32, least / len(pieces), largest / len(pieces))
        factor_of = factor_of * jnp.repeat(jnp.exp(draws), shape[position] // shards_of).reshape((-1,) + (1,) * (len(shape) - 1 - position))
    return factor_of


def length_profile(count, total, reach, skew):
    portions = [(1 << 20) // math.isqrt(grade ** skew) + 1 for grade in range(2, count + 1)]
    rest, given = total - reach - (count - 1), [1] * (count - 1)
    while rest > 0:
        movable = [i for i in range(count - 1) if given[i] < reach]
        pool, remaining = sum([portions[i] for i in movable]), rest
        for i in movable:
            addition = min(reach - given[i], max(1, remaining * portions[i] // pool), rest)
            given[i] = given[i] + addition
            rest = rest - addition
    return np.array([reach] + given)


def ragged(stream_key, amount, total, limit, lean):
    if amount == 2:
        one = jax.random.randint(stream_key, (), max(1, total - limit), min(limit, total - 1) + 1)
        return jnp.stack([one, total - one])
    sizes = jnp.asarray(length_profile(amount, total, limit, lean), jnp.int32)
    pairs = (amount - 1) // 2
    source_of, taker = sizes[1:1 + 2 * pairs:2], sizes[2:2 + 2 * pairs:2]
    slack = jnp.minimum(source_of - 1, limit - taker)
    moved = jax.random.randint(jax.random.fold_in(stream_key, 1), (pairs,), 0, 1 << 20) % (slack + 1)
    sizes = sizes.at[1:1 + 2 * pairs:2].set(source_of - moved).at[2:2 + 2 * pairs:2].set(taker + moved)
    return sizes[jax.random.permutation(jax.random.fold_in(stream_key, 2), amount)]


def bell_draw(key, dims, width, reach, cuts=(), kind=jnp.bfloat16):
    factor_of = levels(key, dims, cuts, -0.22, 0.18) if cuts else 1.0
    array = jax.random.normal(key, dims, jnp.float32) * width * factor_of
    return jnp.minimum(jnp.maximum(array, -reach), reach).astype(kind)


def setup_inputs(seed: int = 0) -> dict:
    streams_of = jax.random.split(jax.random.key(seed), 20)
    enc_out = bell_draw(streams_of[0], (GROUPS * HOLD, ENC, D), 1.0, 6.0, ((0, 8), (1, 4)))
    enc_len = draw_enc_len(jax.random.fold_in(streams_of[19], 71), 0)
    group_docs = ragged(streams_of[2], GROUPS, DOCS, HOLD, 2).astype(jnp.int32)
    list_len = ragged(streams_of[3], QUERY_COUNT, DOCS, min(LIST_MAX, DOCS // 2), 1).astype(jnp.int32)
    relevance = jnp.clip(jnp.exp(jax.random.uniform(streams_of[4], (DOCS,), jnp.float32, math.log(0.1), math.log(10.0))), 0.1, 10.0)
    start_token = bell_draw(streams_of[5], (D,), 1.0, 6.0)
    score_row = bell_draw(streams_of[6], (D,), 1.0, 6.0)
    g_self = jnp.clip(1.0 + 0.18 * jax.random.normal(streams_of[7], (D,), jnp.float32), 0.1, 1.9)
    w_value_self = bell_draw(streams_of[8], (D, HEADS * HEAD_DIM), D ** -0.5, 0.21875, ((1, 4),))
    w_out_self = bell_draw(streams_of[9], (HEADS * HEAD_DIM, D), (HEADS * HEAD_DIM) ** -0.5, 0.21875, ((0, 4),))
    g_cross = jnp.clip(1.0 + 0.18 * jax.random.normal(streams_of[10], (D,), jnp.float32), 0.1, 1.9)
    w_query = bell_draw(streams_of[11], (D, HEADS * HEAD_DIM), (16 * D) ** -0.5, 0.0546875, ((1, 4),))
    w_key = bell_draw(streams_of[12], (D, HEADS * HEAD_DIM), D ** -0.5, 0.21875, ((1, 4),))
    w_value = bell_draw(streams_of[13], (D, HEADS * HEAD_DIM), D ** -0.5, 0.21875, ((1, 4),))
    w_out = bell_draw(streams_of[14], (HEADS * HEAD_DIM, D), (HEADS * HEAD_DIM // 32) ** -0.5, 1.25, ((0, 4),))
    g_ff = jnp.clip(1.0 + 0.18 * jax.random.normal(streams_of[15], (D,), jnp.float32), 0.1, 1.9)
    w_in = bell_draw(streams_of[16], (D, FF), D ** -0.5, 0.21875, ((1, 4),))
    w_down = bell_draw(streams_of[17], (FF, D), FF ** -0.5, 0.109375, ((0, 4),))
    g_final = jnp.clip(1.0 + 0.18 * jax.random.normal(streams_of[18], (D,), jnp.float32), 0.1, 1.9)
    return dict(enc_out=enc_out, enc_len=enc_len, group_docs=group_docs, list_len=list_len, relevance=relevance, start_token=start_token, score_row=score_row, g_self=g_self, w_value_self=w_value_self, w_out_self=w_out_self, g_cross=g_cross, w_query=w_query, w_key=w_key, w_value=w_value, w_out=w_out, g_ff=g_ff, w_in=w_in, w_down=w_down, g_final=g_final)


@jax.custom_vjp
def low(v):
    return lax.optimization_barrier(v.astype(jnp.bfloat16)).astype(jnp.float32)

@jax.custom_vjp
def low_back(v):
    return v

def low_keep(v):
    return (low(v), None)

def low_pass(kept, grad):
    return (grad,)

def back_keep(v):
    return (v, None)

def back_low(kept, grad):
    return (low(grad),)
low.defvjp(low_keep, low_pass)
low_back.defvjp(back_keep, back_low)
EPSILON = 1e-06
MASKED = -1e+30
PRECISE = lax.Precision.HIGHEST

def rms_norm(value_rows, gain):
    scale = lax.rsqrt(lax.optimization_barrier(jnp.mean(value_rows * value_rows, axis=-1, keepdims=True)) + EPSILON)
    return value_rows * scale * gain

def list_loss(all_scores, list_len, relevance):
    list_ends = jnp.cumsum(list_len).astype(jnp.int32)
    begins = (list_ends - list_len).astype(jnp.int32)
    places = jnp.arange(all_scores.shape[0], dtype=jnp.int32)
    member = (places[None, :] >= begins[:, None]) & (places[None, :] < list_ends[:, None])
    owner = lax.optimization_barrier(jnp.sum((places[None, :] >= list_ends[:, None]).astype(jnp.int32), axis=0))
    peak_val = lax.optimization_barrier(jnp.max(jnp.where(member, all_scores[None, :], MASKED), axis=1))
    shifted = jnp.exp(all_scores - peak_val[owner])
    totals = lax.optimization_barrier(jnp.sum(jnp.where(member, shifted[None, :], 0.0), axis=1))
    log_total = peak_val + jnp.log(totals)
    weight_sum = lax.optimization_barrier(jnp.sum(jnp.where(member, relevance[None, :], 0.0), axis=1))
    target = relevance / weight_sum[owner]
    picked = lax.optimization_barrier(jnp.sum(jnp.where(member, (target * all_scores)[None, :], 0.0), axis=1))
    return jnp.mean(log_total - picked)

def slot_docs(group_docs):
    counts = group_docs.astype(jnp.int32)
    starts = (jnp.cumsum(counts) - counts).astype(jnp.int32)
    slot_index = jnp.arange(HOLD, dtype=jnp.int32)
    return jnp.where(slot_index[None, :] < counts[:, None], starts[:, None] + slot_index[None, :], DOCS).astype(jnp.int32)

def reference(enc_out, enc_len, group_docs, list_len, relevance, start_token, score_row, g_self, w_value_self, w_out_self, g_cross, w_query, w_key, w_value, w_out, g_ff, w_in, w_down, g_final):
    slot_ids = slot_docs(group_docs)
    lengths = jnp.concatenate([enc_len.astype(jnp.int32), jnp.ones((1,), jnp.int32)])[slot_ids]
    floats = [item.astype(jnp.float32) for item in (enc_out, start_token, score_row, g_self, w_value_self, w_out_self, g_cross, w_query, w_key, w_value, w_out, g_ff, w_in, w_down, g_final)]

    def forward(enc_f, start_vec, row_vec, gain_self, value_self_w, out_self_w, gain_cross, query_w, key_w, value_w, out_w, gain_ff, inner_w, down_w, gain_final):
        first_in = low(rms_norm(start_vec, gain_self))
        self_value = low(jnp.dot(first_in, value_self_w, precision=PRECISE))
        hidden1 = start_vec + jnp.dot(self_value, out_self_w, precision=PRECISE)
        second_in = low(rms_norm(hidden1, gain_cross))
        query_vec = low(jnp.dot(second_in, query_w, precision=PRECISE)).reshape(HEADS, HEAD_DIM)
        enc_low = low_back(enc_f).reshape(GROUPS, HOLD, ENC, D)

        def group_scores(carried, item_pair):
            enc_g, len_g = item_pair
            key_rows = low_back(low(jnp.einsum('std,de->ste', enc_g, key_w, precision=PRECISE))).reshape(HOLD, ENC, HEADS, HEAD_DIM)
            value_rows = low_back(low(jnp.einsum('std,de->ste', enc_g, value_w, precision=PRECISE))).reshape(HOLD, ENC, HEADS, HEAD_DIM)
            logits = low_back(jnp.einsum('sthd,hd->sht', key_rows, query_vec, precision=PRECISE))
            visible = jnp.arange(ENC, dtype=jnp.int32)[None, :] < len_g[:, None]
            logits = jnp.where(visible[:, None, :], logits, MASKED)
            peak_val = lax.optimization_barrier(jnp.max(logits, axis=-1, keepdims=True))
            raised = jnp.exp(logits - peak_val)
            attn_prob = low(raised / lax.optimization_barrier(jnp.sum(raised, axis=-1, keepdims=True)))
            context = low_back(low(jnp.einsum('sht,sthd->shd', attn_prob, value_rows, precision=PRECISE).reshape(HOLD, HEADS * HEAD_DIM)))
            hidden2 = low_back(hidden1[None, :] + jnp.dot(context, out_w, precision=PRECISE))
            third_in = low(rms_norm(hidden2, gain_ff))
            pre_act = low_back(jnp.dot(third_in, inner_w, precision=PRECISE))
            act_low = low(jax.nn.gelu(pre_act, approximate=False))
            hidden3 = low_back(hidden2 + jnp.dot(act_low, down_w, precision=PRECISE))
            final_vec = rms_norm(hidden3, gain_final)
            return (carried, jnp.dot(final_vec, row_vec, precision=PRECISE) * D ** (-0.5))
        _, scores = lax.scan(jax.checkpoint(group_scores), jnp.zeros((), jnp.float32), (enc_low, lengths))
        all_scores = jnp.zeros((DOCS + 1,), jnp.float32).at[slot_ids.reshape(-1)].set(scores.reshape(-1))[:DOCS]
        return (list_loss(all_scores, list_len, relevance), all_scores)
    loss_value, pullback, all_scores = jax.vjp(forward, *floats, has_aux=True)
    gradients = pullback(jnp.ones_like(loss_value))
    return (all_scores, loss_value, gradients[0].astype(jnp.bfloat16), gradients[1], gradients[2], gradients[3], gradients[4], gradients[5], gradients[6], gradients[7], gradients[8], gradients[9], gradients[10], gradients[11], gradients[12], gradients[13], gradients[14])
```

```python
import functools

import jax
import jax.numpy as jnp
from jax import lax
from jax.experimental import pallas as pl
from jax.experimental.pallas import tpu as pltpu
from jax.sharding import PartitionSpec as P

D = 768
HEADS = 12
HEAD_DIM = 64
ROWS = 16
BLOCK = 16
LANES = 128

EPSILON = 1e-06
MASKED = -1e30
FACTOR = D ** (-0.5)
ROOT_HALF = 0.5**0.5
DENSITY = 0.3989422804014327
f32, bf16, i32 = jnp.float32, jnp.bfloat16, jnp.int32
EXACT = lax.Precision.HIGHEST
MIB = 1 << 20


def nn(a, b, precision=None):
    return lax.dot_general(
        a, b, (((1,), (0,)), ((), ())), precision=precision, preferred_element_type=f32
    )


def nt(a, b, precision=None):
    return lax.dot_general(
        a, b, (((1,), (1,)), ((), ())), precision=precision, preferred_element_type=f32
    )


def tn(a, b, precision=None):
    return lax.dot_general(
        a, b, (((0,), (0,)), ((), ())), precision=precision, preferred_element_type=f32
    )


def iota(shape, dim):
    return lax.broadcasted_iota(i32, shape, dim)


def split2(x):
    high = x.astype(bf16)
    return high, (x - high.astype(f32)).astype(bf16)


def split3(x):
    high = x.astype(bf16)
    rest = x - high.astype(f32)
    mid = rest.astype(bf16)
    return high, mid, (rest - mid.astype(f32)).astype(bf16)


def stack3(row, height=ROWS):
    at = iota((height, row.shape[1]), 0)
    parts = split3(row)
    zero = jnp.zeros((), f32)
    out = jnp.where(at == 0, parts[0].astype(f32), zero)
    out = jnp.where(at == 1, parts[1].astype(f32), out)
    return jnp.where(at == 2, parts[2].astype(f32), out).astype(bf16)


def repeat3(row, height=ROWS):
    at = iota((height, row.shape[1]), 0)
    return jnp.where(at < 3, row.astype(f32), 0.0).astype(bf16)


def rms_parts(rows):
    scale = lax.rsqrt(jnp.mean(rows * rows, axis=-1, keepdims=True) + EPSILON)
    return rows * scale, scale


def rms_back(grad_normed, normed, scale):
    inner = jnp.mean(grad_normed * normed, axis=-1, keepdims=True)
    return scale * (grad_normed - normed * inner)


def phi(z):
    return 0.5 * (1.0 + lax.erf(z * ROOT_HALF))


def gelu_slope(z):
    return phi(z) + z * (DENSITY * jnp.exp(-0.5 * z * z))


def head_of(shape, dim):
    return iota(shape, dim) // HEAD_DIM


def spread(small):
    hot = (iota((LANES, D), 0) == head_of((LANES, D), 1)).astype(f32)
    return nn(small, hot, EXACT)


def self_kernel(start, g_self, wvs, wos, part_out, s1_out, y1_out):
    x0 = start[...].astype(f32)
    n0, _ = rms_parts(x0)
    y1 = jnp.broadcast_to(n0 * g_self[...], (ROWS, D)).astype(bf16)
    s1 = nn(y1, wvs[...]).astype(bf16)
    part_out[...] = nn(s1, wos[...])[:8]
    s1_out[...] = s1
    y1_out[...] = y1


def query_kernel(scal, part_a, part_b, start, g_cross, wq, wk, qk_out, h1_out, q_out, y2_out):
    h1 = start[...].astype(f32) + (part_a[0:1] + part_b[0:1])
    n1, _ = rms_parts(h1)
    y2 = jnp.broadcast_to(n1 * g_cross[...], (ROWS, D)).astype(bf16)
    q = nn(y2, wq[...]).astype(bf16)
    width = q.shape[1]
    first = scal[0] * (width // HEAD_DIM)
    own = iota((ROWS, width), 0) == first + head_of((ROWS, width), 1)
    qm = jnp.where(own, q.astype(f32), 0.0).astype(bf16)
    qk_out[...] = nt(qm, wk[...])
    h1_out[...] = h1
    q_out[...] = qm
    y2_out[...] = y2


def select_docs(height, width):
    r, c = iota((height, width), 0), iota((height, width), 1)
    return (((r // BLOCK) == (c % ROWS)) & ((r % BLOCK) == (c // ROWS))).astype(bf16)


def attend_kernel(scal, qa, qb, enc, wv, p_out, e_out, pay_out, qk_s):
    step = pl.program_id(0)
    tokens = enc.shape[1]
    count = scal[0]
    tall = BLOCK * ROWS

    @pl.when(step == 0)
    def _():
        high, low = split2(qa[...] + qb[...])
        qk_s[0:ROWS] = high
        qk_s[ROWS : 2 * ROWS] = low

    @pl.when(step * BLOCK < count)
    def _():
        rows = enc[...].reshape(BLOCK * tokens, D)
        both = nt(qk_s[...], rows)
        logits = both[:ROWS] + both[ROWS:]
        logits = jnp.concatenate(
            [logits[:, b * tokens : (b + 1) * tokens] for b in range(BLOCK)], axis=0
        )
        lane = iota((ROWS, tokens), 1)
        seen = jnp.concatenate(
            [
                jnp.broadcast_to(scal[8 + step * BLOCK + b], (ROWS, tokens))
                for b in range(BLOCK)
            ],
            axis=0,
        )
        seen = iota((tall, tokens), 1) < seen
        logits = jnp.where(seen, logits, MASKED)
        peak = jnp.max(logits, axis=1, keepdims=True)
        raised = jnp.where(seen, jnp.exp(logits - peak), 0.0)
        total = jnp.sum(raised, axis=1, keepdims=True)
        p_out[...] = raised.reshape(BLOCK, ROWS, tokens)
        low = raised.astype(bf16)
        sums = []
        upper = iota((2 * ROWS, tokens), 0) < ROWS
        zero = jnp.zeros((2 * ROWS, tokens), bf16)
        for k in range(BLOCK // 2):
            pair = low[2 * ROWS * k : 2 * ROWS * (k + 1)]
            left = jnp.concatenate(
                [jnp.where(upper, pair, zero), jnp.where(upper, zero, pair)], axis=1
            )
            sums.append(nn(left, rows[2 * tokens * k : 2 * tokens * (k + 1)]))
        summed = jnp.concatenate(sums, axis=0).astype(bf16)
        e_out[...] = (
            nn(select_docs(HEADS * BLOCK, tall), summed)
            .astype(bf16)
            .reshape(HEADS, BLOCK, D)
        )
        context = nn(summed, wv[...])
        own = (iota((tall, D), 0) % ROWS) == head_of((tall, D), 1)
        context = jnp.where(own, context, 0.0).astype(bf16)
        gather = (iota((BLOCK, tall), 0) == iota((BLOCK, tall), 1) // ROWS).astype(bf16)
        pay_out[:, :D] = nn(gather, context).astype(bf16)
        parts = split3(peak) + split3(total)
        at = iota((tall, LANES), 1)
        extra = jnp.zeros((tall, LANES), f32)
        for k, part in enumerate(parts):
            extra = jnp.where(at // ROWS == k, part.astype(f32), extra)
        extra = jnp.where(at % ROWS == iota((tall, LANES), 0) % ROWS, extra, 0.0)
        pay_out[:, D:] = nn(gather, extra.astype(bf16)).astype(bf16)

    @pl.when(step * BLOCK >= count)
    def _():
        p_out[...] = jnp.zeros_like(p_out)
        e_out[...] = jnp.zeros_like(e_out)
        pay_out[:, :D] = jnp.zeros((BLOCK, D), bf16)
        pay_out[:, D:] = jnp.where(iota((BLOCK, LANES), 1) < ROWS, MASKED, 0.0).astype(bf16)


def decode(pay):
    extra = pay[:, D:].astype(f32)

    def lane(k):
        return pltpu.roll(extra, LANES - k * ROWS, 1) if k else extra

    first = iota(extra.shape, 1) < ROWS
    peak = jnp.where(first, (lane(0) + lane(1)) + lane(2), 0.0)
    total = jnp.where(first, (lane(3) + lane(4)) + lane(5), 0.0)
    return peak, total


def merge(one, two):
    peak1, total1 = decode(one)
    peak2, total2 = decode(two)
    peak = jnp.maximum(peak1, peak2)
    up1, up2 = jnp.exp(peak1 - peak), jnp.exp(peak2 - peak)
    total = up1 * total1 + up2 * total2
    first = iota(peak.shape, 1) < ROWS
    up1, up2 = jnp.where(first, up1, 0.0), jnp.where(first, up2, 0.0)
    context = spread(up1) * one[:, :D].astype(f32) + spread(up2) * two[:, :D].astype(f32)
    return peak, total, context


def ordered(bit, own, other):
    swap = jnp.broadcast_to(bit, own.shape) == 1
    return jnp.where(swap, other, own), jnp.where(swap, own, other)


def merge_kernel(scal, own, other, pay_out):
    one, two = ordered(scal[0], own[...].astype(f32), other[...].astype(f32))
    peak, total, context = merge(one, two)
    pay_out[:, :D] = context.astype(bf16)
    extra = jnp.zeros(peak.shape, f32)
    at = iota(peak.shape, 1) // ROWS
    for k, part in enumerate(split3(peak) + split3(total)):
        part = part.astype(f32)
        extra = jnp.where(at == k, pltpu.roll(part, k * ROWS, 1) if k else part, extra)
    pay_out[:, D:] = extra.astype(bf16)


def forward_kernel(
    scal, own, other, first, h1, wout, g_ff, win, wdown,
    c_out, c32_out, scale_out, h2_out, z_out, part_out,
):
    one, two = ordered(scal[0], own[...].astype(f32), other[...].astype(f32))
    peak, total, context = merge(one, two)
    lanes = iota(peak.shape, 1) < ROWS
    inverse = jnp.where(lanes & (total > 0.0), 1.0 / jnp.where(total > 0.0, total, 1.0), 0.0)
    context = context * spread(inverse)
    mine, _ = decode(first[...].astype(f32))
    scale_out[...] = jnp.exp(jnp.minimum(mine - peak, 0.0)) * inverse
    c32_out[...] = context
    low = context.astype(bf16)
    c_out[...] = low
    h2 = h1[...] + nn(low, wout[...])
    h2_out[...] = h2
    n2, _ = rms_parts(h2)
    y3 = (n2 * g_ff[...]).astype(bf16)
    z = nn(y3, win[...])
    z_out[...] = z
    u = (z * phi(z)).astype(bf16)
    part_out[...] = nn(u, wdown[...]).astype(bf16)


def score_kernel(
    scal, part_a, part_b, h2, z, g_final, row, wdown, win,
    scores_out, n3_out, dh3_out, part_out,
):
    h3 = h2[...] + (part_a[...].astype(f32) + part_b[...].astype(f32))
    n3, r3 = rms_parts(h3)
    n3_out[...] = n3
    row_f = row[...].astype(f32)
    gained = jnp.broadcast_to(g_final[...] * row_f * FACTOR, (8, D))
    scores = nt(gained, n3, EXACT)[0:1]
    slots = n3.shape[0]
    groups = scores_out.shape[0]
    wide = jnp.concatenate([scores, jnp.zeros((1, LANES - slots), f32)], axis=1)
    scores_out[...] = jnp.where(iota((groups, LANES), 0) == scal[1], wide, 0.0)
    dh3 = rms_back(gained[0:1], n3, r3).astype(bf16)
    dh3_out[...] = dh3
    du = nt(dh3, wdown[...])
    dz = (du * gelu_slope(z[...])).astype(bf16)
    part_out[...] = nt(dz, win[...]).astype(bf16)


def list_kernel(scal, sc_a, sc_b, begins, ends, relevance, scores_out, loss_out, ds_out, mine_out):
    groups = sc_a.shape[0]
    docs = scores_out.shape[1]
    wide = docs + LANES
    queries = begins.shape[0]
    scores = sc_a[...] + sc_b[...]
    lane = iota((8, LANES), 1)
    blank = jnp.zeros((8, wide - LANES), f32)
    placed = jnp.zeros((8, wide), f32)
    for g in range(groups):
        start, count = scal[2 + g], scal[2 + groups + g]
        kept = jnp.where(lane < count, scores[g : g + 1], 0.0)
        placed = placed + pltpu.roll(jnp.concatenate([kept, blank], axis=1), start, 1)
    values = placed[0:1, :docs]
    scores_out[...] = values
    place = iota((queries, docs), 1)
    member = (place >= begins[...]) & (place < ends[...])
    peak = jnp.max(jnp.where(member, values, MASKED), axis=1, keepdims=True)
    raised = jnp.where(member, jnp.exp(jnp.where(member, values - peak, 0.0)), 0.0)
    log_total = peak + jnp.log(jnp.sum(raised, axis=1, keepdims=True))
    weight = jnp.sum(jnp.where(member, relevance[...], 0.0), axis=1, keepdims=True)
    target = jnp.where(member, relevance[...] / weight, 0.0)
    picked = jnp.sum(target * values, axis=1, keepdims=True)
    loss_out[...] = jnp.sum(log_total - picked, axis=0, keepdims=True) / queries
    chance = jnp.where(member, jnp.exp(jnp.where(member, values - log_total, 0.0)), 0.0)
    ds = jnp.sum(chance - target, axis=0, keepdims=True) / queries
    ds = jnp.broadcast_to(jnp.concatenate([ds, jnp.zeros((1, LANES), f32)], axis=1), (8, wide))
    at = iota((groups, LANES), 0)
    slotted = jnp.zeros((groups, LANES), f32)
    for g in range(groups):
        start, count = scal[2 + g], scal[2 + groups + g]
        back = pltpu.roll(ds, lax.rem(wide - start, wide), 1)[:, :LANES]
        back = jnp.where(lane < count, back, 0.0)[0:1]
        slotted = jnp.where(at == g, back, slotted)
    ds_out[...] = slotted
    mine = jnp.sum(jnp.where(at == scal[1], slotted, 0.0), axis=0, keepdims=True)
    mine_out[...] = jnp.broadcast_to(mine, (8, LANES))


def context_kernel(
    part_a, part_b, h2, dh3, c32, g_ff, wout, wout_own,
    dh2_out, dc_out, own_out, inner_out, ff_out,
):
    n2, r2 = rms_parts(h2[...])
    dy3 = part_a[...].astype(f32) + part_b[...].astype(f32)
    ff_out[...] = dy3 * n2
    dh2 = (dh3[...].astype(f32) + rms_back(dy3 * g_ff[...], n2, r2)).astype(bf16)
    dh2_out[...] = dh2
    dc = nt(dh2, wout[...]).astype(bf16)
    dc_out[...] = dc
    own_out[...] = nt(dh2, wout_own[...]).astype(bf16)
    hot = (head_of((D, LANES), 0) == iota((D, LANES), 1)).astype(f32)
    inner_out[...] = nn(dc.astype(f32) * c32[...], hot, EXACT)


def column(rows):
    tall = BLOCK * ROWS
    pick = (iota((tall, BLOCK), 0) // ROWS == iota((tall, BLOCK), 1)).astype(f32)
    wide = nn(pick, rows, EXACT)
    own = iota((tall, LANES), 0) % ROWS == iota((tall, LANES), 1)
    return jnp.sum(jnp.where(own, wide, 0.0), axis=1, keepdims=True)


def back_kernel(
    scal, ds, enc, p, scale, inner, dc, wv, dh2, n3, ff,
    dap_out, vd_out, sums_out,
):
    step = pl.program_id(0)
    tokens = enc.shape[1]
    tall = BLOCK * ROWS

    @pl.when(step == 0)
    def _():
        slots = dh2.shape[0]
        row = ds[...][:, :slots] * scal[1].astype(f32) * (1.0 / 1024.0)
        at = iota((ROWS, D), 0)
        out = jnp.where(at == HEADS, nn(row, dh2[...].astype(f32), EXACT)[0:1], 0.0)
        out = jnp.where(at == HEADS + 1, nn(row, n3[...], EXACT)[0:1], out)
        sums_out[...] = jnp.where(at == HEADS + 2, nn(row, ff[...], EXACT)[0:1], out)

    @pl.when(step * BLOCK < scal[0])
    def _():
        rows = enc[...].reshape(BLOCK * tokens, D)
        lane = iota((BLOCK, LANES), 1)
        own_slot = lane == step * BLOCK + iota((BLOCK, LANES), 0)
        ds_col = jnp.sum(jnp.where(own_slot, ds[0:1], 0.0), axis=1, keepdims=True)
        grad = (dc[...].astype(f32) * ds_col).astype(bf16)
        pick = (iota((tall, BLOCK), 0) // ROWS == iota((tall, BLOCK), 1)).astype(bf16)
        own = (iota((tall, D), 0) % ROWS) == head_of((tall, D), 1)
        grad = jnp.where(own, nn(pick, grad), 0.0).astype(bf16)
        vd = nt(grad, wv[...]).astype(bf16)
        vd_out[...] = vd.reshape(BLOCK, ROWS, D)
        grad_probs = []
        for k in range(BLOCK // 2):
            pair = nt(
                vd[2 * ROWS * k : 2 * ROWS * (k + 1)],
                rows[2 * tokens * k : 2 * tokens * (k + 1)],
            )
            grad_probs += [pair[:ROWS, :tokens], pair[ROWS:, tokens:]]
        grad_probs = jnp.concatenate(grad_probs, axis=0)
        prob = p[...].reshape(tall, tokens) * column(scale[...])
        da = (prob * (grad_probs - column(inner[...] * ds_col))).astype(bf16)
        dap_out[:, :ROWS] = da.reshape(BLOCK, ROWS, tokens)
        dap_out[:, ROWS:] = prob.astype(bf16).reshape(BLOCK, ROWS, tokens)
        flat = jnp.concatenate([da[ROWS * b : ROWS * (b + 1)] for b in range(BLOCK)], axis=1)
        sums_out[...] += nn(flat, rows)

    @pl.when(step * BLOCK >= scal[0])
    def _():
        dap_out[...] = jnp.zeros_like(dap_out)
        vd_out[...] = jnp.zeros_like(vd_out)


def enc_grad_kernel(scal, qa, qb, dap, vd, grad_out):
    step = pl.program_id(0)

    @pl.when(step * BLOCK < scal[0])
    def _():
        qk = (qa[...] + qb[...]).astype(bf16)
        for b in range(BLOCK):
            right = jnp.concatenate([qk, vd[b]], axis=0)
            grad_out[b] = tn(dap[b], right).astype(bf16)

    @pl.when(step * BLOCK >= scal[0])
    def _():
        grad_out[...] = jnp.zeros_like(grad_out)


def value_kernel(scal, keep, other, dc, ds, grad_out):
    slots = keep.shape[1]
    own_slot = iota((slots, LANES), 0) == iota((slots, LANES), 1)
    ds_col = jnp.sum(jnp.where(own_slot, ds[0:1], 0.0), axis=1, keepdims=True)
    grad = (dc[...].astype(f32) * ds_col).astype(bf16)
    for h in range(keep.shape[0]):
        summed = (keep[h].astype(f32) + other[h].astype(f32)).astype(bf16)
        part = tn(grad[:, h * HEAD_DIM : (h + 1) * HEAD_DIM], summed)
        grad_out[h * HEAD_DIM : (h + 1) * HEAD_DIM] = part.astype(bf16)


def weights_kernel(
    cd, dh2, c_own, ds, h1, g_ff, wout, win, wdown,
    win_out, wdown_out, wout_out,
):
    @pl.when(pl.program_id(0) == 0)
    def _():
        win_out[...] = jnp.zeros_like(win_out)
        wdown_out[...] = jnp.zeros_like(wdown_out)
        wout_out[...] = jnp.zeros_like(wout_out)

    h2 = h1[...] + nn(cd[:, :D], wout[...])
    n2, _ = rms_parts(h2)
    y3 = (n2 * g_ff[...]).astype(bf16)
    z = nn(y3, win[...])
    u = (z * phi(z)).astype(bf16)
    ds_col = ds[...]
    dh3 = (cd[:, D:].astype(f32) * ds_col).astype(bf16)
    dz = (nt(dh3, wdown[...]) * gelu_slope(z)).astype(bf16)
    win_out[...] += tn(y3, dz)
    wdown_out[...] += tn(u, dh3)
    wout_out[...] += tn(c_own[...], (dh2[...].astype(f32) * ds_col).astype(bf16))


def key_kernel(scal, sum_a, sum_b, wk, wq, qm, y2, key_out, query_out, part_out):
    g = sum_a[...] + sum_b[...]
    g = jnp.where(iota((ROWS, D), 0) < HEADS, g, 0.0)
    high, low = split2(g)
    both = jnp.concatenate([high, low], axis=0)
    dq = nn(both, wk[...])
    dq = dq[:ROWS] + dq[ROWS:]
    width = dq.shape[1]
    first = scal[0] * (width // HEAD_DIM)
    own = iota((ROWS, width), 0) == first + head_of((ROWS, width), 1)
    dq = jnp.sum(jnp.where(own, dq, 0.0), axis=0, keepdims=True)
    key_out[...] = tn(both, jnp.concatenate([qm[...], qm[...]], axis=0))
    dq_parts = stack3(dq)
    query_out[...] = tn(repeat3(y2[0:1]), dq_parts)
    part = jnp.sum(nt(dq_parts, wq[...]), axis=0, keepdims=True)
    part_out[...] = jnp.broadcast_to(part, (8, D))


def hidden_kernel(
    part_a, part_b, sum_a, sum_b, h1, g_cross, s1, y1, wos, wvs, g_final, row,
    cross_out, dh1_out, wos_out, wvs_out, part_out, final_out, row_out, ff_out,
):
    dy2 = part_a[0:1] + part_b[0:1]
    sums = sum_a[...] + sum_b[...]
    n1, r1 = rms_parts(h1[...])
    cross_out[...] = dy2 * n1
    dh1 = sums[HEADS : HEADS + 1] + rms_back(dy2 * g_cross[...], n1, r1)
    dh1_out[...] = dh1
    dh1_parts = stack3(dh1)
    wos_out[...] = tn(repeat3(s1[0:1]), dh1_parts)
    ds1 = jnp.sum(nt(dh1_parts, wos[...]), axis=0, keepdims=True)
    ds1_parts = stack3(ds1)
    wvs_out[...] = tn(repeat3(y1[0:1]), ds1_parts)
    part = jnp.sum(nt(ds1_parts, wvs[...]), axis=0, keepdims=True)
    part_out[...] = jnp.broadcast_to(part, (8, D))
    total = sums[HEADS + 1 : HEADS + 2] * FACTOR
    final_out[...] = total * row[...].astype(f32)
    row_out[...] = total * g_final[...]
    ff_out[...] = sums[HEADS + 2 : HEADS + 3]


def start_kernel(part_a, part_b, dh1, start, g_self, gain_out, start_out):
    dy1 = part_a[0:1] + part_b[0:1]
    n0, r0 = rms_parts(start[...].astype(f32))
    gain_out[...] = dy1 * n0
    start_out[...] = dh1[...] + rms_back(dy1 * g_self[...], n0, r0)


def shape(dims, dtype=f32):
    return jax.ShapeDtypeStruct(dims, dtype)


def whole_spec(memory=pltpu.VMEM):
    return pl.BlockSpec(memory_space=memory)


def plain(kernel, outs, *args, smem=0, flops=0, limit=32):
    size = sum(a.size * a.dtype.itemsize for a in args)
    return pl.pallas_call(
        kernel,
        out_shape=outs,
        in_specs=[whole_spec(pltpu.SMEM if k < smem else pltpu.VMEM) for k in range(len(args))],
        out_specs=jax.tree.map(lambda _: whole_spec(), outs),
        compiler_params=pltpu.CompilerParams(vmem_limit_bytes=limit * MIB),
        cost_estimate=pl.CostEstimate(flops=flops, bytes_accessed=size, transcendentals=0),
        name=kernel.__name__,
    )(*args)


def gridded(kernel, steps, scal, ins, outs, scratch=(), flops=0, limit=40):
    size = sum(a.size * a.dtype.itemsize for a, _, _ in ins)
    size += sum(s.size * s.dtype.itemsize for s, _, _ in outs)
    return pl.pallas_call(
        kernel,
        out_shape=[s for s, _, _ in outs],
        grid_spec=pltpu.PrefetchScalarGridSpec(
            num_scalar_prefetch=1,
            grid=(steps,),
            in_specs=[pl.BlockSpec(block, index) for _, block, index in ins],
            out_specs=[pl.BlockSpec(block, index) for _, block, index in outs],
            scratch_shapes=list(scratch),
        ),
        compiler_params=pltpu.CompilerParams(
            vmem_limit_bytes=limit * MIB, dimension_semantics=("arbitrary",)
        ),
        cost_estimate=pl.CostEstimate(flops=flops, bytes_accessed=size, transcendentals=0),
        name=kernel.__name__,
    )(scal, *[a for a, _, _ in ins])


def bits_of(size):
    return [1 << b for b in range(size.bit_length() - 1)]


def swap(x, axis, bit):
    size = lax.axis_size(axis)
    return lax.ppermute(x, axis, [(i, i ^ bit) for i in range(size)])


def sum_last(x, axes):
    steps = [(axis, bit) for axis in axes for bit in bits_of(lax.axis_size(axis))]
    for axis, bit in steps[:-1]:
        x = (x.astype(f32) + swap(x, axis, bit).astype(f32)).astype(x.dtype)
    axis, bit = steps[-1]
    return x, swap(x, axis, bit)


def gather_rows(x, axis, bits):
    me = lax.axis_index(axis)
    x = x[None]
    for bit in bits:
        other = swap(x, axis, bit)
        mine = (me & bit) > 0
        x = jnp.concatenate([jnp.where(mine, other, x), jnp.where(mine, x, other)], axis=0)
    return x


def gather_all(x, groups):
    me = lax.axis_index("heads")
    half = x.shape[0] // 2
    piece = lax.dynamic_slice_in_dim(x, (me & 1) * half, half)
    pieces = gather_rows(piece, "docs", bits_of(groups))
    halves = gather_rows(pieces, "heads", [1])
    return halves.reshape(2 * groups * half, x.shape[1])


def per_device(
    enc_out,
    enc_len,
    group_docs,
    list_len,
    relevance,
    start_token,
    score_row,
    g_self,
    w_value_self,
    w_out_self,
    g_cross,
    w_query,
    w_key,
    w_value,
    w_out,
    g_ff,
    w_in,
    w_down,
    g_final,
):
    groups = lax.axis_size("docs")
    parts = lax.axis_size("heads")
    me_g = lax.axis_index("docs")
    me_j = lax.axis_index("heads")
    slots, tokens = enc_out.shape[:2]
    docs = enc_len.shape[0]
    queries = list_len.shape[0]
    width = w_value.shape[1]
    own_heads = HEADS // parts
    hidden = w_in.shape[1]
    blocks = slots // BLOCK

    ends = jnp.cumsum(group_docs)
    starts = ends - group_docs
    my_start, my_count = starts[me_g], group_docs[me_g]
    lengths = lax.dynamic_slice_in_dim(
        jnp.concatenate([enc_len, jnp.zeros((slots,), i32)]), my_start, slots
    )
    slot = jnp.arange(slots, dtype=i32)
    seen = jnp.where(slot < my_count, jnp.clip(lengths - me_j * tokens, 0, tokens), 0)
    list_ends = jnp.cumsum(list_len)
    begins = list_ends - list_len
    scal_doc = jnp.concatenate(
        [jnp.stack([my_count] + [jnp.full((), 1024 // parts, i32)] + [me_j] * 6), seen]
    )
    scal_j = jnp.stack([me_j, me_g])
    scal_list = jnp.concatenate([scal_j, starts, group_docs])
    bit_scal = [jnp.stack([(me_j // bit) & 1, me_g]) for bit in bits_of(parts)]

    def as_row(x):
        return x.reshape(1, -1)

    start_row, row = as_row(start_token), as_row(score_row)
    gain0, gain1, gain2, gain3 = (as_row(g) for g in (g_self, g_cross, g_ff, g_final))

    value_full = lax.all_gather(w_value, "heads", axis=1, tiled=True)
    out_full = lax.all_gather(w_out, "heads", axis=0, tiled=True)

    part, s1, y1 = plain(
        self_kernel,
        [shape((8, D)), shape((ROWS, width), bf16), shape((ROWS, D), bf16)],
        start_row,
        gain0,
        w_value_self,
        w_out_self,
    )
    part_a, part_b = sum_last(part, ["heads"])
    qk, h1, qm, y2 = plain(
        query_kernel,
        [shape((ROWS, D)), shape((1, D)), shape((ROWS, width), bf16), shape((ROWS, D), bf16)],
        scal_j,
        part_a,
        part_b,
        start_row,
        gain1,
        w_query,
        w_key,
        smem=1,
    )
    qk_a, qk_b = sum_last(qk, ["heads"])

    def last(scal):
        return jnp.maximum((scal[0] - 1) // BLOCK, 0)

    const2 = lambda i, scal: (0, 0)
    step2 = lambda i, scal: (i, 0)
    step3 = lambda i, scal: (i, 0, 0)
    enc_map = lambda i, scal: (jnp.minimum(i, last(scal)), 0, 0)
    pass_flops = 2 * slots * tokens * D * 256
    prob, summed, pay = gridded(
        attend_kernel,
        blocks,
        scal_doc,
        [
            (qk_a, (ROWS, D), const2),
            (qk_b, (ROWS, D), const2),
            (enc_out, (BLOCK, tokens, D), enc_map),
            (value_full, (D, D), const2),
        ],
        [
            (shape((slots, ROWS, tokens)), (BLOCK, ROWS, tokens), step3),
            (shape((HEADS, slots, D), bf16), (HEADS, BLOCK, D), lambda i, scal: (0, i, 0)),
            (shape((slots, D + LANES), bf16), (BLOCK, D + LANES), step2),
        ],
        scratch=[pltpu.VMEM((2 * ROWS, D), bf16)],
        flops=2 * pass_flops,
    )
    merged = pay
    for bit, scal in zip(bits_of(parts)[:-1], bit_scal[:-1]):
        merged = plain(
            merge_kernel,
            shape(pay.shape, bf16),
            scal,
            merged,
            swap(merged, "heads", bit),
            smem=1,
        )
    other = swap(merged, "heads", bits_of(parts)[-1])

    c, c32, scale, h2, z, part = plain(
        forward_kernel,
        [
            shape((slots, D), bf16),
            shape((slots, D)),
            shape((slots, LANES)),
            shape((slots, D)),
            shape((slots, hidden)),
            shape((slots, D), bf16),
        ],
        bit_scal[-1],
        merged,
        other,
        pay,
        h1,
        out_full,
        gain2,
        w_in,
        w_down,
        smem=1,
    )
    part_a, part_b = sum_last(part, ["heads"])
    scores, n3, dh3, part = plain(
        score_kernel,
        [
            shape((groups, LANES)),
            shape((slots, D)),
            shape((slots, D), bf16),
            shape((slots, D), bf16),
        ],
        scal_j,
        part_a,
        part_b,
        h2,
        z,
        gain3,
        row,
        w_down,
        w_in,
        smem=1,
    )
    score_a, score_b = sum_last(scores, ["docs"])
    all_scores, loss, ds_slots, ds_mine = plain(
        list_kernel,
        [shape((1, docs)), shape((1, 1)), shape((groups, LANES)), shape((8, LANES))],
        scal_list,
        score_a,
        score_b,
        begins.reshape(-1, 1),
        list_ends.reshape(-1, 1),
        as_row(relevance),
        smem=1,
    )
    part_a, part_b = sum_last(part, ["heads"])
    dh2, dc, dc_own, inner, ff = plain(
        context_kernel,
        [
            shape((slots, D), bf16),
            shape((slots, D), bf16),
            shape((slots, width), bf16),
            shape((slots, LANES)),
            shape((slots, D)),
        ],
        part_a,
        part_b,
        h2,
        dh3,
        c32,
        gain2,
        out_full,
        w_out,
    )

    scaled = summed.astype(f32) * scale[:, :HEADS].T[:, :, None]
    piece = scaled.astype(bf16).reshape(parts, own_heads, slots, D)
    keep = piece
    count = parts
    bits = bits_of(parts)
    for k, bit in enumerate(bits):
        mine = (me_j // bit) & 1
        keep = keep.reshape(count // 2, 2, own_heads, slots, D)
        sent = lax.dynamic_index_in_dim(keep, 1 - mine, 1, keepdims=False)
        keep = lax.dynamic_index_in_dim(keep, mine, 1, keepdims=False)
        other = swap(sent, "heads", bit)
        if k < len(bits) - 1:
            keep = (keep.astype(f32) + other.astype(f32)).astype(bf16)
        count //= 2
    keep, other = keep.reshape(own_heads, slots, D), other.reshape(own_heads, slots, D)
    value_part = plain(
        value_kernel,
        shape((width, D), bf16),
        scal_j,
        keep,
        other,
        dc_own,
        ds_mine,
        smem=1,
    )

    dap, vd, sums = gridded(
        back_kernel,
        blocks,
        scal_doc,
        [
            (ds_mine, (8, LANES), const2),
            (enc_out, (BLOCK, tokens, D), enc_map),
            (prob, (BLOCK, ROWS, tokens), step3),
            (scale, (BLOCK, LANES), step2),
            (inner, (BLOCK, LANES), step2),
            (dc, (BLOCK, D), step2),
            (value_full, (D, D), const2),
            (dh2, (slots, D), const2),
            (n3, (slots, D), const2),
            (ff, (slots, D), const2),
        ],
        [
            (shape((slots, 2 * ROWS, tokens), bf16), (BLOCK, 2 * ROWS, tokens), step3),
            (shape((slots, ROWS, D), bf16), (BLOCK, ROWS, D), step3),
            (shape((ROWS, D)), (ROWS, D), const2),
        ],
        flops=2 * pass_flops,
    )
    (enc_grad,) = gridded(
        enc_grad_kernel,
        blocks,
        scal_doc,
        [
            (qk_a, (ROWS, D), const2),
            (qk_b, (ROWS, D), const2),
            (dap, (BLOCK, 2 * ROWS, tokens), step3),
            (vd, (BLOCK, ROWS, D), step3),
        ],
        [(shape(enc_out.shape, bf16), (BLOCK, tokens, D), step3)],
        flops=pass_flops,
    )

    cd_all = gather_all(jnp.concatenate([c, dh3], axis=1), groups)
    dh2_all = gather_all(dh2, groups)
    half = slots // 2
    ds_all = (
        ds_slots[:, :slots].reshape(groups, 2, half).transpose(1, 0, 2).reshape(-1, 1)
    )
    c_own = lax.dynamic_slice_in_dim(cd_all[:, :D], me_j * width, width, axis=1)
    total_rows = groups * slots
    tile = 192
    once = lambda i, scal: (0, 0)
    w_in_grad, w_down_grad, w_out_grad = gridded(
        lambda scal, *refs: weights_kernel(*refs),
        total_rows // tile,
        scal_j,
        [
            (cd_all, (tile, 2 * D), step2),
            (dh2_all, (tile, D), step2),
            (c_own, (tile, width), step2),
            (ds_all, (tile, 1), step2),
            (h1, (1, D), once),
            (gain2, (1, D), once),
            (out_full, (D, D), once),
            (w_in, (D, hidden), once),
            (w_down, (hidden, D), once),
        ],
        [
            (shape((D, hidden)), (D, hidden), once),
            (shape((hidden, D)), (hidden, D), once),
            (shape((width, D)), (width, D), once),
        ],
        flops=10 * total_rows * D * hidden,
        limit=48,
    )

    value_a, value_b = sum_last(value_part, ["docs"])
    value_grad = (value_a.astype(f32) + value_b.astype(f32)).T

    sum_a, sum_b = sum_last(sums, ["heads", "docs"])
    key_grad, query_grad, part = plain(
        key_kernel,
        [shape((D, width)), shape((D, width)), shape((8, D))],
        scal_j,
        sum_a,
        sum_b,
        w_key,
        w_query,
        qm,
        y2,
        smem=1,
    )
    part_a, part_b = sum_last(part, ["heads"])
    cross, dh1, wos_grad, wvs_grad, part, final_gain, row_grad, ff_gain = plain(
        hidden_kernel,
        [shape((1, D))] * 2
        + [shape((width, D)), shape((D, width)), shape((8, D))]
        + [shape((1, D))] * 3,
        part_a,
        part_b,
        sum_a,
        sum_b,
        h1,
        gain1,
        s1,
        y1,
        w_out_self,
        w_value_self,
        gain3,
        row,
    )
    part_a, part_b = sum_last(part, ["heads"])
    self_gain, start_grad = plain(
        start_kernel, [shape((1, D))] * 2, part_a, part_b, dh1, start_row, gain0
    )

    def flat(x):
        return x.reshape(-1)

    return (
        flat(all_scores),
        loss.reshape(()),
        enc_grad,
        flat(start_grad),
        flat(row_grad),
        flat(self_gain),
        wvs_grad,
        wos_grad,
        flat(cross),
        query_grad,
        key_grad,
        value_grad,
        w_out_grad,
        flat(ff_gain),
        w_in_grad,
        w_down_grad,
        flat(final_gain),
    )


def solution(mesh):
    placed = (
        P("docs", "heads", None),
        P(),
        P(),
        P(),
        P(),
        P(),
        P(),
        P(),
        P(None, "heads"),
        P("heads", None),
        P(),
        P(None, "heads"),
        P(None, "heads"),
        P(None, "heads"),
        P("heads", None),
        P(),
        P(None, "heads"),
        P("heads", None),
        P(),
    )
    return jax.shard_map(
        per_device,
        mesh=mesh,
        in_specs=placed,
        out_specs=(
            P(),
            P(),
            P("docs", "heads", None),
            P(),
            P(),
            P(),
            P(None, "heads"),
            P("heads", None),
            P(),
            P(None, "heads"),
            P(None, "heads"),
            P(None, "heads"),
            P("heads", None),
            P(),
            P(None, "heads"),
            P("heads", None),
            P(),
        ),
        check_vma=False,
    )
```

```python
import functools

import jax
import jax.numpy as jnp
from jax import lax
from jax.experimental import pallas as pl
from jax.experimental.pallas import tpu as pltpu
from jax.sharding import PartitionSpec as P

D = 768
HEADS = 12
HEAD_DIM = 64
ROWS = 16
BLOCK = 16
LANES = 128
PARTS = 4

EPSILON = 1e-06
MASKED = -1e30
FACTOR = D ** (-0.5)
ROOT_HALF = 0.5**0.5
DENSITY = 0.3989422804014327
f32, bf16, i32 = jnp.float32, jnp.bfloat16, jnp.int32
EXACT = lax.Precision.HIGHEST
MIB = 1 << 20


def nn(a, b, precision=None):
    return lax.dot_general(
        a, b, (((1,), (0,)), ((), ())), precision=precision, preferred_element_type=f32
    )


def nt(a, b, precision=None):
    return lax.dot_general(
        a, b, (((1,), (1,)), ((), ())), precision=precision, preferred_element_type=f32
    )


def tn(a, b, precision=None):
    return lax.dot_general(
        a, b, (((0,), (0,)), ((), ())), precision=precision, preferred_element_type=f32
    )


def iota(shape, dim):
    return lax.broadcasted_iota(i32, shape, dim)


def split2(x):
    high = x.astype(bf16)
    return high, (x - high.astype(f32)).astype(bf16)


def split3(x):
    high = x.astype(bf16)
    rest = x - high.astype(f32)
    mid = rest.astype(bf16)
    return high, mid, (rest - mid.astype(f32)).astype(bf16)


def stack3(row, height=ROWS):
    at = iota((height, row.shape[1]), 0)
    parts = split3(row)
    zero = jnp.zeros((), f32)
    out = jnp.where(at == 0, parts[0].astype(f32), zero)
    out = jnp.where(at == 1, parts[1].astype(f32), out)
    return jnp.where(at == 2, parts[2].astype(f32), out).astype(bf16)


def repeat3(row, height=ROWS):
    at = iota((height, row.shape[1]), 0)
    return jnp.where(at < 3, row.astype(f32), 0.0).astype(bf16)


def rms_parts(rows):
    scale = lax.rsqrt(jnp.mean(rows * rows, axis=-1, keepdims=True) + EPSILON)
    return rows * scale, scale


def rms_back(grad_normed, normed, scale):
    inner = jnp.mean(grad_normed * normed, axis=-1, keepdims=True)
    return scale * (grad_normed - normed * inner)


def phi(z):
    return 0.5 * (1.0 + lax.erf(z * ROOT_HALF))


def gelu_slope(z):
    return phi(z) + z * (DENSITY * jnp.exp(-0.5 * z * z))


def head_of(shape, dim):
    return iota(shape, dim) // HEAD_DIM


def spread(small):
    hot = (iota((LANES, D), 0) == head_of((LANES, D), 1)).astype(f32)
    return nn(small, hot, EXACT)


def row_of(ref):
    return ref[...].astype(f32).reshape(1, D)


def gained(n, gain):
    return jnp.broadcast_to(n * row_of(gain), (ROWS, D)).astype(bf16)


def self_parts(start, g_self, wvs):
    x0 = row_of(start)
    n0, _ = rms_parts(x0)
    y1 = gained(n0, g_self)
    return y1, nt(y1, wvs[...]).astype(bf16)


def query_parts(scal, h1, g_cross, wq):
    n1, _ = rms_parts(h1[...])
    y2 = gained(n1, g_cross)
    q = nt(y2, wq[...]).astype(bf16)
    width = q.shape[1]
    first = scal[0] * (width // HEAD_DIM)
    own = iota((ROWS, width), 0) == first + head_of((ROWS, width), 1)
    return y2, jnp.where(own, q.astype(f32), 0.0).astype(bf16)


def self_kernel(start, g_self, wvs, wos, part_out):
    _, s1 = self_parts(start, g_self, wvs)
    part_out[...] = nn(s1, wos[...])[:8]


def query_kernel(scal, part_a, part_b, start, g_cross, wq, wk, qk_out, h1_out):
    h1_out[...] = row_of(start) + (part_a[0:1] + part_b[0:1])
    _, qm = query_parts(scal, h1_out, g_cross, wq)
    qk_out[...] = nn(qm, wk[...])


def select_docs(height, width):
    r, c = iota((height, width), 0), iota((height, width), 1)
    return (((r // BLOCK) == (c % ROWS)) & ((r % BLOCK) == (c // ROWS))).astype(bf16)


def load_kernel(lo, hi, scal, sizes, enc, *refs):
    held, sems = refs[-2:]
    count = sizes[scal[1]]

    def piece(k):
        part = pl.ds(lo + k * BLOCK, BLOCK)
        return pltpu.make_async_copy(enc.at[part], held.at[part], sems.at[k])

    for k in range((hi - lo) // BLOCK):

        @pl.when(lo + k * BLOCK < count)
        def _():
            piece(k).start()

    for k in range((hi - lo) // BLOCK):

        @pl.when(lo + k * BLOCK < count)
        def _():
            piece(k).wait()


def first_doc(scal, sizes):
    groups = sizes.shape[0]

    def body(g, total):
        return total + jnp.where(g < scal[1], sizes[g], 0)

    return lax.fori_loop(0, groups, body, jnp.int32(0), unroll=groups <= 8)


def attend_kernel(base, scal, sizes, lengths, qa, qb, enc, *refs):
    p_out, e_out, ext_out, qk_s = refs[-4:]
    step = pl.program_id(0) + base
    tokens = enc.shape[1]
    count = sizes[scal[1]]
    block = pl.ds(step * BLOCK, BLOCK)
    tall = BLOCK * ROWS

    @pl.when(pl.program_id(0) == 0)
    def _():
        high, low = split2(qa[...] + qb[...])
        qk_s[0:ROWS] = high
        qk_s[ROWS : 2 * ROWS] = low

    @pl.when(step * BLOCK < count)
    def _():
        rows = enc[block].reshape(BLOCK * tokens, D)
        both = nt(qk_s[...], rows)
        logits = both[:ROWS] + both[ROWS:]
        logits = jnp.concatenate(
            [logits[:, b * tokens : (b + 1) * tokens] for b in range(BLOCK)], axis=0
        )
        begin = first_doc(scal, sizes)
        shown = []
        for b in range(BLOCK):
            slot = step * BLOCK + b
            doc = jnp.minimum(begin + slot, lengths.shape[0] - 1)
            length = jnp.where(slot < count, lengths[doc] - scal[0] * tokens, 0)
            shown.append(jnp.broadcast_to(length, (ROWS, tokens)))
        seen = jnp.concatenate(shown, axis=0)
        seen = iota((tall, tokens), 1) < seen
        logits = jnp.where(seen, logits, MASKED)
        peak = jnp.max(logits, axis=1, keepdims=True)
        raised = jnp.where(seen, jnp.exp(logits - peak), 0.0)
        total = jnp.sum(raised, axis=1, keepdims=True)
        p_out[...] = raised.reshape(BLOCK, ROWS, tokens)
        low = raised.astype(bf16)
        sums = []
        upper = iota((2 * ROWS, tokens), 0) < ROWS
        zero = jnp.zeros((2 * ROWS, tokens), bf16)
        for k in range(BLOCK // 2):
            pair = low[2 * ROWS * k : 2 * ROWS * (k + 1)]
            left = jnp.concatenate(
                [jnp.where(upper, pair, zero), jnp.where(upper, zero, pair)], axis=1
            )
            sums.append(nn(left, rows[2 * tokens * k : 2 * tokens * (k + 1)]))
        summed = jnp.concatenate(sums, axis=0).astype(bf16)
        e_out[...] = (
            nn(select_docs(HEADS * BLOCK, tall), summed)
            .astype(bf16)
            .reshape(HEADS, BLOCK, D)
        )
        gather = (iota((BLOCK, tall), 0) == iota((BLOCK, tall), 1) // ROWS).astype(bf16)
        parts = split3(peak) + split3(total)
        at = iota((tall, LANES), 1)
        extra = jnp.zeros((tall, LANES), f32)
        for k, part in enumerate(parts):
            extra = jnp.where(at // ROWS == k, part.astype(f32), extra)
        extra = jnp.where(at % ROWS == iota((tall, LANES), 0) % ROWS, extra, 0.0)
        ext_out[...] = nn(gather, extra.astype(bf16)).astype(bf16)

    @pl.when(step * BLOCK >= count)
    def _():
        p_out[...] = jnp.zeros_like(p_out)
        e_out[...] = jnp.zeros_like(e_out)
        ext_out[...] = jnp.where(iota((BLOCK, LANES), 1) < ROWS, MASKED, 0.0).astype(bf16)


def place_parts(scal, full, own, by2, by1, by3):
    height = own.shape[0]
    for mask, piece in ((0, own), (2, by2), (1, by1), (3, by3)):
        at = pl.multiple_of((scal[0] ^ mask) * height, height)
        full[pl.ds(at, height)] = piece[...]


def project_kernel(scal, summed, extra, own, by2, by1, by3, pay_out, wv):
    place_parts(scal, wv, own, by2, by1, by3)
    even = iota((summed.shape[1], LANES), 1) < HEAD_DIM
    for k in range(HEADS // 2):
        pair = wv[k * LANES : (k + 1) * LANES]
        one, two = nt(summed[2 * k], pair), nt(summed[2 * k + 1], pair)
        pay_out[:, k * LANES : (k + 1) * LANES] = jnp.where(even, one, two).astype(bf16)
    pay_out[:, D:] = extra[...]


def decode(pay):
    extra = pay[:, D:].astype(f32)

    def lane(k):
        return pltpu.roll(extra, LANES - k * ROWS, 1) if k else extra

    first = iota(extra.shape, 1) < ROWS
    peak = jnp.where(first, (lane(0) + lane(1)) + lane(2), 0.0)
    total = jnp.where(first, (lane(3) + lane(4)) + lane(5), 0.0)
    return peak, total


def merge(one, two):
    peak1, total1 = decode(one)
    peak2, total2 = decode(two)
    peak = jnp.maximum(peak1, peak2)
    up1, up2 = jnp.exp(peak1 - peak), jnp.exp(peak2 - peak)
    total = up1 * total1 + up2 * total2
    first = iota(peak.shape, 1) < ROWS
    up1, up2 = jnp.where(first, up1, 0.0), jnp.where(first, up2, 0.0)
    context = spread(up1) * one[:, :D].astype(f32) + spread(up2) * two[:, :D].astype(f32)
    return peak, total, context


def ordered(bit, own, other):
    swap = jnp.broadcast_to(bit, own.shape) == 1
    return jnp.where(swap, other, own), jnp.where(swap, own, other)


def merge_kernel(scal, own, other, pay_out):
    one, two = ordered(scal[0] & 1, own[...].astype(f32), other[...].astype(f32))
    peak, total, context = merge(one, two)
    pay_out[:, :D] = context.astype(bf16)
    extra = jnp.zeros(peak.shape, f32)
    at = iota(peak.shape, 1) // ROWS
    for k, part in enumerate(split3(peak) + split3(total)):
        part = part.astype(f32)
        extra = jnp.where(at == k, pltpu.roll(part, k * ROWS, 1) if k else part, extra)
    pay_out[:, D:] = extra.astype(bf16)


def own_half(scal, rows, held, out):
    half = out.shape[0]
    held[...] = rows
    out[...] = held[pl.ds(pl.multiple_of((scal[0] & 1) * half, half), half)]


def forward_kernel(
    scal, own, other, first, h1, wo_own, wo_by2, wo_by1, wo_by3, g_ff, win, wdown,
    c_out, c32_out, scale_out, h2_out, z_out, part_out, wo, c_s,
):
    place_parts(scal, wo, wo_own, wo_by2, wo_by1, wo_by3)
    bit = lax.shift_right_logical(scal[0], 1) & 1
    one, two = ordered(bit, own[...].astype(f32), other[...].astype(f32))
    peak, total, context = merge(one, two)
    lanes = iota(peak.shape, 1) < ROWS
    inverse = jnp.where(lanes & (total > 0.0), 1.0 / jnp.where(total > 0.0, total, 1.0), 0.0)
    context = context * spread(inverse)
    mine, _ = decode(first[...].astype(f32))
    scale_out[...] = jnp.exp(jnp.minimum(mine - peak, 0.0)) * inverse
    c32_out[...] = context
    low = context.astype(bf16)
    own_half(scal, low, c_s, c_out)
    h2 = h1[...] + nn(low, wo[...])
    h2_out[...] = h2
    n2, _ = rms_parts(h2)
    y3 = (n2 * row_of(g_ff)).astype(bf16)
    z = nn(y3, win[...])
    z_out[...] = z
    u = (z * phi(z)).astype(bf16)
    part_out[...] = nn(u, wdown[...]).astype(bf16)


def score_kernel(
    scal, part_a, part_b, h2, z, g_final, row, wdown, win,
    scores_out, n3_out, dh3_out, part_out,
):
    h3 = h2[...] + (part_a[...].astype(f32) + part_b[...].astype(f32))
    n3, r3 = rms_parts(h3)
    n3_out[...] = n3
    wanted = jnp.broadcast_to(row_of(g_final) * row_of(row) * FACTOR, (8, D))
    scores = nt(wanted, n3, EXACT)[0:1]
    slots = n3.shape[0]
    groups = scores_out.shape[0]
    wide = jnp.concatenate([scores, jnp.zeros((1, LANES - slots), f32)], axis=1)
    scores_out[...] = jnp.where(iota((groups, LANES), 0) == scal[1], wide, 0.0)
    dh3 = rms_back(wanted[0:1], n3, r3).astype(bf16)
    dh3_out[...] = dh3
    du = nt(dh3, wdown[...])
    dz = (du * gelu_slope(z[...])).astype(bf16)
    part_out[...] = nt(dz, win[...]).astype(bf16)


def list_kernel(scal, sizes, lens, sc_a, sc_b, rel, scores_out, loss_out, ds_out, mine_out):
    groups = sc_a.shape[0]
    docs = ds_out.shape[1]
    wide = docs + LANES
    queries = lens.shape[0]
    relevance = rel[...].reshape(1, docs)
    scores = sc_a[...] + sc_b[...]
    lane = iota((8, LANES), 1)
    blank = jnp.zeros((8, wide - LANES), f32)
    placed = jnp.zeros((8, wide), f32)
    start = jnp.int32(0)
    for g in range(groups):
        kept = jnp.where(lane < sizes[g], scores[g : g + 1], 0.0)
        placed = placed + pltpu.roll(jnp.concatenate([kept, blank], axis=1), start, 1)
        start = start + sizes[g]
    at = iota((queries, 1), 0)

    def one_list(j, found):
        begin, begins, ends = found
        end = begin + lens[j]
        return end, jnp.where(at == j, begin, begins), jnp.where(at == j, end, ends)

    none = jnp.zeros((queries, 1), i32)
    _, begins, ends = lax.fori_loop(
        0, queries, one_list, (jnp.int32(0), none, none), unroll=queries <= 32
    )
    values = placed[0:1, :docs]
    scores_out[...] = values.reshape(scores_out.shape)
    place = iota((queries, docs), 1)
    member = (place >= begins) & (place < ends)
    peak = jnp.max(jnp.where(member, values, MASKED), axis=1, keepdims=True)
    raised = jnp.where(member, jnp.exp(jnp.where(member, values - peak, 0.0)), 0.0)
    log_total = peak + jnp.log(jnp.sum(raised, axis=1, keepdims=True))
    weight = jnp.sum(jnp.where(member, relevance, 0.0), axis=1, keepdims=True)
    target = jnp.where(member, relevance / weight, 0.0)
    picked = jnp.sum(target * values, axis=1, keepdims=True)
    loss_out[...] = jnp.sum(log_total - picked, axis=0, keepdims=True) / queries
    chance = jnp.where(member, jnp.exp(jnp.where(member, values - log_total, 0.0)), 0.0)
    ds = jnp.sum(chance - target, axis=0, keepdims=True) / queries
    ds_out[...] = ds
    ds = jnp.broadcast_to(jnp.concatenate([ds, jnp.zeros((1, LANES), f32)], axis=1), (8, wide))
    start = first_doc(scal, sizes)
    back = pltpu.roll(ds, lax.rem(wide - start, wide), 1)[:, :LANES]
    mine_out[...] = jnp.where(lane < sizes[scal[1]], back, 0.0)


def context_kernel(
    scal, part_a, part_b, h2, dh3, c32, g_ff, wo_own, wo_by2, wo_by1, wo_by3,
    dh2_out, half_out, dc_out, own_out, inner_out, ff_out, wout, both_s,
):
    place_parts(scal, wout, wo_own, wo_by2, wo_by1, wo_by3)
    n2, r2 = rms_parts(h2[...])
    dy3 = part_a[...].astype(f32) + part_b[...].astype(f32)
    ff_out[...] = dy3 * n2
    dh2 = (dh3[...].astype(f32) + rms_back(dy3 * row_of(g_ff), n2, r2)).astype(bf16)
    dh2_out[...] = dh2
    own_half(scal, jnp.concatenate([dh3[...], dh2], axis=1), both_s, half_out)
    dc = nt(dh2, wout[...]).astype(bf16)
    dc_out[...] = dc
    own_out[...] = nt(dh2, wo_own[...]).astype(bf16)
    hot = (head_of((D, LANES), 0) == iota((D, LANES), 1)).astype(f32)
    inner_out[...] = nn(dc.astype(f32) * c32[...], hot, EXACT)


def column(rows):
    tall = BLOCK * ROWS
    pick = (iota((tall, BLOCK), 0) // ROWS == iota((tall, BLOCK), 1)).astype(f32)
    wide = nn(pick, rows, EXACT)
    own = iota((tall, LANES), 0) % ROWS == iota((tall, LANES), 1)
    return jnp.sum(jnp.where(own, wide, 0.0), axis=1, keepdims=True)


def back_kernel(
    scal, sizes, enc, p, scale, inner, dc, wv_own, wv_by2, wv_by1, wv_by3,
    dap_out, vd_out, wv,
):
    step = pl.program_id(0)

    @pl.when(step == 0)
    def _():
        place_parts(scal, wv, wv_own, wv_by2, wv_by1, wv_by3)

    tokens = enc.shape[1]
    tall = BLOCK * ROWS

    @pl.when(step * BLOCK < sizes[scal[1]])
    def _():
        rows = enc[pl.ds(step * BLOCK, BLOCK)].reshape(BLOCK * tokens, D)
        pick = (iota((tall, BLOCK), 0) // ROWS == iota((tall, BLOCK), 1)).astype(bf16)
        own = (iota((tall, D), 0) % ROWS) == head_of((tall, D), 1)
        grad = jnp.where(own, nn(pick, dc[...]), 0.0).astype(bf16)
        vd = nn(grad, wv[...]).astype(bf16)
        vd_out[...] = vd.reshape(BLOCK, ROWS, D)
        grad_probs = []
        for k in range(BLOCK // 2):
            pair = nt(
                vd[2 * ROWS * k : 2 * ROWS * (k + 1)],
                rows[2 * tokens * k : 2 * tokens * (k + 1)],
            )
            grad_probs += [pair[:ROWS, :tokens], pair[ROWS:, tokens:]]
        grad_probs = jnp.concatenate(grad_probs, axis=0)
        prob = p[...].reshape(tall, tokens) * column(scale[...])
        da = (prob * (grad_probs - column(inner[...]))).astype(bf16)
        dap_out[:, :ROWS] = da.reshape(BLOCK, ROWS, tokens)
        dap_out[:, ROWS:] = prob.astype(bf16).reshape(BLOCK, ROWS, tokens)

    @pl.when(step * BLOCK >= sizes[scal[1]])
    def _():
        dap_out[...] = jnp.zeros_like(dap_out)
        vd_out[...] = jnp.zeros_like(vd_out)


def key_sum_kernel(scal, sizes, ds, enc, da, dh2, n3, ff, sums_out):
    step = pl.program_id(0)
    tokens = enc.shape[1]
    tall = BLOCK * ROWS

    @pl.when(step == 0)
    def _():
        slots = dh2.shape[0]
        row = ds[...][:, :slots] * (1.0 / PARTS)
        at = iota((ROWS, D), 0)
        out = jnp.where(at == HEADS, nn(row, dh2[...].astype(f32), EXACT)[0:1], 0.0)
        out = jnp.where(at == HEADS + 1, nn(row, n3[...], EXACT)[0:1], out)
        sums_out[...] = jnp.where(at == HEADS + 2, nn(row, ff[...], EXACT)[0:1], out)

    @pl.when(step * BLOCK < sizes[scal[1]])
    def _():
        rows = enc[pl.ds(step * BLOCK, BLOCK)].reshape(BLOCK * tokens, D)
        own_slot = iota((tall, LANES), 1) == step * BLOCK + iota((tall, LANES), 0) // ROWS
        ds_col = jnp.sum(jnp.where(own_slot, ds[0:1], 0.0), axis=1, keepdims=True)
        scaled = (da[...].reshape(tall, tokens).astype(f32) * ds_col).astype(bf16)
        flat = jnp.concatenate(
            [scaled[ROWS * b : ROWS * (b + 1)] for b in range(BLOCK)], axis=1
        )
        sums_out[...] += nn(flat, rows)


def enc_grad_kernel(base, scal, sizes, ds, qa, qb, dap, vd, *refs):
    grad_out = refs[-1]
    step = pl.program_id(0) + base

    @pl.when(step * BLOCK < sizes[scal[1]])
    def _():
        qk = qa[...] + qb[...]
        lane = iota((1, LANES), 1)
        for b in range(BLOCK):
            scale = jnp.sum(
                jnp.where(lane == step * BLOCK + b, ds[0:1], 0.0), axis=1, keepdims=True
            )
            right = jnp.concatenate([qk, vd[b].astype(f32)], axis=0) * scale
            grad_out[b] = tn(dap[b], right.astype(bf16)).astype(bf16)

    @pl.when(step * BLOCK >= sizes[scal[1]])
    def _():
        grad_out[...] = jnp.zeros_like(grad_out)


def share_kernel(scal, summed, scale, keep_out, send_out):
    core = scal[0] & 1
    lane = iota(scale.shape, 1)
    for out, bit in ((send_out, 1 - core), (keep_out, core)):
        for y in range(out.shape[0]):
            for k in range(out.shape[1]):
                head = (2 * y + bit) * out.shape[1] + k
                col = jnp.sum(jnp.where(lane == head, scale[...], 0.0), axis=1, keepdims=True)
                out[y, k] = (summed[head].astype(f32) * col).astype(bf16)


def away_kernel(scal, keep, got, out):
    part = 1 - (lax.shift_right_logical(scal[0], 1) & 1)
    for h in range(out.shape[0]):
        out[h] = (keep[part, h].astype(f32) + got[part, h].astype(f32)).astype(bf16)


def value_kernel(scal, keep, got, other, dc, ds, grad_out):
    slots = keep.shape[2]
    part = lax.shift_right_logical(scal[0], 1) & 1
    own_slot = iota((slots, LANES), 0) == iota((slots, LANES), 1)
    ds_col = jnp.sum(jnp.where(own_slot, ds[0:1], 0.0), axis=1, keepdims=True)
    grad = (dc[...].astype(f32) * ds_col).astype(bf16)
    for h in range(keep.shape[1]):
        pair = (keep[part, h].astype(f32) + got[part, h].astype(f32)).astype(bf16)
        summed = (pair.astype(f32) + other[h].astype(f32)).astype(bf16)
        out = tn(grad[:, h * HEAD_DIM : (h + 1) * HEAD_DIM], summed)
        grad_out[h * HEAD_DIM : (h + 1) * HEAD_DIM] = out.astype(bf16)


def document_picks(order, tile, scal, sizes, held, first):
    groups = 1 << len(order)
    half = held // groups
    core = scal[0] & 1
    doc = first + iota((tile, 1), 0)

    def one_group(g, found):
        start, at, upper = found
        mask = g ^ scal[1]
        pos = 0
        for k, bit in enumerate(order):
            pos = pos + (lax.shift_right_logical(mask, bit.bit_length() - 1) & 1) * (1 << k)
        slot = doc - start
        inside = (slot >= 0) & (slot < sizes[g])
        later = (slot >= half).astype(i32)
        at = jnp.where(inside, pos * half + slot - half * later, at)
        return start + sizes[g], at, jnp.where(inside, later, upper)

    zero = jnp.zeros((tile, 1), i32)
    _, at, upper = lax.fori_loop(
        0, groups, one_group, (jnp.int32(0), zero, zero), unroll=groups <= 8
    )
    hit = iota((tile, held), 1) == at
    mine = (hit & (upper == core)).astype(bf16)
    theirs = (hit & (upper != core)).astype(bf16)
    return lambda own, other: (nn(mine, own[...]) + nn(theirs, other[...])).astype(bf16)


def ds_column(ds, first, tile):
    eye = iota((tile, tile), 0) == iota((tile, tile), 1)
    return jnp.sum(jnp.where(eye, ds[0:1, pl.ds(first, tile)], 0.0), axis=1, keepdims=True)


def over_tiles(docs, tile, one_tile):
    one_tile(0, True)
    if docs > tile:

        @pl.loop(1, docs // tile)
        def _(t):
            one_tile(pl.multiple_of(t * tile, tile), False)


def put(out, value, new):
    if new:
        out[...] = value
    else:
        out[...] += value


def weights_kernel(
    order, tile, scal, sizes, c_own, c_other, both_own, both_other, ds,
    h1, g_ff, wo_own, wo_by2, wo_by1, wo_by3, win, wdown,
    win_out, wdown_out, wout_out, wout,
):
    place_parts(scal, wout, wo_own, wo_by2, wo_by1, wo_by3)

    def one_tile(first, new):
        rows = document_picks(order, tile, scal, sizes, c_own.shape[0], first)
        c = rows(c_own, c_other)
        h2 = h1[...] + nn(c, wout[...])
        n2, _ = rms_parts(h2)
        y3 = (n2 * row_of(g_ff)).astype(bf16)
        z = nn(y3, win[...])
        u = (z * phi(z)).astype(bf16)
        both = rows(both_own, both_other).astype(f32) * ds_column(ds, first, tile)
        dh3, dh2 = both[:, :D].astype(bf16), both[:, D:].astype(bf16)
        dz = (nt(dh3, wdown[...]) * gelu_slope(z)).astype(bf16)
        put(win_out, tn(y3, dz), new)
        put(wdown_out, tn(u, dh3), new)
        width = wout_out.shape[0]
        pick = (iota((D, width), 0) == scal[0] * width + iota((D, width), 1)).astype(bf16)
        put(wout_out, tn(nn(c, pick).astype(bf16), dh2), new)

    over_tiles(ds.shape[1], tile, one_tile)


def key_kernel(scal, sum_a, sum_b, h1, g_cross, wk, wq, key_out, query_out, part_out):
    y2, qm = query_parts(scal, h1, g_cross, wq)
    g = sum_a[...] + sum_b[...]
    g = jnp.where(iota((ROWS, D), 0) < HEADS, g, 0.0)
    high, low = split2(g)
    both = jnp.concatenate([high, low], axis=0)
    dq = nt(both, wk[...])
    dq = dq[:ROWS] + dq[ROWS:]
    width = dq.shape[1]
    first = scal[0] * (width // HEAD_DIM)
    own = iota((ROWS, width), 0) == first + head_of((ROWS, width), 1)
    dq = jnp.sum(jnp.where(own, dq, 0.0), axis=0, keepdims=True)
    key_out[...] = tn(jnp.concatenate([qm, qm], axis=0), both)
    dq_parts = stack3(dq)
    query_out[...] = tn(dq_parts, repeat3(y2[0:1]))
    part = jnp.sum(nn(dq_parts, wq[...]), axis=0, keepdims=True)
    part_out[...] = jnp.broadcast_to(part, (8, D))


def hidden_kernel(
    part_a, part_b, sum_a, sum_b, h1, g_cross, start, g_self, wos, wvs, g_final, row,
    dh1_out, wos_out, wvs_out, part_out, cross_out, final_out, row_out, ff_out,
):
    y1, s1 = self_parts(start, g_self, wvs)
    dy2 = part_a[0:1] + part_b[0:1]
    sums = sum_a[...] + sum_b[...]
    n1, r1 = rms_parts(h1[...])
    cross_out[...] = (dy2 * n1).reshape(cross_out.shape)
    dh1 = sums[HEADS : HEADS + 1] + rms_back(dy2 * row_of(g_cross), n1, r1)
    dh1_out[...] = dh1
    dh1_parts = stack3(dh1)
    wos_out[...] = tn(repeat3(s1[0:1]), dh1_parts)
    ds1 = jnp.sum(nt(dh1_parts, wos[...]), axis=0, keepdims=True)
    ds1_parts = stack3(ds1)
    wvs_out[...] = tn(ds1_parts, repeat3(y1[0:1]))
    part = jnp.sum(nn(ds1_parts, wvs[...]), axis=0, keepdims=True)
    part_out[...] = jnp.broadcast_to(part, (8, D))
    total = sums[HEADS + 1 : HEADS + 2] * FACTOR
    final_out[...] = (total * row_of(row)).reshape(final_out.shape)
    row_out[...] = (total * row_of(g_final)).reshape(row_out.shape)
    ff_out[...] = sums[HEADS + 2 : HEADS + 3].reshape(ff_out.shape)


def start_kernel(part_a, part_b, dh1, start, g_self, gain_out, start_out):
    dy1 = part_a[0:1] + part_b[0:1]
    n0, r0 = rms_parts(row_of(start))
    gain_out[...] = (dy1 * n0).reshape(gain_out.shape)
    back = dh1[...] + rms_back(dy1 * row_of(g_self), n0, r0)
    start_out[...] = back.reshape(start_out.shape)


def shape(dims, dtype=f32):
    return jax.ShapeDtypeStruct(dims, dtype)


def whole_spec(memory=pltpu.VMEM):
    return pl.BlockSpec(memory_space=memory)


def name_of(kernel):
    return getattr(kernel, "func", kernel).__name__


def in_hbm(x):
    return pltpu.with_memory_space_constraint(x, pltpu.HBM)


def plain(kernel, outs, *args, smem=0, flops=0, limit=12, scratch=()):
    size = sum(a.size * a.dtype.itemsize for a in args)
    return pl.pallas_call(
        kernel,
        out_shape=outs,
        in_specs=[whole_spec(pltpu.SMEM if k < smem else pltpu.VMEM) for k in range(len(args))],
        out_specs=jax.tree.map(lambda _: whole_spec(), outs),
        scratch_shapes=list(scratch),
        compiler_params=pltpu.CompilerParams(vmem_limit_bytes=limit * MIB),
        cost_estimate=pl.CostEstimate(flops=flops, bytes_accessed=size, transcendentals=0),
        name=name_of(kernel),
    )(*args)


def gridded(kernel, steps, scalars, ins, outs, scratch=(), flops=0, limit=14, onto=()):
    size = sum(a.size * a.dtype.itemsize for a, _, _ in ins)
    size += sum(s.size * s.dtype.itemsize for s, _, _ in outs)
    count = len(scalars) + len(ins)
    return pl.pallas_call(
        kernel,
        out_shape=[s for s, _, _ in outs],
        grid_spec=pltpu.PrefetchScalarGridSpec(
            num_scalar_prefetch=len(scalars),
            grid=(steps,),
            in_specs=[
                pl.BlockSpec(block, index) if block else whole_spec() for _, block, index in ins
            ]
            + [pl.BlockSpec(memory_space=pl.ANY)] * len(onto),
            out_specs=[pl.BlockSpec(block, index) for _, block, index in outs],
            scratch_shapes=list(scratch),
        ),
        input_output_aliases={count + k: k for k in range(len(onto))},
        compiler_params=pltpu.CompilerParams(
            vmem_limit_bytes=limit * MIB, dimension_semantics=("arbitrary",)
        ),
        cost_estimate=pl.CostEstimate(flops=flops, bytes_accessed=size, transcendentals=0),
        name=name_of(kernel),
    )(*scalars, *[a for a, _, _ in ins], *onto)


def bits_of(size):
    return [1 << b for b in range(size.bit_length() - 1)]


def long_first(size):
    bits = bits_of(size)
    return bits[1:] + bits[:1]


def swap(x, axis, bit):
    size = lax.axis_size(axis)
    return lax.ppermute(x, axis, [(i, i ^ bit) for i in range(size)])


def after(x, *deps):
    return lax.optimization_barrier((x, *deps))[0]


def add(x, y):
    return (x.astype(f32) + y.astype(f32)).astype(x.dtype)


def sum_last(x, steps):
    for axis, bit in steps[:-1]:
        x = add(x, swap(x, axis, bit))
    axis, bit = steps[-1]
    return x, swap(x, axis, bit)


def per_device(
    enc_out,
    enc_len,
    group_docs,
    list_len,
    relevance,
    start_token,
    score_row,
    g_self,
    w_value_self,
    w_out_self,
    g_cross,
    w_query,
    w_key,
    w_value,
    w_out,
    g_ff,
    w_in,
    w_down,
    g_final,
):
    groups = lax.axis_size("docs")
    parts = lax.axis_size("heads")
    assert parts == PARTS
    me_g = lax.axis_index("docs")
    me_j = lax.axis_index("heads")
    slots, tokens = enc_out.shape[:2]
    docs = enc_len.shape[0]
    width = w_value.shape[1]
    own_heads = HEADS // parts
    hidden = w_in.shape[1]
    blocks = slots // BLOCK
    over_heads = [("heads", 1), ("heads", 2)]
    order = long_first(groups)
    over_docs = [("docs", bit) for bit in order]

    scal = jnp.stack([me_j, me_g])
    wvs_t, wq_t, wk_t, wv_t = (w.T for w in (w_value_self, w_query, w_key, w_value))

    wv_by1, wo_by1 = swap(wv_t, "heads", 1), swap(w_out, "heads", 1)

    part = plain(
        self_kernel,
        shape((8, D)),
        *map(in_hbm, (start_token, g_self, wvs_t, w_out_self)),
    )

    def load(lo, hi, onto=()):
        return pl.pallas_call(
            functools.partial(load_kernel, lo, hi),
            out_shape=pltpu.VMEM(enc_out.shape, bf16),
            in_specs=[whole_spec(pltpu.SMEM)] * 2
            + [whole_spec(pltpu.HBM)]
            + [whole_spec()] * len(onto),
            out_specs=whole_spec(),
            scratch_shapes=[pltpu.SemaphoreType.DMA(((hi - lo) // BLOCK,))],
            input_output_aliases={3: 0} if onto else {},
            compiler_params=pltpu.CompilerParams(vmem_limit_bytes=MIB),
            cost_estimate=pl.CostEstimate(
                flops=0, bytes_accessed=(hi - lo) * tokens * D * 4, transcendentals=0
            ),
            name="load_kernel",
        )(scal, group_docs, in_hbm(enc_out), *onto)

    middle = slots // 2
    part = add(part, swap(part, "heads", 1))
    part_a, part_b = part, swap(part, "heads", 2)
    held = load(0, middle)
    part_b, held = lax.optimization_barrier((part_b, held))
    qk, h1 = plain(
        query_kernel,
        [shape((ROWS, D)), shape((1, D))],
        scal,
        part_a,
        part_b,
        *map(in_hbm, (start_token, g_cross, wq_t, wk_t)),
        smem=1,
    )
    qk, held = lax.optimization_barrier((qk, held))
    qk_a, qk_b = sum_last(qk, over_heads)
    held = load(middle, slots, (held,))

    const2 = lambda i, *_: (0, 0)
    step2 = lambda i, *_: (i, 0)
    step3 = lambda i, *_: (i, 0, 0)
    pass_flops = 2 * slots * tokens * D * 256

    def attend(base, steps, onto=()):
        return gridded(
            functools.partial(attend_kernel, base),
            steps,
            [scal, group_docs, enc_len],
            [
                (qk_a, (ROWS, D), const2),
                (qk_b, (ROWS, D), const2),
                (held, None, None),
            ],
            [
                (
                    shape((slots, ROWS, tokens)),
                    (BLOCK, ROWS, tokens),
                    lambda i, *_: (i + base, 0, 0),
                ),
                (
                    shape((HEADS, slots, D), bf16),
                    (HEADS, BLOCK, D),
                    lambda i, *_: (0, i + base, 0),
                ),
                (
                    shape((slots, LANES), bf16),
                    (BLOCK, LANES),
                    lambda i, *_: (i + base, 0),
                ),
            ],
            scratch=[pltpu.VMEM((2 * ROWS, D), bf16)],
            flops=2 * pass_flops * steps // blocks,
            onto=onto,
        )

    split = 4
    wv_by2 = swap(after(wv_t, qk_b), "heads", 2)
    prob, summed, extra = attend(0, split)
    prob, wv_by2 = lax.optimization_barrier((prob, wv_by2))
    wv_by3 = swap(wv_by2, "heads", 1)
    wo_by2 = swap(after(w_out, wv_by2), "heads", 2)
    prob, summed, extra = attend(split, blocks - split, (prob, summed, extra))
    wv_parts = (wv_t, wv_by2, wv_by1, wv_by3)
    full = [pltpu.VMEM((D, D), bf16)]
    pay = plain(
        project_kernel,
        shape((slots, D + LANES), bf16),
        scal,
        summed,
        extra,
        *wv_parts,
        smem=1,
        scratch=full,
    )
    wo_by3 = swap(wo_by2, "heads", 1)
    wo_parts = (w_out, wo_by2, wo_by1, wo_by3)
    merged = plain(
        merge_kernel, shape(pay.shape, bf16), scal, pay, swap(pay, "heads", 1), smem=1
    )
    other = swap(merged, "heads", 2)

    c, c32, scale, h2, z, part = plain(
        forward_kernel,
        [
            shape((slots // 2, D), bf16),
            shape((slots, D)),
            shape((slots, LANES)),
            shape((slots, D)),
            shape((slots, hidden)),
            shape((slots, D), bf16),
        ],
        scal,
        merged,
        other,
        pay,
        h1,
        *wo_parts,
        g_ff,
        w_in,
        w_down,
        smem=1,
        scratch=full + [pltpu.VMEM((slots, D), bf16)],
    )

    half = slots // 2

    def grow(x, k):
        return jnp.concatenate([x, swap(x, *over_docs[k])], axis=0)

    def tie(*xs):
        return lax.optimization_barrier(xs)

    last = len(over_docs) - 1
    part = add(part, swap(part, "heads", 1))
    part, c, summed = tie(part, c, summed)
    part_a, part_b = part, swap(part, "heads", 2)
    c_all = grow(c, 0)
    keep, sent = plain(
        share_kernel, [shape((2, own_heads, slots, D), bf16)] * 2, scal, summed, scale, smem=1
    )
    part_b, c_all, sent = tie(part_b, c_all, sent)
    scores, n3, dh3, part = plain(
        score_kernel,
        [
            shape((groups, LANES)),
            shape((slots, D)),
            shape((slots, D), bf16),
            shape((slots, D), bf16),
        ],
        scal,
        part_a,
        part_b,
        h2,
        z,
        g_final,
        score_row,
        w_down,
        w_in,
        smem=1,
    )
    part = add(part, swap(part, "heads", 1))
    got = swap(sent, "heads", 1)
    part_a, part_b = part, swap(part, "heads", 2)
    near_first = [("docs", bit) for bit in bits_of(groups)]
    score_a, score_b = scores, swap(scores, *near_first[0])
    part_b, got, score_b = tie(part_b, got, score_b)
    for k in range(1, last):
        score_a = score_a + score_b
        score_b = swap(score_a, *near_first[k])
    for k in range(1, last):
        c_all = grow(c_all, k)
    dh2, grads, dc, dc_own, inner, ff = plain(
        context_kernel,
        [
            shape((slots, D), bf16),
            shape((half, 2 * D), bf16),
            shape((slots, D), bf16),
            shape((slots, width), bf16),
            shape((slots, LANES)),
            shape((slots, D)),
        ],
        scal,
        part_a,
        part_b,
        h2,
        dh3,
        c32,
        g_ff,
        *wo_parts,
        smem=1,
        scratch=full + [pltpu.VMEM((slots, 2 * D), bf16)],
    )

    away = plain(
        away_kernel, shape((own_heads, slots, D), bf16), scal, keep, got, smem=1
    )
    score_a = score_a + score_b
    score_a, c_all, away, dc, grads = tie(score_a, c_all, away, dc, grads)
    score_b = swap(score_a, *near_first[last])
    other = swap(away, "heads", 2)
    grads = grow(grads, 0)
    c_all = grow(c_all, last)

    dap, vd = gridded(
        back_kernel,
        blocks,
        [scal, group_docs],
        [
            (held, None, None),
            (prob, (BLOCK, ROWS, tokens), step3),
            (scale, (BLOCK, LANES), step2),
            (inner, (BLOCK, LANES), step2),
            (dc, (BLOCK, D), step2),
        ]
        + [(w, (width, D), const2) for w in wv_parts],
        [
            (shape((slots, 2 * ROWS, tokens), bf16), (BLOCK, 2 * ROWS, tokens), step3),
            (shape((slots, ROWS, D), bf16), (BLOCK, ROWS, D), step3),
        ],
        scratch=full,
        flops=pass_flops,
    )
    dap, score_b, grads, c_all, other = tie(dap, score_b, grads, c_all, other)
    all_scores, loss, ds_docs, ds_mine = plain(
        list_kernel,
        [shape((docs,)), shape((1, 1)), shape((1, docs)), shape((8, LANES))],
        scal,
        group_docs,
        list_len,
        score_a,
        score_b,
        in_hbm(relevance),
        smem=3,
    )
    value_part = plain(
        value_kernel,
        shape((width, D), bf16),
        scal,
        keep,
        got,
        other,
        dc_own,
        ds_mine,
        smem=1,
    )
    dap, value_part, grads = tie(dap, value_part, grads)
    value_far = swap(value_part, *near_first[0])
    grads_far = swap(grads, *over_docs[1])
    (sums,) = gridded(
        key_sum_kernel,
        blocks,
        [scal, group_docs],
        [
            (ds_mine, (8, LANES), const2),
            (held, None, None),
            (dap, (BLOCK, ROWS, tokens), step3),
            (dh2, (slots, D), const2),
            (n3, (slots, D), const2),
            (ff, (slots, D), const2),
        ],
        [(shape((ROWS, D)), (ROWS, D), const2)],
        flops=pass_flops,
    )
    sums, value_far = tie(sums, value_far)
    value_part = add(value_part, value_far)

    def enc_grads(base, steps, onto=()):
        def moved(i, *_):
            return (i + base, 0, 0)

        return gridded(
            functools.partial(enc_grad_kernel, base),
            steps,
            [scal, group_docs],
            [
                (ds_mine, (8, LANES), const2),
                (qk_a, (ROWS, D), const2),
                (qk_b, (ROWS, D), const2),
                (dap, (BLOCK, 2 * ROWS, tokens), moved),
                (vd, (BLOCK, ROWS, D), moved),
            ],
            [(shape(enc_out.shape, bf16), (BLOCK, tokens, D), moved)],
            flops=pass_flops * steps // blocks,
            onto=onto,
        )

    sums = add(sums, swap(sums, "heads", 1))
    steps = [over_heads[1]] + near_first
    share = [2, 2, 2] + [0] * len(steps)
    enc_grad, done = (), 0
    sum_a = sums
    value_step, grads_step = 1, 1
    for k, step in enumerate(steps):
        sum_b = swap(sum_a, *step)
        if k == 1:
            value_far = swap(value_part, *near_first[1])
        if share[k]:
            enc_grad = tuple(enc_grads(done, share[k], enc_grad))
            done += share[k]
        if k < len(steps) - 1:
            sum_b, *enc_grad = tie(sum_b, *enc_grad)
            if k >= 2:
                sum_b, value_far, grads_far = tie(sum_b, value_far, grads_far)
                value_part = add(value_part, value_far)
                grads = jnp.concatenate([grads, grads_far], axis=0)
                if k < last:
                    value_far = swap(value_part, *near_first[k])
                    grads_far = swap(grads, *over_docs[k])
            sum_a = sum_a + sum_b
    (enc_grad,) = enc_grad
    value_part, sum_b = tie(value_part, sum_b)
    grads = grow(grads, last)
    c_all, grads = ((x, swap(x, "heads", 1)) for x in (c_all, grads))
    value_a, value_b = value_part, swap(value_part, *near_first[last])
    value_grad = (value_a.astype(f32) + value_b.astype(f32)).T

    w_in_grad, w_down_grad, w_out_grad = plain(
        functools.partial(weights_kernel, order, 384),
        [shape((D, hidden)), shape((hidden, D)), shape((width, D))],
        scal,
        group_docs,
        *c_all,
        *grads,
        ds_docs,
        h1,
        g_ff,
        *wo_parts,
        w_in,
        w_down,
        smem=2,
        flops=10 * docs * D * hidden,
        limit=60 if docs > 384 else 36,
        scratch=full,
    )

    key_grad, query_grad, part = plain(
        key_kernel,
        [shape((width, D)), shape((width, D)), shape((8, D))],
        scal,
        sum_a,
        sum_b,
        h1,
        g_cross,
        wk_t,
        wq_t,
        smem=1,
    )
    part_a, part_b = sum_last(part, over_heads)
    part_b, w_in_grad = tie(part_b, w_in_grad)
    dh1, wos_grad, wvs_grad, part, cross, final_gain, row_grad, ff_gain = plain(
        hidden_kernel,
        [shape((1, D)), shape((width, D)), shape((width, D)), shape((8, D))] + [shape((D,))] * 4,
        part_a,
        part_b,
        sum_a,
        sum_b,
        h1,
        g_cross,
        start_token,
        g_self,
        w_out_self,
        wvs_t,
        g_final,
        score_row,
    )
    part_a, part_b = sum_last(part, over_heads)
    self_gain, start_grad = plain(
        start_kernel, [shape((D,))] * 2, part_a, part_b, dh1, start_token, g_self
    )

    return (
        all_scores,
        loss.reshape(()),
        enc_grad,
        start_grad,
        row_grad,
        self_gain,
        wvs_grad.T,
        wos_grad,
        cross,
        query_grad.T,
        key_grad.T,
        value_grad,
        w_out_grad,
        ff_gain,
        w_in_grad,
        w_down_grad,
        final_gain,
    )


def solution(mesh):
    placed = (
        P("docs", "heads", None),
        P(),
        P(),
        P(),
        P(),
        P(),
        P(),
        P(),
        P(None, "heads"),
        P("heads", None),
        P(),
        P(None, "heads"),
        P(None, "heads"),
        P(None, "heads"),
        P("heads", None),
        P(),
        P(None, "heads"),
        P("heads", None),
        P(),
    )
    return jax.shard_map(
        per_device,
        mesh=mesh,
        in_specs=placed,
        out_specs=(
            P(),
            P(),
            P("docs", "heads", None),
            P(),
            P(),
            P(),
            P(None, "heads"),
            P("heads", None),
            P(),
            P(None, "heads"),
            P(None, "heads"),
            P(None, "heads"),
            P("heads", None),
            P(),
            P(None, "heads"),
            P("heads", None),
            P(),
        ),
        check_vma=False,
    )
```

```python
import functools

import jax
import jax.numpy as jnp
from jax import lax
from jax.experimental import pallas as pl
from jax.experimental.pallas import tpu as pltpu
from jax.sharding import PartitionSpec as P

D = 768
HEADS = 12
HEAD_DIM = 64
ROWS = 16
BLOCK = 16
SPAN = 2 * BLOCK
LANES = 128
PANELS = D // LANES
PARTS = 4

EPSILON = 1e-06
MASKED = -1e30
FACTOR = D ** (-0.5)
ROOT_HALF = 0.5**0.5
DENSITY = 0.3989422804014327
f32, bf16, i32 = jnp.float32, jnp.bfloat16, jnp.int32
EXACT = lax.Precision.HIGHEST
MIB = 1 << 20


def nn(a, b, precision=None):
    return lax.dot_general(
        a, b, (((1,), (0,)), ((), ())), precision=precision, preferred_element_type=f32
    )


def nt(a, b, precision=None):
    return lax.dot_general(
        a, b, (((1,), (1,)), ((), ())), precision=precision, preferred_element_type=f32
    )


def tn(a, b, precision=None):
    return lax.dot_general(
        a, b, (((0,), (0,)), ((), ())), precision=precision, preferred_element_type=f32
    )


def iota(shape, dim):
    return lax.broadcasted_iota(i32, shape, dim)


def split2(x):
    high = x.astype(bf16)
    return high, (x - high.astype(f32)).astype(bf16)


def split3(x):
    high = x.astype(bf16)
    rest = x - high.astype(f32)
    mid = rest.astype(bf16)
    return high, mid, (rest - mid.astype(f32)).astype(bf16)


def stack3(row, height=ROWS):
    at = iota((height, row.shape[1]), 0)
    parts = split3(row)
    zero = jnp.zeros((), f32)
    out = jnp.where(at == 0, parts[0].astype(f32), zero)
    out = jnp.where(at == 1, parts[1].astype(f32), out)
    return jnp.where(at == 2, parts[2].astype(f32), out).astype(bf16)


def repeat3(row, height=ROWS):
    at = iota((height, row.shape[1]), 0)
    return jnp.where(at < 3, row.astype(f32), 0.0).astype(bf16)


def rms_parts(rows):
    scale = lax.rsqrt(jnp.mean(rows * rows, axis=-1, keepdims=True) + EPSILON)
    return rows * scale, scale


def rms_back(grad_normed, normed, scale):
    inner = jnp.mean(grad_normed * normed, axis=-1, keepdims=True)
    return scale * (grad_normed - normed * inner)


def phi(z):
    return 0.5 * (1.0 + lax.erf(z * ROOT_HALF))


def gelu_slope(z):
    return phi(z) + z * (DENSITY * jnp.exp(-0.5 * z * z))


def head_of(shape, dim):
    return iota(shape, dim) // HEAD_DIM


def spread(small):
    hot = (iota((LANES, D), 0) == head_of((LANES, D), 1)).astype(f32)
    return nn(small, hot, EXACT)


def row_of(ref):
    return ref[...].astype(f32).reshape(1, D)


def gained(n, gain):
    return jnp.broadcast_to(n * row_of(gain), (ROWS, D)).astype(bf16)


def self_parts(start, g_self, wvs):
    x0 = row_of(start)
    n0, _ = rms_parts(x0)
    y1 = gained(n0, g_self)
    return y1, nt(y1, wvs[...]).astype(bf16)


def query_parts(scal, h1, g_cross, wq):
    n1, _ = rms_parts(h1[...])
    y2 = gained(n1, g_cross)
    q = nt(y2, wq[...]).astype(bf16)
    width = q.shape[1]
    first = scal[0] * (width // HEAD_DIM)
    own = iota((ROWS, width), 0) == first + head_of((ROWS, width), 1)
    return y2, jnp.where(own, q.astype(f32), 0.0).astype(bf16)


def self_kernel(start, g_self, wvs, wos, part_out):
    _, s1 = self_parts(start, g_self, wvs)
    part_out[...] = nn(s1, wos[...])[:8]


def load_kernel(first, last, enc, since, scal, *refs):
    held, sems = refs[-2:]
    loads = []
    for k in range(first, last):
        part = pl.ds(k * BLOCK, BLOCK)
        loads.append(pltpu.make_async_copy(enc.at[part], held.at[part], sems.at[k - first]))
        loads[-1].start()
    for load in loads:
        load.wait()


def query_kernel(scal, part_a, part_b, start, g_cross, wq, wk, qk_out, h1_out):
    h1_out[...] = row_of(start) + (part_a[0:1] + part_b[0:1])
    _, qm = query_parts(scal, h1_out, g_cross, wq)
    qk_out[...] = nn(qm, wk[...])


def load_kernel(first, last, enc, since, scal, *refs):
    held, sems = refs[-2:]
    loads = []
    for k in range(first, last):
        part = pl.ds(k * BLOCK, BLOCK)
        loads.append(pltpu.make_async_copy(enc.at[part], held.at[part], sems.at[k - first]))
        loads[-1].start()
    for load in loads:
        load.wait()


def query_kernel(scal, part_a, part_b, start, g_cross, wq, wk, qk_out, h1_out):
    h1_out[...] = row_of(start) + (part_a[0:1] + part_b[0:1])
    _, qm = query_parts(scal, h1_out, g_cross, wq)
    qk_out[...] = nn(qm, wk[...])


def select_docs(height, width):
    r, c = iota((height, width), 0), iota((height, width), 1)
    return (((r // BLOCK) == (c % ROWS)) & ((r % BLOCK) == (c // ROWS))).astype(bf16)


def first_doc(scal, sizes):
    groups = sizes.shape[0]

    def body(g, total):
        return total + jnp.where(g < scal[1], sizes[g], 0)

    return lax.fori_loop(0, groups, body, jnp.int32(0), unroll=groups <= 8)


def rounds_of(scal, sizes):
    return (sizes[scal[1]] + SPAN - 1) // SPAN


def attend_kernel(
    loaded, scal, sizes, lengths, qa, qb, enc, _, held, p_out, e_out, ext_out, qk_s, sems
):
    tokens = enc.shape[1]
    blocks = enc.shape[0] // BLOCK
    rounds = rounds_of(scal, sizes)
    per_round = SPAN // BLOCK
    count = sizes[scal[1]]
    begin = first_doc(scal, sizes)
    tall = BLOCK * ROWS

    def piece(k):
        part = pl.ds(k * BLOCK, BLOCK)
        return pltpu.make_async_copy(enc.at[part], held.at[part], sems.at[k])

    for k in range(loaded, blocks):
        pl.when(k // per_round < rounds)(lambda k=k: piece(k).start())
    high, low = split2(qa[...] + qb[...])
    qk_s[0:ROWS] = high
    qk_s[ROWS : 2 * ROWS] = low

    def one_block(step):
        block = pl.ds(pl.multiple_of(step * BLOCK, BLOCK), BLOCK)
        flat = pl.ds(pl.multiple_of(step * tall, tall), tall)
        rows = held[block].reshape(BLOCK * tokens, D)
        both = nt(qk_s[...], rows)
        logits = both[:ROWS] + both[ROWS:]
        logits = jnp.concatenate(
            [logits[:, b * tokens : (b + 1) * tokens] for b in range(BLOCK)], axis=0
        )
        shown = []
        for b in range(BLOCK):
            slot = step * BLOCK + b
            doc = jnp.minimum(begin + slot, lengths.shape[0] - 1)
            length = jnp.where(slot < count, lengths[doc] - scal[0] * tokens, 0)
            shown.append(jnp.broadcast_to(length, (ROWS, tokens)))
        seen = iota((tall, tokens), 1) < jnp.concatenate(shown, axis=0)
        logits = jnp.where(seen, logits, MASKED)
        peak = jnp.max(logits, axis=1, keepdims=True)
        raised = jnp.where(seen, jnp.exp(logits - peak), 0.0)
        total = jnp.sum(raised, axis=1, keepdims=True)
        p_out[block] = raised.reshape(BLOCK, ROWS, tokens)
        low = raised.astype(bf16)
        summed = jnp.concatenate(
            [
                nn(low[ROWS * b : ROWS * (b + 1)], rows[tokens * b : tokens * (b + 1)])
                for b in range(BLOCK)
            ],
            axis=0,
        )
        for k in range(PANELS):
            e_out[k, flat] = summed[:, k * LANES : (k + 1) * LANES]
        gather = (iota((BLOCK, tall), 0) == iota((BLOCK, tall), 1) // ROWS).astype(bf16)
        parts = split3(peak) + split3(total)
        at = iota((tall, LANES), 1)
        extra = jnp.zeros((tall, LANES), f32)
        for k, part in enumerate(parts):
            extra = jnp.where(at // ROWS == k, part.astype(f32), extra)
        extra = jnp.where(at % ROWS == iota((tall, LANES), 0) % ROWS, extra, 0.0)
        ext_out[block] = nn(gather, extra.astype(bf16)).astype(bf16)

    @pl.loop(0, rounds)
    def _(i):
        for j in range(per_round):
            k = i * per_round + j
            pl.when(k >= loaded)(lambda k=k: piece(k).wait())
        for j in range(per_round):
            one_block(i * per_round + j)

    @pl.loop(rounds, enc.shape[0] // SPAN)
    def _(i):
        span = pl.ds(pl.multiple_of(i * SPAN, SPAN), SPAN)
        flat = pl.ds(pl.multiple_of(i * SPAN * ROWS, SPAN * ROWS), SPAN * ROWS)
        p_out[span] = jnp.zeros((SPAN, ROWS, tokens), f32)
        for k in range(PANELS):
            e_out[k, flat] = jnp.zeros((SPAN * ROWS, LANES), f32)
        ext_out[span] = jnp.where(iota((SPAN, LANES), 1) < ROWS, MASKED, 0.0).astype(bf16)


def sums_of_head(summed, head, slots):
    rows = pl.ds(head, slots, stride=ROWS)
    return jnp.concatenate([summed[k, rows, :] for k in range(PANELS)], axis=1)


def place_parts(scal, full, own, by2, by1, by3):
    height = own.shape[0]
    for mask, piece in ((0, own), (2, by2), (1, by1), (3, by3)):
        at = pl.multiple_of((scal[0] ^ mask) * height, height)
        full[pl.ds(at, height)] = piece[...]


def project_kernel(scal, summed, extra, own, by2, by1, by3, pay_out, heads_out, wv):
    place_parts(scal, wv, own, by2, by1, by3)
    slots = pay_out.shape[0]
    even = iota((slots, LANES), 1) < HEAD_DIM
    for k in range(HEADS // 2):
        pair = wv[k * LANES : (k + 1) * LANES]
        for head in (2 * k, 2 * k + 1):
            heads_out[head] = sums_of_head(summed, head, slots).astype(bf16)
        one, two = (nt(heads_out[2 * k + odd], pair) for odd in range(2))
        pay_out[:, k * LANES : (k + 1) * LANES] = jnp.where(even, one, two).astype(bf16)
    pay_out[:, D:] = extra[...]


def decode(pay):
    extra = pay[:, D:].astype(f32)

    def lane(k):
        return pltpu.roll(extra, LANES - k * ROWS, 1) if k else extra

    first = iota(extra.shape, 1) < ROWS
    peak = jnp.where(first, (lane(0) + lane(1)) + lane(2), 0.0)
    total = jnp.where(first, (lane(3) + lane(4)) + lane(5), 0.0)
    return peak, total


def merge(one, two):
    peak1, total1 = decode(one)
    peak2, total2 = decode(two)
    peak = jnp.maximum(peak1, peak2)
    up1, up2 = jnp.exp(peak1 - peak), jnp.exp(peak2 - peak)
    total = up1 * total1 + up2 * total2
    first = iota(peak.shape, 1) < ROWS
    up1, up2 = jnp.where(first, up1, 0.0), jnp.where(first, up2, 0.0)
    context = spread(up1) * one[:, :D].astype(f32) + spread(up2) * two[:, :D].astype(f32)
    return peak, total, context


def ordered(bit, own, other):
    swap = jnp.broadcast_to(bit, own.shape) == 1
    return jnp.where(swap, other, own), jnp.where(swap, own, other)


def merge_kernel(scal, own, other, pay_out):
    one, two = ordered(scal[0] & 1, own[...].astype(f32), other[...].astype(f32))
    peak, total, context = merge(one, two)
    pay_out[:, :D] = context.astype(bf16)
    extra = jnp.zeros(peak.shape, f32)
    at = iota(peak.shape, 1) // ROWS
    for k, part in enumerate(split3(peak) + split3(total)):
        part = part.astype(f32)
        extra = jnp.where(at == k, pltpu.roll(part, k * ROWS, 1) if k else part, extra)
    pay_out[:, D:] = extra.astype(bf16)


def own_half(scal, rows, held, out):
    half = out.shape[0]
    held[...] = rows
    out[...] = held[pl.ds(pl.multiple_of((scal[0] & 1) * half, half), half)]


def forward_kernel(
    scal, own, other, first, h1, wo_own, wo_by2, wo_by1, wo_by3, g_ff, win, wdown,
    c_out, c32_out, scale_out, h2_out, z_out, part_out, wo, c_s,
):
    place_parts(scal, wo, wo_own, wo_by2, wo_by1, wo_by3)
    bit = lax.shift_right_logical(scal[0], 1) & 1
    one, two = ordered(bit, own[...].astype(f32), other[...].astype(f32))
    peak, total, context = merge(one, two)
    lanes = iota(peak.shape, 1) < ROWS
    inverse = jnp.where(lanes & (total > 0.0), 1.0 / jnp.where(total > 0.0, total, 1.0), 0.0)
    context = context * spread(inverse)
    mine, _ = decode(first[...].astype(f32))
    scale_out[...] = jnp.exp(jnp.minimum(mine - peak, 0.0)) * inverse
    c32_out[...] = context
    low = context.astype(bf16)
    own_half(scal, low, c_s, c_out)
    h2 = h1[...] + nn(low, wo[...])
    h2_out[...] = h2
    n2, _ = rms_parts(h2)
    y3 = (n2 * row_of(g_ff)).astype(bf16)
    z = nn(y3, win[...])
    z_out[...] = z
    u = (z * phi(z)).astype(bf16)
    part_out[...] = nn(u, wdown[...]).astype(bf16)


def score_kernel(scal, part_a, part_b, h2, g_final, row, scores_out, n3_out, dh3_out):
    h3 = h2[...] + (part_a[...].astype(f32) + part_b[...].astype(f32))
    n3, r3 = rms_parts(h3)
    n3_out[...] = n3
    wanted = jnp.broadcast_to(row_of(g_final) * row_of(row) * FACTOR, (8, D))
    scores = nt(wanted, n3, EXACT)[0:1]
    slots = n3.shape[0]
    groups = scores_out.shape[0]
    wide = jnp.concatenate([scores, jnp.zeros((1, LANES - slots), f32)], axis=1)
    scores_out[...] = jnp.where(iota((groups, LANES), 0) == scal[1], wide, 0.0)
    dh3_out[...] = rms_back(wanted[0:1], n3, r3).astype(bf16)


def down_kernel(dh3, z, wdown, win, part_out):
    du = nt(dh3[...], wdown[...])
    dz = (du * gelu_slope(z[...])).astype(bf16)
    part_out[...] = nt(dz, win[...]).astype(bf16)


def list_kernel(scal, sizes, lens, sc_a, sc_b, rel, scores_out, loss_out, ds_out, mine_out):
    groups = sc_a.shape[0]
    docs = ds_out.shape[1]
    wide = docs + LANES
    queries = lens.shape[0]
    relevance = rel[...].reshape(1, docs)
    scores = sc_a[...] + sc_b[...]
    lane = iota((8, LANES), 1)
    blank = jnp.zeros((8, wide - LANES), f32)
    placed = jnp.zeros((8, wide), f32)
    start = jnp.int32(0)
    for g in range(groups):
        kept = jnp.where(lane < sizes[g], scores[g : g + 1], 0.0)
        placed = placed + pltpu.roll(jnp.concatenate([kept, blank], axis=1), start, 1)
        start = start + sizes[g]
    at = iota((queries, 1), 0)

    def one_list(j, found):
        begin, begins, ends = found
        end = begin + lens[j]
        return end, jnp.where(at == j, begin, begins), jnp.where(at == j, end, ends)

    none = jnp.zeros((queries, 1), i32)
    _, begins, ends = lax.fori_loop(
        0, queries, one_list, (jnp.int32(0), none, none), unroll=queries <= 32
    )
    values = placed[0:1, :docs]
    scores_out[...] = values.reshape(scores_out.shape)
    place = iota((queries, docs), 1)
    member = (place >= begins) & (place < ends)
    peak = jnp.max(jnp.where(member, values, MASKED), axis=1, keepdims=True)
    raised = jnp.where(member, jnp.exp(jnp.where(member, values - peak, 0.0)), 0.0)
    log_total = peak + jnp.log(jnp.sum(raised, axis=1, keepdims=True))
    weight = jnp.sum(jnp.where(member, relevance, 0.0), axis=1, keepdims=True)
    target = jnp.where(member, relevance / weight, 0.0)
    picked = jnp.sum(target * values, axis=1, keepdims=True)
    loss_out[...] = jnp.sum(log_total - picked, axis=0, keepdims=True) / queries
    chance = jnp.where(member, jnp.exp(jnp.where(member, values - log_total, 0.0)), 0.0)
    ds = jnp.sum(chance - target, axis=0, keepdims=True) / queries
    ds_out[...] = ds
    ds = jnp.broadcast_to(jnp.concatenate([ds, jnp.zeros((1, LANES), f32)], axis=1), (8, wide))
    start = first_doc(scal, sizes)
    back = pltpu.roll(ds, lax.rem(wide - start, wide), 1)[:, :LANES]
    mine_out[...] = jnp.where(lane < sizes[scal[1]], back, 0.0)


def context_kernel(
    scal, part_a, part_b, h2, dh3, c32, g_ff, wo_own, wo_by2, wo_by1, wo_by3,
    dh2_out, half_out, dc_out, own_out, inner_out, ff_out, wout, both_s,
):
    place_parts(scal, wout, wo_own, wo_by2, wo_by1, wo_by3)
    n2, r2 = rms_parts(h2[...])
    dy3 = part_a[...].astype(f32) + part_b[...].astype(f32)
    ff_out[...] = dy3 * n2
    dh2 = (dh3[...].astype(f32) + rms_back(dy3 * row_of(g_ff), n2, r2)).astype(bf16)
    dh2_out[...] = dh2
    own_half(scal, jnp.concatenate([dh3[...], dh2], axis=1), both_s, half_out)
    dc = nt(dh2, wout[...]).astype(bf16)
    dc_out[...] = dc
    own_out[...] = nt(dh2, wo_own[...]).astype(bf16)
    hot = (head_of((D, LANES), 0) == iota((D, LANES), 1)).astype(f32)
    inner_out[...] = nn(dc.astype(f32) * c32[...], hot, EXACT)


def columns(one, two):
    tall = BLOCK * ROWS
    half = LANES // 2
    both = jnp.where(iota((BLOCK, LANES), 1) < half, one, pltpu.roll(two, half, 1))
    parts = jnp.concatenate(split3(both), axis=0)
    r, c = iota((tall, 3 * BLOCK), 0), iota((tall, 3 * BLOCK), 1)
    wide = nn((r // ROWS == c % BLOCK).astype(bf16), parts)
    lane, head = iota((tall, LANES), 1), iota((tall, LANES), 0) % ROWS
    return tuple(
        jnp.sum(jnp.where(lane == head + k * half, wide, 0.0), axis=1, keepdims=True)
        for k in range(2)
    )


def back_kernel(first, last, scal, sizes, enc, p, scale, inner, dc, *refs):
    if first:
        wv, dap_out, vd_out = refs[0], *refs[-2:]
    else:
        dap_out, vd_out, wv = refs[-3:]
        place_parts(scal, wv, *refs[:4])
    tokens = enc.shape[1]
    tall = BLOCK * ROWS
    rounds = jnp.clip(rounds_of(scal, sizes), first, last)

    def one_block(step):
        block = pl.ds(pl.multiple_of(step * BLOCK, BLOCK), BLOCK)
        rows = enc[block].reshape(BLOCK * tokens, D)
        pick = (iota((tall, BLOCK), 0) // ROWS == iota((tall, BLOCK), 1)).astype(bf16)
        own = (iota((tall, D), 0) % ROWS) == head_of((tall, D), 1)
        grad = jnp.where(own, nn(pick, dc[block]), 0.0).astype(bf16)
        vd = nn(grad, wv[...]).astype(bf16)
        vd_out[block] = vd.reshape(BLOCK, ROWS, D)
        grad_probs = []
        for k in range(BLOCK // 2):
            pair = nt(
                vd[2 * ROWS * k : 2 * ROWS * (k + 1)],
                rows[2 * tokens * k : 2 * tokens * (k + 1)],
            )
            grad_probs += [pair[:ROWS, :tokens], pair[ROWS:, tokens:]]
        grad_probs = jnp.concatenate(grad_probs, axis=0)
        scale_col, inner_col = columns(scale[block], inner[block])
        prob = p[block].reshape(tall, tokens) * scale_col
        da = (prob * (grad_probs - inner_col)).astype(bf16)
        dap_out[block, :ROWS] = da.reshape(BLOCK, ROWS, tokens)
        dap_out[block, ROWS:] = prob.astype(bf16).reshape(BLOCK, ROWS, tokens)

    @pl.loop(first, rounds)
    def _(i):
        for j in range(SPAN // BLOCK):
            one_block(i * (SPAN // BLOCK) + j)

    @pl.loop(rounds, last)
    def _(i):
        span = pl.ds(pl.multiple_of(i * SPAN, SPAN), SPAN)
        dap_out[span] = jnp.zeros((SPAN, 2 * ROWS, tokens), bf16)
        vd_out[span] = jnp.zeros((SPAN, ROWS, D), bf16)


def key_sum_kernel(scal, sizes, ds, enc, dap, dh2, n3, ff, sums_out):
    tokens = enc.shape[1]
    tall = BLOCK * ROWS
    slots = dh2.shape[0]
    row = ds[...][:, :slots] * (1.0 / PARTS)
    at = iota((ROWS, D), 0)
    out = jnp.where(at == HEADS, nn(row, dh2[...].astype(f32), EXACT)[0:1], 0.0)
    out = jnp.where(at == HEADS + 1, nn(row, n3[...], EXACT)[0:1], out)
    sums_out[...] = jnp.where(at == HEADS + 2, nn(row, ff[...], EXACT)[0:1], out)

    def one_block(step):
        block = pl.ds(pl.multiple_of(step * BLOCK, BLOCK), BLOCK)
        own_slot = iota((tall, LANES), 1) == step * BLOCK + iota((tall, LANES), 0) // ROWS
        ds_col = jnp.sum(jnp.where(own_slot, ds[0:1], 0.0), axis=1, keepdims=True)
        scaled = (dap[block, :ROWS].reshape(tall, tokens).astype(f32) * ds_col).astype(bf16)
        flat = jnp.concatenate(
            [scaled[ROWS * b : ROWS * (b + 1)] for b in range(BLOCK)], axis=1
        )
        return nn(flat, enc[block].reshape(BLOCK * tokens, D))

    @pl.loop(0, rounds_of(scal, sizes))
    def _(i):
        per_round = SPAN // BLOCK
        total = one_block(i * per_round)
        for j in range(1, per_round):
            total = total + one_block(i * per_round + j)
        sums_out[...] += total


def enc_grad_kernel(first, last, ds, qa, qb, dap, vd, *refs):
    grad_out, slots, sems = refs[-3:]
    pieces, size = slots.shape[:2]
    qk = qa[...] + qb[...]
    lane = iota((1, LANES), 1)
    copies = []
    for k in range((last - first) // size):
        if k >= pieces:
            copies[k - pieces].wait()
        start = first + k * size
        for b in range(size):
            scale = jnp.sum(jnp.where(lane == start + b, ds[0:1], 0.0), axis=1, keepdims=True)
            right = jnp.concatenate([qk, vd[start + b].astype(f32)], axis=0) * scale
            slots[k % pieces, b] = tn(dap[start + b], right.astype(bf16)).astype(bf16)
        copies.append(
            pltpu.make_async_copy(
                slots.at[k % pieces], grad_out.at[pl.ds(start, size)], sems.at[k % pieces]
            )
        )
        copies[-1].start()
    for copy in copies[-pieces:]:
        copy.wait()


def share_kernel(scal, summed, scale, keep_out, send_out):
    core = scal[0] & 1
    lane = iota(scale.shape, 1)
    for out, bit in ((send_out, 1 - core), (keep_out, core)):
        for y in range(out.shape[0]):
            for k in range(out.shape[1]):
                head = (2 * y + bit) * out.shape[1] + k
                col = jnp.sum(jnp.where(lane == head, scale[...], 0.0), axis=1, keepdims=True)
                out[y, k] = (summed[head].astype(f32) * col).astype(bf16)


def away_kernel(scal, keep, got, out):
    part = 1 - (lax.shift_right_logical(scal[0], 1) & 1)
    for h in range(out.shape[0]):
        out[h] = (keep[part, h].astype(f32) + got[part, h].astype(f32)).astype(bf16)


def value_kernel(scal, keep, got, other, dc, ds, grad_out):
    slots = keep.shape[2]
    part = lax.shift_right_logical(scal[0], 1) & 1
    own_slot = iota((slots, LANES), 0) == iota((slots, LANES), 1)
    ds_col = jnp.sum(jnp.where(own_slot, ds[0:1], 0.0), axis=1, keepdims=True)
    grad = (dc[...].astype(f32) * ds_col).astype(bf16)
    for h in range(keep.shape[1]):
        pair = (keep[part, h].astype(f32) + got[part, h].astype(f32)).astype(bf16)
        summed = (pair.astype(f32) + other[h].astype(f32)).astype(bf16)
        out = tn(grad[:, h * HEAD_DIM : (h + 1) * HEAD_DIM], summed)
        grad_out[h * HEAD_DIM : (h + 1) * HEAD_DIM] = out.astype(bf16)


def document_picks(order, tile, scal, sizes, held, first):
    groups = 1 << len(order)
    half = held // groups
    core = scal[0] & 1
    doc = first + iota((tile, 1), 0)

    def one_group(g, found):
        start, at, upper = found
        mask = g ^ scal[1]
        pos = 0
        for k, bit in enumerate(order):
            pos = pos + (lax.shift_right_logical(mask, bit.bit_length() - 1) & 1) * (1 << k)
        slot = doc - start
        inside = (slot >= 0) & (slot < sizes[g])
        later = (slot >= half).astype(i32)
        at = jnp.where(inside, pos * half + slot - half * later, at)
        return start + sizes[g], at, jnp.where(inside, later, upper)

    zero = jnp.zeros((tile, 1), i32)
    _, at, upper = lax.fori_loop(
        0, groups, one_group, (jnp.int32(0), zero, zero), unroll=groups <= 8
    )
    hit = iota((tile, held), 1) == at
    mine = (hit & (upper == core)).astype(bf16)
    theirs = (hit & (upper != core)).astype(bf16)
    return lambda own, other: (nn(mine, own[...]) + nn(theirs, other[...])).astype(bf16)


def ds_column(ds, first, tile):
    eye = iota((tile, tile), 0) == iota((tile, tile), 1)
    return jnp.sum(jnp.where(eye, ds[0:1, pl.ds(first, tile)], 0.0), axis=1, keepdims=True)


def over_tiles(docs, tile, one_tile):
    one_tile(0, True)
    if docs > tile:

        @pl.loop(1, docs // tile)
        def _(t):
            one_tile(pl.multiple_of(t * tile, tile), False)


def put(out, value, new):
    if new:
        out[...] = value
    else:
        out[...] += value


def weights_before_kernel(
    order, tile, scal, sizes, c_own, c_other, h1, g_ff, wo_own, wo_by2, wo_by1, wo_by3, win,
    y3_out, u_out, slope_out, c_out, wout,
):
    place_parts(scal, wout, wo_own, wo_by2, wo_by1, wo_by3)

    def one_tile(first, new):
        here = pl.ds(first, tile)
        rows = document_picks(order, tile, scal, sizes, c_own.shape[0], first)
        c = rows(c_own, c_other)
        h2 = h1[...] + nn(c, wout[...])
        n2, _ = rms_parts(h2)
        y3 = (n2 * row_of(g_ff)).astype(bf16)
        y3_out[here] = y3
        z = nn(y3, win[...])
        u_out[here] = (z * phi(z)).astype(bf16)
        slope_out[here] = gelu_slope(z)
        width = c_out.shape[1]
        pick = (iota((D, width), 0) == scal[0] * width + iota((D, width), 1)).astype(bf16)
        c_out[here] = nn(c, pick).astype(bf16)

    over_tiles(y3_out.shape[0], tile, one_tile)


def weights_kernel(
    order, tile, scal, sizes, y3, slope, both_own, both_other, ds, wdown,
    win_out, grads_out,
):
    def one_tile(first, new):
        here = pl.ds(first, tile)
        rows = document_picks(order, tile, scal, sizes, both_own.shape[0], first)
        both = rows(both_own, both_other).astype(f32) * ds_column(ds, first, tile)
        both = both.astype(bf16)
        grads_out[here] = both
        dz = (nt(both[:, :D], wdown[...]) * slope[here]).astype(bf16)
        put(win_out, tn(y3[here], dz), new)

    over_tiles(ds.shape[1], tile, one_tile)


def weights_after_kernel(tile, u, c, grads, wdown_out, wout_out):
    def one_tile(first, new):
        here = pl.ds(first, tile)
        put(wdown_out, tn(u[here], grads[here, :D]), new)
        put(wout_out, tn(c[here], grads[here, D:]), new)

    over_tiles(u.shape[0], tile, one_tile)


def key_kernel(scal, sum_a, sum_b, h1, g_cross, wk, wq, key_out, query_out, part_out):
    y2, qm = query_parts(scal, h1, g_cross, wq)
    g = sum_a[...] + sum_b[...]
    g = jnp.where(iota((ROWS, D), 0) < HEADS, g, 0.0)
    high, low = split2(g)
    both = jnp.concatenate([high, low], axis=0)
    dq = nt(both, wk[...])
    dq = dq[:ROWS] + dq[ROWS:]
    width = dq.shape[1]
    first = scal[0] * (width // HEAD_DIM)
    own = iota((ROWS, width), 0) == first + head_of((ROWS, width), 1)
    dq = jnp.sum(jnp.where(own, dq, 0.0), axis=0, keepdims=True)
    key_out[...] = tn(jnp.concatenate([qm, qm], axis=0), both)
    dq_parts = stack3(dq)
    query_out[...] = tn(dq_parts, repeat3(y2[0:1]))
    part = jnp.sum(nn(dq_parts, wq[...]), axis=0, keepdims=True)
    part_out[...] = jnp.broadcast_to(part, (8, D))


def hidden_kernel(
    part_a, part_b, sum_a, sum_b, h1, g_cross, start, g_self, wos, wvs, g_final, row,
    dh1_out, wos_out, wvs_out, part_out, cross_out, final_out, row_out, ff_out,
):
    y1, s1 = self_parts(start, g_self, wvs)
    dy2 = part_a[0:1] + part_b[0:1]
    sums = sum_a[...] + sum_b[...]
    n1, r1 = rms_parts(h1[...])
    cross_out[...] = (dy2 * n1).reshape(cross_out.shape)
    dh1 = sums[HEADS : HEADS + 1] + rms_back(dy2 * row_of(g_cross), n1, r1)
    dh1_out[...] = dh1
    dh1_parts = stack3(dh1)
    wos_out[...] = tn(repeat3(s1[0:1]), dh1_parts)
    ds1 = jnp.sum(nt(dh1_parts, wos[...]), axis=0, keepdims=True)
    ds1_parts = stack3(ds1)
    wvs_out[...] = tn(ds1_parts, repeat3(y1[0:1]))
    part = jnp.sum(nn(ds1_parts, wvs[...]), axis=0, keepdims=True)
    part_out[...] = jnp.broadcast_to(part, (8, D))
    total = sums[HEADS + 1 : HEADS + 2] * FACTOR
    final_out[...] = (total * row_of(row)).reshape(final_out.shape)
    row_out[...] = (total * row_of(g_final)).reshape(row_out.shape)
    ff_out[...] = sums[HEADS + 2 : HEADS + 3].reshape(ff_out.shape)


def start_kernel(part_a, part_b, dh1, start, g_self, gain_out, start_out):
    dy1 = part_a[0:1] + part_b[0:1]
    n0, r0 = rms_parts(row_of(start))
    gain_out[...] = (dy1 * n0).reshape(gain_out.shape)
    back = dh1[...] + rms_back(dy1 * row_of(g_self), n0, r0)
    start_out[...] = back.reshape(start_out.shape)


def shape(dims, dtype=f32):
    return jax.ShapeDtypeStruct(dims, dtype)


def whole_spec(memory=pltpu.VMEM):
    return pl.BlockSpec(memory_space=memory)


def name_of(kernel):
    return getattr(kernel, "func", kernel).__name__


def in_hbm(x):
    return pltpu.with_memory_space_constraint(x, pltpu.HBM)


def plain(
    kernel, outs, *args, smem=0, hbm=(), hbm_out=False, onto=None, flops=0, limit=12, scratch=()
):
    size = sum(a.size * a.dtype.itemsize for k, a in enumerate(args) if k not in hbm)
    spaces = [pltpu.SMEM] * smem + [pltpu.VMEM] * (len(args) - smem)
    for k in hbm:
        spaces[k] = pltpu.HBM
    out_space = pltpu.HBM if hbm_out else pltpu.VMEM
    return pl.pallas_call(
        kernel,
        out_shape=outs,
        in_specs=[whole_spec(space) for space in spaces],
        out_specs=[whole_spec(out_space) for _ in outs]
        if isinstance(outs, list)
        else whole_spec(out_space),
        scratch_shapes=list(scratch),
        input_output_aliases=onto or {},
        compiler_params=pltpu.CompilerParams(vmem_limit_bytes=limit * MIB),
        cost_estimate=pl.CostEstimate(flops=flops, bytes_accessed=size, transcendentals=0),
        name=name_of(kernel),
    )(*args)


def bits_of(size):
    return [1 << b for b in range(size.bit_length() - 1)]


def far_first(size):
    return bits_of(size)[::-1]


def swap(x, axis, bit):
    size = lax.axis_size(axis)
    return lax.ppermute(x, axis, [(i, i ^ bit) for i in range(size)])


def after(x, *deps):
    return lax.optimization_barrier((x, *deps))[0]


def add(x, y):
    return (x.astype(f32) + y.astype(f32)).astype(x.dtype)


def sum_last(x, steps):
    for axis, bit in steps[:-1]:
        x = add(x, swap(x, axis, bit))
    axis, bit = steps[-1]
    return x, swap(x, axis, bit)


def per_device(
    enc_out,
    enc_len,
    group_docs,
    list_len,
    relevance,
    start_token,
    score_row,
    g_self,
    w_value_self,
    w_out_self,
    g_cross,
    w_query,
    w_key,
    w_value,
    w_out,
    g_ff,
    w_in,
    w_down,
    g_final,
):
    groups = lax.axis_size("docs")
    parts = lax.axis_size("heads")
    assert parts == PARTS
    me_g = lax.axis_index("docs")
    me_j = lax.axis_index("heads")
    slots, tokens = enc_out.shape[:2]
    docs = enc_len.shape[0]
    width = w_value.shape[1]
    own_heads = HEADS // parts
    hidden = w_in.shape[1]
    over_heads = [("heads", 1), ("heads", 2)]
    order = far_first(groups)
    over_docs = [("docs", bit) for bit in order]

    scal = jnp.stack([me_j, me_g])
    wvs_t, wq_t, wk_t, wv_t = (w.T for w in (w_value_self, w_query, w_key, w_value))

    wv_by1, wo_by1 = swap(wv_t, "heads", 1), swap(w_out, "heads", 1)

    part = plain(
        self_kernel,
        shape((8, D)),
        *map(in_hbm, (start_token, g_self, wvs_t, w_out_self)),
    )


    def load(first, last, since, *onto):
        return pl.pallas_call(
            functools.partial(load_kernel, first, last),
            out_shape=pltpu.VMEM(enc_out.shape, bf16),
            in_specs=[whole_spec(pltpu.HBM), whole_spec(pl.ANY), whole_spec(pltpu.SMEM)]
            + [whole_spec()] * len(onto),
            out_specs=whole_spec(),
            scratch_shapes=[pltpu.SemaphoreType.DMA((last - first,))],
            input_output_aliases={3: 0} if onto else {},
            compiler_params=pltpu.CompilerParams(vmem_limit_bytes=MIB),
            cost_estimate=pl.CostEstimate(
                flops=0, bytes_accessed=(last - first) * BLOCK * tokens * D * 4, transcendentals=0
            ),
            name="load_kernel",
        )(in_hbm(enc_out), since, scal, *onto)

    part = add(part, swap(part, "heads", 1))
    part_a, part_b = part, swap(part, "heads", 2)
    held = load(0, 1, part)
    part_b, held = lax.optimization_barrier((part_b, held))
    wv_by2 = swap(after(wv_t, part_b), "heads", 2)
    qk, h1 = plain(
        query_kernel,
        [shape((ROWS, D)), shape((1, D))],
        scal,
        part_a,
        part_b,
        *map(in_hbm, (start_token, g_cross, wq_t, wk_t)),
        smem=1,
    )
    qk = add(qk, swap(qk, "heads", 1))
    qk, held = lax.optimization_barrier((qk, held))
    qk_a, qk_b = qk, swap(qk, "heads", 2)
    held = load(1, 3, qk, held)
    qk_b, held, wv_by2 = lax.optimization_barrier((qk_b, held, wv_by2))
    wv_by3 = swap(wv_by2, "heads", 1)

    pass_flops = 2 * slots * tokens * D * 256

    wo_by2 = swap(after(w_out, qk_b), "heads", 2)
    held, prob, summed, extra = plain(
        functools.partial(attend_kernel, 3),
        [
            pltpu.VMEM(enc_out.shape, bf16),
            pltpu.VMEM((slots, ROWS, tokens), f32),
            pltpu.VMEM((PANELS, slots * ROWS, LANES), f32),
            shape((slots, LANES), bf16),
        ],
        scal,
        group_docs,
        enc_len,
        qk_a,
        qk_b,
        in_hbm(enc_out),
        held,
        smem=3,
        hbm=(5,),
        onto={6: 0},
        flops=2 * pass_flops,
        scratch=[pltpu.VMEM((2 * ROWS, D), bf16), pltpu.SemaphoreType.DMA((slots // BLOCK,))],
        limit=16,
    )
    summed, wv_by3, wo_by2 = lax.optimization_barrier((summed, wv_by3, wo_by2))
    wv_parts = (wv_t, wv_by2, wv_by1, wv_by3)
    wo_parts = (w_out, wo_by2, wo_by1, swap(wo_by2, "heads", 1))
    full = [pltpu.VMEM((D, D), bf16)]
    pay, summed = plain(
        project_kernel,
        [shape((slots, D + LANES), bf16), shape((HEADS, slots, D), bf16)],
        scal,
        summed,
        extra,
        *wv_parts,
        smem=1,
        scratch=full,
    )
    merged = plain(
        merge_kernel, shape(pay.shape, bf16), scal, pay, swap(pay, "heads", 1), smem=1
    )
    other = swap(merged, "heads", 2)

    c, c32, scale, h2, z, part = plain(
        forward_kernel,
        [
            shape((slots // 2, D), bf16),
            shape((slots, D)),
            shape((slots, LANES)),
            shape((slots, D)),
            shape((slots, hidden)),
            shape((slots, D), bf16),
        ],
        scal,
        merged,
        other,
        pay,
        h1,
        *wo_parts,
        g_ff,
        w_in,
        w_down,
        smem=1,
        scratch=full + [pltpu.VMEM((slots, D), bf16)],
    )

    half = slots // 2

    def grow(x, k):
        return jnp.concatenate([x, swap(x, *over_docs[k])], axis=0)

    def tie(*xs):
        return lax.optimization_barrier(xs)

    last = len(over_docs) - 1
    near_first = over_docs[::-1]
    score_steps = near_first[:1] + over_docs[:-1]
    part = add(part, swap(part, "heads", 1))
    part, c, summed = tie(part, c, summed)
    part_a, part_b = part, swap(part, "heads", 2)
    c_far = swap(c, *over_docs[0])
    keep, sent = plain(
        share_kernel, [shape((2, own_heads, slots, D), bf16)] * 2, scal, summed, scale, smem=1
    )
    got = swap(sent, "heads", 1)
    part_b, keep = tie(part_b, keep)
    scores, n3, dh3 = plain(
        score_kernel,
        [shape((groups, LANES)), shape((slots, D)), shape((slots, D), bf16)],
        scal,
        part_a,
        part_b,
        h2,
        g_final,
        score_row,
        smem=1,
    )
    score_far = swap(scores, *score_steps[0])
    part = plain(down_kernel, shape((slots, D), bf16), dh3, z, w_down, w_in)
    part_far = swap(part, "heads", 1)
    part_far, score_far = tie(part_far, score_far)
    part = add(part, part_far)
    part_a, part_b = part, swap(part, "heads", 2)
    score_a = scores + score_far
    for k in range(1, last):
        score_b = swap(score_a, *score_steps[k])
        if k < last - 1:
            score_a = score_a + score_b
    away = plain(
        away_kernel, shape((own_heads, slots, D), bf16), scal, keep, got, smem=1
    )
    other = swap(away, "heads", 2)
    part_b, score_b, away, c_far = tie(part_b, score_b, away, c_far)
    dh2, grads, dc, dc_own, inner, ff = plain(
        context_kernel,
        [
            shape((slots, D), bf16),
            shape((half, 2 * D), bf16),
            shape((slots, D), bf16),
            shape((slots, width), bf16),
            shape((slots, LANES)),
            shape((slots, D)),
        ],
        scal,
        part_a,
        part_b,
        h2,
        dh3,
        c32,
        g_ff,
        *wo_parts,
        smem=1,
        scratch=full + [pltpu.VMEM((slots, 2 * D), bf16)],
    )

    score_a = score_a + score_b
    c_all = jnp.concatenate([c, c_far], axis=0)
    for k in range(1, last):
        c_all = grow(c_all, k)
    score_a, dc, grads, c_all = tie(score_a, dc, grads, c_all)
    score_b = swap(score_a, *score_steps[last])
    grads_far = swap(grads, *over_docs[0])
    c_far = swap(c_all, *over_docs[last])

    outs = [
        pltpu.VMEM((slots, 2 * ROWS, tokens), bf16),
        pltpu.VMEM((slots, ROWS, D), bf16),
    ]
    rounds = slots // SPAN
    middle = 1
    inputs = (scal, group_docs, held, prob, scale, inner, dc)
    dap, vd, wv_full = plain(
        functools.partial(back_kernel, 0, middle),
        outs + [shape((D, D), bf16)],
        *inputs,
        *wv_parts,
        smem=2,
        flops=pass_flops * middle // rounds,
        limit=16,
    )
    dap, score_b, grads_far, c_far, other = tie(dap, score_b, grads_far, c_far, other)
    all_scores, loss, ds_docs, ds_mine = plain(
        list_kernel,
        [shape((docs,)), shape((1, 1)), shape((1, docs)), shape((8, LANES))],
        scal,
        group_docs,
        list_len,
        score_a,
        score_b,
        in_hbm(relevance),
        smem=3,
    )
    value_part = plain(
        value_kernel,
        shape((width, D), bf16),
        scal,
        keep,
        got,
        other,
        dc_own,
        ds_mine,
        smem=1,
    )
    dap, value_part = tie(dap, value_part)
    value_far = swap(value_part, *near_first[0])
    c_all = jnp.concatenate([c_all, c_far], axis=0)
    c_far = swap(c_all, "heads", 1)
    grads = jnp.concatenate([grads, grads_far], axis=0)
    for m in range(1, last):
        grads_far = swap(grads, *over_docs[m])
        if m < last - 1:
            grads = jnp.concatenate([grads, grads_far], axis=0)
    dap, vd = plain(
        functools.partial(back_kernel, middle, rounds),
        outs,
        *inputs,
        wv_full,
        dap,
        vd,
        smem=2,
        onto={8: 0, 9: 1},
        flops=pass_flops * (rounds - middle) // rounds,
        limit=16,
    )
    dap, value_far, grads_far, c_far = tie(dap, value_far, grads_far, c_far)
    grads = jnp.concatenate([grads, grads_far], axis=0)
    grads_far = swap(grads, *over_docs[last])
    for m in range(1, last):
        value_part = add(value_part, value_far)
        value_far = swap(value_part, *near_first[m])
    sums = plain(
        key_sum_kernel,
        shape((ROWS, D)),
        scal,
        group_docs,
        ds_mine,
        held,
        dap,
        dh2,
        n3,
        ff,
        smem=2,
        flops=pass_flops,
    )

    def enc_grads(first, last, grads=None):
        outs = pltpu.HBM(enc_out.shape, bf16)
        size = 8
        args = (ds_mine, qk_a, qk_b, dap, vd)
        return plain(
            functools.partial(enc_grad_kernel, first, last),
            outs,
            *args,
            *([] if grads is None else [grads]),
            hbm=() if grads is None else (len(args),),
            hbm_out=True,
            onto={} if grads is None else {len(args): 0},
            flops=pass_flops * (last - first) // slots,
            scratch=[pltpu.VMEM((4, size, tokens, D), bf16), pltpu.SemaphoreType.DMA((4,))],
            limit=16,
        )

    sums = add(sums, swap(sums, "heads", 1))
    steps = over_heads[1:] + near_first[:0:-1] + near_first[:1]
    enc_grad = None
    third = slots // 3
    sum_a = sums
    for k, step in enumerate(steps):
        sum_b = swap(sum_a, *step)
        if k < 2 or k == len(steps) - 1:
            part = min(k, 2)
            enc_grad = enc_grads(part * third, (part + 1) * third, enc_grad)
            sum_b, enc_grad = tie(sum_b, enc_grad)
        if k == 1:
            sum_b, value_far = tie(sum_b, value_far)
            value_part = add(value_part, value_far)
        if k == len(steps) - 2:
            ready = plain(
                functools.partial(weights_before_kernel, order, 384),
                [
                    shape((docs, D), bf16),
                    shape((docs, hidden), bf16),
                    shape((docs, hidden)),
                    shape((docs, width), bf16),
                ],
                scal,
                group_docs,
                c_all,
                c_far,
                h1,
                g_ff,
                *wo_parts,
                w_in,
                smem=2,
                flops=4 * docs * D * hidden,
                limit=60 if docs > 384 else 16,
                scratch=full,
            )
            sum_b, value_part, *ready = tie(sum_b, value_part, *ready)
            value_b = swap(value_part, *near_first[last])
        if k == len(steps) - 1:
            sum_b, grads_far = tie(sum_b, grads_far)
            grads = jnp.concatenate([grads, grads_far], axis=0)
            grads_far = swap(grads, "heads", 1)
        if k < len(steps) - 1:
            sum_a = sum_a + sum_b
    key_grad, query_grad, part = plain(
        key_kernel,
        [shape((width, D)), shape((width, D)), shape((8, D))],
        scal,
        sum_a,
        sum_b,
        h1,
        g_cross,
        wk_t,
        wq_t,
        smem=1,
    )
    part_a, part_b = sum_last(part, over_heads)
    y3, u, slope, c_own = ready
    w_in_grad, grads_docs = plain(
        functools.partial(weights_kernel, order, 384),
        [shape((D, hidden)), shape((docs, 2 * D), bf16)],
        scal,
        group_docs,
        y3,
        slope,
        grads,
        grads_far,
        ds_docs,
        w_down,
        smem=2,
        flops=4 * docs * D * hidden,
        limit=60 if docs > 384 else 16,
    )
    part_b, w_in_grad, grads_docs = tie(part_b, w_in_grad, grads_docs)
    dh1, wos_grad, wvs_grad, part, cross, final_gain, row_grad, ff_gain = plain(
        hidden_kernel,
        [shape((1, D)), shape((width, D)), shape((width, D)), shape((8, D))] + [shape((D,))] * 4,
        part_a,
        part_b,
        sum_a,
        sum_b,
        h1,
        g_cross,
        start_token,
        g_self,
        w_out_self,
        wvs_t,
        g_final,
        score_row,
    )
    part_a, part_b = sum_last(part, over_heads)
    w_down_grad, w_out_grad = plain(
        functools.partial(weights_after_kernel, 384),
        [shape((hidden, D)), shape((width, D))],
        u,
        c_own,
        grads_docs,
        flops=4 * docs * D * hidden,
        limit=60 if docs > 384 else 16,
    )
    part_b, w_down_grad, value_b = tie(part_b, w_down_grad, value_b)
    value_grad = (value_part.astype(f32) + value_b.astype(f32)).T
    self_gain, start_grad = plain(
        start_kernel, [shape((D,))] * 2, part_a, part_b, dh1, start_token, g_self
    )

    return (
        all_scores,
        loss.reshape(()),
        enc_grad,
        start_grad,
        row_grad,
        self_gain,
        wvs_grad.T,
        wos_grad,
        cross,
        query_grad.T,
        key_grad.T,
        value_grad,
        w_out_grad,
        ff_gain,
        w_in_grad,
        w_down_grad,
        final_gain,
    )


def solution(mesh):
    placed = (
        P("docs", "heads", None),
        P(),
        P(),
        P(),
        P(),
        P(),
        P(),
        P(),
        P(None, "heads"),
        P("heads", None),
        P(),
        P(None, "heads"),
        P(None, "heads"),
        P(None, "heads"),
        P("heads", None),
        P(),
        P(None, "heads"),
        P("heads", None),
        P(),
    )
    return jax.shard_map(
        per_device,
        mesh=mesh,
        in_specs=placed,
        out_specs=(
            P(),
            P(),
            P("docs", "heads", None),
            P(),
            P(),
            P(),
            P(None, "heads"),
            P("heads", None),
            P(),
            P(None, "heads"),
            P(None, "heads"),
            P(None, "heads"),
            P("heads", None),
            P(),
            P(None, "heads"),
            P("heads", None),
            P(),
        ),
        check_vma=False,
    )
```

```python
import functools

import jax
import jax.numpy as jnp
from jax import lax
from jax.experimental import pallas as pl
from jax.experimental.pallas import tpu as pltpu
from jax.sharding import PartitionSpec as P

D = 768
HEADS = 12
HEAD_DIM = 64
ROWS = 16
BLOCK = 16
SPAN = 2 * BLOCK
LANES = 128
PANELS = D // LANES
PARTS = 4

EPSILON = 1e-06
MASKED = -1e30
FACTOR = D ** (-0.5)
ROOT_HALF = 0.5**0.5
DENSITY = 0.3989422804014327
f32, bf16, i32 = jnp.float32, jnp.bfloat16, jnp.int32
EXACT = lax.Precision.HIGHEST
MIB = 1 << 20


def nn(a, b, precision=None):
    return lax.dot_general(
        a, b, (((1,), (0,)), ((), ())), precision=precision, preferred_element_type=f32
    )


def nt(a, b, precision=None):
    return lax.dot_general(
        a, b, (((1,), (1,)), ((), ())), precision=precision, preferred_element_type=f32
    )


def tn(a, b, precision=None):
    return lax.dot_general(
        a, b, (((0,), (0,)), ((), ())), precision=precision, preferred_element_type=f32
    )


def iota(shape, dim):
    return lax.broadcasted_iota(i32, shape, dim)


def split2(x):
    high = x.astype(bf16)
    return high, (x - high.astype(f32)).astype(bf16)


def split3(x):
    high = x.astype(bf16)
    rest = x - high.astype(f32)
    mid = rest.astype(bf16)
    return high, mid, (rest - mid.astype(f32)).astype(bf16)


def stack3(row, height=ROWS):
    at = iota((height, row.shape[1]), 0)
    parts = split3(row)
    zero = jnp.zeros((), f32)
    out = jnp.where(at == 0, parts[0].astype(f32), zero)
    out = jnp.where(at == 1, parts[1].astype(f32), out)
    return jnp.where(at == 2, parts[2].astype(f32), out).astype(bf16)


def repeat3(row, height=ROWS):
    at = iota((height, row.shape[1]), 0)
    return jnp.where(at < 3, row.astype(f32), 0.0).astype(bf16)


def rms_parts(rows):
    scale = lax.rsqrt(jnp.mean(rows * rows, axis=-1, keepdims=True) + EPSILON)
    return rows * scale, scale


def rms_back(grad_normed, normed, scale):
    inner = jnp.mean(grad_normed * normed, axis=-1, keepdims=True)
    return scale * (grad_normed - normed * inner)


def phi(z):
    return 0.5 * (1.0 + lax.erf(z * ROOT_HALF))


def gelu_slope(z):
    return phi(z) + z * (DENSITY * jnp.exp(-0.5 * z * z))


def head_of(shape, dim):
    return iota(shape, dim) // HEAD_DIM


def spread(small):
    high, mid, low = (part.astype(f32) for part in split3(small))
    packed = high + pltpu.roll(mid, ROWS, 1) + pltpu.roll(low, 2 * ROWS, 1)
    lane = iota((LANES, D), 0)
    hot = (lane < 3 * ROWS) & (lane % ROWS == head_of((LANES, D), 1))
    return nn(packed.astype(bf16), hot.astype(bf16))


def row_dot(row, right):
    high, low = split2(right)
    parts = stack3(row)
    return jnp.sum(nn(parts, high) + nn(parts, low), axis=0, keepdims=True)


def row_of(ref):
    return ref[...].astype(f32).reshape(1, D)


def gained(n, gain):
    return jnp.broadcast_to(n * row_of(gain), (ROWS, D)).astype(bf16)


def self_parts(start, g_self, wvs):
    x0 = row_of(start)
    n0, _ = rms_parts(x0)
    y1 = gained(n0, g_self)
    return y1, nt(y1, wvs[...]).astype(bf16)


def query_parts(scal, h1, g_cross, wq):
    n1, _ = rms_parts(h1[...])
    y2 = gained(n1, g_cross)
    q = nt(y2, wq[...]).astype(bf16)
    width = q.shape[1]
    first = scal[0] * (width // HEAD_DIM)
    own = iota((ROWS, width), 0) == first + head_of((ROWS, width), 1)
    return y2, jnp.where(own, q.astype(f32), 0.0).astype(bf16)


def self_kernel(start, g_self, wvs, wos, part_out):
    _, s1 = self_parts(start, g_self, wvs)
    part_out[...] = nn(s1, wos[...])[:8]


def load_kernel(first, last, enc, since, scal, *refs):
    held, sems = refs[-2:]
    loads = []
    for k in range(first, last):
        part = pl.ds(k * BLOCK, BLOCK)
        loads.append(pltpu.make_async_copy(enc.at[part], held.at[part], sems.at[k - first]))
        loads[-1].start()
    for load in loads:
        load.wait()


def query_kernel(scal, part_a, part_b, start, g_cross, wq, wk, qk_out, h1_out):
    h1_out[...] = row_of(start) + (part_a[0:1] + part_b[0:1])
    _, qm = query_parts(scal, h1_out, g_cross, wq)
    qk_out[...] = nn(qm, wk[...])


def load_kernel(first, last, enc, since, scal, *refs):
    held, sems = refs[-2:]
    loads = []
    for k in range(first, last):
        part = pl.ds(k * BLOCK, BLOCK)
        loads.append(pltpu.make_async_copy(enc.at[part], held.at[part], sems.at[k - first]))
        loads[-1].start()
    for load in loads:
        load.wait()


def query_kernel(scal, part_a, part_b, start, g_cross, wq, wk, qk_out, h1_out):
    h1_out[...] = row_of(start) + (part_a[0:1] + part_b[0:1])
    _, qm = query_parts(scal, h1_out, g_cross, wq)
    qk_out[...] = nn(qm, wk[...])


def select_docs(height, width):
    r, c = iota((height, width), 0), iota((height, width), 1)
    return (((r // BLOCK) == (c % ROWS)) & ((r % BLOCK) == (c // ROWS))).astype(bf16)


def first_doc(scal, sizes):
    groups = sizes.shape[0]

    def body(g, total):
        return total + jnp.where(g < scal[1], sizes[g], 0)

    return lax.fori_loop(0, groups, body, jnp.int32(0), unroll=groups <= 8)


def rounds_of(scal, sizes):
    return (sizes[scal[1]] + SPAN - 1) // SPAN


def attend_kernel(
    loaded, scal, sizes, lengths, qa, qb, enc, _, held, p_out, e_out, ext_out, qk_s, sems
):
    tokens = enc.shape[1]
    blocks = enc.shape[0] // BLOCK
    rounds = rounds_of(scal, sizes)
    per_round = SPAN // BLOCK
    count = sizes[scal[1]]
    begin = first_doc(scal, sizes)
    tall = BLOCK * ROWS

    def piece(k):
        part = pl.ds(k * BLOCK, BLOCK)
        return pltpu.make_async_copy(enc.at[part], held.at[part], sems.at[k])

    for k in range(loaded, blocks):
        pl.when(k // per_round < rounds)(lambda k=k: piece(k).start())
    high, low = split2(qa[...] + qb[...])
    qk_s[0:ROWS] = high
    qk_s[ROWS : 2 * ROWS] = low

    def one_block(step):
        block = pl.ds(pl.multiple_of(step * BLOCK, BLOCK), BLOCK)
        flat = pl.ds(pl.multiple_of(step * tall, tall), tall)
        rows = held[block].reshape(BLOCK * tokens, D)
        both = nt(qk_s[...], rows)
        logits = both[:ROWS] + both[ROWS:]
        logits = jnp.concatenate(
            [logits[:, b * tokens : (b + 1) * tokens] for b in range(BLOCK)], axis=0
        )
        shown = []
        for b in range(BLOCK):
            slot = step * BLOCK + b
            doc = jnp.minimum(begin + slot, lengths.shape[0] - 1)
            length = jnp.where(slot < count, lengths[doc] - scal[0] * tokens, 0)
            shown.append(jnp.broadcast_to(length, (ROWS, tokens)))
        seen = iota((tall, tokens), 1) < jnp.concatenate(shown, axis=0)
        logits = jnp.where(seen, logits, MASKED)
        peak = jnp.max(logits, axis=1, keepdims=True)
        raised = jnp.where(seen, jnp.exp(logits - peak), 0.0)
        total = jnp.sum(raised, axis=1, keepdims=True)
        p_out[block] = raised.reshape(BLOCK, ROWS, tokens)
        low = raised.astype(bf16)
        summed = jnp.concatenate(
            [
                nn(low[ROWS * b : ROWS * (b + 1)], rows[tokens * b : tokens * (b + 1)])
                for b in range(BLOCK)
            ],
            axis=0,
        )
        for k in range(PANELS):
            e_out[k, flat] = summed[:, k * LANES : (k + 1) * LANES]
        gather = (iota((BLOCK, tall), 0) == iota((BLOCK, tall), 1) // ROWS).astype(bf16)
        parts = split3(peak) + split3(total)
        at = iota((tall, LANES), 1)
        extra = jnp.zeros((tall, LANES), f32)
        for k, part in enumerate(parts):
            extra = jnp.where(at // ROWS == k, part.astype(f32), extra)
        extra = jnp.where(at % ROWS == iota((tall, LANES), 0) % ROWS, extra, 0.0)
        ext_out[block] = nn(gather, extra.astype(bf16)).astype(bf16)

    @pl.loop(0, rounds)
    def _(i):
        for j in range(per_round):
            k = i * per_round + j
            pl.when(k >= loaded)(lambda k=k: piece(k).wait())
        for j in range(per_round):
            one_block(i * per_round + j)

    @pl.loop(rounds, enc.shape[0] // SPAN)
    def _(i):
        span = pl.ds(pl.multiple_of(i * SPAN, SPAN), SPAN)
        flat = pl.ds(pl.multiple_of(i * SPAN * ROWS, SPAN * ROWS), SPAN * ROWS)
        p_out[span] = jnp.zeros((SPAN, ROWS, tokens), f32)
        for k in range(PANELS):
            e_out[k, flat] = jnp.zeros((SPAN * ROWS, LANES), f32)
        ext_out[span] = jnp.where(iota((SPAN, LANES), 1) < ROWS, MASKED, 0.0).astype(bf16)


def sums_of_head(summed, head, slots):
    rows = pl.ds(head, slots, stride=ROWS)
    return jnp.concatenate([summed[k, rows, :] for k in range(PANELS)], axis=1)


def place_parts(scal, full, own, by2, by1, by3):
    height = own.shape[0]
    for mask, piece in ((0, own), (2, by2), (1, by1), (3, by3)):
        at = pl.multiple_of((scal[0] ^ mask) * height, height)
        full[pl.ds(at, height)] = piece[...]


def arrange_kernel(scal, own, by2, by1, by3, full_out):
    place_parts(scal, full_out, own, by2, by1, by3)


def project_kernel(scal, summed, extra, own, by2, by1, by3, pay_out, heads_out, wv):
    place_parts(scal, wv, own, by2, by1, by3)
    slots = pay_out.shape[0]
    even = iota((slots, LANES), 1) < HEAD_DIM
    for k in range(HEADS // 2):
        pair = wv[k * LANES : (k + 1) * LANES]
        for head in (2 * k, 2 * k + 1):
            heads_out[head] = sums_of_head(summed, head, slots).astype(bf16)
        one, two = (nt(heads_out[2 * k + odd], pair) for odd in range(2))
        pay_out[:, k * LANES : (k + 1) * LANES] = jnp.where(even, one, two).astype(bf16)
    pay_out[:, D:] = extra[...]


def decode(pay):
    extra = pay[:, D:].astype(f32)

    def lane(k):
        return pltpu.roll(extra, LANES - k * ROWS, 1) if k else extra

    first = iota(extra.shape, 1) < ROWS
    peak = jnp.where(first, (lane(0) + lane(1)) + lane(2), 0.0)
    total = jnp.where(first, (lane(3) + lane(4)) + lane(5), 0.0)
    return peak, total


def merge(one, two, last=False):
    peak1, total1 = decode(one)
    peak2, total2 = decode(two)
    peak = jnp.maximum(peak1, peak2)
    up1, up2 = jnp.exp(peak1 - peak), jnp.exp(peak2 - peak)
    total = up1 * total1 + up2 * total2
    first = iota(peak.shape, 1) < ROWS
    if last:
        some = first & (total > 0.0)
        total = jnp.where(some, 1.0 / jnp.where(some, total, 1.0), 0.0)
        up1, up2 = up1 * total, up2 * total
    up1, up2 = jnp.where(first, up1, 0.0), jnp.where(first, up2, 0.0)
    context = spread(up1) * one[:, :D].astype(f32) + spread(up2) * two[:, :D].astype(f32)
    return peak, total, context


def ordered(bit, own, other):
    swap = jnp.broadcast_to(bit, own.shape) == 1
    return jnp.where(swap, other, own), jnp.where(swap, own, other)


def merge_kernel(scal, own, other, pay_out):
    one, two = ordered(scal[0] & 1, own[...].astype(f32), other[...].astype(f32))
    peak, total, context = merge(one, two)
    pay_out[:, :D] = context.astype(bf16)
    extra = jnp.zeros(peak.shape, f32)
    at = iota(peak.shape, 1) // ROWS
    for k, part in enumerate(split3(peak) + split3(total)):
        part = part.astype(f32)
        extra = jnp.where(at == k, pltpu.roll(part, k * ROWS, 1) if k else part, extra)
    pay_out[:, D:] = extra.astype(bf16)


def own_half(scal, rows, held, out):
    half = out.shape[0]
    held[...] = rows
    out[...] = held[pl.ds(pl.multiple_of((scal[0] & 1) * half, half), half)]


def forward_kernel(
    scal, own, other, first, h1, wo, g_ff, win, wdown,
    c_out, c32_out, scale_out, h2_out, z_out, part_out, c_s,
):
    bit = lax.shift_right_logical(scal[0], 1) & 1
    one, two = ordered(bit, own[...].astype(f32), other[...].astype(f32))
    peak, inverse, context = merge(one, two, True)
    mine, _ = decode(first[...].astype(f32))
    scale_out[...] = jnp.exp(jnp.minimum(mine - peak, 0.0)) * inverse
    c32_out[...] = context
    low = context.astype(bf16)
    own_half(scal, low, c_s, c_out)
    h2 = h1[...] + nn(low, wo[...])
    h2_out[...] = h2
    n2, _ = rms_parts(h2)
    y3 = (n2 * row_of(g_ff)).astype(bf16)
    z = nn(y3, win[...])
    z_out[...] = z
    u = (z * phi(z)).astype(bf16)
    part_out[...] = nn(u, wdown[...]).astype(bf16)


def score_kernel(part_a, part_b, h2, g_final, row, c, pay_out, n3_out, dh3_out):
    h3 = h2[...] + (part_a[...].astype(f32) + part_b[...].astype(f32))
    n3, r3 = rms_parts(h3)
    n3_out[...] = n3
    wanted = jnp.broadcast_to(row_of(g_final) * row_of(row) * FACTOR, (8, D))
    scores = nt(wanted, n3, EXACT)[0:1]
    wide = jnp.concatenate([scores, jnp.zeros((1, LANES - n3.shape[0]), f32)], axis=1)
    pay_out[:, :D] = c[...]
    pay_out[:, D:] = stack3(wide, c.shape[0])
    dh3_out[...] = rms_back(wanted[0:1], n3, r3).astype(bf16)


def down_kernel(dh3, z, wdown, win, part_out):
    du = nt(dh3[...], wdown[...])
    dz = (du * gelu_slope(z[...])).astype(bf16)
    part_out[...] = nt(dz, win[...]).astype(bf16)


def target_kernel(lens, rel, target_out, member_out):
    queries, docs = target_out.shape
    relevance = rel[...].reshape(1, docs)
    at = iota((queries, 1), 0)

    def one_list(j, found):
        begin, begins, ends = found
        end = begin + lens[j]
        return end, jnp.where(at == j, begin, begins), jnp.where(at == j, end, ends)

    none = jnp.zeros((queries, 1), i32)
    _, begins, ends = lax.fori_loop(
        0, queries, one_list, (jnp.int32(0), none, none), unroll=queries <= 32
    )
    place = iota((queries, docs), 1)
    member = (place >= begins) & (place < ends)
    weight = jnp.sum(jnp.where(member, relevance, 0.0), axis=1, keepdims=True)
    target_out[...] = jnp.where(member, relevance / weight, 0.0)
    member_out[...] = member.astype(f32)


def place_of(order, mask):
    pos = 0
    for k, bit in enumerate(order):
        pos = pos + (lax.shift_right_logical(mask, bit.bit_length() - 1) & 1) * (1 << k)
    return pos


def list_kernel(order, scal, sizes, rows, targets, members, scores_out, loss_out, ds_out, mine_out):
    groups = 1 << len(order)
    docs = ds_out.shape[1]
    wide = docs + LANES
    queries = targets.shape[0]
    half = rows.shape[0] // groups
    lane = iota((8, LANES), 1)
    blank = jnp.zeros((8, wide - LANES), f32)

    def one_group(g, found):
        start, placed = found
        at = pl.multiple_of(place_of(order, g ^ scal[1]) * half, half)
        parts = rows[pl.ds(at, ROWS), D:].astype(f32)
        score = (parts[0:1] + parts[1:2]) + parts[2:3]
        kept = jnp.where(lane < sizes[g], score, 0.0)
        kept = pltpu.roll(jnp.concatenate([kept, blank], axis=1), start, 1)
        return start + sizes[g], placed + kept

    _, placed = lax.fori_loop(
        0,
        groups,
        one_group,
        (jnp.int32(0), jnp.zeros((8, wide), f32)),
        unroll=groups <= 8,
    )
    values = placed[0:1, :docs]
    scores_out[...] = values.reshape(scores_out.shape)
    member = members[...] > 0.0
    target = targets[...]
    peak = jnp.max(jnp.where(member, values, MASKED), axis=1, keepdims=True)
    raised = jnp.where(member, jnp.exp(jnp.where(member, values - peak, 0.0)), 0.0)
    log_total = peak + jnp.log(jnp.sum(raised, axis=1, keepdims=True))
    picked = jnp.sum(target * values, axis=1, keepdims=True)
    loss_out[...] = jnp.sum(log_total - picked, axis=0, keepdims=True) / queries
    chance = jnp.where(member, jnp.exp(jnp.where(member, values - log_total, 0.0)), 0.0)
    ds = jnp.sum(chance - target, axis=0, keepdims=True) / queries
    ds_out[...] = ds
    ds = jnp.broadcast_to(jnp.concatenate([ds, jnp.zeros((1, LANES), f32)], axis=1), (8, wide))
    start = first_doc(scal, sizes)
    back = pltpu.roll(ds, lax.rem(wide - start, wide), 1)[:, :LANES]
    mine_out[...] = jnp.where(lane < sizes[scal[1]], back, 0.0)


def context_kernel(
    scal, part_a, part_b, h2, dh3, c32, g_ff, wout, wo_own,
    dh2_out, half_out, dc_out, own_out, inner_out, ff_out, both_s,
):
    n2, r2 = rms_parts(h2[...])
    dy3 = part_a[...].astype(f32) + part_b[...].astype(f32)
    ff_out[...] = dy3 * n2
    dh2 = (dh3[...].astype(f32) + rms_back(dy3 * row_of(g_ff), n2, r2)).astype(bf16)
    dh2_out[...] = dh2
    own_half(scal, jnp.concatenate([dh3[...], dh2], axis=1), both_s, half_out)
    dc = nt(dh2, wout[...]).astype(bf16)
    dc_out[...] = dc
    own_out[...] = nt(dh2, wo_own[...]).astype(bf16)
    hot = (head_of((D, LANES), 0) == iota((D, LANES), 1)).astype(bf16)
    high, low = split2(dc.astype(f32) * c32[...])
    inner_out[...] = nn(high, hot) + nn(low, hot)


def columns(one, two):
    tall = BLOCK * ROWS
    half = LANES // 2
    both = jnp.where(iota((BLOCK, LANES), 1) < half, one, pltpu.roll(two, half, 1))
    parts = jnp.concatenate(split3(both), axis=0)
    r, c = iota((tall, 3 * BLOCK), 0), iota((tall, 3 * BLOCK), 1)
    wide = nn((r // ROWS == c % BLOCK).astype(bf16), parts)
    lane, head = iota((tall, LANES), 1), iota((tall, LANES), 0) % ROWS
    return tuple(
        jnp.sum(jnp.where(lane == head + k * half, wide, 0.0), axis=1, keepdims=True)
        for k in range(2)
    )


def back_kernel(first, last, scal, sizes, enc, p, scale, inner, dc, wv, *refs):
    dap_out, vd_out = refs[-2:]
    tokens = enc.shape[1]
    tall = BLOCK * ROWS
    rounds = jnp.clip(rounds_of(scal, sizes), first, last)

    def one_block(step):
        block = pl.ds(pl.multiple_of(step * BLOCK, BLOCK), BLOCK)
        rows = enc[block].reshape(BLOCK * tokens, D)
        pick = (iota((tall, BLOCK), 0) // ROWS == iota((tall, BLOCK), 1)).astype(bf16)
        own = (iota((tall, D), 0) % ROWS) == head_of((tall, D), 1)
        grad = jnp.where(own, nn(pick, dc[block]), 0.0).astype(bf16)
        vd = nn(grad, wv[...]).astype(bf16)
        vd_out[block] = vd.reshape(BLOCK, ROWS, D)
        grad_probs = []
        for k in range(BLOCK // 2):
            pair = nt(
                vd[2 * ROWS * k : 2 * ROWS * (k + 1)],
                rows[2 * tokens * k : 2 * tokens * (k + 1)],
            )
            grad_probs += [pair[:ROWS, :tokens], pair[ROWS:, tokens:]]
        grad_probs = jnp.concatenate(grad_probs, axis=0)
        scale_col, inner_col = columns(scale[block], inner[block])
        prob = p[block].reshape(tall, tokens) * scale_col
        da = (prob * (grad_probs - inner_col)).astype(bf16)
        dap_out[block, :ROWS] = da.reshape(BLOCK, ROWS, tokens)
        dap_out[block, ROWS:] = prob.astype(bf16).reshape(BLOCK, ROWS, tokens)

    @pl.loop(first, rounds)
    def _(i):
        for j in range(SPAN // BLOCK):
            one_block(i * (SPAN // BLOCK) + j)

    @pl.loop(rounds, last)
    def _(i):
        span = pl.ds(pl.multiple_of(i * SPAN, SPAN), SPAN)
        dap_out[span] = jnp.zeros((SPAN, 2 * ROWS, tokens), bf16)
        vd_out[span] = jnp.zeros((SPAN, ROWS, D), bf16)


def key_sum_kernel(scal, sizes, ds, enc, dap, dh2, n3, ff, sums_out):
    tokens = enc.shape[1]
    tall = BLOCK * ROWS
    slots = dh2.shape[0]
    row = ds[...][:, :slots] * (1.0 / PARTS)
    at = iota((ROWS, D), 0)
    row = row[0:1]
    out = jnp.where(at == HEADS, jnp.sum(nn(stack3(row), dh2[...]), axis=0, keepdims=True), 0.0)
    out = jnp.where(at == HEADS + 1, row_dot(row, n3[...]), out)
    sums_out[...] = jnp.where(at == HEADS + 2, row_dot(row, ff[...]), out)

    def one_block(step):
        block = pl.ds(pl.multiple_of(step * BLOCK, BLOCK), BLOCK)
        own_slot = iota((tall, LANES), 1) == step * BLOCK + iota((tall, LANES), 0) // ROWS
        ds_col = jnp.sum(jnp.where(own_slot, ds[0:1], 0.0), axis=1, keepdims=True)
        scaled = (dap[block, :ROWS].reshape(tall, tokens).astype(f32) * ds_col).astype(bf16)
        flat = jnp.concatenate(
            [scaled[ROWS * b : ROWS * (b + 1)] for b in range(BLOCK)], axis=1
        )
        return nn(flat, enc[block].reshape(BLOCK * tokens, D))

    @pl.loop(0, rounds_of(scal, sizes))
    def _(i):
        per_round = SPAN // BLOCK
        total = one_block(i * per_round)
        for j in range(1, per_round):
            total = total + one_block(i * per_round + j)
        sums_out[...] += total


def enc_grad_kernel(first, last, ds, qa, qb, dap, vd, *refs):
    grad_out, slots, sems = refs[-3:]
    pieces, size = slots.shape[:2]
    qk = qa[...] + qb[...]
    lane = iota((1, LANES), 1)
    copies = []
    for k in range((last - first) // size):
        if k >= pieces:
            copies[k - pieces].wait()
        start = first + k * size
        for b in range(size):
            scale = jnp.sum(jnp.where(lane == start + b, ds[0:1], 0.0), axis=1, keepdims=True)
            right = jnp.concatenate([qk, vd[start + b].astype(f32)], axis=0) * scale
            slots[k % pieces, b] = tn(dap[start + b], right.astype(bf16)).astype(bf16)
        copies.append(
            pltpu.make_async_copy(
                slots.at[k % pieces], grad_out.at[pl.ds(start, size)], sems.at[k % pieces]
            )
        )
        copies[-1].start()
    for copy in copies[-pieces:]:
        copy.wait()


def share_kernel(scal, summed, scale, keep_out, send_out):
    core = scal[0] & 1
    lane = iota(scale.shape, 1)
    for out, bit in ((send_out, 1 - core), (keep_out, core)):
        for y in range(out.shape[0]):
            for k in range(out.shape[1]):
                head = (2 * y + bit) * out.shape[1] + k
                col = jnp.sum(jnp.where(lane == head, scale[...], 0.0), axis=1, keepdims=True)
                out[y, k] = (summed[head].astype(f32) * col).astype(bf16)


def away_kernel(scal, keep, got, out):
    part = 1 - (lax.shift_right_logical(scal[0], 1) & 1)
    for h in range(out.shape[0]):
        out[h] = (keep[part, h].astype(f32) + got[part, h].astype(f32)).astype(bf16)


def value_kernel(scal, keep, got, other, dc, ds, grad_out):
    slots = keep.shape[2]
    part = lax.shift_right_logical(scal[0], 1) & 1
    own_slot = iota((slots, LANES), 0) == iota((slots, LANES), 1)
    ds_col = jnp.sum(jnp.where(own_slot, ds[0:1], 0.0), axis=1, keepdims=True)
    grad = (dc[...].astype(f32) * ds_col).astype(bf16)
    for h in range(keep.shape[1]):
        pair = (keep[part, h].astype(f32) + got[part, h].astype(f32)).astype(bf16)
        summed = (pair.astype(f32) + other[h].astype(f32)).astype(bf16)
        out = tn(grad[:, h * HEAD_DIM : (h + 1) * HEAD_DIM], summed)
        grad_out[h * HEAD_DIM : (h + 1) * HEAD_DIM] = out.astype(bf16)


def document_picks(order, tile, scal, sizes, held, first):
    groups = 1 << len(order)
    half = held // groups
    core = scal[0] & 1
    doc = first + iota((tile, 1), 0)

    def one_group(g, found):
        start, at, upper = found
        pos = place_of(order, g ^ scal[1])
        slot = doc - start
        inside = (slot >= 0) & (slot < sizes[g])
        later = (slot >= half).astype(i32)
        at = jnp.where(inside, pos * half + slot - half * later, at)
        return start + sizes[g], at, jnp.where(inside, later, upper)

    zero = jnp.zeros((tile, 1), i32)
    _, at, upper = lax.fori_loop(
        0, groups, one_group, (jnp.int32(0), zero, zero), unroll=groups <= 8
    )
    hit = iota((tile, held), 1) == at
    mine = (hit & (upper == core)).astype(bf16)
    theirs = (hit & (upper != core)).astype(bf16)

    def rows(own, other, width):
        return (nn(mine, own[:, :width]) + nn(theirs, other[:, :width])).astype(bf16)

    return rows


def ds_column(ds, first, tile):
    eye = iota((tile, tile), 0) == iota((tile, tile), 1)
    return jnp.sum(jnp.where(eye, ds[0:1, pl.ds(first, tile)], 0.0), axis=1, keepdims=True)


def over_tiles(docs, tile, one_tile):
    one_tile(0, True)
    if docs > tile:

        @pl.loop(1, docs // tile)
        def _(t):
            one_tile(pl.multiple_of(t * tile, tile), False)


def put(out, value, new):
    if new:
        out[...] = value
    else:
        out[...] += value


def weights_before_kernel(
    order, tile, scal, sizes, c_own, c_other, h1, g_ff, wout, win,
    y3_out, u_out, slope_out, c_out,
):
    def one_tile(first, new):
        here = pl.ds(first, tile)
        rows = document_picks(order, tile, scal, sizes, c_own.shape[0], first)
        c = rows(c_own, c_other, D)
        h2 = h1[...] + nn(c, wout[...])
        n2, _ = rms_parts(h2)
        y3 = (n2 * row_of(g_ff)).astype(bf16)
        y3_out[here] = y3
        z = nn(y3, win[...])
        u_out[here] = (z * phi(z)).astype(bf16)
        slope_out[here] = gelu_slope(z)
        width = c_out.shape[1]
        pick = (iota((D, width), 0) == scal[0] * width + iota((D, width), 1)).astype(bf16)
        c_out[here] = nn(c, pick).astype(bf16)

    over_tiles(y3_out.shape[0], tile, one_tile)


def weights_kernel(
    order, tile, scal, sizes, y3, slope, both_own, both_other, ds, wdown,
    win_out, grads_out,
):
    def one_tile(first, new):
        here = pl.ds(first, tile)
        rows = document_picks(order, tile, scal, sizes, both_own.shape[0], first)
        both = rows(both_own, both_other, 2 * D).astype(f32) * ds_column(ds, first, tile)
        both = both.astype(bf16)
        grads_out[here] = both
        dz = (nt(both[:, :D], wdown[...]) * slope[here]).astype(bf16)
        put(win_out, tn(y3[here], dz), new)

    over_tiles(ds.shape[1], tile, one_tile)


def weights_after_kernel(tile, u, c, grads, wdown_out, wout_out):
    def one_tile(first, new):
        here = pl.ds(first, tile)
        put(wdown_out, tn(u[here], grads[here, :D]), new)
        put(wout_out, tn(c[here], grads[here, D:]), new)

    over_tiles(u.shape[0], tile, one_tile)


def key_kernel(scal, sum_a, sum_b, h1, g_cross, wk, wq, key_out, query_out, part_out):
    y2, qm = query_parts(scal, h1, g_cross, wq)
    g = sum_a[...] + sum_b[...]
    g = jnp.where(iota((ROWS, D), 0) < HEADS, g, 0.0)
    high, low = split2(g)
    both = jnp.concatenate([high, low], axis=0)
    dq = nt(both, wk[...])
    dq = dq[:ROWS] + dq[ROWS:]
    width = dq.shape[1]
    first = scal[0] * (width // HEAD_DIM)
    own = iota((ROWS, width), 0) == first + head_of((ROWS, width), 1)
    dq = jnp.sum(jnp.where(own, dq, 0.0), axis=0, keepdims=True)
    key_out[...] = tn(jnp.concatenate([qm, qm], axis=0), both)
    dq_parts = stack3(dq)
    query_out[...] = tn(dq_parts, repeat3(y2[0:1]))
    part = jnp.sum(nn(dq_parts, wq[...]), axis=0, keepdims=True)
    part_out[...] = jnp.broadcast_to(part, (8, D))


def hidden_kernel(
    part_a, part_b, sum_a, sum_b, h1, g_cross, start, g_self, wos, wvs, g_final, row,
    dh1_out, wos_out, wvs_out, part_out, cross_out, final_out, row_out, ff_out,
):
    y1, s1 = self_parts(start, g_self, wvs)
    dy2 = part_a[0:1] + part_b[0:1]
    sums = sum_a[...] + sum_b[...]
    n1, r1 = rms_parts(h1[...])
    cross_out[...] = (dy2 * n1).reshape(cross_out.shape)
    dh1 = sums[HEADS : HEADS + 1] + rms_back(dy2 * row_of(g_cross), n1, r1)
    dh1_out[...] = dh1
    dh1_parts = stack3(dh1)
    wos_out[...] = tn(repeat3(s1[0:1]), dh1_parts)
    ds1 = jnp.sum(nt(dh1_parts, wos[...]), axis=0, keepdims=True)
    ds1_parts = stack3(ds1)
    wvs_out[...] = tn(ds1_parts, repeat3(y1[0:1]))
    part = jnp.sum(nn(ds1_parts, wvs[...]), axis=0, keepdims=True)
    part_out[...] = jnp.broadcast_to(part, (8, D))
    total = sums[HEADS + 1 : HEADS + 2] * FACTOR
    final_out[...] = (total * row_of(row)).reshape(final_out.shape)
    row_out[...] = (total * row_of(g_final)).reshape(row_out.shape)
    ff_out[...] = sums[HEADS + 2 : HEADS + 3].reshape(ff_out.shape)


def start_kernel(part_a, part_b, dh1, start, g_self, gain_out, start_out):
    dy1 = part_a[0:1] + part_b[0:1]
    n0, r0 = rms_parts(row_of(start))
    gain_out[...] = (dy1 * n0).reshape(gain_out.shape)
    back = dh1[...] + rms_back(dy1 * row_of(g_self), n0, r0)
    start_out[...] = back.reshape(start_out.shape)


def shape(dims, dtype=f32):
    return jax.ShapeDtypeStruct(dims, dtype)


def whole_spec(memory=pltpu.VMEM):
    return pl.BlockSpec(memory_space=memory)


def name_of(kernel):
    return getattr(kernel, "func", kernel).__name__


def in_hbm(x):
    return pltpu.with_memory_space_constraint(x, pltpu.HBM)


def plain(
    kernel, outs, *args, smem=0, hbm=(), hbm_out=False, onto=None, limit=12, scratch=()
):
    spaces = [pltpu.SMEM] * smem + [pltpu.VMEM] * (len(args) - smem)
    for k in hbm:
        spaces[k] = pltpu.HBM
    out_space = pltpu.HBM if hbm_out else pltpu.VMEM
    return pl.pallas_call(
        kernel,
        out_shape=outs,
        in_specs=[whole_spec(space) for space in spaces],
        out_specs=[whole_spec(out_space) for _ in outs]
        if isinstance(outs, list)
        else whole_spec(out_space),
        scratch_shapes=list(scratch),
        input_output_aliases=onto or {},
        compiler_params=pltpu.CompilerParams(vmem_limit_bytes=limit * MIB),
        cost_estimate=pl.CostEstimate(flops=0, bytes_accessed=0, transcendentals=0),
        name=name_of(kernel),
    )(*args)


def bits_of(size):
    return [1 << b for b in range(size.bit_length() - 1)]


def far_first(size):
    return bits_of(size)[::-1]


def swap(x, axis, bit):
    size = lax.axis_size(axis)
    return lax.ppermute(x, axis, [(i, i ^ bit) for i in range(size)])


def after(x, *deps):
    return lax.optimization_barrier((x, *deps))[0]


def add(x, y):
    return (x.astype(f32) + y.astype(f32)).astype(x.dtype)


def sum_last(x, steps):
    for axis, bit in steps[:-1]:
        x = add(x, swap(x, axis, bit))
    axis, bit = steps[-1]
    return x, swap(x, axis, bit)


def per_device(
    enc_out,
    enc_len,
    group_docs,
    list_len,
    relevance,
    start_token,
    score_row,
    g_self,
    w_value_self,
    w_out_self,
    g_cross,
    w_query,
    w_key,
    w_value,
    w_out,
    g_ff,
    w_in,
    w_down,
    g_final,
):
    groups = lax.axis_size("docs")
    parts = lax.axis_size("heads")
    assert parts == PARTS
    me_g = lax.axis_index("docs")
    me_j = lax.axis_index("heads")
    slots, tokens = enc_out.shape[:2]
    docs = enc_len.shape[0]
    width = w_value.shape[1]
    own_heads = HEADS // parts
    hidden = w_in.shape[1]
    over_heads = [("heads", 1), ("heads", 2)]
    order = far_first(groups)
    over_docs = [("docs", bit) for bit in order]

    scal = jnp.stack([me_j, me_g])
    wvs_t, wq_t, wk_t, wv_t = (w.T for w in (w_value_self, w_query, w_key, w_value))

    wv_by1, wo_by1 = swap(wv_t, "heads", 1), swap(w_out, "heads", 1)

    part = plain(
        self_kernel,
        shape((8, D)),
        *map(in_hbm, (start_token, g_self, wvs_t, w_out_self)),
    )


    def load(first, last, since, *onto):
        return pl.pallas_call(
            functools.partial(load_kernel, first, last),
            out_shape=pltpu.VMEM(enc_out.shape, bf16),
            in_specs=[whole_spec(pltpu.HBM), whole_spec(pl.ANY), whole_spec(pltpu.SMEM)]
            + [whole_spec()] * len(onto),
            out_specs=whole_spec(),
            scratch_shapes=[pltpu.SemaphoreType.DMA((last - first,))],
            input_output_aliases={3: 0} if onto else {},
            compiler_params=pltpu.CompilerParams(vmem_limit_bytes=MIB),
            cost_estimate=pl.CostEstimate(flops=0, bytes_accessed=0, transcendentals=0),
            name="load_kernel",
        )(in_hbm(enc_out), since, scal, *onto)

    part = add(part, swap(part, "heads", 1))
    part_a, part_b = part, swap(part, "heads", 2)
    held = load(0, 1, part)
    part_b, held = lax.optimization_barrier((part_b, held))
    wv_by2 = swap(after(wv_t, part_b), "heads", 2)
    qk, h1 = plain(
        query_kernel,
        [shape((ROWS, D)), shape((1, D))],
        scal,
        part_a,
        part_b,
        *map(in_hbm, (start_token, g_cross, wq_t, wk_t)),
        smem=1,
    )
    qk = add(qk, swap(qk, "heads", 1))
    qk, held = lax.optimization_barrier((qk, held))
    qk_a, qk_b = qk, swap(qk, "heads", 2)
    held = load(1, 3, qk, held)
    qk_b, held, wv_by2 = lax.optimization_barrier((qk_b, held, wv_by2))
    wv_by3 = swap(wv_by2, "heads", 1)

    wo_by2 = swap(after(w_out, qk_b), "heads", 2)
    held, prob, summed, extra = plain(
        functools.partial(attend_kernel, 3),
        [
            pltpu.VMEM(enc_out.shape, bf16),
            pltpu.VMEM((slots, ROWS, tokens), f32),
            pltpu.VMEM((PANELS, slots * ROWS, LANES), f32),
            shape((slots, LANES), bf16),
        ],
        scal,
        group_docs,
        enc_len,
        qk_a,
        qk_b,
        in_hbm(enc_out),
        held,
        smem=3,
        hbm=(5,),
        onto={6: 0},
        scratch=[pltpu.VMEM((2 * ROWS, D), bf16), pltpu.SemaphoreType.DMA((slots // BLOCK,))],
        limit=16,
    )
    summed, wv_by3, wo_by2 = lax.optimization_barrier((summed, wv_by3, wo_by2))
    wv_parts = (wv_t, wv_by2, wv_by1, wv_by3)
    wo_parts = (w_out, wo_by2, wo_by1, swap(wo_by2, "heads", 1))
    pay, summed, wv_full = plain(
        project_kernel,
        [
            shape((slots, D + LANES), bf16),
            shape((HEADS, slots, D), bf16),
            shape((D, D), bf16),
        ],
        scal,
        summed,
        extra,
        *wv_parts,
        smem=1,
    )
    merged = plain(
        merge_kernel, shape(pay.shape, bf16), scal, pay, swap(pay, "heads", 1), smem=1
    )
    other = swap(merged, "heads", 2)
    wo_full = plain(arrange_kernel, shape((D, D), bf16), scal, *wo_parts, smem=1)
    target, member = plain(
        target_kernel, [shape((list_len.shape[0], docs))] * 2, list_len, relevance, smem=1
    )
    other, wo_full, target, member = lax.optimization_barrier((other, wo_full, target, member))

    c, c32, scale, h2, z, part = plain(
        forward_kernel,
        [
            shape((slots // 2, D), bf16),
            shape((slots, D)),
            shape((slots, LANES)),
            shape((slots, D)),
            shape((slots, hidden)),
            shape((slots, D), bf16),
        ],
        scal,
        merged,
        other,
        pay,
        h1,
        wo_full,
        g_ff,
        w_in,
        w_down,
        smem=1,
        scratch=[pltpu.VMEM((slots, D), bf16)],
    )

    half = slots // 2

    def grow(x, k):
        return jnp.concatenate([x, swap(x, *over_docs[k])], axis=0)

    def tie(*xs):
        return lax.optimization_barrier(xs)

    last = len(over_docs) - 1
    near_first = over_docs[::-1]
    part = add(part, swap(part, "heads", 1))
    part_a, part_b = part, swap(part, "heads", 2)
    c_all, n3, dh3 = plain(
        score_kernel,
        [shape((half, D + LANES), bf16), shape((slots, D)), shape((slots, D), bf16)],
        part_a,
        part_b,
        h2,
        g_final,
        score_row,
        c,
    )
    part = plain(down_kernel, shape((slots, D), bf16), dh3, z, w_down, w_in)
    part = add(part, swap(part, "heads", 1))
    part, summed = tie(part, summed)
    part_a, part_b = part, swap(part, "heads", 2)
    c_far = swap(c_all, *over_docs[0])
    keep, sent = plain(
        share_kernel, [shape((2, own_heads, slots, D), bf16)] * 2, scal, summed, scale, smem=1
    )
    got = swap(sent, "heads", 1)
    away = plain(
        away_kernel, shape((own_heads, slots, D), bf16), scal, keep, got, smem=1
    )
    other = swap(away, "heads", 2)
    part_b, away = tie(part_b, away)
    dh2, grads, dc, dc_own, inner, ff = plain(
        context_kernel,
        [
            shape((slots, D), bf16),
            shape((half, 2 * D), bf16),
            shape((slots, D), bf16),
            shape((slots, width), bf16),
            shape((slots, LANES)),
            shape((slots, D)),
        ],
        scal,
        part_a,
        part_b,
        h2,
        dh3,
        c32,
        g_ff,
        wo_full,
        w_out,
        smem=1,
        scratch=[pltpu.VMEM((slots, 2 * D), bf16)],
    )

    c_all, c_far, dc, grads = tie(c_all, c_far, dc, grads)
    c_all = jnp.concatenate([c_all, c_far], axis=0)
    for k in range(1, last):
        c_far = swap(c_all, *over_docs[k])
        if k < last - 1:
            c_all = jnp.concatenate([c_all, c_far], axis=0)
    grads_far = swap(grads, *over_docs[0])

    outs = [
        pltpu.VMEM((slots, 2 * ROWS, tokens), bf16),
        pltpu.VMEM((slots, ROWS, D), bf16),
    ]
    rounds = slots // SPAN
    inputs = (scal, group_docs, held, prob, scale, inner, dc, wv_full)

    def back(first, last, *onto):
        return plain(
            functools.partial(back_kernel, first, last),
            outs,
            *inputs,
            *onto,
            smem=2,
            onto={8: 0, 9: 1} if onto else None,
            limit=16,
        )

    dap, vd = back(0, 1)
    dap, c_far = tie(dap, c_far)
    c_all = jnp.concatenate([c_all, c_far], axis=0)
    c_far = swap(c_all, *over_docs[last])
    dap, vd = back(1, rounds, dap, vd)
    dap, c_far, other, grads_far = tie(dap, c_far, other, grads_far)
    grads = jnp.concatenate([grads, grads_far], axis=0)
    for m in range(1, last):
        grads_far = swap(grads, *over_docs[m])
        if m < last - 1:
            grads = jnp.concatenate([grads, grads_far], axis=0)
    c_all = jnp.concatenate([c_all, c_far], axis=0)
    all_scores, loss, ds_docs, ds_mine = plain(
        functools.partial(list_kernel, order),
        [shape((docs,)), shape((1, 1)), shape((1, docs)), shape((8, LANES))],
        scal,
        group_docs,
        c_all,
        target,
        member,
        smem=2,
    )
    value_part = plain(
        value_kernel,
        shape((width, D), bf16),
        scal,
        keep,
        got,
        other,
        dc_own,
        ds_mine,
        smem=1,
    )
    dap, value_part = tie(dap, value_part)
    value_far = swap(value_part, *near_first[0])
    c_far = swap(c_all, "heads", 1)
    sums = plain(
        key_sum_kernel,
        shape((ROWS, D)),
        scal,
        group_docs,
        ds_mine,
        held,
        dap,
        dh2,
        n3,
        ff,
        smem=2,
    )

    def enc_grads(first, last, grads=None):
        outs = pltpu.HBM(enc_out.shape, bf16)
        size = 8
        args = (ds_mine, qk_a, qk_b, dap, vd)
        return plain(
            functools.partial(enc_grad_kernel, first, last),
            outs,
            *args,
            *([] if grads is None else [grads]),
            hbm=() if grads is None else (len(args),),
            hbm_out=True,
            onto={} if grads is None else {len(args): 0},
            scratch=[pltpu.VMEM((4, size, tokens, D), bf16), pltpu.SemaphoreType.DMA((4,))],
            limit=16,
        )

    sums = add(sums, swap(sums, "heads", 1))
    steps = near_first[:0:-1] + over_heads[1:] + near_first[:1]
    sums, grads_far = tie(sums, grads_far)
    grads = jnp.concatenate([grads, grads_far], axis=0)
    grads_far = swap(grads, *over_docs[last])
    enc_grad = None
    third = slots // 3
    sum_a = sums
    for k, step in enumerate(steps):
        ds_mine, sum_a = tie(ds_mine, sum_a)
        sum_b = swap(sum_a, *step)
        if k < 3:
            enc_grad = enc_grads(k * third, (k + 1) * third, enc_grad)
            sum_b, enc_grad = tie(sum_b, enc_grad)
        if k == 1:
            sum_b, value_far, c_far = tie(sum_b, value_far, c_far)
            for step in near_first[1:-1]:
                value_part = add(value_part, value_far)
                value_far = swap(value_part, *step)
        if k < len(steps) - 1:
            sum_a = sum_a + sum_b
    y3, u, slope, c_own = plain(
        functools.partial(weights_before_kernel, order, 384),
        [
            shape((docs, D), bf16),
            shape((docs, hidden), bf16),
            shape((docs, hidden)),
            shape((docs, width), bf16),
        ],
        scal,
        group_docs,
        c_all,
        c_far,
        h1,
        g_ff,
        wo_full,
        w_in,
        smem=2,
        limit=60 if docs > 384 else 16,
    )
    sum_b, grads_far, value_far, y3, u, slope, c_own = tie(
        sum_b, grads_far, value_far, y3, u, slope, c_own
    )
    value_part = add(value_part, value_far)
    value_far = swap(value_part, *near_first[-1])
    grads = jnp.concatenate([grads, grads_far], axis=0)
    grads_far = swap(grads, "heads", 1)

    key_grad, query_grad, part = plain(
        key_kernel,
        [shape((width, D)), shape((width, D)), shape((8, D))],
        scal,
        sum_a,
        sum_b,
        h1,
        g_cross,
        wk_t,
        wq_t,
        smem=1,
    )
    part = add(part, swap(part, "heads", 1))
    part, grads_far = tie(part, grads_far)
    part_a, part_b = part, swap(part, "heads", 2)
    w_in_grad, grads_docs = plain(
        functools.partial(weights_kernel, order, 384),
        [shape((D, hidden)), shape((docs, 2 * D), bf16)],
        scal,
        group_docs,
        y3,
        slope,
        grads,
        grads_far,
        ds_docs,
        w_down,
        smem=2,
        limit=60 if docs > 384 else 16,
    )
    part_b, w_in_grad, grads_docs = tie(part_b, w_in_grad, grads_docs)
    dh1, wos_grad, wvs_grad, part, cross, final_gain, row_grad, ff_gain = plain(
        hidden_kernel,
        [shape((1, D)), shape((width, D)), shape((width, D)), shape((8, D))] + [shape((D,))] * 4,
        part_a,
        part_b,
        sum_a,
        sum_b,
        h1,
        g_cross,
        start_token,
        g_self,
        w_out_self,
        wvs_t,
        g_final,
        score_row,
    )
    part_a, part_b = sum_last(part, over_heads)
    w_down_grad, w_out_grad = plain(
        functools.partial(weights_after_kernel, 384),
        [shape((hidden, D)), shape((width, D))],
        u,
        c_own,
        grads_docs,
        limit=60 if docs > 384 else 16,
    )
    part_b, w_down_grad, value_far = tie(part_b, w_down_grad, value_far)
    value_grad = (value_part.astype(f32) + value_far.astype(f32)).T
    self_gain, start_grad = plain(
        start_kernel, [shape((D,))] * 2, part_a, part_b, dh1, start_token, g_self
    )

    return (
        all_scores,
        loss.reshape(()),
        enc_grad,
        start_grad,
        row_grad,
        self_gain,
        wvs_grad.T,
        wos_grad,
        cross,
        query_grad.T,
        key_grad.T,
        value_grad,
        w_out_grad,
        ff_gain,
        w_in_grad,
        w_down_grad,
        final_gain,
    )


def solution(mesh):
    placed = (
        P("docs", "heads", None),
        P(),
        P(),
        P(),
        P(),
        P(),
        P(),
        P(),
        P(None, "heads"),
        P("heads", None),
        P(),
        P(None, "heads"),
        P(None, "heads"),
        P(None, "heads"),
        P("heads", None),
        P(),
        P(None, "heads"),
        P("heads", None),
        P(),
    )
    return jax.shard_map(
        per_device,
        mesh=mesh,
        in_specs=placed,
        out_specs=(
            P(),
            P(),
            P("docs", "heads", None),
            P(),
            P(),
            P(),
            P(None, "heads"),
            P("heads", None),
            P(),
            P(None, "heads"),
            P(None, "heads"),
            P(None, "heads"),
            P("heads", None),
            P(),
            P(None, "heads"),
            P("heads", None),
            P(),
        ),
        check_vma=False,
    )
```

```python
import functools

import jax
import jax.numpy as jnp
from jax import lax
from jax.experimental import pallas as pl
from jax.experimental.pallas import tpu as pltpu
from jax.sharding import PartitionSpec as P

D = 768
HEADS = 12
HEAD_DIM = 64
ROWS = 16
BLOCK = 16
SPAN = 2 * BLOCK
LANES = 128
PANELS = D // LANES
COLUMNS = 256
PARTS = 4

EPSILON = 1e-06
MASKED = -1e30
FACTOR = D ** (-0.5)
ROOT_HALF = 0.5**0.5
DENSITY = 0.3989422804014327
f32, bf16, i32 = jnp.float32, jnp.bfloat16, jnp.int32
EXACT = lax.Precision.HIGHEST
MIB = 1 << 20


def nn(a, b, precision=None):
    return lax.dot_general(
        a, b, (((1,), (0,)), ((), ())), precision=precision, preferred_element_type=f32
    )


def nt(a, b, precision=None):
    return lax.dot_general(
        a, b, (((1,), (1,)), ((), ())), precision=precision, preferred_element_type=f32
    )


def tn(a, b, precision=None):
    return lax.dot_general(
        a, b, (((0,), (0,)), ((), ())), precision=precision, preferred_element_type=f32
    )


def iota(shape, dim):
    return lax.broadcasted_iota(i32, shape, dim)


def split2(x):
    high = x.astype(bf16)
    return high, (x - high.astype(f32)).astype(bf16)


def split3(x):
    high = x.astype(bf16)
    rest = x - high.astype(f32)
    mid = rest.astype(bf16)
    return high, mid, (rest - mid.astype(f32)).astype(bf16)


def stack3(row, height=ROWS):
    at = iota((height, row.shape[1]), 0)
    parts = split3(row)
    zero = jnp.zeros((), f32)
    out = jnp.where(at == 0, parts[0].astype(f32), zero)
    out = jnp.where(at == 1, parts[1].astype(f32), out)
    return jnp.where(at == 2, parts[2].astype(f32), out).astype(bf16)


def repeat3(row, height=ROWS):
    at = iota((height, row.shape[1]), 0)
    return jnp.where(at < 3, row.astype(f32), 0.0).astype(bf16)


def rms_parts(rows):
    scale = lax.rsqrt(jnp.mean(rows * rows, axis=-1, keepdims=True) + EPSILON)
    return rows * scale, scale


def rms_back(grad_normed, normed, scale):
    inner = jnp.mean(grad_normed * normed, axis=-1, keepdims=True)
    return scale * (grad_normed - normed * inner)


def phi(z):
    return 0.5 * (1.0 + lax.erf(z * ROOT_HALF))


def gelu_slope(z):
    return phi(z) + z * (DENSITY * jnp.exp(-0.5 * z * z))


def head_of(shape, dim):
    return iota(shape, dim) // HEAD_DIM


def spread(small):
    high, mid, low = (part.astype(f32) for part in split3(small))
    packed = high + pltpu.roll(mid, ROWS, 1) + pltpu.roll(low, 2 * ROWS, 1)
    lane = iota((LANES, D), 0)
    hot = (lane < 3 * ROWS) & (lane % ROWS == head_of((LANES, D), 1))
    return nn(packed.astype(bf16), hot.astype(bf16))


def row_dot(row, right):
    high, low = split2(right)
    parts = stack3(row)
    return jnp.sum(nn(parts, high) + nn(parts, low), axis=0, keepdims=True)


def row_of(ref):
    return ref[...].astype(f32).reshape(1, D)


def gained(n, gain):
    return jnp.broadcast_to(n * row_of(gain), (ROWS, D)).astype(bf16)


def self_parts(start, g_self, wvs):
    x0 = row_of(start)
    n0, _ = rms_parts(x0)
    y1 = gained(n0, g_self)
    return y1, nt(y1, wvs[...]).astype(bf16)


def query_parts(scal, h1, g_cross, wq):
    n1, _ = rms_parts(h1[...])
    y2 = gained(n1, g_cross)
    q = nt(y2, wq[...]).astype(bf16)
    width = q.shape[1]
    first = scal[0] * (width // HEAD_DIM)
    own = iota((ROWS, width), 0) == first + head_of((ROWS, width), 1)
    return y2, jnp.where(own, q.astype(f32), 0.0).astype(bf16)


def self_kernel(start, g_self, wvs, wos, part_out):
    _, s1 = self_parts(start, g_self, wvs)
    part_out[...] = nn(s1, wos[...])[:8]


def load_kernel(first, last, enc, since, scal, *refs):
    held, sems = refs[-2:]
    loads = []
    for k in range(first, last):
        part = pl.ds(k * BLOCK, BLOCK)
        loads.append(pltpu.make_async_copy(enc.at[part], held.at[part], sems.at[k - first]))
        loads[-1].start()
    for load in loads:
        load.wait()


def query_kernel(scal, part_a, part_b, start, g_cross, wq, wk, qk_out, h1_out):
    h1_out[...] = row_of(start) + (part_a[0:1] + part_b[0:1])
    _, qm = query_parts(scal, h1_out, g_cross, wq)
    qk_out[...] = nn(qm, wk[...])


def load_kernel(first, last, enc, since, scal, *refs):
    held, sems = refs[-2:]
    loads = []
    for k in range(first, last):
        part = pl.ds(k * BLOCK, BLOCK)
        loads.append(pltpu.make_async_copy(enc.at[part], held.at[part], sems.at[k - first]))
        loads[-1].start()
    for load in loads:
        load.wait()


def query_kernel(scal, part_a, part_b, start, g_cross, wq, wk, qk_out, h1_out):
    h1_out[...] = row_of(start) + (part_a[0:1] + part_b[0:1])
    _, qm = query_parts(scal, h1_out, g_cross, wq)
    qk_out[...] = nn(qm, wk[...])


def select_docs(height, width):
    r, c = iota((height, width), 0), iota((height, width), 1)
    return (((r // BLOCK) == (c % ROWS)) & ((r % BLOCK) == (c // ROWS))).astype(bf16)


def first_doc(scal, sizes):
    groups = sizes.shape[0]

    def body(g, total):
        return total + jnp.where(g < scal[1], sizes[g], 0)

    return lax.fori_loop(0, groups, body, jnp.int32(0), unroll=groups <= 8)


def rounds_of(scal, sizes):
    return (sizes[scal[1]] + SPAN - 1) // SPAN


def attend_kernel(
    loaded, scal, sizes, lengths, qa, qb, enc, _, held, p_out, e_out, ext_out, qk_s, sems
):
    tokens = enc.shape[1]
    blocks = enc.shape[0] // BLOCK
    rounds = rounds_of(scal, sizes)
    per_round = SPAN // BLOCK
    count = sizes[scal[1]]
    begin = first_doc(scal, sizes)
    tall = BLOCK * ROWS

    def piece(k):
        part = pl.ds(k * BLOCK, BLOCK)
        return pltpu.make_async_copy(enc.at[part], held.at[part], sems.at[k])

    for k in range(loaded, blocks):
        pl.when(k // per_round < rounds)(lambda k=k: piece(k).start())
    high, low = split2(qa[...] + qb[...])
    qk_s[0:ROWS] = high
    qk_s[ROWS : 2 * ROWS] = low

    def one_block(step):
        block = pl.ds(pl.multiple_of(step * BLOCK, BLOCK), BLOCK)
        flat = pl.ds(pl.multiple_of(step * tall, tall), tall)
        rows = held[block].reshape(BLOCK * tokens, D)
        both = nt(qk_s[...], rows)
        logits = both[:ROWS] + both[ROWS:]
        logits = jnp.concatenate(
            [logits[:, b * tokens : (b + 1) * tokens] for b in range(BLOCK)], axis=0
        )
        shown = []
        for b in range(BLOCK):
            slot = step * BLOCK + b
            doc = jnp.minimum(begin + slot, lengths.shape[0] - 1)
            length = jnp.where(slot < count, lengths[doc] - scal[0] * tokens, 0)
            shown.append(jnp.broadcast_to(length, (ROWS, tokens)))
        seen = iota((tall, tokens), 1) < jnp.concatenate(shown, axis=0)
        logits = jnp.where(seen, logits, MASKED)
        peak = jnp.max(logits, axis=1, keepdims=True)
        raised = jnp.where(seen, jnp.exp(logits - peak), 0.0)
        total = jnp.sum(raised, axis=1, keepdims=True)
        p_out[block] = raised.reshape(BLOCK, ROWS, tokens)
        low = raised.astype(bf16)
        summed = jnp.concatenate(
            [
                nn(low[ROWS * b : ROWS * (b + 1)], rows[tokens * b : tokens * (b + 1)])
                for b in range(BLOCK)
            ],
            axis=0,
        )
        for k in range(PANELS):
            e_out[k, flat] = summed[:, k * LANES : (k + 1) * LANES]
        gather = (iota((BLOCK, tall), 0) == iota((BLOCK, tall), 1) // ROWS).astype(bf16)
        parts = split3(peak) + split3(total)
        at = iota((tall, LANES), 1)
        extra = jnp.zeros((tall, LANES), f32)
        for k, part in enumerate(parts):
            extra = jnp.where(at // ROWS == k, part.astype(f32), extra)
        extra = jnp.where(at % ROWS == iota((tall, LANES), 0) % ROWS, extra, 0.0)
        ext_out[block] = nn(gather, extra.astype(bf16)).astype(bf16)

    @pl.loop(0, rounds)
    def _(i):
        for j in range(per_round):
            k = i * per_round + j
            pl.when(k >= loaded)(lambda k=k: piece(k).wait())
        for j in range(per_round):
            one_block(i * per_round + j)

    @pl.loop(rounds, enc.shape[0] // SPAN)
    def _(i):
        span = pl.ds(pl.multiple_of(i * SPAN, SPAN), SPAN)
        flat = pl.ds(pl.multiple_of(i * SPAN * ROWS, SPAN * ROWS), SPAN * ROWS)
        p_out[span] = jnp.zeros((SPAN, ROWS, tokens), f32)
        for k in range(PANELS):
            e_out[k, flat] = jnp.zeros((SPAN * ROWS, LANES), f32)
        ext_out[span] = jnp.where(iota((SPAN, LANES), 1) < ROWS, MASKED, 0.0).astype(bf16)


def sums_of_head(summed, head, slots):
    rows = pl.ds(head, slots, stride=ROWS)
    return jnp.concatenate([summed[k, rows, :] for k in range(PANELS)], axis=1)


def place_parts(scal, full, own, by2, by1, by3):
    height = own.shape[0]
    for mask, piece in ((0, own), (2, by2), (1, by1), (3, by3)):
        at = pl.multiple_of((scal[0] ^ mask) * height, height)
        full[pl.ds(at, height)] = piece[...]


def arrange_kernel(scal, own, by2, by1, by3, full_out):
    place_parts(scal, full_out, own, by2, by1, by3)


def project_kernel(scal, summed, extra, own, by2, by1, by3, pay_out, heads_out, wv):
    place_parts(scal, wv, own, by2, by1, by3)
    slots = pay_out.shape[0]
    even = iota((slots, LANES), 1) < HEAD_DIM
    for k in range(HEADS // 2):
        pair = wv[k * LANES : (k + 1) * LANES]
        for head in (2 * k, 2 * k + 1):
            heads_out[head] = sums_of_head(summed, head, slots).astype(bf16)
        one, two = (nt(heads_out[2 * k + odd], pair) for odd in range(2))
        pay_out[:, k * LANES : (k + 1) * LANES] = jnp.where(even, one, two).astype(bf16)
    pay_out[:, D:] = extra[...]


def decode(pay):
    extra = pay[:, D:].astype(f32)

    def lane(k):
        return pltpu.roll(extra, LANES - k * ROWS, 1) if k else extra

    first = iota(extra.shape, 1) < ROWS
    peak = jnp.where(first, (lane(0) + lane(1)) + lane(2), 0.0)
    total = jnp.where(first, (lane(3) + lane(4)) + lane(5), 0.0)
    return peak, total


def merge(one, two, last=False):
    peak1, total1 = decode(one)
    peak2, total2 = decode(two)
    peak = jnp.maximum(peak1, peak2)
    up1, up2 = jnp.exp(peak1 - peak), jnp.exp(peak2 - peak)
    total = up1 * total1 + up2 * total2
    first = iota(peak.shape, 1) < ROWS
    if last:
        some = first & (total > 0.0)
        total = jnp.where(some, 1.0 / jnp.where(some, total, 1.0), 0.0)
        up1, up2 = up1 * total, up2 * total
    up1, up2 = jnp.where(first, up1, 0.0), jnp.where(first, up2, 0.0)
    context = spread(up1) * one[:, :D].astype(f32) + spread(up2) * two[:, :D].astype(f32)
    return peak, total, context


def ordered(bit, own, other):
    swap = jnp.broadcast_to(bit, own.shape) == 1
    return jnp.where(swap, other, own), jnp.where(swap, own, other)


def merge_kernel(scal, own, other, pay_out):
    one, two = ordered(scal[0] & 1, own[...].astype(f32), other[...].astype(f32))
    peak, total, context = merge(one, two)
    pay_out[:, :D] = context.astype(bf16)
    extra = jnp.zeros(peak.shape, f32)
    at = iota(peak.shape, 1) // ROWS
    for k, part in enumerate(split3(peak) + split3(total)):
        part = part.astype(f32)
        extra = jnp.where(at == k, pltpu.roll(part, k * ROWS, 1) if k else part, extra)
    pay_out[:, D:] = extra.astype(bf16)


def own_half(scal, rows, held, out):
    half = out.shape[0]
    held[...] = rows
    out[...] = held[pl.ds(pl.multiple_of((scal[0] & 1) * half, half), half)]


def forward_kernel(
    scal, own, other, first, h1, wo, g_ff, win, wdown,
    c_out, c32_out, scale_out, h2_out, z_out, part_out, c_s,
):
    bit = lax.shift_right_logical(scal[0], 1) & 1
    one, two = ordered(bit, own[...].astype(f32), other[...].astype(f32))
    peak, inverse, context = merge(one, two, True)
    mine, _ = decode(first[...].astype(f32))
    scale_out[...] = jnp.exp(jnp.minimum(mine - peak, 0.0)) * inverse
    c32_out[...] = context
    low = context.astype(bf16)
    own_half(scal, low, c_s, c_out)
    h2 = h1[...] + nn(low, wo[...])
    h2_out[...] = h2
    n2, _ = rms_parts(h2)
    y3 = (n2 * row_of(g_ff)).astype(bf16)
    z = nn(y3, win[...])
    z_out[...] = z
    u = (z * phi(z)).astype(bf16)
    part_out[...] = nn(u, wdown[...]).astype(bf16)


def score_kernel(part_a, part_b, h2, g_final, row, c, pay_out, n3_out, dh3_out):
    h3 = h2[...] + (part_a[...].astype(f32) + part_b[...].astype(f32))
    n3, r3 = rms_parts(h3)
    n3_out[...] = n3
    wanted = jnp.broadcast_to(row_of(g_final) * row_of(row) * FACTOR, (8, D))
    scores = nt(wanted, n3, EXACT)[0:1]
    wide = jnp.concatenate([scores, jnp.zeros((1, LANES - n3.shape[0]), f32)], axis=1)
    pay_out[:, :D] = c[...]
    pay_out[:, D:] = stack3(wide, c.shape[0])
    dh3_out[...] = rms_back(wanted[0:1], n3, r3).astype(bf16)


def down_kernel(dh3, z, wdown, win, part_out):
    du = nt(dh3[...], wdown[...])
    dz = (du * gelu_slope(z[...])).astype(bf16)
    part_out[...] = nt(dz, win[...]).astype(bf16)


def target_kernel(order, scal, sizes, lens, rel, target_out, member_out, *picks_out):
    if picks_out:
        tile, held = picks_out[0].shape
        for out, pick in zip(picks_out, document_picks(order, tile, scal, sizes, held, 0)):
            out[...] = pick
    queries, docs = target_out.shape
    relevance = rel[...].reshape(1, docs)
    at = iota((queries, 1), 0)

    def one_list(j, found):
        begin, begins, ends = found
        end = begin + lens[j]
        return end, jnp.where(at == j, begin, begins), jnp.where(at == j, end, ends)

    none = jnp.zeros((queries, 1), i32)
    _, begins, ends = lax.fori_loop(
        0, queries, one_list, (jnp.int32(0), none, none), unroll=queries <= 32
    )
    place = iota((queries, docs), 1)
    member = (place >= begins) & (place < ends)
    weight = jnp.sum(jnp.where(member, relevance, 0.0), axis=1, keepdims=True)
    target_out[...] = jnp.where(member, relevance / weight, 0.0)
    member_out[...] = member.astype(f32)


def place_of(order, mask):
    pos = 0
    for k, bit in enumerate(order):
        pos = pos + (lax.shift_right_logical(mask, bit.bit_length() - 1) & 1) * (1 << k)
    return pos


def list_kernel(order, scal, sizes, rows, targets, members, scores_out, loss_out, ds_out, mine_out):
    groups = 1 << len(order)
    docs = ds_out.shape[1]
    wide = docs + LANES
    queries = targets.shape[0]
    half = rows.shape[0] // groups
    lane = iota((8, LANES), 1)
    blank = jnp.zeros((8, wide - LANES), f32)

    def one_group(g, found):
        start, placed = found
        at = pl.multiple_of(place_of(order, g ^ scal[1]) * half, half)
        parts = rows[pl.ds(at, ROWS), D:].astype(f32)
        score = (parts[0:1] + parts[1:2]) + parts[2:3]
        kept = jnp.where(lane < sizes[g], score, 0.0)
        kept = pltpu.roll(jnp.concatenate([kept, blank], axis=1), start, 1)
        return start + sizes[g], placed + kept

    _, placed = lax.fori_loop(
        0,
        groups,
        one_group,
        (jnp.int32(0), jnp.zeros((8, wide), f32)),
        unroll=groups <= 8,
    )
    values = placed[0:1, :docs]
    scores_out[...] = values.reshape(scores_out.shape)
    member = members[...] > 0.0
    target = targets[...]
    peak = jnp.max(jnp.where(member, values, MASKED), axis=1, keepdims=True)
    raised = jnp.where(member, jnp.exp(jnp.where(member, values - peak, 0.0)), 0.0)
    log_total = peak + jnp.log(jnp.sum(raised, axis=1, keepdims=True))
    picked = jnp.sum(target * values, axis=1, keepdims=True)
    loss_out[...] = jnp.sum(log_total - picked, axis=0, keepdims=True) / queries
    chance = jnp.where(member, jnp.exp(jnp.where(member, values - log_total, 0.0)), 0.0)
    ds = jnp.sum(chance - target, axis=0, keepdims=True) / queries
    ds_out[...] = ds
    ds = jnp.broadcast_to(jnp.concatenate([ds, jnp.zeros((1, LANES), f32)], axis=1), (8, wide))
    start = first_doc(scal, sizes)
    back = pltpu.roll(ds, lax.rem(wide - start, wide), 1)[:, :LANES]
    mine_out[...] = jnp.where(lane < sizes[scal[1]], back, 0.0)


def context_kernel(
    scal, part_a, part_b, h2, dh3, c32, g_ff, wout, wo_own,
    dh2_out, half_out, dc_out, own_out, inner_out, ff_out, both_s,
):
    n2, r2 = rms_parts(h2[...])
    dy3 = part_a[...].astype(f32) + part_b[...].astype(f32)
    ff_out[...] = dy3 * n2
    dh2 = (dh3[...].astype(f32) + rms_back(dy3 * row_of(g_ff), n2, r2)).astype(bf16)
    dh2_out[...] = dh2
    own_half(scal, jnp.concatenate([dh3[...], dh2], axis=1), both_s, half_out)
    dc = nt(dh2, wout[...]).astype(bf16)
    dc_out[...] = dc
    own_out[...] = nt(dh2, wo_own[...]).astype(bf16)
    hot = (head_of((D, LANES), 0) == iota((D, LANES), 1)).astype(bf16)
    high, low = split2(dc.astype(f32) * c32[...])
    inner_out[...] = nn(high, hot) + nn(low, hot)


def columns(one, two):
    tall = BLOCK * ROWS
    half = LANES // 2
    both = jnp.where(iota((BLOCK, LANES), 1) < half, one, pltpu.roll(two, half, 1))
    parts = jnp.concatenate(split3(both), axis=0)
    r, c = iota((tall, 3 * BLOCK), 0), iota((tall, 3 * BLOCK), 1)
    wide = nn((r // ROWS == c % BLOCK).astype(bf16), parts)
    lane, head = iota((tall, LANES), 1), iota((tall, LANES), 0) % ROWS
    return tuple(
        jnp.sum(jnp.where(lane == head + k * half, wide, 0.0), axis=1, keepdims=True)
        for k in range(2)
    )


def back_kernel(first, last, scal, sizes, enc, p, scale, inner, dc, wv, *refs):
    dap_out, vd_out = refs[-2:]
    tokens = enc.shape[1]
    tall = BLOCK * ROWS
    rounds = jnp.clip(rounds_of(scal, sizes), first, last)

    def one_block(step):
        block = pl.ds(pl.multiple_of(step * BLOCK, BLOCK), BLOCK)
        rows = enc[block].reshape(BLOCK * tokens, D)
        pick = (iota((tall, BLOCK), 0) // ROWS == iota((tall, BLOCK), 1)).astype(bf16)
        own = (iota((tall, D), 0) % ROWS) == head_of((tall, D), 1)
        grad = jnp.where(own, nn(pick, dc[block]), 0.0).astype(bf16)
        vd = nn(grad, wv[...]).astype(bf16)
        vd_out[block] = vd.reshape(BLOCK, ROWS, D)
        grad_probs = []
        for k in range(BLOCK // 2):
            pair = nt(
                vd[2 * ROWS * k : 2 * ROWS * (k + 1)],
                rows[2 * tokens * k : 2 * tokens * (k + 1)],
            )
            grad_probs += [pair[:ROWS, :tokens], pair[ROWS:, tokens:]]
        grad_probs = jnp.concatenate(grad_probs, axis=0)
        scale_col, inner_col = columns(scale[block], inner[block])
        prob = p[block].reshape(tall, tokens) * scale_col
        da = (prob * (grad_probs - inner_col)).astype(bf16)
        dap_out[block, :ROWS] = da.reshape(BLOCK, ROWS, tokens)
        dap_out[block, ROWS:] = prob.astype(bf16).reshape(BLOCK, ROWS, tokens)

    @pl.loop(first, rounds)
    def _(i):
        for j in range(SPAN // BLOCK):
            one_block(i * (SPAN // BLOCK) + j)

    @pl.loop(rounds, last)
    def _(i):
        span = pl.ds(pl.multiple_of(i * SPAN, SPAN), SPAN)
        dap_out[span] = jnp.zeros((SPAN, 2 * ROWS, tokens), bf16)
        vd_out[span] = jnp.zeros((SPAN, ROWS, D), bf16)


def key_sum_kernel(scal, sizes, ds, enc, dap, dh2, n3, ff, sums_out):
    tokens = enc.shape[1]
    tall = BLOCK * ROWS
    slots = dh2.shape[0]
    row = ds[...][:, :slots] * (1.0 / PARTS)
    at = iota((ROWS, D), 0)
    row = row[0:1]
    out = jnp.where(at == HEADS, jnp.sum(nn(stack3(row), dh2[...]), axis=0, keepdims=True), 0.0)
    out = jnp.where(at == HEADS + 1, row_dot(row, n3[...]), out)
    sums_out[...] = jnp.where(at == HEADS + 2, row_dot(row, ff[...]), out)

    def one_block(step):
        block = pl.ds(pl.multiple_of(step * BLOCK, BLOCK), BLOCK)
        own_slot = iota((tall, LANES), 1) == step * BLOCK + iota((tall, LANES), 0) // ROWS
        ds_col = jnp.sum(jnp.where(own_slot, ds[0:1], 0.0), axis=1, keepdims=True)
        scaled = (dap[block, :ROWS].reshape(tall, tokens).astype(f32) * ds_col).astype(bf16)
        flat = jnp.concatenate(
            [scaled[ROWS * b : ROWS * (b + 1)] for b in range(BLOCK)], axis=1
        )
        return nn(flat, enc[block].reshape(BLOCK * tokens, D))

    @pl.loop(0, rounds_of(scal, sizes))
    def _(i):
        per_round = SPAN // BLOCK
        total = one_block(i * per_round)
        for j in range(1, per_round):
            total = total + one_block(i * per_round + j)
        sums_out[...] += total


def enc_grad_kernel(first, last, ds, qa, qb, dap, vd, *refs):
    grad_out, slots, sems = refs[-3:]
    pieces, size = slots.shape[:2]
    qk = qa[...] + qb[...]
    lane = iota((1, LANES), 1)
    copies = []
    for k in range((last - first) // size):
        if k >= pieces:
            copies[k - pieces].wait()
        start = first + k * size
        for b in range(size):
            scale = jnp.sum(jnp.where(lane == start + b, ds[0:1], 0.0), axis=1, keepdims=True)
            right = jnp.concatenate([qk, vd[start + b].astype(f32)], axis=0) * scale
            slots[k % pieces, b] = tn(dap[start + b], right.astype(bf16)).astype(bf16)
        copies.append(
            pltpu.make_async_copy(
                slots.at[k % pieces], grad_out.at[pl.ds(start, size)], sems.at[k % pieces]
            )
        )
        copies[-1].start()
    for copy in copies[-pieces:]:
        copy.wait()


def share_kernel(scal, summed, scale, keep_out, send_out):
    core = scal[0] & 1
    lane = iota(scale.shape, 1)
    for out, bit in ((send_out, 1 - core), (keep_out, core)):
        for y in range(out.shape[0]):
            for k in range(out.shape[1]):
                head = (2 * y + bit) * out.shape[1] + k
                col = jnp.sum(jnp.where(lane == head, scale[...], 0.0), axis=1, keepdims=True)
                out[y, k] = (summed[head].astype(f32) * col).astype(bf16)


def away_kernel(scal, keep, got, out):
    part = 1 - (lax.shift_right_logical(scal[0], 1) & 1)
    for h in range(out.shape[0]):
        out[h] = (keep[part, h].astype(f32) + got[part, h].astype(f32)).astype(bf16)


def value_kernel(scal, keep, got, other, dc, ds, grad_out):
    slots = keep.shape[2]
    part = lax.shift_right_logical(scal[0], 1) & 1
    own_slot = iota((slots, LANES), 0) == iota((slots, LANES), 1)
    ds_col = jnp.sum(jnp.where(own_slot, ds[0:1], 0.0), axis=1, keepdims=True)
    grad = (dc[...].astype(f32) * ds_col).astype(bf16)
    for h in range(keep.shape[1]):
        pair = (keep[part, h].astype(f32) + got[part, h].astype(f32)).astype(bf16)
        summed = (pair.astype(f32) + other[h].astype(f32)).astype(bf16)
        out = tn(grad[:, h * HEAD_DIM : (h + 1) * HEAD_DIM], summed)
        grad_out[h * HEAD_DIM : (h + 1) * HEAD_DIM] = out.astype(bf16)


def document_picks(order, tile, scal, sizes, held, first):
    groups = 1 << len(order)
    half = held // groups
    core = scal[0] & 1
    doc = first + iota((tile, 1), 0)

    def one_group(g, found):
        start, at, upper = found
        pos = place_of(order, g ^ scal[1])
        slot = doc - start
        inside = (slot >= 0) & (slot < sizes[g])
        later = (slot >= half).astype(i32)
        at = jnp.where(inside, pos * half + slot - half * later, at)
        return start + sizes[g], at, jnp.where(inside, later, upper)

    zero = jnp.zeros((tile, 1), i32)
    _, at, upper = lax.fori_loop(
        0, groups, one_group, (jnp.int32(0), zero, zero), unroll=groups <= 8
    )
    hit = iota((tile, held), 1) == at
    return (hit & (upper == core)).astype(bf16), (hit & (upper != core)).astype(bf16)


def in_order(picks, own, other, width):
    mine, theirs = picks
    return (nn(mine, own[:, :width]) + nn(theirs, other[:, :width])).astype(bf16)


def picks_of(order, tile, scal, sizes, held, first, ready):
    if ready:
        return tuple(pick[...] for pick in ready)
    return document_picks(order, tile, scal, sizes, held, first)


def ds_column(ds, first, tile):
    eye = iota((tile, tile), 0) == iota((tile, tile), 1)
    return jnp.sum(jnp.where(eye, ds[0:1, pl.ds(first, tile)], 0.0), axis=1, keepdims=True)


def over_tiles(docs, tile, one_tile):
    one_tile(0, True)
    if docs > tile:

        @pl.loop(1, docs // tile)
        def _(t):
            one_tile(pl.multiple_of(t * tile, tile), False)


def put(out, value, new):
    if new:
        out[...] = value
    else:
        out[...] += value


def weights_before_kernel(
    order, tile, scal, sizes, c_own, c_other, h1, g_ff, wout, win, *refs
):
    ready, (y3_out, u_out, slope_out, c_out) = refs[:-4], refs[-4:]

    def one_tile(first, new):
        here = pl.ds(first, tile)
        picks = picks_of(order, tile, scal, sizes, c_own.shape[0], first, ready)
        c = in_order(picks, c_own, c_other, D)
        h2 = h1[...] + nn(c, wout[...])
        n2, _ = rms_parts(h2)
        y3 = (n2 * row_of(g_ff)).astype(bf16)
        y3_out[here] = y3
        z = nn(y3, win[...])
        u_out[here] = (z * phi(z)).astype(bf16)
        slope_out[here] = gelu_slope(z)
        width = c_out.shape[1]
        pick = (iota((D, width), 0) == scal[0] * width + iota((D, width), 1)).astype(bf16)
        c_out[here] = nn(c, pick).astype(bf16)

    over_tiles(y3_out.shape[0], tile, one_tile)


def grads_kernel(order, tile, scal, sizes, slope, both_own, both_other, ds, wdown, *refs):
    ready, (dz_out, both_out) = refs[:-2], refs[-2:]

    def one_tile(first, new):
        here = pl.ds(first, tile)
        picks = picks_of(order, tile, scal, sizes, both_own.shape[0], first, ready)
        both = in_order(picks, both_own, both_other, 2 * D).astype(f32)
        both = (both * ds_column(ds, first, tile)).astype(bf16)
        both_out[here] = both
        dz_out[here] = (nt(both[:, :D], wdown[...]) * slope[here]).astype(bf16)

    over_tiles(ds.shape[1], tile, one_tile)


def outer_kernel(
    tile, y3, dz, u, c, both, left1, right1, left2, right2,
    win_out, wdown_out, wout_out, key_out, query_out, wos_out, wvs_out,
    win_s, wdown_s, wout_s, key_s, query_s, wos_s, wvs_s, sems,
):
    copies = []

    def leave(held, out):
        copies.append(pltpu.make_async_copy(held, out, sems.at[len(copies)]))
        copies[-1].start()

    docs = y3.shape[0]

    def total(held, left, right):
        held[...] = tn(left[:tile], right[:tile])
        if docs > tile:

            @pl.loop(1, docs // tile)
            def _(t):
                here = pl.ds(pl.multiple_of(t * tile, tile), tile)
                held[...] += tn(left[here], right[here])

    def by_parts(held, out, left, right):
        for k in range(held.shape[0] // COLUMNS):
            part = pl.ds(k * COLUMNS, COLUMNS)
            total(held.at[part], left.at[:, part], right)
            leave(held.at[part], out.at[part])

    key_s[...] = tn(left1[: 2 * ROWS], right1[: 2 * ROWS])
    leave(key_s, key_out)
    query_s[...] = tn(left1[2 * ROWS :], right1[2 * ROWS :])
    leave(query_s, query_out)
    wos_s[...] = tn(left2[:ROWS], right2[:ROWS])
    leave(wos_s, wos_out)
    wvs_s[...] = tn(left2[ROWS:], right2[ROWS:])
    leave(wvs_s, wvs_out)
    total(wout_s, c, both.at[:, D:])
    leave(wout_s, wout_out)
    by_parts(win_s, win_out, y3, dz)
    by_parts(wdown_s, wdown_out, u, both.at[:, :D])
    for copy in copies:
        copy.wait()


def key_kernel(scal, sum_a, sum_b, h1, g_cross, wk, wq, part_out, left_out, right_out):
    y2, qm = query_parts(scal, h1, g_cross, wq)
    g = sum_a[...] + sum_b[...]
    g = jnp.where(iota((ROWS, D), 0) < HEADS, g, 0.0)
    high, low = split2(g)
    both = jnp.concatenate([high, low], axis=0)
    dq = nt(both, wk[...])
    dq = dq[:ROWS] + dq[ROWS:]
    width = dq.shape[1]
    first = scal[0] * (width // HEAD_DIM)
    own = iota((ROWS, width), 0) == first + head_of((ROWS, width), 1)
    dq = jnp.sum(jnp.where(own, dq, 0.0), axis=0, keepdims=True)
    dq_parts = stack3(dq)
    left_out[...] = jnp.concatenate([qm, qm, dq_parts], axis=0)
    right_out[...] = jnp.concatenate([both, repeat3(y2[0:1])], axis=0)
    part = jnp.sum(nn(dq_parts, wq[...]), axis=0, keepdims=True)
    part_out[...] = jnp.broadcast_to(part, (8, D))


def hidden_kernel(
    part_a, part_b, sum_a, sum_b, h1, g_cross, start, g_self, wos, wvs, g_final, row,
    dh1_out, part_out, left_out, right_out, cross_out, final_out, row_out, ff_out,
):
    y1, s1 = self_parts(start, g_self, wvs)
    dy2 = part_a[0:1] + part_b[0:1]
    sums = sum_a[...] + sum_b[...]
    n1, r1 = rms_parts(h1[...])
    cross_out[...] = (dy2 * n1).reshape(cross_out.shape)
    dh1 = sums[HEADS : HEADS + 1] + rms_back(dy2 * row_of(g_cross), n1, r1)
    dh1_out[...] = dh1
    dh1_parts = stack3(dh1)
    ds1 = jnp.sum(nt(dh1_parts, wos[...]), axis=0, keepdims=True)
    ds1_parts = stack3(ds1)
    left_out[...] = jnp.concatenate([repeat3(s1[0:1]), ds1_parts], axis=0)
    right_out[...] = jnp.concatenate([dh1_parts, repeat3(y1[0:1])], axis=0)
    part = jnp.sum(nn(ds1_parts, wvs[...]), axis=0, keepdims=True)
    part_out[...] = jnp.broadcast_to(part, (8, D))
    total = sums[HEADS + 1 : HEADS + 2] * FACTOR
    final_out[...] = (total * row_of(row)).reshape(final_out.shape)
    row_out[...] = (total * row_of(g_final)).reshape(row_out.shape)
    ff_out[...] = sums[HEADS + 2 : HEADS + 3].reshape(ff_out.shape)


def start_kernel(
    part_a, part_b, dh1, start, g_self, value_a, value_b, gain_out, start_out, value_out
):
    value_out[...] = value_a[...].astype(f32) + value_b[...].astype(f32)
    dy1 = part_a[0:1] + part_b[0:1]
    n0, r0 = rms_parts(row_of(start))
    gain_out[...] = (dy1 * n0).reshape(gain_out.shape)
    back = dh1[...] + rms_back(dy1 * row_of(g_self), n0, r0)
    start_out[...] = back.reshape(start_out.shape)


def shape(dims, dtype=f32):
    return jax.ShapeDtypeStruct(dims, dtype)


def whole_spec(memory=pltpu.VMEM):
    return pl.BlockSpec(memory_space=memory)


def name_of(kernel):
    return getattr(kernel, "func", kernel).__name__


def in_hbm(x):
    return pltpu.with_memory_space_constraint(x, pltpu.HBM)


def plain(
    kernel, outs, *args, smem=0, hbm=(), hbm_out=False, onto=None, limit=12, scratch=()
):
    spaces = [pltpu.SMEM] * smem + [pltpu.VMEM] * (len(args) - smem)
    for k in hbm:
        spaces[k] = pltpu.HBM
    out_space = pltpu.HBM if hbm_out else pltpu.VMEM
    return pl.pallas_call(
        kernel,
        out_shape=outs,
        in_specs=[whole_spec(space) for space in spaces],
        out_specs=[whole_spec(out_space) for _ in outs]
        if isinstance(outs, list)
        else whole_spec(out_space),
        scratch_shapes=list(scratch),
        input_output_aliases=onto or {},
        compiler_params=pltpu.CompilerParams(vmem_limit_bytes=limit * MIB),
        cost_estimate=pl.CostEstimate(flops=0, bytes_accessed=0, transcendentals=0),
        name=name_of(kernel),
    )(*args)


def bits_of(size):
    return [1 << b for b in range(size.bit_length() - 1)]


def far_first(size):
    return bits_of(size)[::-1]


def swap(x, axis, bit):
    size = lax.axis_size(axis)
    return lax.ppermute(x, axis, [(i, i ^ bit) for i in range(size)])


def after(x, *deps):
    return lax.optimization_barrier((x, *deps))[0]


def add(x, y):
    return (x.astype(f32) + y.astype(f32)).astype(x.dtype)


def sum_last(x, steps):
    for axis, bit in steps[:-1]:
        x = add(x, swap(x, axis, bit))
    axis, bit = steps[-1]
    return x, swap(x, axis, bit)


def per_device(
    enc_out,
    enc_len,
    group_docs,
    list_len,
    relevance,
    start_token,
    score_row,
    g_self,
    w_value_self,
    w_out_self,
    g_cross,
    w_query,
    w_key,
    w_value,
    w_out,
    g_ff,
    w_in,
    w_down,
    g_final,
):
    groups = lax.axis_size("docs")
    parts = lax.axis_size("heads")
    assert parts == PARTS
    me_g = lax.axis_index("docs")
    me_j = lax.axis_index("heads")
    slots, tokens = enc_out.shape[:2]
    docs = enc_len.shape[0]
    width = w_value.shape[1]
    own_heads = HEADS // parts
    hidden = w_in.shape[1]
    over_heads = [("heads", 1), ("heads", 2)]
    order = far_first(groups)
    over_docs = [("docs", bit) for bit in order]

    scal = jnp.stack([me_j, me_g])
    wvs_t, wq_t, wk_t, wv_t = (w.T for w in (w_value_self, w_query, w_key, w_value))

    wv_by1, wo_by1 = swap(wv_t, "heads", 1), swap(w_out, "heads", 1)

    part = plain(
        self_kernel,
        shape((8, D)),
        *map(in_hbm, (start_token, g_self, wvs_t, w_out_self)),
    )


    def load(first, last, since, *onto):
        return pl.pallas_call(
            functools.partial(load_kernel, first, last),
            out_shape=pltpu.VMEM(enc_out.shape, bf16),
            in_specs=[whole_spec(pltpu.HBM), whole_spec(pl.ANY), whole_spec(pltpu.SMEM)]
            + [whole_spec()] * len(onto),
            out_specs=whole_spec(),
            scratch_shapes=[pltpu.SemaphoreType.DMA((last - first,))],
            input_output_aliases={3: 0} if onto else {},
            compiler_params=pltpu.CompilerParams(vmem_limit_bytes=MIB),
            cost_estimate=pl.CostEstimate(flops=0, bytes_accessed=0, transcendentals=0),
            name="load_kernel",
        )(in_hbm(enc_out), since, scal, *onto)

    part = add(part, swap(part, "heads", 1))
    part_a, part_b = part, swap(part, "heads", 2)
    held = load(0, 1, part)
    part_b, held = lax.optimization_barrier((part_b, held))
    wv_by2 = swap(after(wv_t, part_b), "heads", 2)
    qk, h1 = plain(
        query_kernel,
        [shape((ROWS, D)), shape((1, D))],
        scal,
        part_a,
        part_b,
        *map(in_hbm, (start_token, g_cross, wq_t, wk_t)),
        smem=1,
    )
    qk = add(qk, swap(qk, "heads", 1))
    qk, held = lax.optimization_barrier((qk, held))
    qk_a, qk_b = qk, swap(qk, "heads", 2)
    held = load(1, 3, qk, held)
    qk_b, held, wv_by2 = lax.optimization_barrier((qk_b, held, wv_by2))
    wv_by3 = swap(wv_by2, "heads", 1)

    wo_by2 = swap(after(w_out, qk_b), "heads", 2)
    held, prob, summed, extra = plain(
        functools.partial(attend_kernel, 3),
        [
            pltpu.VMEM(enc_out.shape, bf16),
            pltpu.VMEM((slots, ROWS, tokens), f32),
            pltpu.VMEM((PANELS, slots * ROWS, LANES), f32),
            shape((slots, LANES), bf16),
        ],
        scal,
        group_docs,
        enc_len,
        qk_a,
        qk_b,
        in_hbm(enc_out),
        held,
        smem=3,
        hbm=(5,),
        onto={6: 0},
        scratch=[pltpu.VMEM((2 * ROWS, D), bf16), pltpu.SemaphoreType.DMA((slots // BLOCK,))],
        limit=16,
    )
    summed, wv_by3, wo_by2 = lax.optimization_barrier((summed, wv_by3, wo_by2))
    wv_parts = (wv_t, wv_by2, wv_by1, wv_by3)
    wo_parts = (w_out, wo_by2, wo_by1, swap(wo_by2, "heads", 1))
    pay, summed, wv_full = plain(
        project_kernel,
        [
            shape((slots, D + LANES), bf16),
            shape((HEADS, slots, D), bf16),
            shape((D, D), bf16),
        ],
        scal,
        summed,
        extra,
        *wv_parts,
        smem=1,
    )
    merged = plain(
        merge_kernel, shape(pay.shape, bf16), scal, pay, swap(pay, "heads", 1), smem=1
    )
    other = swap(merged, "heads", 2)
    wo_full = plain(arrange_kernel, shape((D, D), bf16), scal, *wo_parts, smem=1)
    tile = 384
    held_rows = groups * slots // 2
    picks_shape = [shape((tile, held_rows), bf16)] * 2 if docs == tile else []
    target, member, *picks = plain(
        functools.partial(target_kernel, order),
        [shape((list_len.shape[0], docs))] * 2 + picks_shape,
        scal,
        group_docs,
        list_len,
        relevance,
        smem=3,
    )
    other, wo_full, target, member, *picks = lax.optimization_barrier(
        (other, wo_full, target, member, *picks)
    )

    c, c32, scale, h2, z, part = plain(
        forward_kernel,
        [
            shape((slots // 2, D), bf16),
            shape((slots, D)),
            shape((slots, LANES)),
            shape((slots, D)),
            shape((slots, hidden)),
            shape((slots, D), bf16),
        ],
        scal,
        merged,
        other,
        pay,
        h1,
        wo_full,
        g_ff,
        w_in,
        w_down,
        smem=1,
        scratch=[pltpu.VMEM((slots, D), bf16)],
    )

    half = slots // 2

    def grow(x, k):
        return jnp.concatenate([x, swap(x, *over_docs[k])], axis=0)

    def tie(*xs):
        return lax.optimization_barrier(xs)

    last = len(over_docs) - 1
    near_first = over_docs[::-1]
    part = add(part, swap(part, "heads", 1))
    part_a, part_b = part, swap(part, "heads", 2)
    c_all, n3, dh3 = plain(
        score_kernel,
        [shape((half, D + LANES), bf16), shape((slots, D)), shape((slots, D), bf16)],
        part_a,
        part_b,
        h2,
        g_final,
        score_row,
        c,
    )
    part = plain(down_kernel, shape((slots, D), bf16), dh3, z, w_down, w_in)
    part = add(part, swap(part, "heads", 1))
    part, summed = tie(part, summed)
    part_a, part_b = part, swap(part, "heads", 2)
    c_far = swap(c_all, *over_docs[0])
    keep, sent = plain(
        share_kernel, [shape((2, own_heads, slots, D), bf16)] * 2, scal, summed, scale, smem=1
    )
    got = swap(sent, "heads", 1)
    away = plain(
        away_kernel, shape((own_heads, slots, D), bf16), scal, keep, got, smem=1
    )
    other = swap(away, "heads", 2)
    part_b, away = tie(part_b, away)
    dh2, grads, dc, dc_own, inner, ff = plain(
        context_kernel,
        [
            shape((slots, D), bf16),
            shape((half, 2 * D), bf16),
            shape((slots, D), bf16),
            shape((slots, width), bf16),
            shape((slots, LANES)),
            shape((slots, D)),
        ],
        scal,
        part_a,
        part_b,
        h2,
        dh3,
        c32,
        g_ff,
        wo_full,
        w_out,
        smem=1,
        scratch=[pltpu.VMEM((slots, 2 * D), bf16)],
    )

    c_all, c_far, dc, grads = tie(c_all, c_far, dc, grads)
    c_all = jnp.concatenate([c_all, c_far], axis=0)
    for k in range(1, last):
        c_far = swap(c_all, *over_docs[k])
        if k < last - 1:
            c_all = jnp.concatenate([c_all, c_far], axis=0)
    grads_far = swap(grads, *over_docs[0])

    outs = [
        pltpu.VMEM((slots, 2 * ROWS, tokens), bf16),
        pltpu.VMEM((slots, ROWS, D), bf16),
    ]
    rounds = slots // SPAN
    inputs = (scal, group_docs, held, prob, scale, inner, dc, wv_full)

    def back(first, last, *onto):
        return plain(
            functools.partial(back_kernel, first, last),
            outs,
            *inputs,
            *onto,
            smem=2,
            onto={8: 0, 9: 1} if onto else None,
            limit=16,
        )

    dap, vd = back(0, 1)
    dap, c_far = tie(dap, c_far)
    c_all = jnp.concatenate([c_all, c_far], axis=0)
    c_far = swap(c_all, *over_docs[last])
    dap, vd = back(1, rounds, dap, vd)
    dap, c_far, other, grads_far = tie(dap, c_far, other, grads_far)
    grads = jnp.concatenate([grads, grads_far], axis=0)
    for m in range(1, last):
        grads_far = swap(grads, *over_docs[m])
        if m < last - 1:
            grads = jnp.concatenate([grads, grads_far], axis=0)
    c_all = jnp.concatenate([c_all, c_far], axis=0)
    all_scores, loss, ds_docs, ds_mine = plain(
        functools.partial(list_kernel, order),
        [shape((docs,)), shape((1, 1)), shape((1, docs)), shape((8, LANES))],
        scal,
        group_docs,
        c_all,
        target,
        member,
        smem=2,
    )
    value_part = plain(
        value_kernel,
        shape((width, D), bf16),
        scal,
        keep,
        got,
        other,
        dc_own,
        ds_mine,
        smem=1,
    )
    dap, value_part = tie(dap, value_part)
    value_far = swap(value_part, *near_first[0])
    c_far = swap(c_all, "heads", 1)
    sums = plain(
        key_sum_kernel,
        shape((ROWS, D)),
        scal,
        group_docs,
        ds_mine,
        held,
        dap,
        dh2,
        n3,
        ff,
        smem=2,
    )

    def enc_grads(first, last, grads=None):
        outs = pltpu.HBM(enc_out.shape, bf16)
        size = 8
        args = (ds_mine, qk_a, qk_b, dap, vd)
        return plain(
            functools.partial(enc_grad_kernel, first, last),
            outs,
            *args,
            *([] if grads is None else [grads]),
            hbm=() if grads is None else (len(args),),
            hbm_out=True,
            onto={} if grads is None else {len(args): 0},
            scratch=[pltpu.VMEM((4, size, tokens, D), bf16), pltpu.SemaphoreType.DMA((4,))],
            limit=16,
        )

    sums = add(sums, swap(sums, "heads", 1))
    steps = near_first[:0:-1] + over_heads[1:] + near_first[:1]
    sums, grads_far = tie(sums, grads_far)
    grads = jnp.concatenate([grads, grads_far], axis=0)
    grads_far = swap(grads, *over_docs[last])
    enc_grad = None
    third = slots // 3
    sum_a = sums
    for k, step in enumerate(steps):
        ds_mine, sum_a = tie(ds_mine, sum_a)
        sum_b = swap(sum_a, *step)
        if k < 3:
            enc_grad = enc_grads(k * third, (k + 1) * third, enc_grad)
            sum_b, enc_grad = tie(sum_b, enc_grad)
        if k == 1:
            sum_b, value_far, c_far = tie(sum_b, value_far, c_far)
            for step in near_first[1:-1]:
                value_part = add(value_part, value_far)
                value_far = swap(value_part, *step)
        if k < len(steps) - 1:
            sum_a = sum_a + sum_b
    y3, u, slope, c_own = plain(
        functools.partial(weights_before_kernel, order, tile),
        [
            shape((docs, D), bf16),
            shape((docs, hidden), bf16),
            shape((docs, hidden)),
            shape((docs, width), bf16),
        ],
        scal,
        group_docs,
        c_all,
        c_far,
        h1,
        g_ff,
        wo_full,
        w_in,
        *picks,
        smem=2,
        limit=60 if docs > 384 else 16,
    )
    sum_b, grads_far, value_far, y3, u, slope, c_own = tie(
        sum_b, grads_far, value_far, y3, u, slope, c_own
    )
    value_part = add(value_part, value_far)
    value_far = swap(value_part, *near_first[-1])
    grads = jnp.concatenate([grads, grads_far], axis=0)
    grads_far = swap(grads, "heads", 1)

    part, left1, right1 = plain(
        key_kernel,
        [shape((8, D)), shape((3 * ROWS, width), bf16), shape((3 * ROWS, D), bf16)],
        scal,
        sum_a,
        sum_b,
        h1,
        g_cross,
        wk_t,
        wq_t,
        smem=1,
    )
    part = add(part, swap(part, "heads", 1))
    part, grads_far = tie(part, grads_far)
    part_a, part_b = part, swap(part, "heads", 2)
    dz, both = plain(
        functools.partial(grads_kernel, order, tile),
        [shape((docs, hidden), bf16), shape((docs, 2 * D), bf16)],
        scal,
        group_docs,
        slope,
        grads,
        grads_far,
        ds_docs,
        w_down,
        *picks,
        smem=2,
        limit=60 if docs > 384 else 16,
    )
    part_b, dz, both = tie(part_b, dz, both)
    dh1, part, left2, right2, cross, final_gain, row_grad, ff_gain = plain(
        hidden_kernel,
        [
            shape((1, D)),
            shape((8, D)),
            shape((2 * ROWS, width), bf16),
            shape((2 * ROWS, D), bf16),
        ]
        + [shape((D,))] * 4,
        part_a,
        part_b,
        sum_a,
        sum_b,
        h1,
        g_cross,
        start_token,
        g_self,
        w_out_self,
        wvs_t,
        g_final,
        score_row,
    )
    part_a, part_b = sum_last(part, over_heads)
    dims = [(D, hidden), (hidden, D), (width, D)] + [(width, D)] * 4
    w_in_grad, w_down_grad, w_out_grad, key_grad, query_grad, wos_grad, wvs_grad = plain(
        functools.partial(outer_kernel, tile),
        [pltpu.HBM(dim, f32) for dim in dims],
        y3,
        dz,
        u,
        c_own,
        both,
        left1,
        right1,
        left2,
        right2,
        hbm_out=True,
        scratch=[pltpu.VMEM(dim, f32) for dim in dims] + [pltpu.SemaphoreType.DMA((16,))],
        limit=60 if docs > 384 else 24,
    )
    part_b, w_down_grad, value_far = tie(part_b, w_down_grad, value_far)
    self_gain, start_grad, value_grad = plain(
        start_kernel,
        [shape((D,)), shape((D,)), shape((width, D))],
        part_a,
        part_b,
        dh1,
        start_token,
        g_self,
        value_part,
        value_far,
    )

    return (
        all_scores,
        loss.reshape(()),
        enc_grad,
        start_grad,
        row_grad,
        self_gain,
        wvs_grad.T,
        wos_grad,
        cross,
        query_grad.T,
        key_grad.T,
        value_grad.T,
        w_out_grad,
        ff_gain,
        w_in_grad,
        w_down_grad,
        final_gain,
    )


def solution(mesh):
    placed = (
        P("docs", "heads", None),
        P(),
        P(),
        P(),
        P(),
        P(),
        P(),
        P(),
        P(None, "heads"),
        P("heads", None),
        P(),
        P(None, "heads"),
        P(None, "heads"),
        P(None, "heads"),
        P("heads", None),
        P(),
        P(None, "heads"),
        P("heads", None),
        P(),
    )
    return jax.shard_map(
        per_device,
        mesh=mesh,
        in_specs=placed,
        out_specs=(
            P(),
            P(),
            P("docs", "heads", None),
            P(),
            P(),
            P(),
            P(None, "heads"),
            P("heads", None),
            P(),
            P(None, "heads"),
            P(None, "heads"),
            P(None, "heads"),
            P("heads", None),
            P(),
            P(None, "heads"),
            P("heads", None),
            P(),
        ),
        check_vma=False,
    )
```

```python
import functools

import jax
import jax.numpy as jnp
from jax import lax
from jax.experimental import pallas as pl
from jax.experimental.pallas import tpu as pltpu
from jax.sharding import PartitionSpec as P

D = 768
HEADS = 12
HEAD_DIM = 64
ROWS = 16
BLOCK = 16
SPAN = 2 * BLOCK
LANES = 128
PANELS = D // LANES
COLUMNS = 256
PARTS = 4

EPSILON = 1e-06
MASKED = -1e30
FACTOR = D ** (-0.5)
ROOT_HALF = 0.5**0.5
DENSITY = 0.3989422804014327
f32, bf16, i32 = jnp.float32, jnp.bfloat16, jnp.int32
EXACT = lax.Precision.HIGHEST
MIB = 1 << 20


def nn(a, b, precision=None):
    return lax.dot_general(
        a, b, (((1,), (0,)), ((), ())), precision=precision, preferred_element_type=f32
    )


def nt(a, b, precision=None):
    return lax.dot_general(
        a, b, (((1,), (1,)), ((), ())), precision=precision, preferred_element_type=f32
    )


def tn(a, b, precision=None):
    return lax.dot_general(
        a, b, (((0,), (0,)), ((), ())), precision=precision, preferred_element_type=f32
    )


def iota(shape, dim):
    return lax.broadcasted_iota(i32, shape, dim)


def split2(x):
    high = x.astype(bf16)
    return high, (x - high.astype(f32)).astype(bf16)


def split3(x):
    high = x.astype(bf16)
    rest = x - high.astype(f32)
    mid = rest.astype(bf16)
    return high, mid, (rest - mid.astype(f32)).astype(bf16)


def stack3(row, height=ROWS):
    at = iota((height, row.shape[1]), 0)
    parts = split3(row)
    zero = jnp.zeros((), f32)
    out = jnp.where(at == 0, parts[0].astype(f32), zero)
    out = jnp.where(at == 1, parts[1].astype(f32), out)
    return jnp.where(at == 2, parts[2].astype(f32), out).astype(bf16)


def repeat3(row, height=ROWS):
    at = iota((height, row.shape[1]), 0)
    return jnp.where(at < 3, row.astype(f32), 0.0).astype(bf16)


def rms_parts(rows):
    scale = lax.rsqrt(jnp.mean(rows * rows, axis=-1, keepdims=True) + EPSILON)
    return rows * scale, scale


def rms_back(grad_normed, normed, scale):
    inner = jnp.mean(grad_normed * normed, axis=-1, keepdims=True)
    return scale * (grad_normed - normed * inner)


def phi(z):
    return 0.5 * (1.0 + lax.erf(z * ROOT_HALF))


def gelu_slope(z):
    return phi(z) + z * (DENSITY * jnp.exp(-0.5 * z * z))


def head_of(shape, dim):
    return iota(shape, dim) // HEAD_DIM


def spread(small):
    high, mid, low = (part.astype(f32) for part in split3(small))
    packed = high + pltpu.roll(mid, ROWS, 1) + pltpu.roll(low, 2 * ROWS, 1)
    lane = iota((LANES, D), 0)
    hot = (lane < 3 * ROWS) & (lane % ROWS == head_of((LANES, D), 1))
    return nn(packed.astype(bf16), hot.astype(bf16))


def row_dot(row, right):
    high, low = split2(right)
    parts = stack3(row)
    return jnp.sum(nn(parts, high) + nn(parts, low), axis=0, keepdims=True)


def row_of(ref):
    return ref[...].astype(f32).reshape(1, D)


def gained(n, gain):
    return jnp.broadcast_to(n * row_of(gain), (ROWS, D)).astype(bf16)


def self_parts(start, g_self, wvs):
    x0 = row_of(start)
    n0, _ = rms_parts(x0)
    y1 = gained(n0, g_self)
    return y1, nt(y1, wvs[...]).astype(bf16)


def query_parts(scal, h1, g_cross, wq):
    n1, _ = rms_parts(h1[...])
    y2 = gained(n1, g_cross)
    q = nt(y2, wq[...]).astype(bf16)
    width = q.shape[1]
    first = scal[0] * (width // HEAD_DIM)
    own = iota((ROWS, width), 0) == first + head_of((ROWS, width), 1)
    return y2, jnp.where(own, q.astype(f32), 0.0).astype(bf16)


def self_kernel(start, g_self, wvs, wos, part_out):
    _, s1 = self_parts(start, g_self, wvs)
    part_out[...] = nn(s1, wos[...])[:8]


def load_kernel(first, last, enc, since, scal, *refs):
    held, sems = refs[-2:]
    loads = []
    for k in range(first, last):
        part = pl.ds(k * BLOCK, BLOCK)
        loads.append(pltpu.make_async_copy(enc.at[part], held.at[part], sems.at[k - first]))
        loads[-1].start()
    for load in loads:
        load.wait()


def query_kernel(scal, part_a, part_b, start, g_cross, wq, wk, qk_out, h1_out):
    h1_out[...] = row_of(start) + (part_a[0:1] + part_b[0:1])
    _, qm = query_parts(scal, h1_out, g_cross, wq)
    qk_out[...] = nn(qm, wk[...])


def load_kernel(first, last, enc, since, scal, *refs):
    held, sems = refs[-2:]
    loads = []
    for k in range(first, last):
        part = pl.ds(k * BLOCK, BLOCK)
        loads.append(pltpu.make_async_copy(enc.at[part], held.at[part], sems.at[k - first]))
        loads[-1].start()
    for load in loads:
        load.wait()


def query_kernel(scal, part_a, part_b, start, g_cross, wq, wk, qk_out, h1_out):
    h1_out[...] = row_of(start) + (part_a[0:1] + part_b[0:1])
    _, qm = query_parts(scal, h1_out, g_cross, wq)
    qk_out[...] = nn(qm, wk[...])


def select_docs(height, width):
    r, c = iota((height, width), 0), iota((height, width), 1)
    return (((r // BLOCK) == (c % ROWS)) & ((r % BLOCK) == (c // ROWS))).astype(bf16)


def first_doc(scal, sizes):
    groups = sizes.shape[0]

    def body(g, total):
        return total + jnp.where(g < scal[1], sizes[g], 0)

    return lax.fori_loop(0, groups, body, jnp.int32(0), unroll=groups <= 8)


def rounds_of(scal, sizes):
    return (sizes[scal[1]] + SPAN - 1) // SPAN


def attend_kernel(
    loaded, scal, sizes, lengths, qa, qb, enc, _, held, p_out, e_out, ext_out, qk_s, sems
):
    tokens = enc.shape[1]
    blocks = enc.shape[0] // BLOCK
    rounds = rounds_of(scal, sizes)
    per_round = SPAN // BLOCK
    count = sizes[scal[1]]
    begin = first_doc(scal, sizes)
    tall = BLOCK * ROWS

    def piece(k):
        part = pl.ds(k * BLOCK, BLOCK)
        return pltpu.make_async_copy(enc.at[part], held.at[part], sems.at[k])

    for k in range(loaded, blocks):
        pl.when(k // per_round < rounds)(lambda k=k: piece(k).start())
    high, low = split2(qa[...] + qb[...])
    qk_s[0:ROWS] = high
    qk_s[ROWS : 2 * ROWS] = low

    def one_block(step):
        block = pl.ds(pl.multiple_of(step * BLOCK, BLOCK), BLOCK)
        flat = pl.ds(pl.multiple_of(step * tall, tall), tall)
        rows = held[block].reshape(BLOCK * tokens, D)
        both = nt(qk_s[...], rows)
        logits = both[:ROWS] + both[ROWS:]
        logits = jnp.concatenate(
            [logits[:, b * tokens : (b + 1) * tokens] for b in range(BLOCK)], axis=0
        )
        shown = []
        for b in range(BLOCK):
            slot = step * BLOCK + b
            doc = jnp.minimum(begin + slot, lengths.shape[0] - 1)
            length = jnp.where(slot < count, lengths[doc] - scal[0] * tokens, 0)
            shown.append(jnp.broadcast_to(length, (ROWS, tokens)))
        seen = iota((tall, tokens), 1) < jnp.concatenate(shown, axis=0)
        logits = jnp.where(seen, logits, MASKED)
        peak = jnp.max(logits, axis=1, keepdims=True)
        raised = jnp.where(seen, jnp.exp(logits - peak), 0.0)
        total = jnp.sum(raised, axis=1, keepdims=True)
        p_out[block] = raised.reshape(BLOCK, ROWS, tokens)
        low = raised.astype(bf16)
        summed = jnp.concatenate(
            [
                nn(low[ROWS * b : ROWS * (b + 1)], rows[tokens * b : tokens * (b + 1)])
                for b in range(BLOCK)
            ],
            axis=0,
        )
        for k in range(PANELS):
            e_out[k, flat] = summed[:, k * LANES : (k + 1) * LANES]
        gather = (iota((BLOCK, tall), 0) == iota((BLOCK, tall), 1) // ROWS).astype(bf16)
        parts = split3(peak) + split3(total)
        at = iota((tall, LANES), 1)
        extra = jnp.zeros((tall, LANES), f32)
        for k, part in enumerate(parts):
            extra = jnp.where(at // ROWS == k, part.astype(f32), extra)
        extra = jnp.where(at % ROWS == iota((tall, LANES), 0) % ROWS, extra, 0.0)
        ext_out[block] = nn(gather, extra.astype(bf16)).astype(bf16)

    @pl.loop(0, rounds)
    def _(i):
        for j in range(per_round):
            k = i * per_round + j
            pl.when(k >= loaded)(lambda k=k: piece(k).wait())
        for j in range(per_round):
            one_block(i * per_round + j)

    @pl.loop(rounds, enc.shape[0] // SPAN)
    def _(i):
        span = pl.ds(pl.multiple_of(i * SPAN, SPAN), SPAN)
        flat = pl.ds(pl.multiple_of(i * SPAN * ROWS, SPAN * ROWS), SPAN * ROWS)
        p_out[span] = jnp.zeros((SPAN, ROWS, tokens), f32)
        for k in range(PANELS):
            e_out[k, flat] = jnp.zeros((SPAN * ROWS, LANES), f32)
        ext_out[span] = jnp.where(iota((SPAN, LANES), 1) < ROWS, MASKED, 0.0).astype(bf16)


def sums_of_head(summed, head, slots):
    rows = pl.ds(head, slots, stride=ROWS)
    return jnp.concatenate([summed[k, rows, :] for k in range(PANELS)], axis=1)


def place_parts(scal, full, own, by2, by1, by3):
    height = own.shape[0]
    for mask, piece in ((0, own), (2, by2), (1, by1), (3, by3)):
        at = pl.multiple_of((scal[0] ^ mask) * height, height)
        full[pl.ds(at, height)] = piece[...]


def arrange_kernel(scal, own, by2, by1, by3, full_out):
    place_parts(scal, full_out, own, by2, by1, by3)


def project_kernel(scal, summed, extra, own, by2, by1, by3, pay_out, heads_out, wv):
    place_parts(scal, wv, own, by2, by1, by3)
    slots = pay_out.shape[0]
    even = iota((slots, LANES), 1) < HEAD_DIM
    for k in range(HEADS // 2):
        pair = wv[k * LANES : (k + 1) * LANES]
        for head in (2 * k, 2 * k + 1):
            heads_out[head] = sums_of_head(summed, head, slots).astype(bf16)
        one, two = (nt(heads_out[2 * k + odd], pair) for odd in range(2))
        pay_out[:, k * LANES : (k + 1) * LANES] = jnp.where(even, one, two).astype(bf16)
    pay_out[:, D:] = extra[...]


def decode(pay):
    extra = pay[:, D:].astype(f32)

    def lane(k):
        return pltpu.roll(extra, LANES - k * ROWS, 1) if k else extra

    first = iota(extra.shape, 1) < ROWS
    peak = jnp.where(first, (lane(0) + lane(1)) + lane(2), 0.0)
    total = jnp.where(first, (lane(3) + lane(4)) + lane(5), 0.0)
    return peak, total


def merge(one, two, last=False):
    peak1, total1 = decode(one)
    peak2, total2 = decode(two)
    peak = jnp.maximum(peak1, peak2)
    up1, up2 = jnp.exp(peak1 - peak), jnp.exp(peak2 - peak)
    total = up1 * total1 + up2 * total2
    first = iota(peak.shape, 1) < ROWS
    if last:
        some = first & (total > 0.0)
        total = jnp.where(some, 1.0 / jnp.where(some, total, 1.0), 0.0)
        up1, up2 = up1 * total, up2 * total
    up1, up2 = jnp.where(first, up1, 0.0), jnp.where(first, up2, 0.0)
    context = spread(up1) * one[:, :D].astype(f32) + spread(up2) * two[:, :D].astype(f32)
    return peak, total, context


def ordered(bit, own, other):
    swap = jnp.broadcast_to(bit, own.shape) == 1
    return jnp.where(swap, other, own), jnp.where(swap, own, other)


def merge_kernel(scal, own, other, pay_out):
    one, two = ordered(scal[0] & 1, own[...].astype(f32), other[...].astype(f32))
    peak, total, context = merge(one, two)
    pay_out[:, :D] = context.astype(bf16)
    extra = jnp.zeros(peak.shape, f32)
    at = iota(peak.shape, 1) // ROWS
    for k, part in enumerate(split3(peak) + split3(total)):
        part = part.astype(f32)
        extra = jnp.where(at == k, pltpu.roll(part, k * ROWS, 1) if k else part, extra)
    pay_out[:, D:] = extra.astype(bf16)


def own_half(scal, rows, held, out):
    half = out.shape[0]
    held[...] = rows
    out[...] = held[pl.ds(pl.multiple_of((scal[0] & 1) * half, half), half)]


def forward_kernel(
    scal, own, other, first, h1, wo, g_ff, win, wdown,
    c_out, c32_out, scale_out, h2_out, z_out, part_out, c_s,
):
    bit = lax.shift_right_logical(scal[0], 1) & 1
    one, two = ordered(bit, own[...].astype(f32), other[...].astype(f32))
    peak, inverse, context = merge(one, two, True)
    mine, _ = decode(first[...].astype(f32))
    scale_out[...] = jnp.exp(jnp.minimum(mine - peak, 0.0)) * inverse
    c32_out[...] = context
    low = context.astype(bf16)
    own_half(scal, low, c_s, c_out)
    h2 = h1[...] + nn(low, wo[...])
    h2_out[...] = h2
    n2, _ = rms_parts(h2)
    y3 = (n2 * row_of(g_ff)).astype(bf16)
    z = nn(y3, win[...])
    z_out[...] = z
    u = (z * phi(z)).astype(bf16)
    part_out[...] = nn(u, wdown[...]).astype(bf16)


def score_kernel(part_a, part_b, h2, g_final, row, c, pay_out, n3_out, dh3_out):
    h3 = h2[...] + (part_a[...].astype(f32) + part_b[...].astype(f32))
    n3, r3 = rms_parts(h3)
    n3_out[...] = n3
    wanted = jnp.broadcast_to(row_of(g_final) * row_of(row) * FACTOR, (8, D))
    scores = nt(wanted, n3, EXACT)[0:1]
    wide = jnp.concatenate([scores, jnp.zeros((1, LANES - n3.shape[0]), f32)], axis=1)
    pay_out[:, :D] = c[...]
    pay_out[:, D:] = stack3(wide, c.shape[0])
    dh3_out[...] = rms_back(wanted[0:1], n3, r3).astype(bf16)


def down_kernel(dh3, z, wdown, win, part_out):
    du = nt(dh3[...], wdown[...])
    dz = (du * gelu_slope(z[...])).astype(bf16)
    part_out[...] = nt(dz, win[...]).astype(bf16)


def target_kernel(order, scal, sizes, lens, rel, target_out, member_out, *picks_out):
    if picks_out:
        tile, held = picks_out[0].shape
        for out, pick in zip(picks_out, document_picks(order, tile, scal, sizes, held, 0)):
            out[...] = pick
    queries, docs = target_out.shape
    relevance = rel[...].reshape(1, docs)
    at = iota((queries, 1), 0)

    def one_list(j, found):
        begin, begins, ends = found
        end = begin + lens[j]
        return end, jnp.where(at == j, begin, begins), jnp.where(at == j, end, ends)

    none = jnp.zeros((queries, 1), i32)
    _, begins, ends = lax.fori_loop(
        0, queries, one_list, (jnp.int32(0), none, none), unroll=queries <= 32
    )
    place = iota((queries, docs), 1)
    member = (place >= begins) & (place < ends)
    weight = jnp.sum(jnp.where(member, relevance, 0.0), axis=1, keepdims=True)
    target_out[...] = jnp.where(member, relevance / weight, 0.0)
    member_out[...] = member.astype(f32)


def place_of(order, mask):
    pos = 0
    for k, bit in enumerate(order):
        pos = pos + (lax.shift_right_logical(mask, bit.bit_length() - 1) & 1) * (1 << k)
    return pos


def list_kernel(order, scal, sizes, rows, targets, members, scores_out, loss_out, ds_out, mine_out):
    groups = 1 << len(order)
    docs = ds_out.shape[1]
    wide = docs + LANES
    queries = targets.shape[0]
    half = rows.shape[0] // groups
    lane = iota((8, LANES), 1)
    blank = jnp.zeros((8, wide - LANES), f32)

    def one_group(g, found):
        start, placed = found
        at = pl.multiple_of(place_of(order, g ^ scal[1]) * half, half)
        parts = rows[pl.ds(at, ROWS), D:].astype(f32)
        score = (parts[0:1] + parts[1:2]) + parts[2:3]
        kept = jnp.where(lane < sizes[g], score, 0.0)
        kept = pltpu.roll(jnp.concatenate([kept, blank], axis=1), start, 1)
        return start + sizes[g], placed + kept

    _, placed = lax.fori_loop(
        0,
        groups,
        one_group,
        (jnp.int32(0), jnp.zeros((8, wide), f32)),
        unroll=groups <= 8,
    )
    values = placed[0:1, :docs]
    scores_out[...] = values.reshape(scores_out.shape)
    member = members[...] > 0.0
    target = targets[...]
    peak = jnp.max(jnp.where(member, values, MASKED), axis=1, keepdims=True)
    raised = jnp.where(member, jnp.exp(jnp.where(member, values - peak, 0.0)), 0.0)
    log_total = peak + jnp.log(jnp.sum(raised, axis=1, keepdims=True))
    picked = jnp.sum(target * values, axis=1, keepdims=True)
    loss_out[...] = jnp.sum(log_total - picked, axis=0, keepdims=True) / queries
    chance = jnp.where(member, jnp.exp(jnp.where(member, values - log_total, 0.0)), 0.0)
    ds = jnp.sum(chance - target, axis=0, keepdims=True) / queries
    ds_out[...] = ds
    ds = jnp.broadcast_to(jnp.concatenate([ds, jnp.zeros((1, LANES), f32)], axis=1), (8, wide))
    start = first_doc(scal, sizes)
    back = pltpu.roll(ds, lax.rem(wide - start, wide), 1)[:, :LANES]
    mine_out[...] = jnp.where(lane < sizes[scal[1]], back, 0.0)


def context_kernel(
    scal, part_a, part_b, h2, dh3, c32, g_ff, wout, wo_own,
    dh2_out, half_out, dc_out, own_out, inner_out, ff_out, both_s,
):
    n2, r2 = rms_parts(h2[...])
    dy3 = part_a[...].astype(f32) + part_b[...].astype(f32)
    ff_out[...] = dy3 * n2
    dh2 = (dh3[...].astype(f32) + rms_back(dy3 * row_of(g_ff), n2, r2)).astype(bf16)
    dh2_out[...] = dh2
    own_half(scal, jnp.concatenate([dh3[...], dh2], axis=1), both_s, half_out)
    dc = nt(dh2, wout[...]).astype(bf16)
    dc_out[...] = dc
    own_out[...] = nt(dh2, wo_own[...]).astype(bf16)
    hot = (head_of((D, LANES), 0) == iota((D, LANES), 1)).astype(bf16)
    high, low = split2(dc.astype(f32) * c32[...])
    inner_out[...] = nn(high, hot) + nn(low, hot)


def columns(one, two):
    tall = BLOCK * ROWS
    half = LANES // 2
    both = jnp.where(iota((BLOCK, LANES), 1) < half, one, pltpu.roll(two, half, 1))
    parts = jnp.concatenate(split3(both), axis=0)
    r, c = iota((tall, 3 * BLOCK), 0), iota((tall, 3 * BLOCK), 1)
    wide = nn((r // ROWS == c % BLOCK).astype(bf16), parts)
    lane, head = iota((tall, LANES), 1), iota((tall, LANES), 0) % ROWS
    return tuple(
        jnp.sum(jnp.where(lane == head + k * half, wide, 0.0), axis=1, keepdims=True)
        for k in range(2)
    )


def back_kernel(first, last, scal, sizes, enc, p, scale, inner, dc, wv, *refs):
    dap_out, vd_out = refs[-2:]
    tokens = enc.shape[1]
    tall = BLOCK * ROWS
    rounds = jnp.clip(rounds_of(scal, sizes), first, last)

    def one_block(step):
        block = pl.ds(pl.multiple_of(step * BLOCK, BLOCK), BLOCK)
        rows = enc[block].reshape(BLOCK * tokens, D)
        pick = (iota((tall, BLOCK), 0) // ROWS == iota((tall, BLOCK), 1)).astype(bf16)
        own = (iota((tall, D), 0) % ROWS) == head_of((tall, D), 1)
        grad = jnp.where(own, nn(pick, dc[block]), 0.0).astype(bf16)
        vd = nn(grad, wv[...]).astype(bf16)
        vd_out[block] = vd.reshape(BLOCK, ROWS, D)
        grad_probs = []
        for k in range(BLOCK // 2):
            pair = nt(
                vd[2 * ROWS * k : 2 * ROWS * (k + 1)],
                rows[2 * tokens * k : 2 * tokens * (k + 1)],
            )
            grad_probs += [pair[:ROWS, :tokens], pair[ROWS:, tokens:]]
        grad_probs = jnp.concatenate(grad_probs, axis=0)
        scale_col, inner_col = columns(scale[block], inner[block])
        prob = p[block].reshape(tall, tokens) * scale_col
        da = (prob * (grad_probs - inner_col)).astype(bf16)
        dap_out[block, :ROWS] = da.reshape(BLOCK, ROWS, tokens)
        dap_out[block, ROWS:] = prob.astype(bf16).reshape(BLOCK, ROWS, tokens)

    @pl.loop(first, rounds)
    def _(i):
        for j in range(SPAN // BLOCK):
            one_block(i * (SPAN // BLOCK) + j)

    @pl.loop(rounds, last)
    def _(i):
        span = pl.ds(pl.multiple_of(i * SPAN, SPAN), SPAN)
        dap_out[span] = jnp.zeros((SPAN, 2 * ROWS, tokens), bf16)
        vd_out[span] = jnp.zeros((SPAN, ROWS, D), bf16)


def key_sum_kernel(scal, sizes, ds, enc, dap, dh2, n3, ff, sums_out):
    tokens = enc.shape[1]
    tall = BLOCK * ROWS
    slots = dh2.shape[0]
    row = ds[...][:, :slots] * (1.0 / PARTS)
    at = iota((ROWS, D), 0)
    row = row[0:1]
    out = jnp.where(at == HEADS, jnp.sum(nn(stack3(row), dh2[...]), axis=0, keepdims=True), 0.0)
    out = jnp.where(at == HEADS + 1, row_dot(row, n3[...]), out)
    sums_out[...] = jnp.where(at == HEADS + 2, row_dot(row, ff[...]), out)

    def one_block(step):
        block = pl.ds(pl.multiple_of(step * BLOCK, BLOCK), BLOCK)
        own_slot = iota((tall, LANES), 1) == step * BLOCK + iota((tall, LANES), 0) // ROWS
        ds_col = jnp.sum(jnp.where(own_slot, ds[0:1], 0.0), axis=1, keepdims=True)
        scaled = (dap[block, :ROWS].reshape(tall, tokens).astype(f32) * ds_col).astype(bf16)
        flat = jnp.concatenate(
            [scaled[ROWS * b : ROWS * (b + 1)] for b in range(BLOCK)], axis=1
        )
        return nn(flat, enc[block].reshape(BLOCK * tokens, D))

    @pl.loop(0, rounds_of(scal, sizes))
    def _(i):
        per_round = SPAN // BLOCK
        total = one_block(i * per_round)
        for j in range(1, per_round):
            total = total + one_block(i * per_round + j)
        sums_out[...] += total


def enc_grad_kernel(first, last, ds, qa, qb, dap, vd, *refs):
    grad_out, slots, sems = refs[-3:]
    pieces, size = slots.shape[:2]
    qk = qa[...] + qb[...]
    lane = iota((1, LANES), 1)
    copies = []
    for k in range((last - first) // size):
        if k >= pieces:
            copies[k - pieces].wait()
        start = first + k * size
        for b in range(size):
            scale = jnp.sum(jnp.where(lane == start + b, ds[0:1], 0.0), axis=1, keepdims=True)
            right = jnp.concatenate([qk, vd[start + b].astype(f32)], axis=0) * scale
            slots[k % pieces, b] = tn(dap[start + b], right.astype(bf16)).astype(bf16)
        copies.append(
            pltpu.make_async_copy(
                slots.at[k % pieces], grad_out.at[pl.ds(start, size)], sems.at[k % pieces]
            )
        )
        copies[-1].start()
    for copy in copies[-pieces:]:
        copy.wait()


def share_kernel(scal, summed, scale, keep_out, send_out):
    core = scal[0] & 1
    lane = iota(scale.shape, 1)
    for out, bit in ((send_out, 1 - core), (keep_out, core)):
        for y in range(out.shape[0]):
            for k in range(out.shape[1]):
                head = (2 * y + bit) * out.shape[1] + k
                col = jnp.sum(jnp.where(lane == head, scale[...], 0.0), axis=1, keepdims=True)
                out[y, k] = (summed[head].astype(f32) * col).astype(bf16)


def away_kernel(scal, keep, got, out):
    part = 1 - (lax.shift_right_logical(scal[0], 1) & 1)
    for h in range(out.shape[0]):
        out[h] = (keep[part, h].astype(f32) + got[part, h].astype(f32)).astype(bf16)


def value_kernel(scal, keep, got, other, dc, ds, grad_out):
    slots = keep.shape[2]
    part = lax.shift_right_logical(scal[0], 1) & 1
    own_slot = iota((slots, LANES), 0) == iota((slots, LANES), 1)
    ds_col = jnp.sum(jnp.where(own_slot, ds[0:1], 0.0), axis=1, keepdims=True)
    grad = (dc[...].astype(f32) * ds_col).astype(bf16)
    for h in range(keep.shape[1]):
        pair = (keep[part, h].astype(f32) + got[part, h].astype(f32)).astype(bf16)
        summed = (pair.astype(f32) + other[h].astype(f32)).astype(bf16)
        out = tn(grad[:, h * HEAD_DIM : (h + 1) * HEAD_DIM], summed)
        grad_out[h * HEAD_DIM : (h + 1) * HEAD_DIM] = out.astype(bf16)


def document_picks(order, tile, scal, sizes, held, first):
    groups = 1 << len(order)
    half = held // groups
    core = scal[0] & 1
    doc = first + iota((tile, 1), 0)

    def one_group(g, found):
        start, at, upper = found
        pos = place_of(order, g ^ scal[1])
        slot = doc - start
        inside = (slot >= 0) & (slot < sizes[g])
        later = (slot >= half).astype(i32)
        at = jnp.where(inside, pos * half + slot - half * later, at)
        return start + sizes[g], at, jnp.where(inside, later, upper)

    zero = jnp.zeros((tile, 1), i32)
    _, at, upper = lax.fori_loop(
        0, groups, one_group, (jnp.int32(0), zero, zero), unroll=groups <= 8
    )
    hit = iota((tile, held), 1) == at
    return (hit & (upper == core)).astype(bf16), (hit & (upper != core)).astype(bf16)


def in_order(picks, own, other, width):
    mine, theirs = picks
    return (nn(mine, own[:, :width]) + nn(theirs, other[:, :width])).astype(bf16)


def picks_of(order, tile, scal, sizes, held, first, ready):
    if ready:
        return tuple(pick[...] for pick in ready)
    return document_picks(order, tile, scal, sizes, held, first)


def ds_column(ds, first, tile):
    eye = iota((tile, tile), 0) == iota((tile, tile), 1)
    return jnp.sum(jnp.where(eye, ds[0:1, pl.ds(first, tile)], 0.0), axis=1, keepdims=True)


def over_tiles(docs, tile, one_tile):
    one_tile(0, True)
    if docs > tile:

        @pl.loop(1, docs // tile)
        def _(t):
            one_tile(pl.multiple_of(t * tile, tile), False)


def put(out, value, new):
    if new:
        out[...] = value
    else:
        out[...] += value


def weights_before_kernel(
    order, tile, scal, sizes, c_own, c_other, h1, g_ff, wout, win, *refs
):
    ready, (y3_out, u_out, slope_out, c_out) = refs[:-4], refs[-4:]

    def one_tile(first, new):
        here = pl.ds(first, tile)
        picks = picks_of(order, tile, scal, sizes, c_own.shape[0], first, ready)
        c = in_order(picks, c_own, c_other, D)
        h2 = h1[...] + nn(c, wout[...])
        n2, _ = rms_parts(h2)
        y3 = (n2 * row_of(g_ff)).astype(bf16)
        y3_out[here] = y3
        z = nn(y3, win[...])
        u_out[here] = (z * phi(z)).astype(bf16)
        slope_out[here] = gelu_slope(z)
        width = c_out.shape[1]
        pick = (iota((D, width), 0) == scal[0] * width + iota((D, width), 1)).astype(bf16)
        c_out[here] = nn(c, pick).astype(bf16)

    over_tiles(y3_out.shape[0], tile, one_tile)


def grads_kernel(order, tile, scal, sizes, slope, both_own, both_other, ds, wdown, *refs):
    ready, (dz_out, both_out) = refs[:-2], refs[-2:]

    def one_tile(first, new):
        here = pl.ds(first, tile)
        picks = picks_of(order, tile, scal, sizes, both_own.shape[0], first, ready)
        both = in_order(picks, both_own, both_other, 2 * D).astype(f32)
        both = (both * ds_column(ds, first, tile)).astype(bf16)
        both_out[here] = both
        dz_out[here] = (nt(both[:, :D], wdown[...]) * slope[here]).astype(bf16)

    over_tiles(ds.shape[1], tile, one_tile)


def outer_kernel(
    tile, y3, dz, u, c, both, left1, right1, left2, right2,
    win_out, wdown_out, wout_out, key_out, query_out, wos_out, wvs_out,
    win_s, wdown_s, wout_s, key_s, query_s, wos_s, wvs_s, sems,
):
    copies = []

    def leave(held, out):
        copies.append(pltpu.make_async_copy(held, out, sems.at[len(copies)]))
        copies[-1].start()

    docs = y3.shape[0]

    def total(held, left, right):
        held[...] = tn(left[:tile], right[:tile])
        if docs > tile:

            @pl.loop(1, docs // tile)
            def _(t):
                here = pl.ds(pl.multiple_of(t * tile, tile), tile)
                held[...] += tn(left[here], right[here])

    def by_parts(held, out, left, right):
        for k in range(held.shape[0] // COLUMNS):
            part = pl.ds(k * COLUMNS, COLUMNS)
            total(held.at[part], left.at[:, part], right)
            leave(held.at[part], out.at[part])

    key_s[...] = tn(left1[: 2 * ROWS], right1[: 2 * ROWS])
    leave(key_s, key_out)
    query_s[...] = tn(left1[2 * ROWS :], right1[2 * ROWS :])
    leave(query_s, query_out)
    wos_s[...] = tn(left2[:ROWS], right2[:ROWS])
    leave(wos_s, wos_out)
    wvs_s[...] = tn(left2[ROWS:], right2[ROWS:])
    leave(wvs_s, wvs_out)
    total(wout_s, c, both.at[:, D:])
    leave(wout_s, wout_out)
    by_parts(win_s, win_out, y3, dz)
    by_parts(wdown_s, wdown_out, u, both.at[:, :D])
    for copy in copies:
        copy.wait()


def key_kernel(scal, sum_a, sum_b, h1, g_cross, wk, wq, part_out, left_out, right_out):
    y2, qm = query_parts(scal, h1, g_cross, wq)
    g = sum_a[...] + sum_b[...]
    g = jnp.where(iota((ROWS, D), 0) < HEADS, g, 0.0)
    high, low = split2(g)
    both = jnp.concatenate([high, low], axis=0)
    dq = nt(both, wk[...])
    dq = dq[:ROWS] + dq[ROWS:]
    width = dq.shape[1]
    first = scal[0] * (width // HEAD_DIM)
    own = iota((ROWS, width), 0) == first + head_of((ROWS, width), 1)
    dq = jnp.sum(jnp.where(own, dq, 0.0), axis=0, keepdims=True)
    dq_parts = stack3(dq)
    left_out[...] = jnp.concatenate([qm, qm, dq_parts], axis=0)
    right_out[...] = jnp.concatenate([both, repeat3(y2[0:1])], axis=0)
    part = jnp.sum(nn(dq_parts, wq[...]), axis=0, keepdims=True)
    part_out[...] = jnp.broadcast_to(part, (8, D))


def hidden_kernel(
    part_a, part_b, sum_a, sum_b, h1, g_cross, start, g_self, wos, wvs, g_final, row,
    dh1_out, part_out, left_out, right_out, cross_out, final_out, row_out, ff_out,
):
    y1, s1 = self_parts(start, g_self, wvs)
    dy2 = part_a[0:1] + part_b[0:1]
    sums = sum_a[...] + sum_b[...]
    n1, r1 = rms_parts(h1[...])
    cross_out[...] = (dy2 * n1).reshape(cross_out.shape)
    dh1 = sums[HEADS : HEADS + 1] + rms_back(dy2 * row_of(g_cross), n1, r1)
    dh1_out[...] = dh1
    dh1_parts = stack3(dh1)
    ds1 = jnp.sum(nt(dh1_parts, wos[...]), axis=0, keepdims=True)
    ds1_parts = stack3(ds1)
    left_out[...] = jnp.concatenate([repeat3(s1[0:1]), ds1_parts], axis=0)
    right_out[...] = jnp.concatenate([dh1_parts, repeat3(y1[0:1])], axis=0)
    part = jnp.sum(nn(ds1_parts, wvs[...]), axis=0, keepdims=True)
    part_out[...] = jnp.broadcast_to(part, (8, D))
    total = sums[HEADS + 1 : HEADS + 2] * FACTOR
    final_out[...] = (total * row_of(row)).reshape(final_out.shape)
    row_out[...] = (total * row_of(g_final)).reshape(row_out.shape)
    ff_out[...] = sums[HEADS + 2 : HEADS + 3].reshape(ff_out.shape)


def start_kernel(
    part_a, part_b, dh1, start, g_self, value_a, value_b, gain_out, start_out, value_out
):
    value_out[...] = value_a[...].astype(f32) + value_b[...].astype(f32)
    dy1 = part_a[0:1] + part_b[0:1]
    n0, r0 = rms_parts(row_of(start))
    gain_out[...] = (dy1 * n0).reshape(gain_out.shape)
    back = dh1[...] + rms_back(dy1 * row_of(g_self), n0, r0)
    start_out[...] = back.reshape(start_out.shape)


def shape(dims, dtype=f32):
    return jax.ShapeDtypeStruct(dims, dtype)


def whole_spec(memory=pltpu.VMEM):
    return pl.BlockSpec(memory_space=memory)


def name_of(kernel):
    return getattr(kernel, "func", kernel).__name__


def in_hbm(x):
    return pltpu.with_memory_space_constraint(x, pltpu.HBM)


def plain(
    kernel, outs, *args, smem=0, hbm=(), hbm_out=False, onto=None, limit=12, scratch=()
):
    spaces = [pltpu.SMEM] * smem + [pltpu.VMEM] * (len(args) - smem)
    for k in hbm:
        spaces[k] = pltpu.HBM
    out_space = pltpu.HBM if hbm_out else pltpu.VMEM
    return pl.pallas_call(
        kernel,
        out_shape=outs,
        in_specs=[whole_spec(space) for space in spaces],
        out_specs=[whole_spec(out_space) for _ in outs]
        if isinstance(outs, list)
        else whole_spec(out_space),
        scratch_shapes=list(scratch),
        input_output_aliases=onto or {},
        compiler_params=pltpu.CompilerParams(vmem_limit_bytes=limit * MIB),
        cost_estimate=pl.CostEstimate(flops=0, bytes_accessed=0, transcendentals=0),
        name=name_of(kernel),
    )(*args)


def bits_of(size):
    return [1 << b for b in range(size.bit_length() - 1)]


def far_first(size):
    return bits_of(size)[::-1]


def swap(x, axis, bit):
    size = lax.axis_size(axis)
    return lax.ppermute(x, axis, [(i, i ^ bit) for i in range(size)])


def after(x, *deps):
    return lax.optimization_barrier((x, *deps))[0]


def add(x, y):
    return (x.astype(f32) + y.astype(f32)).astype(x.dtype)


def sum_last(x, steps):
    for axis, bit in steps[:-1]:
        x = add(x, swap(x, axis, bit))
    axis, bit = steps[-1]
    return x, swap(x, axis, bit)


def per_device(
    enc_out,
    enc_len,
    group_docs,
    list_len,
    relevance,
    start_token,
    score_row,
    g_self,
    w_value_self,
    w_out_self,
    g_cross,
    w_query,
    w_key,
    w_value,
    w_out,
    g_ff,
    w_in,
    w_down,
    g_final,
):
    groups = lax.axis_size("docs")
    parts = lax.axis_size("heads")
    assert parts == PARTS
    me_g = lax.axis_index("docs")
    me_j = lax.axis_index("heads")
    slots, tokens = enc_out.shape[:2]
    docs = enc_len.shape[0]
    width = w_value.shape[1]
    own_heads = HEADS // parts
    hidden = w_in.shape[1]
    over_heads = [("heads", 1), ("heads", 2)]
    order = far_first(groups)
    over_docs = [("docs", bit) for bit in order]

    scal = jnp.stack([me_j, me_g])
    wvs_t, wq_t, wk_t, wv_t = (w.T for w in (w_value_self, w_query, w_key, w_value))

    wv_by1, wo_by1 = swap(wv_t, "heads", 1), swap(w_out, "heads", 1)

    part = plain(
        self_kernel,
        shape((8, D)),
        *map(in_hbm, (start_token, g_self, wvs_t, w_out_self)),
    )


    def load(first, last, since, *onto):
        return pl.pallas_call(
            functools.partial(load_kernel, first, last),
            out_shape=pltpu.VMEM(enc_out.shape, bf16),
            in_specs=[whole_spec(pltpu.HBM), whole_spec(pl.ANY), whole_spec(pltpu.SMEM)]
            + [whole_spec()] * len(onto),
            out_specs=whole_spec(),
            scratch_shapes=[pltpu.SemaphoreType.DMA((last - first,))],
            input_output_aliases={3: 0} if onto else {},
            compiler_params=pltpu.CompilerParams(vmem_limit_bytes=MIB),
            cost_estimate=pl.CostEstimate(flops=0, bytes_accessed=0, transcendentals=0),
            name="load_kernel",
        )(in_hbm(enc_out), since, scal, *onto)

    part = add(part, swap(part, "heads", 1))
    part_a, part_b = part, swap(part, "heads", 2)
    held = load(0, 1, part)
    part_b, held = lax.optimization_barrier((part_b, held))
    wv_by2 = swap(after(wv_t, part_b), "heads", 2)
    qk, h1 = plain(
        query_kernel,
        [shape((ROWS, D)), shape((1, D))],
        scal,
        part_a,
        part_b,
        *map(in_hbm, (start_token, g_cross, wq_t, wk_t)),
        smem=1,
    )
    qk = add(qk, swap(qk, "heads", 1))
    qk, held = lax.optimization_barrier((qk, held))
    qk_a, qk_b = qk, swap(qk, "heads", 2)
    held = load(1, 3, qk, held)
    qk_b, held, wv_by2 = lax.optimization_barrier((qk_b, held, wv_by2))
    wv_by3 = swap(wv_by2, "heads", 1)

    wo_by2 = swap(after(w_out, qk_b), "heads", 2)
    held, prob, summed, extra = plain(
        functools.partial(attend_kernel, 3),
        [
            pltpu.VMEM(enc_out.shape, bf16),
            pltpu.VMEM((slots, ROWS, tokens), f32),
            pltpu.VMEM((PANELS, slots * ROWS, LANES), f32),
            shape((slots, LANES), bf16),
        ],
        scal,
        group_docs,
        enc_len,
        qk_a,
        qk_b,
        in_hbm(enc_out),
        held,
        smem=3,
        hbm=(5,),
        onto={6: 0},
        scratch=[pltpu.VMEM((2 * ROWS, D), bf16), pltpu.SemaphoreType.DMA((slots // BLOCK,))],
        limit=16,
    )
    summed, wv_by3, wo_by2 = lax.optimization_barrier((summed, wv_by3, wo_by2))
    wv_parts = (wv_t, wv_by2, wv_by1, wv_by3)
    wo_parts = (w_out, wo_by2, wo_by1, swap(wo_by2, "heads", 1))
    pay, summed, wv_full = plain(
        project_kernel,
        [
            shape((slots, D + LANES), bf16),
            shape((HEADS, slots, D), bf16),
            shape((D, D), bf16),
        ],
        scal,
        summed,
        extra,
        *wv_parts,
        smem=1,
    )
    merged = plain(
        merge_kernel, shape(pay.shape, bf16), scal, pay, swap(pay, "heads", 1), smem=1
    )
    other = swap(merged, "heads", 2)
    wo_full = plain(arrange_kernel, shape((D, D), bf16), scal, *wo_parts, smem=1)
    tile = 384
    held_rows = groups * slots // 2
    picks_shape = [shape((tile, held_rows), bf16)] * 2 if docs == tile else []
    target, member, *picks = plain(
        functools.partial(target_kernel, order),
        [shape((list_len.shape[0], docs))] * 2 + picks_shape,
        scal,
        group_docs,
        list_len,
        relevance,
        smem=3,
    )
    other, wo_full, target, member, *picks = lax.optimization_barrier(
        (other, wo_full, target, member, *picks)
    )

    c, c32, scale, h2, z, part = plain(
        forward_kernel,
        [
            shape((slots // 2, D), bf16),
            shape((slots, D)),
            shape((slots, LANES)),
            shape((slots, D)),
            shape((slots, hidden)),
            shape((slots, D), bf16),
        ],
        scal,
        merged,
        other,
        pay,
        h1,
        wo_full,
        g_ff,
        w_in,
        w_down,
        smem=1,
        scratch=[pltpu.VMEM((slots, D), bf16)],
    )

    half = slots // 2

    def grow(x, k):
        return jnp.concatenate([x, swap(x, *over_docs[k])], axis=0)

    def tie(*xs):
        return lax.optimization_barrier(xs)

    last = len(over_docs) - 1
    near_first = over_docs[::-1]
    part = add(part, swap(part, "heads", 1))
    part_a, part_b = part, swap(part, "heads", 2)
    keep, sent = plain(
        share_kernel, [shape((2, own_heads, slots, D), bf16)] * 2, scal, summed, scale, smem=1
    )
    part_b, keep, sent = tie(part_b, keep, sent)
    c_all, n3, dh3 = plain(
        score_kernel,
        [shape((half, D + LANES), bf16), shape((slots, D)), shape((slots, D), bf16)],
        part_a,
        part_b,
        h2,
        g_final,
        score_row,
        c,
    )
    part = plain(down_kernel, shape((slots, D), bf16), dh3, z, w_down, w_in)
    part = add(part, swap(part, "heads", 1))
    part_a, part_b = part, swap(part, "heads", 2)
    c_far = swap(c_all, *over_docs[0])
    got = swap(sent, "heads", 1)
    away = plain(
        away_kernel, shape((own_heads, slots, D), bf16), scal, keep, got, smem=1
    )
    other = swap(away, "heads", 2)
    part_b, away = tie(part_b, away)
    dh2, grads, dc, dc_own, inner, ff = plain(
        context_kernel,
        [
            shape((slots, D), bf16),
            shape((half, 2 * D), bf16),
            shape((slots, D), bf16),
            shape((slots, width), bf16),
            shape((slots, LANES)),
            shape((slots, D)),
        ],
        scal,
        part_a,
        part_b,
        h2,
        dh3,
        c32,
        g_ff,
        wo_full,
        w_out,
        smem=1,
        scratch=[pltpu.VMEM((slots, 2 * D), bf16)],
    )

    c_all, c_far, dc, grads = tie(c_all, c_far, dc, grads)
    c_all = jnp.concatenate([c_all, c_far], axis=0)
    for k in range(1, last):
        c_far = swap(c_all, *over_docs[k])
        if k < last - 1:
            c_all = jnp.concatenate([c_all, c_far], axis=0)
    grads_far = swap(grads, *over_docs[0])

    outs = [
        pltpu.VMEM((slots, 2 * ROWS, tokens), bf16),
        pltpu.VMEM((slots, ROWS, D), bf16),
    ]
    rounds = slots // SPAN
    inputs = (scal, group_docs, held, prob, scale, inner, dc, wv_full)

    def back(first, last, *onto):
        return plain(
            functools.partial(back_kernel, first, last),
            outs,
            *inputs,
            *onto,
            smem=2,
            onto={8: 0, 9: 1} if onto else None,
            limit=16,
        )

    dap, vd = back(0, 1)
    dap, c_far = tie(dap, c_far)
    c_all = jnp.concatenate([c_all, c_far], axis=0)
    c_far = swap(c_all, *over_docs[last])
    dap, vd = back(1, rounds, dap, vd)
    dap, c_far, other, grads_far = tie(dap, c_far, other, grads_far)
    grads = jnp.concatenate([grads, grads_far], axis=0)
    for m in range(1, last):
        grads_far = swap(grads, *over_docs[m])
        if m < last - 1:
            grads = jnp.concatenate([grads, grads_far], axis=0)
    c_all = jnp.concatenate([c_all, c_far], axis=0)
    all_scores, loss, ds_docs, ds_mine = plain(
        functools.partial(list_kernel, order),
        [shape((docs,)), shape((1, 1)), shape((1, docs)), shape((8, LANES))],
        scal,
        group_docs,
        c_all,
        target,
        member,
        smem=2,
    )
    sums = plain(
        key_sum_kernel,
        shape((ROWS, D)),
        scal,
        group_docs,
        ds_mine,
        held,
        dap,
        dh2,
        n3,
        ff,
        smem=2,
    )

    def enc_grads(first, last, grads=None):
        outs = pltpu.HBM(enc_out.shape, bf16)
        size = 8
        args = (ds_mine, qk_a, qk_b, dap, vd)
        return plain(
            functools.partial(enc_grad_kernel, first, last),
            outs,
            *args,
            *([] if grads is None else [grads]),
            hbm=() if grads is None else (len(args),),
            hbm_out=True,
            onto={} if grads is None else {len(args): 0},
            scratch=[pltpu.VMEM((4, size, tokens, D), bf16), pltpu.SemaphoreType.DMA((4,))],
            limit=16,
        )

    sums, dc_own = tie(sums, dc_own)
    value_part = plain(
        value_kernel,
        shape((width, D), bf16),
        scal,
        keep,
        got,
        other,
        dc_own,
        ds_mine,
        smem=1,
    )
    value_far = swap(value_part, *near_first[0])
    c_far = swap(c_all, "heads", 1)
    sums = add(sums, swap(sums, "heads", 1))
    steps = near_first[:0:-1] + over_heads[1:] + near_first[:1]
    sums, grads_far = tie(sums, grads_far)
    grads = jnp.concatenate([grads, grads_far], axis=0)
    grads_far = swap(grads, *over_docs[last])
    enc_grad = None
    third = slots // 3
    sum_a = sums
    for k, step in enumerate(steps):
        ds_mine, sum_a = tie(ds_mine, sum_a)
        sum_b = swap(sum_a, *step)
        if k < 3:
            enc_grad = enc_grads(k * third, (k + 1) * third, enc_grad)
            sum_b, enc_grad = tie(sum_b, enc_grad)
        if k == 1:
            sum_b, value_far, c_far = tie(sum_b, value_far, c_far)
            for step in near_first[1:-1]:
                value_part = add(value_part, value_far)
                value_far = swap(value_part, *step)
        if k < len(steps) - 1:
            sum_a = sum_a + sum_b
    y3, u, slope, c_own = plain(
        functools.partial(weights_before_kernel, order, tile),
        [
            shape((docs, D), bf16),
            shape((docs, hidden), bf16),
            shape((docs, hidden)),
            shape((docs, width), bf16),
        ],
        scal,
        group_docs,
        c_all,
        c_far,
        h1,
        g_ff,
        wo_full,
        w_in,
        *picks,
        smem=2,
        limit=60 if docs > 384 else 16,
    )
    sum_b, grads_far, value_far, y3, u, slope, c_own = tie(
        sum_b, grads_far, value_far, y3, u, slope, c_own
    )
    value_part = add(value_part, value_far)
    value_far = swap(value_part, *near_first[-1])
    grads = jnp.concatenate([grads, grads_far], axis=0)
    grads_far = swap(grads, "heads", 1)

    part, left1, right1 = plain(
        key_kernel,
        [shape((8, D)), shape((3 * ROWS, width), bf16), shape((3 * ROWS, D), bf16)],
        scal,
        sum_a,
        sum_b,
        h1,
        g_cross,
        wk_t,
        wq_t,
        smem=1,
    )
    part = add(part, swap(part, "heads", 1))
    part, grads_far = tie(part, grads_far)
    part_a, part_b = part, swap(part, "heads", 2)
    dz, both = plain(
        functools.partial(grads_kernel, order, tile),
        [shape((docs, hidden), bf16), shape((docs, 2 * D), bf16)],
        scal,
        group_docs,
        slope,
        grads,
        grads_far,
        ds_docs,
        w_down,
        *picks,
        smem=2,
        limit=60 if docs > 384 else 16,
    )
    part_b, dz, both = tie(part_b, dz, both)
    dh1, part, left2, right2, cross, final_gain, row_grad, ff_gain = plain(
        hidden_kernel,
        [
            shape((1, D)),
            shape((8, D)),
            shape((2 * ROWS, width), bf16),
            shape((2 * ROWS, D), bf16),
        ]
        + [shape((D,))] * 4,
        part_a,
        part_b,
        sum_a,
        sum_b,
        h1,
        g_cross,
        start_token,
        g_self,
        w_out_self,
        wvs_t,
        g_final,
        score_row,
    )
    part_a, part_b = sum_last(part, over_heads)
    dims = [(D, hidden), (hidden, D), (width, D)] + [(width, D)] * 4
    w_in_grad, w_down_grad, w_out_grad, key_grad, query_grad, wos_grad, wvs_grad = plain(
        functools.partial(outer_kernel, tile),
        [pltpu.HBM(dim, f32) for dim in dims],
        y3,
        dz,
        u,
        c_own,
        both,
        left1,
        right1,
        left2,
        right2,
        hbm_out=True,
        scratch=[pltpu.VMEM(dim, f32) for dim in dims] + [pltpu.SemaphoreType.DMA((16,))],
        limit=60 if docs > 384 else 24,
    )
    part_b, w_down_grad, value_far = tie(part_b, w_down_grad, value_far)
    self_gain, start_grad, value_grad = plain(
        start_kernel,
        [shape((D,)), shape((D,)), shape((width, D))],
        part_a,
        part_b,
        dh1,
        start_token,
        g_self,
        value_part,
        value_far,
    )

    return (
        all_scores,
        loss.reshape(()),
        enc_grad,
        start_grad,
        row_grad,
        self_gain,
        wvs_grad.T,
        wos_grad,
        cross,
        query_grad.T,
        key_grad.T,
        value_grad.T,
        w_out_grad,
        ff_gain,
        w_in_grad,
        w_down_grad,
        final_gain,
    )


def solution(mesh):
    placed = (
        P("docs", "heads", None),
        P(),
        P(),
        P(),
        P(),
        P(),
        P(),
        P(),
        P(None, "heads"),
        P("heads", None),
        P(),
        P(None, "heads"),
        P(None, "heads"),
        P(None, "heads"),
        P("heads", None),
        P(),
        P(None, "heads"),
        P("heads", None),
        P(),
    )
    return jax.shard_map(
        per_device,
        mesh=mesh,
        in_specs=placed,
        out_specs=(
            P(),
            P(),
            P("docs", "heads", None),
            P(),
            P(),
            P(),
            P(None, "heads"),
            P("heads", None),
            P(),
            P(None, "heads"),
            P(None, "heads"),
            P(None, "heads"),
            P("heads", None),
            P(),
            P(None, "heads"),
            P("heads", None),
            P(),
        ),
        check_vma=False,
    )
```

```python
import functools

import jax
import jax.numpy as jnp
from jax import lax
from jax.experimental import pallas as pl
from jax.experimental.pallas import tpu as pltpu
from jax.sharding import PartitionSpec as P

D = 768
HEADS = 12
HEAD_DIM = 64
ROWS = 16
BLOCK = 16
SPAN = 2 * BLOCK
LANES = 128
PANELS = D // LANES
COLUMNS = 256
PARTS = 4

EPSILON = 1e-06
MASKED = -1e30
FACTOR = D ** (-0.5)
ROOT_HALF = 0.5**0.5
DENSITY = 0.3989422804014327
f32, bf16, i32 = jnp.float32, jnp.bfloat16, jnp.int32
EXACT = lax.Precision.HIGHEST
MIB = 1 << 20


def nn(a, b, precision=None):
    return lax.dot_general(
        a, b, (((1,), (0,)), ((), ())), precision=precision, preferred_element_type=f32
    )


def nt(a, b, precision=None):
    return lax.dot_general(
        a, b, (((1,), (1,)), ((), ())), precision=precision, preferred_element_type=f32
    )


def tn(a, b, precision=None):
    return lax.dot_general(
        a, b, (((0,), (0,)), ((), ())), precision=precision, preferred_element_type=f32
    )


def iota(shape, dim):
    return lax.broadcasted_iota(i32, shape, dim)


def split2(x):
    high = x.astype(bf16)
    return high, (x - high.astype(f32)).astype(bf16)


def split3(x):
    high = x.astype(bf16)
    rest = x - high.astype(f32)
    mid = rest.astype(bf16)
    return high, mid, (rest - mid.astype(f32)).astype(bf16)


def stack3(row, height=ROWS):
    at = iota((height, row.shape[1]), 0)
    parts = split3(row)
    zero = jnp.zeros((), f32)
    out = jnp.where(at == 0, parts[0].astype(f32), zero)
    out = jnp.where(at == 1, parts[1].astype(f32), out)
    return jnp.where(at == 2, parts[2].astype(f32), out).astype(bf16)


def repeat3(row, height=ROWS):
    at = iota((height, row.shape[1]), 0)
    return jnp.where(at < 3, row.astype(f32), 0.0).astype(bf16)


def rms_parts(rows):
    scale = lax.rsqrt(jnp.mean(rows * rows, axis=-1, keepdims=True) + EPSILON)
    return rows * scale, scale


def rms_back(grad_normed, normed, scale):
    inner = jnp.mean(grad_normed * normed, axis=-1, keepdims=True)
    return scale * (grad_normed - normed * inner)


def phi(z):
    return 0.5 * (1.0 + lax.erf(z * ROOT_HALF))


def gelu_slope(z):
    return phi(z) + z * (DENSITY * jnp.exp(-0.5 * z * z))


def head_of(shape, dim):
    return iota(shape, dim) // HEAD_DIM


def spread(small):
    high, mid, low = (part.astype(f32) for part in split3(small))
    packed = high + pltpu.roll(mid, ROWS, 1) + pltpu.roll(low, 2 * ROWS, 1)
    lane = iota((LANES, D), 0)
    hot = (lane < 3 * ROWS) & (lane % ROWS == head_of((LANES, D), 1))
    return nn(packed.astype(bf16), hot.astype(bf16))


def row_dot(row, right):
    high, low = split2(right)
    parts = stack3(row)
    return jnp.sum(nn(parts, high) + nn(parts, low), axis=0, keepdims=True)


def row_of(ref):
    return ref[...].astype(f32).reshape(1, D)


def gained(n, gain):
    return jnp.broadcast_to(n * row_of(gain), (ROWS, D)).astype(bf16)


def self_parts(start, g_self, wvs):
    x0 = row_of(start)
    n0, _ = rms_parts(x0)
    y1 = gained(n0, g_self)
    return y1, nt(y1, wvs[...]).astype(bf16)


def query_parts(scal, h1, g_cross, wq):
    n1, _ = rms_parts(h1[...])
    y2 = gained(n1, g_cross)
    q = nt(y2, wq[...]).astype(bf16)
    width = q.shape[1]
    first = scal[0] * (width // HEAD_DIM)
    own = iota((ROWS, width), 0) == first + head_of((ROWS, width), 1)
    return y2, jnp.where(own, q.astype(f32), 0.0).astype(bf16)


def self_kernel(start, g_self, wvs, wos, part_out):
    _, s1 = self_parts(start, g_self, wvs)
    part_out[...] = nn(s1, wos[...])[:8]


def load_kernel(first, last, enc, since, scal, *refs):
    held, sems = refs[-2:]
    loads = []
    for k in range(first, last):
        part = pl.ds(k * BLOCK, BLOCK)
        loads.append(pltpu.make_async_copy(enc.at[part], held.at[part], sems.at[k - first]))
        loads[-1].start()
    for load in loads:
        load.wait()


def query_kernel(scal, part_a, part_b, start, g_cross, wq, wk, qk_out, h1_out):
    h1_out[...] = row_of(start) + (part_a[0:1] + part_b[0:1])
    _, qm = query_parts(scal, h1_out, g_cross, wq)
    qk_out[...] = nn(qm, wk[...])


def load_kernel(first, last, enc, since, scal, *refs):
    held, sems = refs[-2:]
    loads = []
    for k in range(first, last):
        part = pl.ds(k * BLOCK, BLOCK)
        loads.append(pltpu.make_async_copy(enc.at[part], held.at[part], sems.at[k - first]))
        loads[-1].start()
    for load in loads:
        load.wait()


def query_kernel(scal, part_a, part_b, start, g_cross, wq, wk, qk_out, h1_out):
    h1_out[...] = row_of(start) + (part_a[0:1] + part_b[0:1])
    _, qm = query_parts(scal, h1_out, g_cross, wq)
    qk_out[...] = nn(qm, wk[...])


def select_docs(height, width):
    r, c = iota((height, width), 0), iota((height, width), 1)
    return (((r // BLOCK) == (c % ROWS)) & ((r % BLOCK) == (c // ROWS))).astype(bf16)


def first_doc(scal, sizes):
    groups = sizes.shape[0]

    def body(g, total):
        return total + jnp.where(g < scal[1], sizes[g], 0)

    return lax.fori_loop(0, groups, body, jnp.int32(0), unroll=groups <= 8)


def rounds_of(scal, sizes):
    return (sizes[scal[1]] + SPAN - 1) // SPAN


def attend_kernel(
    loaded, scal, sizes, lengths, qa, qb, enc, _, held, p_out, e_out, ext_out, qk_s, sems
):
    tokens = enc.shape[1]
    blocks = enc.shape[0] // BLOCK
    rounds = rounds_of(scal, sizes)
    per_round = SPAN // BLOCK
    count = sizes[scal[1]]
    begin = first_doc(scal, sizes)
    tall = BLOCK * ROWS

    def piece(k):
        part = pl.ds(k * BLOCK, BLOCK)
        return pltpu.make_async_copy(enc.at[part], held.at[part], sems.at[k])

    for k in range(loaded, blocks):
        pl.when(k // per_round < rounds)(lambda k=k: piece(k).start())
    high, low = split2(qa[...] + qb[...])
    qk_s[0:ROWS] = high
    qk_s[ROWS : 2 * ROWS] = low

    def one_block(step):
        block = pl.ds(pl.multiple_of(step * BLOCK, BLOCK), BLOCK)
        flat = pl.ds(pl.multiple_of(step * tall, tall), tall)
        rows = held[block].reshape(BLOCK * tokens, D)
        both = nt(qk_s[...], rows)
        logits = both[:ROWS] + both[ROWS:]
        logits = jnp.concatenate(
            [logits[:, b * tokens : (b + 1) * tokens] for b in range(BLOCK)], axis=0
        )
        shown = []
        for b in range(BLOCK):
            slot = step * BLOCK + b
            doc = jnp.minimum(begin + slot, lengths.shape[0] - 1)
            length = jnp.where(slot < count, lengths[doc] - scal[0] * tokens, 0)
            shown.append(jnp.broadcast_to(length, (ROWS, tokens)))
        seen = iota((tall, tokens), 1) < jnp.concatenate(shown, axis=0)
        logits = jnp.where(seen, logits, MASKED)
        peak = jnp.max(logits, axis=1, keepdims=True)
        raised = jnp.where(seen, jnp.exp(logits - peak), 0.0)
        total = jnp.sum(raised, axis=1, keepdims=True)
        p_out[block] = raised.reshape(BLOCK, ROWS, tokens)
        low = raised.astype(bf16)
        summed = jnp.concatenate(
            [
                nn(low[ROWS * b : ROWS * (b + 1)], rows[tokens * b : tokens * (b + 1)])
                for b in range(BLOCK)
            ],
            axis=0,
        )
        for k in range(PANELS):
            e_out[k, flat] = summed[:, k * LANES : (k + 1) * LANES]
        gather = (iota((BLOCK, tall), 0) == iota((BLOCK, tall), 1) // ROWS).astype(bf16)
        parts = split3(peak) + split3(total)
        at = iota((tall, LANES), 1)
        extra = jnp.zeros((tall, LANES), f32)
        for k, part in enumerate(parts):
            extra = jnp.where(at // ROWS == k, part.astype(f32), extra)
        extra = jnp.where(at % ROWS == iota((tall, LANES), 0) % ROWS, extra, 0.0)
        ext_out[block] = nn(gather, extra.astype(bf16)).astype(bf16)

    @pl.loop(0, rounds)
    def _(i):
        for j in range(per_round):
            k = i * per_round + j
            pl.when(k >= loaded)(lambda k=k: piece(k).wait())
        for j in range(per_round):
            one_block(i * per_round + j)

    @pl.loop(rounds, enc.shape[0] // SPAN)
    def _(i):
        span = pl.ds(pl.multiple_of(i * SPAN, SPAN), SPAN)
        flat = pl.ds(pl.multiple_of(i * SPAN * ROWS, SPAN * ROWS), SPAN * ROWS)
        p_out[span] = jnp.zeros((SPAN, ROWS, tokens), f32)
        for k in range(PANELS):
            e_out[k, flat] = jnp.zeros((SPAN * ROWS, LANES), f32)
        ext_out[span] = jnp.where(iota((SPAN, LANES), 1) < ROWS, MASKED, 0.0).astype(bf16)


def sums_of_head(summed, head, slots):
    rows = pl.ds(head, slots, stride=ROWS)
    return jnp.concatenate([summed[k, rows, :] for k in range(PANELS)], axis=1)


def place_parts(scal, full, own, by2, by1, by3):
    height = own.shape[0]
    for mask, piece in ((0, own), (2, by2), (1, by1), (3, by3)):
        at = pl.multiple_of((scal[0] ^ mask) * height, height)
        full[pl.ds(at, height)] = piece[...]


def arrange_kernel(scal, own, by2, by1, by3, full_out):
    place_parts(scal, full_out, own, by2, by1, by3)


def project_kernel(scal, summed, extra, own, by2, by1, by3, pay_out, heads_out, wv):
    place_parts(scal, wv, own, by2, by1, by3)
    slots = pay_out.shape[0]
    even = iota((slots, LANES), 1) < HEAD_DIM
    for k in range(HEADS // 2):
        pair = wv[k * LANES : (k + 1) * LANES]
        for head in (2 * k, 2 * k + 1):
            heads_out[head] = sums_of_head(summed, head, slots).astype(bf16)
        one, two = (nt(heads_out[2 * k + odd], pair) for odd in range(2))
        pay_out[:, k * LANES : (k + 1) * LANES] = jnp.where(even, one, two).astype(bf16)
    pay_out[:, D:] = extra[...]


def decode(pay):
    extra = pay[:, D:].astype(f32)

    def lane(k):
        return pltpu.roll(extra, LANES - k * ROWS, 1) if k else extra

    first = iota(extra.shape, 1) < ROWS
    peak = jnp.where(first, (lane(0) + lane(1)) + lane(2), 0.0)
    total = jnp.where(first, (lane(3) + lane(4)) + lane(5), 0.0)
    return peak, total


def merge(one, two, last=False):
    peak1, total1 = decode(one)
    peak2, total2 = decode(two)
    peak = jnp.maximum(peak1, peak2)
    up1, up2 = jnp.exp(peak1 - peak), jnp.exp(peak2 - peak)
    total = up1 * total1 + up2 * total2
    first = iota(peak.shape, 1) < ROWS
    if last:
        some = first & (total > 0.0)
        total = jnp.where(some, 1.0 / jnp.where(some, total, 1.0), 0.0)
        up1, up2 = up1 * total, up2 * total
    up1, up2 = jnp.where(first, up1, 0.0), jnp.where(first, up2, 0.0)
    context = spread(up1) * one[:, :D].astype(f32) + spread(up2) * two[:, :D].astype(f32)
    return peak, total, context


def ordered(bit, own, other):
    swap = jnp.broadcast_to(bit, own.shape) == 1
    return jnp.where(swap, other, own), jnp.where(swap, own, other)


def merge_kernel(scal, own, other, pay_out):
    one, two = ordered(scal[0] & 1, own[...].astype(f32), other[...].astype(f32))
    peak, total, context = merge(one, two)
    pay_out[:, :D] = context.astype(bf16)
    extra = jnp.zeros(peak.shape, f32)
    at = iota(peak.shape, 1) // ROWS
    for k, part in enumerate(split3(peak) + split3(total)):
        part = part.astype(f32)
        extra = jnp.where(at == k, pltpu.roll(part, k * ROWS, 1) if k else part, extra)
    pay_out[:, D:] = extra.astype(bf16)


def own_half(scal, rows, held, out):
    half = out.shape[0]
    held[...] = rows
    out[...] = held[pl.ds(pl.multiple_of((scal[0] & 1) * half, half), half)]


def forward_kernel(
    scal, own, other, first, h1, wo, g_ff, win, wdown,
    c_out, c32_out, scale_out, h2_out, z_out, part_out, c_s,
):
    bit = lax.shift_right_logical(scal[0], 1) & 1
    one, two = ordered(bit, own[...].astype(f32), other[...].astype(f32))
    peak, inverse, context = merge(one, two, True)
    mine, _ = decode(first[...].astype(f32))
    scale_out[...] = jnp.exp(jnp.minimum(mine - peak, 0.0)) * inverse
    c32_out[...] = context
    low = context.astype(bf16)
    own_half(scal, low, c_s, c_out)
    h2 = h1[...] + nn(low, wo[...])
    h2_out[...] = h2
    n2, _ = rms_parts(h2)
    y3 = (n2 * row_of(g_ff)).astype(bf16)
    z = nn(y3, win[...])
    z_out[...] = z
    u = (z * phi(z)).astype(bf16)
    part_out[...] = nn(u, wdown[...]).astype(bf16)


def score_kernel(part_a, part_b, h2, g_final, row, c, pay_out, n3_out, dh3_out):
    h3 = h2[...] + (part_a[...].astype(f32) + part_b[...].astype(f32))
    n3, r3 = rms_parts(h3)
    n3_out[...] = n3
    wanted = jnp.broadcast_to(row_of(g_final) * row_of(row) * FACTOR, (8, D))
    scores = nt(wanted, n3, EXACT)[0:1]
    wide = jnp.concatenate([scores, jnp.zeros((1, LANES - n3.shape[0]), f32)], axis=1)
    pay_out[:, :D] = c[...]
    pay_out[:, D:] = stack3(wide, c.shape[0])
    dh3_out[...] = rms_back(wanted[0:1], n3, r3).astype(bf16)


def down_kernel(dh3, z, wdown, win, part_out):
    du = nt(dh3[...], wdown[...])
    dz = (du * gelu_slope(z[...])).astype(bf16)
    part_out[...] = nt(dz, win[...]).astype(bf16)


def target_kernel(order, scal, sizes, lens, rel, target_out, member_out, *picks_out):
    if picks_out:
        tile, held = picks_out[0].shape
        for out, pick in zip(picks_out, document_picks(order, tile, scal, sizes, held, 0)):
            out[...] = pick
    queries, docs = target_out.shape
    relevance = rel[...].reshape(1, docs)
    at = iota((queries, 1), 0)

    def one_list(j, found):
        begin, begins, ends = found
        end = begin + lens[j]
        return end, jnp.where(at == j, begin, begins), jnp.where(at == j, end, ends)

    none = jnp.zeros((queries, 1), i32)
    _, begins, ends = lax.fori_loop(
        0, queries, one_list, (jnp.int32(0), none, none), unroll=queries <= 32
    )
    place = iota((queries, docs), 1)
    member = (place >= begins) & (place < ends)
    weight = jnp.sum(jnp.where(member, relevance, 0.0), axis=1, keepdims=True)
    target_out[...] = jnp.where(member, relevance / weight, 0.0)
    member_out[...] = member.astype(f32)


def place_of(order, mask):
    pos = 0
    for k, bit in enumerate(order):
        pos = pos + (lax.shift_right_logical(mask, bit.bit_length() - 1) & 1) * (1 << k)
    return pos


def list_kernel(order, scal, sizes, rows, targets, members, scores_out, loss_out, ds_out, mine_out):
    groups = 1 << len(order)
    docs = ds_out.shape[1]
    wide = docs + LANES
    queries = targets.shape[0]
    half = rows.shape[0] // groups
    lane = iota((8, LANES), 1)
    blank = jnp.zeros((8, wide - LANES), f32)

    def one_group(g, found):
        start, placed = found
        at = pl.multiple_of(place_of(order, g ^ scal[1]) * half, half)
        parts = rows[pl.ds(at, ROWS), D:].astype(f32)
        score = (parts[0:1] + parts[1:2]) + parts[2:3]
        kept = jnp.where(lane < sizes[g], score, 0.0)
        kept = pltpu.roll(jnp.concatenate([kept, blank], axis=1), start, 1)
        return start + sizes[g], placed + kept

    _, placed = lax.fori_loop(
        0,
        groups,
        one_group,
        (jnp.int32(0), jnp.zeros((8, wide), f32)),
        unroll=groups <= 8,
    )
    values = placed[0:1, :docs]
    scores_out[...] = values.reshape(scores_out.shape)
    member = members[...] > 0.0
    target = targets[...]
    peak = jnp.max(jnp.where(member, values, MASKED), axis=1, keepdims=True)
    raised = jnp.where(member, jnp.exp(jnp.where(member, values - peak, 0.0)), 0.0)
    log_total = peak + jnp.log(jnp.sum(raised, axis=1, keepdims=True))
    picked = jnp.sum(target * values, axis=1, keepdims=True)
    loss_out[...] = jnp.sum(log_total - picked, axis=0, keepdims=True) / queries
    chance = jnp.where(member, jnp.exp(jnp.where(member, values - log_total, 0.0)), 0.0)
    ds = jnp.sum(chance - target, axis=0, keepdims=True) / queries
    ds_out[...] = ds
    ds = jnp.broadcast_to(jnp.concatenate([ds, jnp.zeros((1, LANES), f32)], axis=1), (8, wide))
    start = first_doc(scal, sizes)
    back = pltpu.roll(ds, lax.rem(wide - start, wide), 1)[:, :LANES]
    mine_out[...] = jnp.where(lane < sizes[scal[1]], back, 0.0)


def context_kernel(
    scal, part_a, part_b, h2, dh3, c32, g_ff, wout, wo_own,
    dh2_out, half_out, dc_out, own_out, inner_out, ff_out, both_s,
):
    n2, r2 = rms_parts(h2[...])
    dy3 = part_a[...].astype(f32) + part_b[...].astype(f32)
    ff_out[...] = dy3 * n2
    dh2 = (dh3[...].astype(f32) + rms_back(dy3 * row_of(g_ff), n2, r2)).astype(bf16)
    dh2_out[...] = dh2
    own_half(scal, jnp.concatenate([dh3[...], dh2], axis=1), both_s, half_out)
    dc = nt(dh2, wout[...]).astype(bf16)
    dc_out[...] = dc
    own_out[...] = nt(dh2, wo_own[...]).astype(bf16)
    hot = (head_of((D, LANES), 0) == iota((D, LANES), 1)).astype(bf16)
    high, low = split2(dc.astype(f32) * c32[...])
    inner_out[...] = nn(high, hot) + nn(low, hot)


def columns(one, two):
    tall = BLOCK * ROWS
    half = LANES // 2
    both = jnp.where(iota((BLOCK, LANES), 1) < half, one, pltpu.roll(two, half, 1))
    parts = jnp.concatenate(split3(both), axis=0)
    r, c = iota((tall, 3 * BLOCK), 0), iota((tall, 3 * BLOCK), 1)
    wide = nn((r // ROWS == c % BLOCK).astype(bf16), parts)
    lane, head = iota((tall, LANES), 1), iota((tall, LANES), 0) % ROWS
    return tuple(
        jnp.sum(jnp.where(lane == head + k * half, wide, 0.0), axis=1, keepdims=True)
        for k in range(2)
    )


def back_kernel(first, last, scal, sizes, enc, p, scale, inner, dc, wv, *refs):
    dap_out, vd_out = refs[-2:]
    tokens = enc.shape[1]
    tall = BLOCK * ROWS
    rounds = jnp.clip(rounds_of(scal, sizes), first, last)

    def one_block(step):
        block = pl.ds(pl.multiple_of(step * BLOCK, BLOCK), BLOCK)
        rows = enc[block].reshape(BLOCK * tokens, D)
        pick = (iota((tall, BLOCK), 0) // ROWS == iota((tall, BLOCK), 1)).astype(bf16)
        own = (iota((tall, D), 0) % ROWS) == head_of((tall, D), 1)
        grad = jnp.where(own, nn(pick, dc[block]), 0.0).astype(bf16)
        vd = nn(grad, wv[...]).astype(bf16)
        vd_out[block] = vd.reshape(BLOCK, ROWS, D)
        grad_probs = []
        for k in range(BLOCK // 2):
            pair = nt(
                vd[2 * ROWS * k : 2 * ROWS * (k + 1)],
                rows[2 * tokens * k : 2 * tokens * (k + 1)],
            )
            grad_probs += [pair[:ROWS, :tokens], pair[ROWS:, tokens:]]
        grad_probs = jnp.concatenate(grad_probs, axis=0)
        scale_col, inner_col = columns(scale[block], inner[block])
        prob = p[block].reshape(tall, tokens) * scale_col
        da = (prob * (grad_probs - inner_col)).astype(bf16)
        dap_out[block, :ROWS] = da.reshape(BLOCK, ROWS, tokens)
        dap_out[block, ROWS:] = prob.astype(bf16).reshape(BLOCK, ROWS, tokens)

    @pl.loop(first, rounds)
    def _(i):
        for j in range(SPAN // BLOCK):
            one_block(i * (SPAN // BLOCK) + j)

    @pl.loop(rounds, last)
    def _(i):
        span = pl.ds(pl.multiple_of(i * SPAN, SPAN), SPAN)
        dap_out[span] = jnp.zeros((SPAN, 2 * ROWS, tokens), bf16)
        vd_out[span] = jnp.zeros((SPAN, ROWS, D), bf16)


def key_sum_kernel(scal, sizes, ds, enc, dap, dh2, n3, ff, sums_out):
    tokens = enc.shape[1]
    tall = BLOCK * ROWS
    slots = dh2.shape[0]
    row = ds[...][:, :slots] * (1.0 / PARTS)
    at = iota((ROWS, D), 0)
    row = row[0:1]
    out = jnp.where(at == HEADS, jnp.sum(nn(stack3(row), dh2[...]), axis=0, keepdims=True), 0.0)
    out = jnp.where(at == HEADS + 1, row_dot(row, n3[...]), out)
    sums_out[...] = jnp.where(at == HEADS + 2, row_dot(row, ff[...]), out)

    def one_block(step):
        block = pl.ds(pl.multiple_of(step * BLOCK, BLOCK), BLOCK)
        own_slot = iota((tall, LANES), 1) == step * BLOCK + iota((tall, LANES), 0) // ROWS
        ds_col = jnp.sum(jnp.where(own_slot, ds[0:1], 0.0), axis=1, keepdims=True)
        scaled = (dap[block, :ROWS].reshape(tall, tokens).astype(f32) * ds_col).astype(bf16)
        flat = jnp.concatenate(
            [scaled[ROWS * b : ROWS * (b + 1)] for b in range(BLOCK)], axis=1
        )
        return nn(flat, enc[block].reshape(BLOCK * tokens, D))

    @pl.loop(0, rounds_of(scal, sizes))
    def _(i):
        per_round = SPAN // BLOCK
        total = one_block(i * per_round)
        for j in range(1, per_round):
            total = total + one_block(i * per_round + j)
        sums_out[...] += total


def enc_grad_kernel(first, last, ds, qa, qb, dap, vd, *refs):
    grad_out, held, sems = refs[-3:]
    qk = qa[...] + qb[...]
    lane = iota((1, LANES), 1)
    copies = []
    begin = first
    while begin < last:
        size = 4
        for b in range(begin, begin + size):
            scale = jnp.sum(jnp.where(lane == b, ds[0:1], 0.0), axis=1, keepdims=True)
            right = jnp.concatenate([qk, vd[b].astype(f32)], axis=0) * scale
            held[b - first] = tn(dap[b], right.astype(bf16)).astype(bf16)
        copies.append(
            pltpu.make_async_copy(
                held.at[pl.ds(begin - first, size)],
                grad_out.at[pl.ds(begin, size)],
                sems.at[len(copies)],
            )
        )
        copies[-1].start()
        begin += size
    for copy in copies:
        copy.wait()


def share_kernel(scal, summed, scale, keep_out, send_out):
    core = scal[0] & 1
    lane = iota(scale.shape, 1)
    for out, bit in ((send_out, 1 - core), (keep_out, core)):
        for y in range(out.shape[0]):
            for k in range(out.shape[1]):
                head = (2 * y + bit) * out.shape[1] + k
                col = jnp.sum(jnp.where(lane == head, scale[...], 0.0), axis=1, keepdims=True)
                out[y, k] = (summed[head].astype(f32) * col).astype(bf16)


def away_kernel(scal, keep, got, out):
    part = 1 - (lax.shift_right_logical(scal[0], 1) & 1)
    for h in range(out.shape[0]):
        out[h] = (keep[part, h].astype(f32) + got[part, h].astype(f32)).astype(bf16)


def value_kernel(scal, keep, got, other, dc, ds, grad_out):
    slots = keep.shape[2]
    part = lax.shift_right_logical(scal[0], 1) & 1
    own_slot = iota((slots, LANES), 0) == iota((slots, LANES), 1)
    ds_col = jnp.sum(jnp.where(own_slot, ds[0:1], 0.0), axis=1, keepdims=True)
    grad = (dc[...].astype(f32) * ds_col).astype(bf16)
    for h in range(keep.shape[1]):
        pair = (keep[part, h].astype(f32) + got[part, h].astype(f32)).astype(bf16)
        summed = (pair.astype(f32) + other[h].astype(f32)).astype(bf16)
        out = tn(grad[:, h * HEAD_DIM : (h + 1) * HEAD_DIM], summed)
        grad_out[h * HEAD_DIM : (h + 1) * HEAD_DIM] = out.astype(bf16)


def document_picks(order, tile, scal, sizes, held, first):
    groups = 1 << len(order)
    half = held // groups
    core = scal[0] & 1
    doc = first + iota((tile, 1), 0)

    def one_group(g, found):
        start, at, upper = found
        pos = place_of(order, g ^ scal[1])
        slot = doc - start
        inside = (slot >= 0) & (slot < sizes[g])
        later = (slot >= half).astype(i32)
        at = jnp.where(inside, pos * half + slot - half * later, at)
        return start + sizes[g], at, jnp.where(inside, later, upper)

    zero = jnp.zeros((tile, 1), i32)
    _, at, upper = lax.fori_loop(
        0, groups, one_group, (jnp.int32(0), zero, zero), unroll=groups <= 8
    )
    hit = iota((tile, held), 1) == at
    return (hit & (upper == core)).astype(bf16), (hit & (upper != core)).astype(bf16)


def in_order(picks, own, other, width):
    mine, theirs = picks
    return (nn(mine, own[:, :width]) + nn(theirs, other[:, :width])).astype(bf16)


def picks_of(order, tile, scal, sizes, held, first, ready):
    if ready:
        return tuple(pick[...] for pick in ready)
    return document_picks(order, tile, scal, sizes, held, first)


def ds_column(ds, first, tile):
    eye = iota((tile, tile), 0) == iota((tile, tile), 1)
    return jnp.sum(jnp.where(eye, ds[0:1, pl.ds(first, tile)], 0.0), axis=1, keepdims=True)


def over_tiles(docs, tile, one_tile):
    one_tile(0, True)
    if docs > tile:

        @pl.loop(1, docs // tile)
        def _(t):
            one_tile(pl.multiple_of(t * tile, tile), False)


def put(out, value, new):
    if new:
        out[...] = value
    else:
        out[...] += value


def weights_before_kernel(
    order, tile, scal, sizes, c_own, c_other, h1, g_ff, wout, win, *refs
):
    ready, (y3_out, u_out, slope_out, c_out) = refs[:-4], refs[-4:]

    def one_tile(first, new):
        here = pl.ds(first, tile)
        picks = picks_of(order, tile, scal, sizes, c_own.shape[0], first, ready)
        c = in_order(picks, c_own, c_other, D)
        h2 = h1[...] + nn(c, wout[...])
        n2, _ = rms_parts(h2)
        y3 = (n2 * row_of(g_ff)).astype(bf16)
        y3_out[here] = y3
        z = nn(y3, win[...])
        u_out[here] = (z * phi(z)).astype(bf16)
        slope_out[here] = gelu_slope(z)
        width = c_out.shape[1]
        pick = (iota((D, width), 0) == scal[0] * width + iota((D, width), 1)).astype(bf16)
        c_out[here] = nn(c, pick).astype(bf16)

    over_tiles(y3_out.shape[0], tile, one_tile)


def grads_kernel(order, tile, scal, sizes, slope, both_own, both_other, ds, wdown, *refs):
    ready, (dz_out, both_out) = refs[:-2], refs[-2:]

    def one_tile(first, new):
        here = pl.ds(first, tile)
        picks = picks_of(order, tile, scal, sizes, both_own.shape[0], first, ready)
        both = in_order(picks, both_own, both_other, 2 * D).astype(f32)
        both = (both * ds_column(ds, first, tile)).astype(bf16)
        both_out[here] = both
        dz_out[here] = (nt(both[:, :D], wdown[...]) * slope[here]).astype(bf16)

    over_tiles(ds.shape[1], tile, one_tile)


def outer_kernel(
    tile, y3, dz, u, c, both, left1, right1, left2, right2,
    win_out, wdown_out, wout_out, key_out, query_out, wos_out, wvs_out,
    win_s, wdown_s, wout_s, key_s, query_s, wos_s, wvs_s, sems,
):
    copies = []

    def leave(held, out):
        copies.append(pltpu.make_async_copy(held, out, sems.at[len(copies)]))
        copies[-1].start()

    docs = y3.shape[0]

    def total(held, left, right):
        held[...] = tn(left[:tile], right[:tile])
        if docs > tile:

            @pl.loop(1, docs // tile)
            def _(t):
                here = pl.ds(pl.multiple_of(t * tile, tile), tile)
                held[...] += tn(left[here], right[here])

    def by_parts(held, out, left, right):
        for k in range(held.shape[0] // COLUMNS):
            part = pl.ds(k * COLUMNS, COLUMNS)
            total(held.at[part], left.at[:, part], right)
            leave(held.at[part], out.at[part])

    key_s[...] = tn(left1[: 2 * ROWS], right1[: 2 * ROWS])
    leave(key_s, key_out)
    query_s[...] = tn(left1[2 * ROWS :], right1[2 * ROWS :])
    leave(query_s, query_out)
    wos_s[...] = tn(left2[:ROWS], right2[:ROWS])
    leave(wos_s, wos_out)
    wvs_s[...] = tn(left2[ROWS:], right2[ROWS:])
    leave(wvs_s, wvs_out)
    total(wout_s, c, both.at[:, D:])
    leave(wout_s, wout_out)
    by_parts(win_s, win_out, y3, dz)
    by_parts(wdown_s, wdown_out, u, both.at[:, :D])
    for copy in copies:
        copy.wait()


def key_kernel(scal, sum_a, sum_b, h1, g_cross, wk, wq, part_out, left_out, right_out):
    y2, qm = query_parts(scal, h1, g_cross, wq)
    g = sum_a[...] + sum_b[...]
    g = jnp.where(iota((ROWS, D), 0) < HEADS, g, 0.0)
    high, low = split2(g)
    both = jnp.concatenate([high, low], axis=0)
    dq = nt(both, wk[...])
    dq = dq[:ROWS] + dq[ROWS:]
    width = dq.shape[1]
    first = scal[0] * (width // HEAD_DIM)
    own = iota((ROWS, width), 0) == first + head_of((ROWS, width), 1)
    dq = jnp.sum(jnp.where(own, dq, 0.0), axis=0, keepdims=True)
    dq_parts = stack3(dq)
    left_out[...] = jnp.concatenate([qm, qm, dq_parts], axis=0)
    right_out[...] = jnp.concatenate([both, repeat3(y2[0:1])], axis=0)
    part = jnp.sum(nn(dq_parts, wq[...]), axis=0, keepdims=True)
    part_out[...] = jnp.broadcast_to(part, (8, D))


def hidden_kernel(
    part_a, part_b, sum_a, sum_b, h1, g_cross, start, g_self, wos, wvs, g_final, row,
    dh1_out, part_out, left_out, right_out, cross_out, final_out, row_out, ff_out,
):
    y1, s1 = self_parts(start, g_self, wvs)
    dy2 = part_a[0:1] + part_b[0:1]
    sums = sum_a[...] + sum_b[...]
    n1, r1 = rms_parts(h1[...])
    cross_out[...] = (dy2 * n1).reshape(cross_out.shape)
    dh1 = sums[HEADS : HEADS + 1] + rms_back(dy2 * row_of(g_cross), n1, r1)
    dh1_out[...] = dh1
    dh1_parts = stack3(dh1)
    ds1 = jnp.sum(nt(dh1_parts, wos[...]), axis=0, keepdims=True)
    ds1_parts = stack3(ds1)
    left_out[...] = jnp.concatenate([repeat3(s1[0:1]), ds1_parts], axis=0)
    right_out[...] = jnp.concatenate([dh1_parts, repeat3(y1[0:1])], axis=0)
    part = jnp.sum(nn(ds1_parts, wvs[...]), axis=0, keepdims=True)
    part_out[...] = jnp.broadcast_to(part, (8, D))
    total = sums[HEADS + 1 : HEADS + 2] * FACTOR
    final_out[...] = (total * row_of(row)).reshape(final_out.shape)
    row_out[...] = (total * row_of(g_final)).reshape(row_out.shape)
    ff_out[...] = sums[HEADS + 2 : HEADS + 3].reshape(ff_out.shape)


def start_kernel(
    part_a, part_b, dh1, start, g_self, value_a, value_b, gain_out, start_out, value_out
):
    value_out[...] = value_a[...].astype(f32) + value_b[...].astype(f32)
    dy1 = part_a[0:1] + part_b[0:1]
    n0, r0 = rms_parts(row_of(start))
    gain_out[...] = (dy1 * n0).reshape(gain_out.shape)
    back = dh1[...] + rms_back(dy1 * row_of(g_self), n0, r0)
    start_out[...] = back.reshape(start_out.shape)


def shape(dims, dtype=f32):
    return jax.ShapeDtypeStruct(dims, dtype)


def whole_spec(memory=pltpu.VMEM):
    return pl.BlockSpec(memory_space=memory)


def name_of(kernel):
    return getattr(kernel, "func", kernel).__name__


def in_hbm(x):
    return pltpu.with_memory_space_constraint(x, pltpu.HBM)


def plain(
    kernel, outs, *args, smem=0, hbm=(), hbm_out=False, onto=None, limit=12, scratch=()
):
    spaces = [pltpu.SMEM] * smem + [pltpu.VMEM] * (len(args) - smem)
    for k in hbm:
        spaces[k] = pltpu.HBM
    out_space = pltpu.HBM if hbm_out else pltpu.VMEM
    return pl.pallas_call(
        kernel,
        out_shape=outs,
        in_specs=[whole_spec(space) for space in spaces],
        out_specs=[whole_spec(out_space) for _ in outs]
        if isinstance(outs, list)
        else whole_spec(out_space),
        scratch_shapes=list(scratch),
        input_output_aliases=onto or {},
        compiler_params=pltpu.CompilerParams(vmem_limit_bytes=limit * MIB),
        cost_estimate=pl.CostEstimate(flops=0, bytes_accessed=0, transcendentals=0),
        name=name_of(kernel),
    )(*args)


def bits_of(size):
    return [1 << b for b in range(size.bit_length() - 1)]


def far_first(size):
    return bits_of(size)[::-1]


def swap(x, axis, bit):
    size = lax.axis_size(axis)
    return lax.ppermute(x, axis, [(i, i ^ bit) for i in range(size)])


def after(x, *deps):
    return lax.optimization_barrier((x, *deps))[0]


def add(x, y):
    return (x.astype(f32) + y.astype(f32)).astype(x.dtype)


def sum_last(x, steps):
    for axis, bit in steps[:-1]:
        x = add(x, swap(x, axis, bit))
    axis, bit = steps[-1]
    return x, swap(x, axis, bit)


def per_device(
    enc_out,
    enc_len,
    group_docs,
    list_len,
    relevance,
    start_token,
    score_row,
    g_self,
    w_value_self,
    w_out_self,
    g_cross,
    w_query,
    w_key,
    w_value,
    w_out,
    g_ff,
    w_in,
    w_down,
    g_final,
):
    groups = lax.axis_size("docs")
    parts = lax.axis_size("heads")
    assert parts == PARTS
    me_g = lax.axis_index("docs")
    me_j = lax.axis_index("heads")
    slots, tokens = enc_out.shape[:2]
    docs = enc_len.shape[0]
    width = w_value.shape[1]
    own_heads = HEADS // parts
    hidden = w_in.shape[1]
    over_heads = [("heads", 1), ("heads", 2)]
    order = far_first(groups)
    over_docs = [("docs", bit) for bit in order]

    scal = jnp.stack([me_j, me_g])
    wvs_t, wq_t, wk_t, wv_t = (w.T for w in (w_value_self, w_query, w_key, w_value))

    wv_by1, wo_by1 = swap(wv_t, "heads", 1), swap(w_out, "heads", 1)

    part = plain(
        self_kernel,
        shape((8, D)),
        *map(in_hbm, (start_token, g_self, wvs_t, w_out_self)),
    )


    def load(first, last, since, *onto):
        return pl.pallas_call(
            functools.partial(load_kernel, first, last),
            out_shape=pltpu.VMEM(enc_out.shape, bf16),
            in_specs=[whole_spec(pltpu.HBM), whole_spec(pl.ANY), whole_spec(pltpu.SMEM)]
            + [whole_spec()] * len(onto),
            out_specs=whole_spec(),
            scratch_shapes=[pltpu.SemaphoreType.DMA((last - first,))],
            input_output_aliases={3: 0} if onto else {},
            compiler_params=pltpu.CompilerParams(vmem_limit_bytes=MIB),
            cost_estimate=pl.CostEstimate(flops=0, bytes_accessed=0, transcendentals=0),
            name="load_kernel",
        )(in_hbm(enc_out), since, scal, *onto)

    part = add(part, swap(part, "heads", 1))
    part_a, part_b = part, swap(part, "heads", 2)
    held = load(0, 1, part)
    part_b, held = lax.optimization_barrier((part_b, held))
    wv_by2 = swap(after(wv_t, part_b), "heads", 2)
    qk, h1 = plain(
        query_kernel,
        [shape((ROWS, D)), shape((1, D))],
        scal,
        part_a,
        part_b,
        *map(in_hbm, (start_token, g_cross, wq_t, wk_t)),
        smem=1,
    )
    qk = add(qk, swap(qk, "heads", 1))
    qk, held = lax.optimization_barrier((qk, held))
    qk_a, qk_b = qk, swap(qk, "heads", 2)
    held = load(1, 3, qk, held)
    qk_b, held, wv_by2 = lax.optimization_barrier((qk_b, held, wv_by2))
    wv_by3 = swap(wv_by2, "heads", 1)

    wo_by2 = swap(after(w_out, qk_b), "heads", 2)
    held, prob, summed, extra = plain(
        functools.partial(attend_kernel, 3),
        [
            pltpu.VMEM(enc_out.shape, bf16),
            pltpu.VMEM((slots, ROWS, tokens), f32),
            pltpu.VMEM((PANELS, slots * ROWS, LANES), f32),
            shape((slots, LANES), bf16),
        ],
        scal,
        group_docs,
        enc_len,
        qk_a,
        qk_b,
        in_hbm(enc_out),
        held,
        smem=3,
        hbm=(5,),
        onto={6: 0},
        scratch=[pltpu.VMEM((2 * ROWS, D), bf16), pltpu.SemaphoreType.DMA((slots // BLOCK,))],
        limit=16,
    )
    summed, wv_by3, wo_by2 = lax.optimization_barrier((summed, wv_by3, wo_by2))
    wv_parts = (wv_t, wv_by2, wv_by1, wv_by3)
    wo_parts = (w_out, wo_by2, wo_by1, swap(wo_by2, "heads", 1))
    pay, summed, wv_full = plain(
        project_kernel,
        [
            shape((slots, D + LANES), bf16),
            shape((HEADS, slots, D), bf16),
            shape((D, D), bf16),
        ],
        scal,
        summed,
        extra,
        *wv_parts,
        smem=1,
    )
    merged = plain(
        merge_kernel, shape(pay.shape, bf16), scal, pay, swap(pay, "heads", 1), smem=1
    )
    other = swap(merged, "heads", 2)
    wo_full = plain(arrange_kernel, shape((D, D), bf16), scal, *wo_parts, smem=1)
    tile = 384
    held_rows = groups * slots // 2
    picks_shape = [shape((tile, held_rows), bf16)] * 2 if docs == tile else []
    target, member, *picks = plain(
        functools.partial(target_kernel, order),
        [shape((list_len.shape[0], docs))] * 2 + picks_shape,
        scal,
        group_docs,
        list_len,
        relevance,
        smem=3,
    )
    other, wo_full, target, member, *picks = lax.optimization_barrier(
        (other, wo_full, target, member, *picks)
    )

    c, c32, scale, h2, z, part = plain(
        forward_kernel,
        [
            shape((slots // 2, D), bf16),
            shape((slots, D)),
            shape((slots, LANES)),
            shape((slots, D)),
            shape((slots, hidden)),
            shape((slots, D), bf16),
        ],
        scal,
        merged,
        other,
        pay,
        h1,
        wo_full,
        g_ff,
        w_in,
        w_down,
        smem=1,
        scratch=[pltpu.VMEM((slots, D), bf16)],
    )

    half = slots // 2

    def grow(x, k):
        return jnp.concatenate([x, swap(x, *over_docs[k])], axis=0)

    def tie(*xs):
        return lax.optimization_barrier(xs)

    last = len(over_docs) - 1
    near_first = over_docs[::-1]
    part = add(part, swap(part, "heads", 1))
    part_a, part_b = part, swap(part, "heads", 2)
    keep, sent = plain(
        share_kernel, [shape((2, own_heads, slots, D), bf16)] * 2, scal, summed, scale, smem=1
    )
    part_b, keep, sent = tie(part_b, keep, sent)
    c_all, n3, dh3 = plain(
        score_kernel,
        [shape((half, D + LANES), bf16), shape((slots, D)), shape((slots, D), bf16)],
        part_a,
        part_b,
        h2,
        g_final,
        score_row,
        c,
    )
    part = plain(down_kernel, shape((slots, D), bf16), dh3, z, w_down, w_in)
    part = add(part, swap(part, "heads", 1))
    part_a, part_b = part, swap(part, "heads", 2)
    c_far = swap(c_all, *over_docs[0])
    got = swap(sent, "heads", 1)
    away = plain(
        away_kernel, shape((own_heads, slots, D), bf16), scal, keep, got, smem=1
    )
    part_b, away = tie(part_b, away)
    dh2, grads, dc, dc_own, inner, ff = plain(
        context_kernel,
        [
            shape((slots, D), bf16),
            shape((half, 2 * D), bf16),
            shape((slots, D), bf16),
            shape((slots, width), bf16),
            shape((slots, LANES)),
            shape((slots, D)),
        ],
        scal,
        part_a,
        part_b,
        h2,
        dh3,
        c32,
        g_ff,
        wo_full,
        w_out,
        smem=1,
        scratch=[pltpu.VMEM((slots, 2 * D), bf16)],
    )

    c_all, c_far, dc, grads = tie(c_all, c_far, dc, grads)
    c_all = jnp.concatenate([c_all, c_far], axis=0)
    for k in range(1, last):
        c_far = swap(c_all, *over_docs[k])
        if k < last - 1:
            c_all = jnp.concatenate([c_all, c_far], axis=0)
    grads_far = swap(grads, *over_docs[0])

    outs = [
        pltpu.VMEM((slots, 2 * ROWS, tokens), bf16),
        pltpu.VMEM((slots, ROWS, D), bf16),
    ]
    rounds = slots // SPAN
    inputs = (scal, group_docs, held, prob, scale, inner, dc, wv_full)

    def back(first, last, *onto):
        return plain(
            functools.partial(back_kernel, first, last),
            outs,
            *inputs,
            *onto,
            smem=2,
            onto={8: 0, 9: 1} if onto else None,
            limit=16,
        )

    dap, vd = back(0, 1)
    dap, away = tie(dap, away)
    other = swap(away, "heads", 2)
    dap, c_far = tie(dap, c_far)
    c_all = jnp.concatenate([c_all, c_far], axis=0)
    c_far = swap(c_all, *over_docs[last])
    dap, vd = back(1, rounds, dap, vd)
    dap, c_far, other, grads_far = tie(dap, c_far, other, grads_far)
    grads = jnp.concatenate([grads, grads_far], axis=0)
    for m in range(1, last):
        grads_far = swap(grads, *over_docs[m])
        if m < last - 1:
            grads = jnp.concatenate([grads, grads_far], axis=0)
    c_all = jnp.concatenate([c_all, c_far], axis=0)
    all_scores, loss, ds_docs, ds_mine = plain(
        functools.partial(list_kernel, order),
        [shape((docs,)), shape((1, 1)), shape((1, docs)), shape((8, LANES))],
        scal,
        group_docs,
        c_all,
        target,
        member,
        smem=2,
    )
    sums = plain(
        key_sum_kernel,
        shape((ROWS, D)),
        scal,
        group_docs,
        ds_mine,
        held,
        dap,
        dh2,
        n3,
        ff,
        smem=2,
    )

    def enc_grads(first, last, grads=None):
        outs = pltpu.HBM(enc_out.shape, bf16)
        args = (ds_mine, qk_a, qk_b, dap, vd)
        return plain(
            functools.partial(enc_grad_kernel, first, last),
            outs,
            *args,
            *([] if grads is None else [grads]),
            hbm=() if grads is None else (len(args),),
            hbm_out=True,
            onto={} if grads is None else {len(args): 0},
            scratch=[pltpu.VMEM((last - first, tokens, D), bf16), pltpu.SemaphoreType.DMA((8,))],
            limit=16,
        )

    sums, dc_own = tie(sums, dc_own)
    value_part = plain(
        value_kernel,
        shape((width, D), bf16),
        scal,
        keep,
        got,
        other,
        dc_own,
        ds_mine,
        smem=1,
    )
    value_far = swap(value_part, *near_first[0])
    c_far = swap(c_all, "heads", 1)
    sums = add(sums, swap(sums, "heads", 1))
    steps = near_first[:0:-1] + over_heads[1:] + near_first[:1]
    sums, grads_far = tie(sums, grads_far)
    grads = jnp.concatenate([grads, grads_far], axis=0)
    grads_far = swap(grads, *over_docs[last])
    enc_grad = None
    third = slots // 3
    sum_a = sums
    for k, step in enumerate(steps):
        ds_mine, sum_a = tie(ds_mine, sum_a)
        sum_b = swap(sum_a, *step)
        if k < 3:
            enc_grad = enc_grads(k * third, (k + 1) * third, enc_grad)
            sum_b, enc_grad = tie(sum_b, enc_grad)
        if k == 1:
            sum_b, value_far, c_far = tie(sum_b, value_far, c_far)
            for step in near_first[1:-1]:
                value_part = add(value_part, value_far)
                value_far = swap(value_part, *step)
        if k < len(steps) - 1:
            sum_a = sum_a + sum_b
    y3, u, slope, c_own = plain(
        functools.partial(weights_before_kernel, order, tile),
        [
            shape((docs, D), bf16),
            shape((docs, hidden), bf16),
            shape((docs, hidden)),
            shape((docs, width), bf16),
        ],
        scal,
        group_docs,
        c_all,
        c_far,
        h1,
        g_ff,
        wo_full,
        w_in,
        *picks,
        smem=2,
        limit=60 if docs > 384 else 16,
    )
    sum_b, grads_far, value_far, y3, u, slope, c_own = tie(
        sum_b, grads_far, value_far, y3, u, slope, c_own
    )
    value_part = add(value_part, value_far)
    value_far = swap(value_part, *near_first[-1])
    grads = jnp.concatenate([grads, grads_far], axis=0)
    grads_far = swap(grads, "heads", 1)

    part, left1, right1 = plain(
        key_kernel,
        [shape((8, D)), shape((3 * ROWS, width), bf16), shape((3 * ROWS, D), bf16)],
        scal,
        sum_a,
        sum_b,
        h1,
        g_cross,
        wk_t,
        wq_t,
        smem=1,
    )
    part = add(part, swap(part, "heads", 1))
    part, grads_far = tie(part, grads_far)
    part_a, part_b = part, swap(part, "heads", 2)
    dz, both = plain(
        functools.partial(grads_kernel, order, tile),
        [shape((docs, hidden), bf16), shape((docs, 2 * D), bf16)],
        scal,
        group_docs,
        slope,
        grads,
        grads_far,
        ds_docs,
        w_down,
        *picks,
        smem=2,
        limit=60 if docs > 384 else 16,
    )
    part_b, dz, both = tie(part_b, dz, both)
    dh1, part, left2, right2, cross, final_gain, row_grad, ff_gain = plain(
        hidden_kernel,
        [
            shape((1, D)),
            shape((8, D)),
            shape((2 * ROWS, width), bf16),
            shape((2 * ROWS, D), bf16),
        ]
        + [shape((D,))] * 4,
        part_a,
        part_b,
        sum_a,
        sum_b,
        h1,
        g_cross,
        start_token,
        g_self,
        w_out_self,
        wvs_t,
        g_final,
        score_row,
    )
    part_a, part_b = sum_last(part, over_heads)
    dims = [(D, hidden), (hidden, D), (width, D)] + [(width, D)] * 4
    w_in_grad, w_down_grad, w_out_grad, key_grad, query_grad, wos_grad, wvs_grad = plain(
        functools.partial(outer_kernel, tile),
        [pltpu.HBM(dim, f32) for dim in dims],
        y3,
        dz,
        u,
        c_own,
        both,
        left1,
        right1,
        left2,
        right2,
        hbm_out=True,
        scratch=[pltpu.VMEM(dim, f32) for dim in dims] + [pltpu.SemaphoreType.DMA((16,))],
        limit=60 if docs > 384 else 24,
    )
    part_b, w_down_grad, value_far = tie(part_b, w_down_grad, value_far)
    self_gain, start_grad, value_grad = plain(
        start_kernel,
        [shape((D,)), shape((D,)), shape((width, D))],
        part_a,
        part_b,
        dh1,
        start_token,
        g_self,
        value_part,
        value_far,
    )

    return (
        all_scores,
        loss.reshape(()),
        enc_grad,
        start_grad,
        row_grad,
        self_gain,
        wvs_grad.T,
        wos_grad,
        cross,
        query_grad.T,
        key_grad.T,
        value_grad.T,
        w_out_grad,
        ff_gain,
        w_in_grad,
        w_down_grad,
        final_gain,
    )


def solution(mesh):
    placed = (
        P("docs", "heads", None),
        P(),
        P(),
        P(),
        P(),
        P(),
        P(),
        P(),
        P(None, "heads"),
        P("heads", None),
        P(),
        P(None, "heads"),
        P(None, "heads"),
        P(None, "heads"),
        P("heads", None),
        P(),
        P(None, "heads"),
        P("heads", None),
        P(),
    )
    return jax.shard_map(
        per_device,
        mesh=mesh,
        in_specs=placed,
        out_specs=(
            P(),
            P(),
            P("docs", "heads", None),
            P(),
            P(),
            P(),
            P(None, "heads"),
            P("heads", None),
            P(),
            P(None, "heads"),
            P(None, "heads"),
            P(None, "heads"),
            P("heads", None),
            P(),
            P(None, "heads"),
            P("heads", None),
            P(),
        ),
        check_vma=False,
    )
```

```python
import functools

import jax
import jax.numpy as jnp
from jax import lax
from jax.experimental import pallas as pl
from jax.experimental.pallas import tpu as pltpu
from jax.sharding import PartitionSpec as P

D = 768
HEADS = 12
HEAD_DIM = 64
ROWS = 16
BLOCK = 16
SPAN = 2 * BLOCK
LANES = 128
PANELS = D // LANES
COLUMNS = 384
PARTS = 4

EPSILON = 1e-06
MASKED = -1e30
FACTOR = D ** (-0.5)
ROOT_HALF = 0.5**0.5
DENSITY = 0.3989422804014327
f32, bf16, i32 = jnp.float32, jnp.bfloat16, jnp.int32
EXACT = lax.Precision.HIGHEST
MIB = 1 << 20


def nn(a, b, precision=None):
    return lax.dot_general(
        a, b, (((1,), (0,)), ((), ())), precision=precision, preferred_element_type=f32
    )


def nt(a, b, precision=None):
    return lax.dot_general(
        a, b, (((1,), (1,)), ((), ())), precision=precision, preferred_element_type=f32
    )


def tn(a, b, precision=None):
    return lax.dot_general(
        a, b, (((0,), (0,)), ((), ())), precision=precision, preferred_element_type=f32
    )


def iota(shape, dim):
    return lax.broadcasted_iota(i32, shape, dim)


def split2(x):
    high = x.astype(bf16)
    return high, (x - high.astype(f32)).astype(bf16)


def split3(x):
    high = x.astype(bf16)
    rest = x - high.astype(f32)
    mid = rest.astype(bf16)
    return high, mid, (rest - mid.astype(f32)).astype(bf16)


def stack3(row, height=ROWS):
    at = iota((height, row.shape[1]), 0)
    parts = split3(row)
    zero = jnp.zeros((), f32)
    out = jnp.where(at == 0, parts[0].astype(f32), zero)
    out = jnp.where(at == 1, parts[1].astype(f32), out)
    return jnp.where(at == 2, parts[2].astype(f32), out).astype(bf16)


def repeat3(row, height=ROWS):
    at = iota((height, row.shape[1]), 0)
    return jnp.where(at < 3, row.astype(f32), 0.0).astype(bf16)


def rms_parts(rows):
    scale = lax.rsqrt(jnp.mean(rows * rows, axis=-1, keepdims=True) + EPSILON)
    return rows * scale, scale


def rms_back(grad_normed, normed, scale):
    inner = jnp.mean(grad_normed * normed, axis=-1, keepdims=True)
    return scale * (grad_normed - normed * inner)


def phi(z):
    return 0.5 * (1.0 + lax.erf(z * ROOT_HALF))


def gelu_slope(z):
    return phi(z) + z * (DENSITY * jnp.exp(-0.5 * z * z))


def head_of(shape, dim):
    return iota(shape, dim) // HEAD_DIM


def spread(small):
    high, mid, low = (part.astype(f32) for part in split3(small))
    packed = high + pltpu.roll(mid, ROWS, 1) + pltpu.roll(low, 2 * ROWS, 1)
    lane = iota((LANES, D), 0)
    hot = (lane < 3 * ROWS) & (lane % ROWS == head_of((LANES, D), 1))
    return nn(packed.astype(bf16), hot.astype(bf16))


def row_dot(row, right):
    high, low = split2(right)
    parts = stack3(row)
    return jnp.sum(nn(parts, high) + nn(parts, low), axis=0, keepdims=True)


def row_of(ref):
    return ref[...].astype(f32).reshape(1, D)


def gained(n, gain):
    return jnp.broadcast_to(n * row_of(gain), (ROWS, D)).astype(bf16)


def self_parts(start, g_self, wvs):
    x0 = row_of(start)
    n0, _ = rms_parts(x0)
    y1 = gained(n0, g_self)
    return y1, nt(y1, wvs[...]).astype(bf16)


def query_parts(scal, h1, g_cross, wq):
    n1, _ = rms_parts(h1[...])
    y2 = gained(n1, g_cross)
    q = nt(y2, wq[...]).astype(bf16)
    width = q.shape[1]
    first = scal[0] * (width // HEAD_DIM)
    own = iota((ROWS, width), 0) == first + head_of((ROWS, width), 1)
    return y2, jnp.where(own, q.astype(f32), 0.0).astype(bf16)


def self_kernel(start, g_self, wvs, wos, part_out):
    _, s1 = self_parts(start, g_self, wvs)
    part_out[...] = nn(s1, wos[...])[:8]


def load_kernel(first, last, enc, since, scal, *refs):
    held, sems = refs[-2:]
    loads = []
    for k in range(first, last):
        part = pl.ds(k * BLOCK, BLOCK)
        loads.append(pltpu.make_async_copy(enc.at[part], held.at[part], sems.at[k - first]))
        loads[-1].start()
    for load in loads:
        load.wait()


def query_kernel(scal, part_a, part_b, start, g_cross, wq, wk, qk_out, h1_out):
    h1_out[...] = row_of(start) + (part_a[0:1] + part_b[0:1])
    _, qm = query_parts(scal, h1_out, g_cross, wq)
    qk_out[...] = nn(qm, wk[...])


def load_kernel(first, last, enc, since, scal, *refs):
    held, sems = refs[-2:]
    loads = []
    for k in range(first, last):
        part = pl.ds(k * BLOCK, BLOCK)
        loads.append(pltpu.make_async_copy(enc.at[part], held.at[part], sems.at[k - first]))
        loads[-1].start()
    for load in loads:
        load.wait()


def query_kernel(scal, part_a, part_b, start, g_cross, wq, wk, qk_out, h1_out):
    h1_out[...] = row_of(start) + (part_a[0:1] + part_b[0:1])
    _, qm = query_parts(scal, h1_out, g_cross, wq)
    qk_out[...] = nn(qm, wk[...])


def select_docs(height, width):
    r, c = iota((height, width), 0), iota((height, width), 1)
    return (((r // BLOCK) == (c % ROWS)) & ((r % BLOCK) == (c // ROWS))).astype(bf16)


def first_doc(scal, sizes):
    groups = sizes.shape[0]

    def body(g, total):
        return total + jnp.where(g < scal[1], sizes[g], 0)

    return lax.fori_loop(0, groups, body, jnp.int32(0), unroll=groups <= 8)


def rounds_of(scal, sizes):
    return (sizes[scal[1]] + SPAN - 1) // SPAN


def attend_kernel(
    loaded, scal, sizes, lengths, qa, qb, enc, _, held, p_out, e_out, ext_out, qk_s, sems
):
    tokens = enc.shape[1]
    blocks = enc.shape[0] // BLOCK
    rounds = rounds_of(scal, sizes)
    per_round = SPAN // BLOCK
    count = sizes[scal[1]]
    begin = first_doc(scal, sizes)
    tall = BLOCK * ROWS

    def piece(k):
        part = pl.ds(k * BLOCK, BLOCK)
        return pltpu.make_async_copy(enc.at[part], held.at[part], sems.at[k])

    for k in range(loaded, blocks):
        pl.when(k // per_round < rounds)(lambda k=k: piece(k).start())
    high, low = split2(qa[...] + qb[...])
    qk_s[0:ROWS] = high
    qk_s[ROWS : 2 * ROWS] = low

    def one_block(step):
        block = pl.ds(pl.multiple_of(step * BLOCK, BLOCK), BLOCK)
        flat = pl.ds(pl.multiple_of(step * tall, tall), tall)
        rows = held[block].reshape(BLOCK * tokens, D)
        both = nt(qk_s[...], rows)
        logits = both[:ROWS] + both[ROWS:]
        logits = jnp.concatenate(
            [logits[:, b * tokens : (b + 1) * tokens] for b in range(BLOCK)], axis=0
        )
        shown = []
        for b in range(BLOCK):
            slot = step * BLOCK + b
            doc = jnp.minimum(begin + slot, lengths.shape[0] - 1)
            length = jnp.where(slot < count, lengths[doc] - scal[0] * tokens, 0)
            shown.append(jnp.broadcast_to(length, (ROWS, tokens)))
        seen = iota((tall, tokens), 1) < jnp.concatenate(shown, axis=0)
        logits = jnp.where(seen, logits, MASKED)
        peak = jnp.max(logits, axis=1, keepdims=True)
        raised = jnp.where(seen, jnp.exp(logits - peak), 0.0)
        total = jnp.sum(raised, axis=1, keepdims=True)
        p_out[block] = raised.reshape(BLOCK, ROWS, tokens)
        low = raised.astype(bf16)
        summed = jnp.concatenate(
            [
                nn(low[ROWS * b : ROWS * (b + 1)], rows[tokens * b : tokens * (b + 1)])
                for b in range(BLOCK)
            ],
            axis=0,
        )
        for k in range(PANELS):
            e_out[k, flat] = summed[:, k * LANES : (k + 1) * LANES]
        gather = (iota((BLOCK, tall), 0) == iota((BLOCK, tall), 1) // ROWS).astype(bf16)
        parts = split3(peak) + split3(total)
        at = iota((tall, LANES), 1)
        extra = jnp.zeros((tall, LANES), f32)
        for k, part in enumerate(parts):
            extra = jnp.where(at // ROWS == k, part.astype(f32), extra)
        extra = jnp.where(at % ROWS == iota((tall, LANES), 0) % ROWS, extra, 0.0)
        ext_out[block] = nn(gather, extra.astype(bf16)).astype(bf16)

    @pl.loop(0, rounds)
    def _(i):
        for j in range(per_round):
            k = i * per_round + j
            pl.when(k >= loaded)(lambda k=k: piece(k).wait())
        for j in range(per_round):
            one_block(i * per_round + j)

    @pl.loop(rounds, enc.shape[0] // SPAN)
    def _(i):
        span = pl.ds(pl.multiple_of(i * SPAN, SPAN), SPAN)
        flat = pl.ds(pl.multiple_of(i * SPAN * ROWS, SPAN * ROWS), SPAN * ROWS)
        p_out[span] = jnp.zeros((SPAN, ROWS, tokens), f32)
        for k in range(PANELS):
            e_out[k, flat] = jnp.zeros((SPAN * ROWS, LANES), f32)
        ext_out[span] = jnp.where(iota((SPAN, LANES), 1) < ROWS, MASKED, 0.0).astype(bf16)


def sums_of_head(summed, head, slots):
    rows = pl.ds(head, slots, stride=ROWS)
    return jnp.concatenate([summed[k, rows, :] for k in range(PANELS)], axis=1)


def place_parts(scal, full, own, by2, by1, by3):
    height = own.shape[0]
    for mask, piece in ((0, own), (2, by2), (1, by1), (3, by3)):
        at = pl.multiple_of((scal[0] ^ mask) * height, height)
        full[pl.ds(at, height)] = piece[...]


def arrange_kernel(scal, own, by2, by1, by3, full_out):
    place_parts(scal, full_out, own, by2, by1, by3)


def project_kernel(scal, summed, extra, own, by2, by1, by3, pay_out, heads_out, wv):
    place_parts(scal, wv, own, by2, by1, by3)
    slots = pay_out.shape[0]
    even = iota((slots, LANES), 1) < HEAD_DIM
    for k in range(HEADS // 2):
        pair = wv[k * LANES : (k + 1) * LANES]
        for head in (2 * k, 2 * k + 1):
            heads_out[head] = sums_of_head(summed, head, slots).astype(bf16)
        one, two = (nt(heads_out[2 * k + odd], pair) for odd in range(2))
        pay_out[:, k * LANES : (k + 1) * LANES] = jnp.where(even, one, two).astype(bf16)
    pay_out[:, D:] = extra[...]


def decode(pay):
    extra = pay[:, D:].astype(f32)

    def lane(k):
        return pltpu.roll(extra, LANES - k * ROWS, 1) if k else extra

    first = iota(extra.shape, 1) < ROWS
    peak = jnp.where(first, (lane(0) + lane(1)) + lane(2), 0.0)
    total = jnp.where(first, (lane(3) + lane(4)) + lane(5), 0.0)
    return peak, total


def merge(one, two, last=False):
    peak1, total1 = decode(one)
    peak2, total2 = decode(two)
    peak = jnp.maximum(peak1, peak2)
    up1, up2 = jnp.exp(peak1 - peak), jnp.exp(peak2 - peak)
    total = up1 * total1 + up2 * total2
    first = iota(peak.shape, 1) < ROWS
    if last:
        some = first & (total > 0.0)
        total = jnp.where(some, 1.0 / jnp.where(some, total, 1.0), 0.0)
        up1, up2 = up1 * total, up2 * total
    up1, up2 = jnp.where(first, up1, 0.0), jnp.where(first, up2, 0.0)
    context = spread(up1) * one[:, :D].astype(f32) + spread(up2) * two[:, :D].astype(f32)
    return peak, total, context


def ordered(bit, own, other):
    swap = jnp.broadcast_to(bit, own.shape) == 1
    return jnp.where(swap, other, own), jnp.where(swap, own, other)


def merge_kernel(scal, own, other, pay_out):
    one, two = ordered(scal[0] & 1, own[...].astype(f32), other[...].astype(f32))
    peak, total, context = merge(one, two)
    pay_out[:, :D] = context.astype(bf16)
    extra = jnp.zeros(peak.shape, f32)
    at = iota(peak.shape, 1) // ROWS
    for k, part in enumerate(split3(peak) + split3(total)):
        part = part.astype(f32)
        extra = jnp.where(at == k, pltpu.roll(part, k * ROWS, 1) if k else part, extra)
    pay_out[:, D:] = extra.astype(bf16)


def own_half(scal, rows, held, out):
    half = out.shape[0]
    held[...] = rows
    out[...] = held[pl.ds(pl.multiple_of((scal[0] & 1) * half, half), half)]


def forward_kernel(
    scal, own, other, first, h1, wo, g_ff, win, wdown,
    c_out, c32_out, scale_out, h2_out, z_out, part_out, c_s,
):
    bit = lax.shift_right_logical(scal[0], 1) & 1
    one, two = ordered(bit, own[...].astype(f32), other[...].astype(f32))
    peak, inverse, context = merge(one, two, True)
    mine, _ = decode(first[...].astype(f32))
    scale_out[...] = jnp.exp(jnp.minimum(mine - peak, 0.0)) * inverse
    c32_out[...] = context
    low = context.astype(bf16)
    own_half(scal, low, c_s, c_out)
    h2 = h1[...] + nn(low, wo[...])
    h2_out[...] = h2
    n2, _ = rms_parts(h2)
    y3 = (n2 * row_of(g_ff)).astype(bf16)
    z = nn(y3, win[...])
    z_out[...] = z
    u = (z * phi(z)).astype(bf16)
    part_out[...] = nn(u, wdown[...]).astype(bf16)


def score_kernel(part_a, part_b, h2, g_final, row, c, pay_out, n3_out, dh3_out):
    h3 = h2[...] + (part_a[...].astype(f32) + part_b[...].astype(f32))
    n3, r3 = rms_parts(h3)
    n3_out[...] = n3
    wanted = jnp.broadcast_to(row_of(g_final) * row_of(row) * FACTOR, (8, D))
    scores = nt(wanted, n3, EXACT)[0:1]
    wide = jnp.concatenate([scores, jnp.zeros((1, LANES - n3.shape[0]), f32)], axis=1)
    pay_out[:, :D] = c[...]
    pay_out[:, D:] = stack3(wide, c.shape[0])
    dh3_out[...] = rms_back(wanted[0:1], n3, r3).astype(bf16)


def down_kernel(dh3, z, wdown, win, part_out):
    du = nt(dh3[...], wdown[...])
    dz = (du * gelu_slope(z[...])).astype(bf16)
    part_out[...] = nt(dz, win[...]).astype(bf16)


def target_kernel(order, scal, sizes, lens, rel, target_out, member_out, *picks_out):
    if picks_out:
        tile, held = picks_out[0].shape
        for out, pick in zip(picks_out, document_picks(order, tile, scal, sizes, held, 0)):
            out[...] = pick
    queries, docs = target_out.shape
    relevance = rel[...].reshape(1, docs)
    at = iota((queries, 1), 0)

    def one_list(j, found):
        begin, begins, ends = found
        end = begin + lens[j]
        return end, jnp.where(at == j, begin, begins), jnp.where(at == j, end, ends)

    none = jnp.zeros((queries, 1), i32)
    _, begins, ends = lax.fori_loop(
        0, queries, one_list, (jnp.int32(0), none, none), unroll=queries <= 32
    )
    place = iota((queries, docs), 1)
    member = (place >= begins) & (place < ends)
    weight = jnp.sum(jnp.where(member, relevance, 0.0), axis=1, keepdims=True)
    target_out[...] = jnp.where(member, relevance / weight, 0.0)
    member_out[...] = member.astype(f32)


def place_of(order, mask):
    pos = 0
    for k, bit in enumerate(order):
        pos = pos + (lax.shift_right_logical(mask, bit.bit_length() - 1) & 1) * (1 << k)
    return pos


def list_kernel(order, scal, sizes, rows, targets, members, scores_out, loss_out, ds_out, mine_out):
    groups = 1 << len(order)
    docs = ds_out.shape[1]
    wide = docs + LANES
    queries = targets.shape[0]
    half = rows.shape[0] // groups
    lane = iota((8, LANES), 1)
    blank = jnp.zeros((8, wide - LANES), f32)

    def one_group(g, found):
        start, placed = found
        at = pl.multiple_of(place_of(order, g ^ scal[1]) * half, half)
        parts = rows[pl.ds(at, ROWS), D:].astype(f32)
        score = (parts[0:1] + parts[1:2]) + parts[2:3]
        kept = jnp.where(lane < sizes[g], score, 0.0)
        kept = pltpu.roll(jnp.concatenate([kept, blank], axis=1), start, 1)
        return start + sizes[g], placed + kept

    _, placed = lax.fori_loop(
        0,
        groups,
        one_group,
        (jnp.int32(0), jnp.zeros((8, wide), f32)),
        unroll=groups <= 8,
    )
    values = placed[0:1, :docs]
    scores_out[...] = values.reshape(scores_out.shape)
    member = members[...] > 0.0
    target = targets[...]
    peak = jnp.max(jnp.where(member, values, MASKED), axis=1, keepdims=True)
    raised = jnp.where(member, jnp.exp(jnp.where(member, values - peak, 0.0)), 0.0)
    log_total = peak + jnp.log(jnp.sum(raised, axis=1, keepdims=True))
    picked = jnp.sum(target * values, axis=1, keepdims=True)
    loss_out[...] = jnp.sum(log_total - picked, axis=0, keepdims=True) / queries
    chance = jnp.where(member, jnp.exp(jnp.where(member, values - log_total, 0.0)), 0.0)
    ds = jnp.sum(chance - target, axis=0, keepdims=True) / queries
    ds_out[...] = ds
    ds = jnp.broadcast_to(jnp.concatenate([ds, jnp.zeros((1, LANES), f32)], axis=1), (8, wide))
    start = first_doc(scal, sizes)
    back = pltpu.roll(ds, lax.rem(wide - start, wide), 1)[:, :LANES]
    mine_out[...] = jnp.where(lane < sizes[scal[1]], back, 0.0)


def context_kernel(
    scal, part_a, part_b, h2, dh3, c32, g_ff, wout, wo_own,
    dh2_out, half_out, dc_out, own_out, inner_out, ff_out, both_s,
):
    n2, r2 = rms_parts(h2[...])
    dy3 = part_a[...].astype(f32) + part_b[...].astype(f32)
    ff_out[...] = dy3 * n2
    dh2 = (dh3[...].astype(f32) + rms_back(dy3 * row_of(g_ff), n2, r2)).astype(bf16)
    dh2_out[...] = dh2
    own_half(scal, jnp.concatenate([dh3[...], dh2], axis=1), both_s, half_out)
    dc = nt(dh2, wout[...]).astype(bf16)
    dc_out[...] = dc
    own_out[...] = nt(dh2, wo_own[...]).astype(bf16)
    hot = (head_of((D, LANES), 0) == iota((D, LANES), 1)).astype(bf16)
    high, low = split2(dc.astype(f32) * c32[...])
    inner_out[...] = nn(high, hot) + nn(low, hot)


def columns(one, two):
    tall = BLOCK * ROWS
    half = LANES // 2
    both = jnp.where(iota((BLOCK, LANES), 1) < half, one, pltpu.roll(two, half, 1))
    parts = jnp.concatenate(split3(both), axis=0)
    r, c = iota((tall, 3 * BLOCK), 0), iota((tall, 3 * BLOCK), 1)
    wide = nn((r // ROWS == c % BLOCK).astype(bf16), parts)
    lane, head = iota((tall, LANES), 1), iota((tall, LANES), 0) % ROWS
    return tuple(
        jnp.sum(jnp.where(lane == head + k * half, wide, 0.0), axis=1, keepdims=True)
        for k in range(2)
    )


def back_kernel(first, last, scal, sizes, enc, p, scale, inner, dc, wv, *refs):
    dap_out, vd_out = refs[-2:]
    tokens = enc.shape[1]
    tall = BLOCK * ROWS
    rounds = jnp.clip(rounds_of(scal, sizes), first, last)

    def one_block(step):
        block = pl.ds(pl.multiple_of(step * BLOCK, BLOCK), BLOCK)
        rows = enc[block].reshape(BLOCK * tokens, D)
        pick = (iota((tall, BLOCK), 0) // ROWS == iota((tall, BLOCK), 1)).astype(bf16)
        own = (iota((tall, D), 0) % ROWS) == head_of((tall, D), 1)
        grad = jnp.where(own, nn(pick, dc[block]), 0.0).astype(bf16)
        vd = nn(grad, wv[...]).astype(bf16)
        vd_out[block] = vd.reshape(BLOCK, ROWS, D)
        grad_probs = []
        for k in range(BLOCK // 2):
            pair = nt(
                vd[2 * ROWS * k : 2 * ROWS * (k + 1)],
                rows[2 * tokens * k : 2 * tokens * (k + 1)],
            )
            grad_probs += [pair[:ROWS, :tokens], pair[ROWS:, tokens:]]
        grad_probs = jnp.concatenate(grad_probs, axis=0)
        scale_col, inner_col = columns(scale[block], inner[block])
        prob = p[block].reshape(tall, tokens) * scale_col
        da = (prob * (grad_probs - inner_col)).astype(bf16)
        dap_out[block, :ROWS] = da.reshape(BLOCK, ROWS, tokens)
        dap_out[block, ROWS:] = prob.astype(bf16).reshape(BLOCK, ROWS, tokens)

    @pl.loop(first, rounds)
    def _(i):
        for j in range(SPAN // BLOCK):
            one_block(i * (SPAN // BLOCK) + j)

    @pl.loop(rounds, last)
    def _(i):
        span = pl.ds(pl.multiple_of(i * SPAN, SPAN), SPAN)
        dap_out[span] = jnp.zeros((SPAN, 2 * ROWS, tokens), bf16)
        vd_out[span] = jnp.zeros((SPAN, ROWS, D), bf16)


def key_sum_kernel(scal, sizes, ds, enc, dap, dh2, n3, ff, sums_out):
    tokens = enc.shape[1]
    tall = BLOCK * ROWS
    slots = dh2.shape[0]
    row = ds[...][:, :slots] * (1.0 / PARTS)
    at = iota((ROWS, D), 0)
    row = row[0:1]
    out = jnp.where(at == HEADS, jnp.sum(nn(stack3(row), dh2[...]), axis=0, keepdims=True), 0.0)
    out = jnp.where(at == HEADS + 1, row_dot(row, n3[...]), out)
    sums_out[...] = jnp.where(at == HEADS + 2, row_dot(row, ff[...]), out)

    def one_block(step):
        block = pl.ds(pl.multiple_of(step * BLOCK, BLOCK), BLOCK)
        own_slot = iota((tall, LANES), 1) == step * BLOCK + iota((tall, LANES), 0) // ROWS
        ds_col = jnp.sum(jnp.where(own_slot, ds[0:1], 0.0), axis=1, keepdims=True)
        scaled = (dap[block, :ROWS].reshape(tall, tokens).astype(f32) * ds_col).astype(bf16)
        flat = jnp.concatenate(
            [scaled[ROWS * b : ROWS * (b + 1)] for b in range(BLOCK)], axis=1
        )
        return nn(flat, enc[block].reshape(BLOCK * tokens, D))

    @pl.loop(0, rounds_of(scal, sizes))
    def _(i):
        per_round = SPAN // BLOCK
        total = one_block(i * per_round)
        for j in range(1, per_round):
            total = total + one_block(i * per_round + j)
        sums_out[...] += total


def enc_grad_kernel(first, last, ds, qa, qb, dap, vd, *refs):
    grad_out, held, sems = refs[-3:]
    qk = qa[...] + qb[...]
    lane = iota((1, LANES), 1)
    copies = []
    begin = first
    while begin < last:
        size = 4
        for b in range(begin, begin + size):
            scale = jnp.sum(jnp.where(lane == b, ds[0:1], 0.0), axis=1, keepdims=True)
            right = jnp.concatenate([qk, vd[b].astype(f32)], axis=0) * scale
            held[b - first] = tn(dap[b], right.astype(bf16)).astype(bf16)
        copies.append(
            pltpu.make_async_copy(
                held.at[pl.ds(begin - first, size)],
                grad_out.at[pl.ds(begin, size)],
                sems.at[len(copies)],
            )
        )
        copies[-1].start()
        begin += size
    for copy in copies:
        copy.wait()


def share_kernel(scal, summed, scale, keep_out, send_out):
    core = scal[0] & 1
    lane = iota(scale.shape, 1)
    for out, bit in ((send_out, 1 - core), (keep_out, core)):
        for y in range(out.shape[0]):
            for k in range(out.shape[1]):
                head = (2 * y + bit) * out.shape[1] + k
                col = jnp.sum(jnp.where(lane == head, scale[...], 0.0), axis=1, keepdims=True)
                out[y, k] = (summed[head].astype(f32) * col).astype(bf16)


def away_kernel(scal, keep, got, out):
    part = 1 - (lax.shift_right_logical(scal[0], 1) & 1)
    for h in range(out.shape[0]):
        out[h] = (keep[part, h].astype(f32) + got[part, h].astype(f32)).astype(bf16)


def value_kernel(scal, keep, got, other, dc, ds, grad_out):
    slots = keep.shape[2]
    part = lax.shift_right_logical(scal[0], 1) & 1
    own_slot = iota((slots, LANES), 0) == iota((slots, LANES), 1)
    ds_col = jnp.sum(jnp.where(own_slot, ds[0:1], 0.0), axis=1, keepdims=True)
    grad = (dc[...].astype(f32) * ds_col).astype(bf16)
    for h in range(keep.shape[1]):
        pair = (keep[part, h].astype(f32) + got[part, h].astype(f32)).astype(bf16)
        summed = (pair.astype(f32) + other[h].astype(f32)).astype(bf16)
        out = tn(grad[:, h * HEAD_DIM : (h + 1) * HEAD_DIM], summed)
        grad_out[h * HEAD_DIM : (h + 1) * HEAD_DIM] = out.astype(bf16)


def document_picks(order, tile, scal, sizes, held, first):
    groups = 1 << len(order)
    half = held // groups
    core = scal[0] & 1
    doc = first + iota((tile, 1), 0)

    def one_group(g, found):
        start, at, upper = found
        pos = place_of(order, g ^ scal[1])
        slot = doc - start
        inside = (slot >= 0) & (slot < sizes[g])
        later = (slot >= half).astype(i32)
        at = jnp.where(inside, pos * half + slot - half * later, at)
        return start + sizes[g], at, jnp.where(inside, later, upper)

    zero = jnp.zeros((tile, 1), i32)
    _, at, upper = lax.fori_loop(
        0, groups, one_group, (jnp.int32(0), zero, zero), unroll=groups <= 8
    )
    hit = iota((tile, held), 1) == at
    return (hit & (upper == core)).astype(bf16), (hit & (upper != core)).astype(bf16)


def in_order(picks, own, other, width):
    mine, theirs = picks
    return (nn(mine, own[:, :width]) + nn(theirs, other[:, :width])).astype(bf16)


def picks_of(order, tile, scal, sizes, held, first, ready):
    if ready:
        return tuple(pick[...] for pick in ready)
    return document_picks(order, tile, scal, sizes, held, first)


def ds_column(ds, first, tile):
    eye = iota((tile, tile), 0) == iota((tile, tile), 1)
    return jnp.sum(jnp.where(eye, ds[0:1, pl.ds(first, tile)], 0.0), axis=1, keepdims=True)


def over_tiles(docs, tile, one_tile):
    one_tile(0, True)
    if docs > tile:

        @pl.loop(1, docs // tile)
        def _(t):
            one_tile(pl.multiple_of(t * tile, tile), False)


def put(out, value, new):
    if new:
        out[...] = value
    else:
        out[...] += value


def weights_before_kernel(
    order, tile, scal, sizes, c_own, c_other, h1, g_ff, wout, win, *refs
):
    ready, (y3_out, u_out, slope_out, c_out) = refs[:-4], refs[-4:]

    def one_tile(first, new):
        here = pl.ds(first, tile)
        picks = picks_of(order, tile, scal, sizes, c_own.shape[0], first, ready)
        c = in_order(picks, c_own, c_other, D)
        h2 = h1[...] + nn(c, wout[...])
        n2, _ = rms_parts(h2)
        y3 = (n2 * row_of(g_ff)).astype(bf16)
        y3_out[here] = y3
        z = nn(y3, win[...])
        u_out[here] = (z * phi(z)).astype(bf16)
        slope_out[here] = gelu_slope(z)
        width = c_out.shape[1]
        pick = (iota((D, width), 0) == scal[0] * width + iota((D, width), 1)).astype(bf16)
        c_out[here] = nn(c, pick).astype(bf16)

    over_tiles(y3_out.shape[0], tile, one_tile)


def grads_kernel(order, tile, scal, sizes, slope, both_own, both_other, ds, wdown, *refs):
    ready, (dz_out, both_out) = refs[:-2], refs[-2:]

    def one_tile(first, new):
        here = pl.ds(first, tile)
        picks = picks_of(order, tile, scal, sizes, both_own.shape[0], first, ready)
        both = in_order(picks, both_own, both_other, 2 * D).astype(f32)
        both = (both * ds_column(ds, first, tile)).astype(bf16)
        both_out[here] = both
        dz_out[here] = (nt(both[:, :D], wdown[...]) * slope[here]).astype(bf16)

    over_tiles(ds.shape[1], tile, one_tile)


def outer_kernel(
    tile, y3, dz, u, c, both, left1, right1, left2, right2,
    win_out, wdown_out, wout_out, key_out, query_out, wos_out, wvs_out,
    win_s, wdown_s, wout_s, key_s, query_s, wos_s, wvs_s, sems,
):
    copies = []

    def leave(held, out):
        copies.append(pltpu.make_async_copy(held, out, sems.at[len(copies)]))
        copies[-1].start()

    docs = y3.shape[0]

    def total(held, left, right):
        held[...] = tn(left[:tile], right[:tile])
        if docs > tile:

            @pl.loop(1, docs // tile)
            def _(t):
                here = pl.ds(pl.multiple_of(t * tile, tile), tile)
                held[...] += tn(left[here], right[here])

    def by_parts(held, out, left, right):
        for k in range(held.shape[0] // COLUMNS):
            part = pl.ds(k * COLUMNS, COLUMNS)
            total(held.at[part], left.at[:, part], right)
            leave(held.at[part], out.at[part])

    key_s[...] = tn(left1[: 2 * ROWS], right1[: 2 * ROWS])
    leave(key_s, key_out)
    query_s[...] = tn(left1[2 * ROWS :], right1[2 * ROWS :])
    leave(query_s, query_out)
    wos_s[...] = tn(left2[:ROWS], right2[:ROWS])
    leave(wos_s, wos_out)
    wvs_s[...] = tn(left2[ROWS:], right2[ROWS:])
    leave(wvs_s, wvs_out)
    total(wout_s, c, both.at[:, D:])
    leave(wout_s, wout_out)
    by_parts(win_s, win_out, y3, dz)
    by_parts(wdown_s, wdown_out, u, both.at[:, :D])
    for copy in copies:
        copy.wait()


def key_kernel(scal, sum_a, sum_b, h1, g_cross, wk, wq, part_out, left_out, right_out):
    y2, qm = query_parts(scal, h1, g_cross, wq)
    g = sum_a[...] + sum_b[...]
    g = jnp.where(iota((ROWS, D), 0) < HEADS, g, 0.0)
    high, low = split2(g)
    both = jnp.concatenate([high, low], axis=0)
    dq = nt(both, wk[...])
    dq = dq[:ROWS] + dq[ROWS:]
    width = dq.shape[1]
    first = scal[0] * (width // HEAD_DIM)
    own = iota((ROWS, width), 0) == first + head_of((ROWS, width), 1)
    dq = jnp.sum(jnp.where(own, dq, 0.0), axis=0, keepdims=True)
    dq_parts = stack3(dq)
    left_out[...] = jnp.concatenate([qm, qm, dq_parts], axis=0)
    right_out[...] = jnp.concatenate([both, repeat3(y2[0:1])], axis=0)
    part = jnp.sum(nn(dq_parts, wq[...]), axis=0, keepdims=True)
    part_out[...] = jnp.broadcast_to(part, (8, D))


def hidden_kernel(
    part_a, part_b, sum_a, sum_b, h1, g_cross, start, g_self, wos, wvs, g_final, row,
    dh1_out, part_out, left_out, right_out, cross_out, final_out, row_out, ff_out,
):
    y1, s1 = self_parts(start, g_self, wvs)
    dy2 = part_a[0:1] + part_b[0:1]
    sums = sum_a[...] + sum_b[...]
    n1, r1 = rms_parts(h1[...])
    cross_out[...] = (dy2 * n1).reshape(cross_out.shape)
    dh1 = sums[HEADS : HEADS + 1] + rms_back(dy2 * row_of(g_cross), n1, r1)
    dh1_out[...] = dh1
    dh1_parts = stack3(dh1)
    ds1 = jnp.sum(nt(dh1_parts, wos[...]), axis=0, keepdims=True)
    ds1_parts = stack3(ds1)
    left_out[...] = jnp.concatenate([repeat3(s1[0:1]), ds1_parts], axis=0)
    right_out[...] = jnp.concatenate([dh1_parts, repeat3(y1[0:1])], axis=0)
    part = jnp.sum(nn(ds1_parts, wvs[...]), axis=0, keepdims=True)
    part_out[...] = jnp.broadcast_to(part, (8, D))
    total = sums[HEADS + 1 : HEADS + 2] * FACTOR
    final_out[...] = (total * row_of(row)).reshape(final_out.shape)
    row_out[...] = (total * row_of(g_final)).reshape(row_out.shape)
    ff_out[...] = sums[HEADS + 2 : HEADS + 3].reshape(ff_out.shape)


def start_kernel(
    part_a, part_b, dh1, start, g_self, value_a, value_b, gain_out, start_out, value_out
):
    value_out[...] = value_a[...].astype(f32) + value_b[...].astype(f32)
    dy1 = part_a[0:1] + part_b[0:1]
    n0, r0 = rms_parts(row_of(start))
    gain_out[...] = (dy1 * n0).reshape(gain_out.shape)
    back = dh1[...] + rms_back(dy1 * row_of(g_self), n0, r0)
    start_out[...] = back.reshape(start_out.shape)


def shape(dims, dtype=f32):
    return jax.ShapeDtypeStruct(dims, dtype)


def whole_spec(memory=pltpu.VMEM):
    return pl.BlockSpec(memory_space=memory)


def name_of(kernel):
    return getattr(kernel, "func", kernel).__name__


def in_hbm(x):
    return pltpu.with_memory_space_constraint(x, pltpu.HBM)


def plain(
    kernel, outs, *args, smem=0, hbm=(), hbm_out=False, onto=None, limit=12, scratch=()
):
    spaces = [pltpu.SMEM] * smem + [pltpu.VMEM] * (len(args) - smem)
    for k in hbm:
        spaces[k] = pltpu.HBM
    out_space = pltpu.HBM if hbm_out else pltpu.VMEM
    return pl.pallas_call(
        kernel,
        out_shape=outs,
        in_specs=[whole_spec(space) for space in spaces],
        out_specs=[whole_spec(out_space) for _ in outs]
        if isinstance(outs, list)
        else whole_spec(out_space),
        scratch_shapes=list(scratch),
        input_output_aliases=onto or {},
        compiler_params=pltpu.CompilerParams(vmem_limit_bytes=limit * MIB),
        cost_estimate=pl.CostEstimate(flops=0, bytes_accessed=0, transcendentals=0),
        name=name_of(kernel),
    )(*args)


def bits_of(size):
    return [1 << b for b in range(size.bit_length() - 1)]


def far_first(size):
    return bits_of(size)[::-1]


def swap(x, axis, bit):
    size = lax.axis_size(axis)
    return lax.ppermute(x, axis, [(i, i ^ bit) for i in range(size)])


def after(x, *deps):
    return lax.optimization_barrier((x, *deps))[0]


def add(x, y):
    return (x.astype(f32) + y.astype(f32)).astype(x.dtype)


def sum_last(x, steps):
    for axis, bit in steps[:-1]:
        x = add(x, swap(x, axis, bit))
    axis, bit = steps[-1]
    return x, swap(x, axis, bit)


def per_device(
    enc_out,
    enc_len,
    group_docs,
    list_len,
    relevance,
    start_token,
    score_row,
    g_self,
    w_value_self,
    w_out_self,
    g_cross,
    w_query,
    w_key,
    w_value,
    w_out,
    g_ff,
    w_in,
    w_down,
    g_final,
):
    groups = lax.axis_size("docs")
    parts = lax.axis_size("heads")
    assert parts == PARTS
    me_g = lax.axis_index("docs")
    me_j = lax.axis_index("heads")
    slots, tokens = enc_out.shape[:2]
    docs = enc_len.shape[0]
    width = w_value.shape[1]
    own_heads = HEADS // parts
    hidden = w_in.shape[1]
    over_heads = [("heads", 1), ("heads", 2)]
    order = far_first(groups)
    over_docs = [("docs", bit) for bit in order]

    scal = jnp.stack([me_j, me_g])
    wvs_t, wq_t, wk_t, wv_t = (w.T for w in (w_value_self, w_query, w_key, w_value))

    wv_by1, wo_by1 = swap(wv_t, "heads", 1), swap(w_out, "heads", 1)

    part = plain(
        self_kernel,
        shape((8, D)),
        *map(in_hbm, (start_token, g_self, wvs_t, w_out_self)),
    )


    def load(first, last, since, *onto):
        return pl.pallas_call(
            functools.partial(load_kernel, first, last),
            out_shape=pltpu.VMEM(enc_out.shape, bf16),
            in_specs=[whole_spec(pltpu.HBM), whole_spec(pl.ANY), whole_spec(pltpu.SMEM)]
            + [whole_spec()] * len(onto),
            out_specs=whole_spec(),
            scratch_shapes=[pltpu.SemaphoreType.DMA((last - first,))],
            input_output_aliases={3: 0} if onto else {},
            compiler_params=pltpu.CompilerParams(vmem_limit_bytes=MIB),
            cost_estimate=pl.CostEstimate(flops=0, bytes_accessed=0, transcendentals=0),
            name="load_kernel",
        )(in_hbm(enc_out), since, scal, *onto)

    part = add(part, swap(part, "heads", 1))
    part_a, part_b = part, swap(part, "heads", 2)
    held = load(0, 1, part)
    part_b, held = lax.optimization_barrier((part_b, held))
    wv_by2 = swap(after(wv_t, part_b), "heads", 2)
    qk, h1 = plain(
        query_kernel,
        [shape((ROWS, D)), shape((1, D))],
        scal,
        part_a,
        part_b,
        *map(in_hbm, (start_token, g_cross, wq_t, wk_t)),
        smem=1,
    )
    qk = add(qk, swap(qk, "heads", 1))
    qk, held = lax.optimization_barrier((qk, held))
    qk_a, qk_b = qk, swap(qk, "heads", 2)
    held = load(1, 3, qk, held)
    qk_b, held, wv_by2 = lax.optimization_barrier((qk_b, held, wv_by2))
    wv_by3 = swap(wv_by2, "heads", 1)

    wo_by2 = swap(after(w_out, qk_b), "heads", 2)
    held, prob, summed, extra = plain(
        functools.partial(attend_kernel, 3),
        [
            pltpu.VMEM(enc_out.shape, bf16),
            pltpu.VMEM((slots, ROWS, tokens), f32),
            pltpu.VMEM((PANELS, slots * ROWS, LANES), f32),
            shape((slots, LANES), bf16),
        ],
        scal,
        group_docs,
        enc_len,
        qk_a,
        qk_b,
        in_hbm(enc_out),
        held,
        smem=3,
        hbm=(5,),
        onto={6: 0},
        scratch=[pltpu.VMEM((2 * ROWS, D), bf16), pltpu.SemaphoreType.DMA((slots // BLOCK,))],
        limit=16,
    )
    summed, wv_by3, wo_by2 = lax.optimization_barrier((summed, wv_by3, wo_by2))
    wv_parts = (wv_t, wv_by2, wv_by1, wv_by3)
    wo_parts = (w_out, wo_by2, wo_by1, swap(wo_by2, "heads", 1))
    pay, summed, wv_full = plain(
        project_kernel,
        [
            shape((slots, D + LANES), bf16),
            shape((HEADS, slots, D), bf16),
            shape((D, D), bf16),
        ],
        scal,
        summed,
        extra,
        *wv_parts,
        smem=1,
    )
    merged = plain(
        merge_kernel, shape(pay.shape, bf16), scal, pay, swap(pay, "heads", 1), smem=1
    )
    other = swap(merged, "heads", 2)
    wo_full = plain(arrange_kernel, shape((D, D), bf16), scal, *wo_parts, smem=1)
    tile = 384
    held_rows = groups * slots // 2
    picks_shape = [shape((tile, held_rows), bf16)] * 2 if docs == tile else []
    target, member, *picks = plain(
        functools.partial(target_kernel, order),
        [shape((list_len.shape[0], docs))] * 2 + picks_shape,
        scal,
        group_docs,
        list_len,
        relevance,
        smem=3,
    )
    other, wo_full, target, member, *picks = lax.optimization_barrier(
        (other, wo_full, target, member, *picks)
    )

    c, c32, scale, h2, z, part = plain(
        forward_kernel,
        [
            shape((slots // 2, D), bf16),
            shape((slots, D)),
            shape((slots, LANES)),
            shape((slots, D)),
            shape((slots, hidden)),
            shape((slots, D), bf16),
        ],
        scal,
        merged,
        other,
        pay,
        h1,
        wo_full,
        g_ff,
        w_in,
        w_down,
        smem=1,
        scratch=[pltpu.VMEM((slots, D), bf16)],
    )

    half = slots // 2

    def grow(x, k):
        return jnp.concatenate([x, swap(x, *over_docs[k])], axis=0)

    def tie(*xs):
        return lax.optimization_barrier(xs)

    last = len(over_docs) - 1
    near_first = over_docs[::-1]
    part = add(part, swap(part, "heads", 1))
    part_a, part_b = part, swap(part, "heads", 2)
    keep, sent = plain(
        share_kernel, [shape((2, own_heads, slots, D), bf16)] * 2, scal, summed, scale, smem=1
    )
    part_b, keep, sent = tie(part_b, keep, sent)
    c_all, n3, dh3 = plain(
        score_kernel,
        [shape((half, D + LANES), bf16), shape((slots, D)), shape((slots, D), bf16)],
        part_a,
        part_b,
        h2,
        g_final,
        score_row,
        c,
    )
    part = plain(down_kernel, shape((slots, D), bf16), dh3, z, w_down, w_in)
    part = add(part, swap(part, "heads", 1))
    part_a, part_b = part, swap(part, "heads", 2)
    c_far = swap(c_all, *over_docs[0])
    got = swap(sent, "heads", 1)
    away = plain(
        away_kernel, shape((own_heads, slots, D), bf16), scal, keep, got, smem=1
    )
    part_b, away = tie(part_b, away)
    dh2, grads, dc, dc_own, inner, ff = plain(
        context_kernel,
        [
            shape((slots, D), bf16),
            shape((half, 2 * D), bf16),
            shape((slots, D), bf16),
            shape((slots, width), bf16),
            shape((slots, LANES)),
            shape((slots, D)),
        ],
        scal,
        part_a,
        part_b,
        h2,
        dh3,
        c32,
        g_ff,
        wo_full,
        w_out,
        smem=1,
        scratch=[pltpu.VMEM((slots, 2 * D), bf16)],
    )

    c_all, c_far, dc, grads = tie(c_all, c_far, dc, grads)
    c_all = jnp.concatenate([c_all, c_far], axis=0)
    for k in range(1, last):
        c_far = swap(c_all, *over_docs[k])
        if k < last - 1:
            c_all = jnp.concatenate([c_all, c_far], axis=0)
    grads_far = swap(grads, *over_docs[0])

    outs = [
        pltpu.VMEM((slots, 2 * ROWS, tokens), bf16),
        pltpu.VMEM((slots, ROWS, D), bf16),
    ]
    rounds = slots // SPAN
    inputs = (scal, group_docs, held, prob, scale, inner, dc, wv_full)

    def back(first, last, *onto):
        return plain(
            functools.partial(back_kernel, first, last),
            outs,
            *inputs,
            *onto,
            smem=2,
            onto={8: 0, 9: 1} if onto else None,
            limit=16,
        )

    dap, vd = back(0, 1)
    dap, away = tie(dap, away)
    other = swap(away, "heads", 2)
    dap, c_far = tie(dap, c_far)
    c_all = jnp.concatenate([c_all, c_far], axis=0)
    c_far = swap(c_all, *over_docs[last])
    dap, vd = back(1, rounds, dap, vd)
    dap, c_far, other, grads_far = tie(dap, c_far, other, grads_far)
    grads = jnp.concatenate([grads, grads_far], axis=0)
    for m in range(1, last):
        grads_far = swap(grads, *over_docs[m])
        if m < last - 1:
            grads = jnp.concatenate([grads, grads_far], axis=0)
    c_all = jnp.concatenate([c_all, c_far], axis=0)
    all_scores, loss, ds_docs, ds_mine = plain(
        functools.partial(list_kernel, order),
        [shape((docs,)), shape((1, 1)), shape((1, docs)), shape((8, LANES))],
        scal,
        group_docs,
        c_all,
        target,
        member,
        smem=2,
    )
    sums = plain(
        key_sum_kernel,
        shape((ROWS, D)),
        scal,
        group_docs,
        ds_mine,
        held,
        dap,
        dh2,
        n3,
        ff,
        smem=2,
    )

    def enc_grads(first, last, grads=None):
        outs = pltpu.HBM(enc_out.shape, bf16)
        args = (ds_mine, qk_a, qk_b, dap, vd)
        return plain(
            functools.partial(enc_grad_kernel, first, last),
            outs,
            *args,
            *([] if grads is None else [grads]),
            hbm=() if grads is None else (len(args),),
            hbm_out=True,
            onto={} if grads is None else {len(args): 0},
            scratch=[pltpu.VMEM((last - first, tokens, D), bf16), pltpu.SemaphoreType.DMA((8,))],
            limit=16,
        )

    sums, dc_own = tie(sums, dc_own)
    value_part = plain(
        value_kernel,
        shape((width, D), bf16),
        scal,
        keep,
        got,
        other,
        dc_own,
        ds_mine,
        smem=1,
    )
    value_far = swap(value_part, *near_first[0])
    c_far = swap(c_all, "heads", 1)
    sums = add(sums, swap(sums, "heads", 1))
    steps = near_first[:0:-1] + over_heads[1:] + near_first[:1]
    sums, grads_far = tie(sums, grads_far)
    grads = jnp.concatenate([grads, grads_far], axis=0)
    grads_far = swap(grads, *over_docs[last])
    enc_grad = None
    third = slots // 3
    sum_a = sums
    for k, step in enumerate(steps):
        ds_mine, sum_a = tie(ds_mine, sum_a)
        sum_b = swap(sum_a, *step)
        if k < 3:
            enc_grad = enc_grads(k * third, (k + 1) * third, enc_grad)
            sum_b, enc_grad = tie(sum_b, enc_grad)
        if k == 1:
            sum_b, value_far, c_far = tie(sum_b, value_far, c_far)
            for step in near_first[1:-1]:
                value_part = add(value_part, value_far)
                value_far = swap(value_part, *step)
        if k < len(steps) - 1:
            sum_a = sum_a + sum_b
    y3, u, slope, c_own = plain(
        functools.partial(weights_before_kernel, order, tile),
        [
            shape((docs, D), bf16),
            shape((docs, hidden), bf16),
            shape((docs, hidden)),
            shape((docs, width), bf16),
        ],
        scal,
        group_docs,
        c_all,
        c_far,
        h1,
        g_ff,
        wo_full,
        w_in,
        *picks,
        smem=2,
        limit=60 if docs > 384 else 16,
    )
    sum_b, grads_far, value_far, y3, u, slope, c_own = tie(
        sum_b, grads_far, value_far, y3, u, slope, c_own
    )
    value_part = add(value_part, value_far)
    value_far = swap(value_part, *near_first[-1])
    grads = jnp.concatenate([grads, grads_far], axis=0)
    grads_far = swap(grads, "heads", 1)

    part, left1, right1 = plain(
        key_kernel,
        [shape((8, D)), shape((3 * ROWS, width), bf16), shape((3 * ROWS, D), bf16)],
        scal,
        sum_a,
        sum_b,
        h1,
        g_cross,
        wk_t,
        wq_t,
        smem=1,
    )
    part = add(part, swap(part, "heads", 1))
    part, grads_far = tie(part, grads_far)
    part_a, part_b = part, swap(part, "heads", 2)
    dz, both = plain(
        functools.partial(grads_kernel, order, tile),
        [shape((docs, hidden), bf16), shape((docs, 2 * D), bf16)],
        scal,
        group_docs,
        slope,
        grads,
        grads_far,
        ds_docs,
        w_down,
        *picks,
        smem=2,
        limit=60 if docs > 384 else 16,
    )
    part_b, dz, both = tie(part_b, dz, both)
    dh1, part, left2, right2, cross, final_gain, row_grad, ff_gain = plain(
        hidden_kernel,
        [
            shape((1, D)),
            shape((8, D)),
            shape((2 * ROWS, width), bf16),
            shape((2 * ROWS, D), bf16),
        ]
        + [shape((D,))] * 4,
        part_a,
        part_b,
        sum_a,
        sum_b,
        h1,
        g_cross,
        start_token,
        g_self,
        w_out_self,
        wvs_t,
        g_final,
        score_row,
    )
    part_a, part_b = sum_last(part, over_heads)
    dims = [(D, hidden), (hidden, D), (width, D)] + [(width, D)] * 4
    w_in_grad, w_down_grad, w_out_grad, key_grad, query_grad, wos_grad, wvs_grad = plain(
        functools.partial(outer_kernel, tile),
        [pltpu.HBM(dim, f32) for dim in dims],
        y3,
        dz,
        u,
        c_own,
        both,
        left1,
        right1,
        left2,
        right2,
        hbm_out=True,
        scratch=[pltpu.VMEM(dim, f32) for dim in dims] + [pltpu.SemaphoreType.DMA((16,))],
        limit=60 if docs > 384 else 24,
    )
    part_b, w_down_grad, value_far = tie(part_b, w_down_grad, value_far)
    self_gain, start_grad, value_grad = plain(
        start_kernel,
        [shape((D,)), shape((D,)), shape((width, D))],
        part_a,
        part_b,
        dh1,
        start_token,
        g_self,
        value_part,
        value_far,
    )

    return (
        all_scores,
        loss.reshape(()),
        enc_grad,
        start_grad,
        row_grad,
        self_gain,
        wvs_grad.T,
        wos_grad,
        cross,
        query_grad.T,
        key_grad.T,
        value_grad.T,
        w_out_grad,
        ff_gain,
        w_in_grad,
        w_down_grad,
        final_gain,
    )


def solution(mesh):
    placed = (
        P("docs", "heads", None),
        P(),
        P(),
        P(),
        P(),
        P(),
        P(),
        P(),
        P(None, "heads"),
        P("heads", None),
        P(),
        P(None, "heads"),
        P(None, "heads"),
        P(None, "heads"),
        P("heads", None),
        P(),
        P(None, "heads"),
        P("heads", None),
        P(),
    )
    return jax.shard_map(
        per_device,
        mesh=mesh,
        in_specs=placed,
        out_specs=(
            P(),
            P(),
            P("docs", "heads", None),
            P(),
            P(),
            P(),
            P(None, "heads"),
            P("heads", None),
            P(),
            P(None, "heads"),
            P(None, "heads"),
            P(None, "heads"),
            P("heads", None),
            P(),
            P(None, "heads"),
            P("heads", None),
            P(),
        ),
        check_vma=False,
    )
```
